32 devices in a mesh: rep: 4 (over x, core), shard: 8 (over z, y).
Axes of the slice: x: 2, y: 2, z: 4, core: 2. Of those that a mesh axis runs over, the one named last changes fastest.
Arguments:
- tokens: bfloat16 [8, 4, 1024, 768], P('shard', 'rep'), may hold values from -6 to 6
- cotangent: bfloat16 [8, 4, 1024, 768], P('shard', 'rep'), may hold values from -6 to 6
- teacher: bfloat16 [8, 4, 1024, 768], P('shard', 'rep'), may hold values from -20 to 20
- valid_mask: int32 [8, 4, 1024], P('shard', 'rep'), may hold values 0 or 1
- valid_count: int32 [], replicated, may hold values from 16384 to 32767
- query_weight: bfloat16 [768, 768], P('shard'), may hold values from -0.3125 to 0.3125
- query_bias: bfloat16 [768], P('shard'), may hold values from -0.8984375 to 0.8984375
- key_weight: bfloat16 [768, 768], P('shard'), may hold values from -0.21875 to 0.21875
- value_weight: bfloat16 [768, 768], P('shard'), may hold values from -0.21875 to 0.21875
- value_bias: bfloat16 [768], P('shard'), may hold values from -0.29882812 to 0.29882812
- attn_weight: bfloat16 [768, 768], P('shard'), may hold values from -2.5 to 2.5
- attn_bias: bfloat16 [768], P('shard'), may hold values from -0.59765625 to 0.59765625
- first_gain: bfloat16 [768], P('shard'), may hold values from 0.5 to 1.5
- first_shift: bfloat16 [768], P('shard'), may hold values from -0.59765625 to 0.59765625
- up_weight: bfloat16 [768, 3072], P('shard'), may hold values from -0.21875 to 0.21875
- up_bias: bfloat16 [3072], P('shard'), may hold values from -0.59765625 to 0.59765625
- down_weight: bfloat16 [3072, 768], P('shard'), may hold values from -0.109375 to 0.109375
- down_bias: bfloat16 [768], P('shard'), may hold values from -0.59765625 to 0.59765625
- second_gain: bfloat16 [768], P('shard'), may hold values from 0.5 to 1.5
- second_shift: bfloat16 [768], P('shard'), may hold values from -0.59765625 to 0.59765625
Outputs:
- layer_out: bfloat16 [8, 4, 1024, 768], P('shard', 'rep')
- loss_value: float32 [], replicated
- tokens_grad: bfloat16 [8, 4, 1024, 768], P('shard', 'rep')
- query_weight_grad: float32 [768, 768], P('shard')
- query_bias_grad: float32 [768], P('shard')
- key_weight_grad: float32 [768, 768], P('shard')
- value_weight_grad: float32 [768, 768], P('shard')
- value_bias_grad: float32 [768], P('shard')
- attn_weight_grad: float32 [768, 768], P('shard')
- attn_bias_grad: float32 [768], P('shard')
- first_gain_grad: float32 [768], P('shard')
- first_shift_grad: float32 [768], P('shard')
- up_weight_grad: float32 [768, 3072], P('shard')
- up_bias_grad: float32 [3072], P('shard')
- down_weight_grad: float32 [3072, 768], P('shard')
- down_bias_grad: float32 [768], P('shard')
- second_gain_grad: float32 [768], P('shard')
- second_shift_grad: float32 [768], P('shard')
The draws below stay inside these ranges and needn't reach their ends.
All inputs are finite; a program needn't handle non-finite values. No bound on the sum of `valid_mask` on one device may be relied on, other than what follows from the above.
Results may differ from the reference program's by a relative error of at most 0.019.
Values may be sent and summed in bfloat16 or wider, within the bound.
A program may use at most 192 MiB of HBM per device.

```python
import math
import jax
import jax.numpy as jnp
from jax import lax

D = 768
HEADS = 12
HDIM = 64
FF = 3072
PPIECE = 512
CLEN = 256
MEMBERS = 4
GROUPS = 8
TOK_DEV = 1024
KEYS = 2560
TOKENS = 32768


def draw_teacher(key, part):
    shape = (GROUPS, MEMBERS, TOK_DEV, D)
    places = jnp.arange(GROUPS * MEMBERS, dtype=jnp.float32).reshape(GROUPS, MEMBERS, 1, 1) / max(GROUPS * MEMBERS - 1, 1)
    level = jax.random.uniform(jax.random.fold_in(key, 7), (), jnp.float32, -0.5, 0.5)
    base = jax.random.truncated_normal(key, -4.0, 4.0, shape, jnp.float32)
    factor = (1.0 + 2.0 * places) * jnp.exp(level)
    return (base * factor).astype(jnp.bfloat16)


def touch_ends(entries, rng, smallest, high):
    dims = entries.shape
    index_at = [jax.random.randint(jax.random.fold_in(rng, axis), (), 0, dims[axis]) for axis in range(len(dims))]
    entries = entries.at[tuple(index_at)].set(smallest)
    longest = dims.index(max(dims))
    index_at[longest] = (index_at[longest] + 1) % dims[longest]
    return entries.at[tuple(index_at)].set(high)


def block_levels(rng, extent, split, low, high):
    level = 1.0
    for axis_at, parts in split:
        heights = jax.random.uniform(jax.random.fold_in(jax.random.fold_in(rng, 6), axis_at), (parts,), jnp.float32, low / len(split), high / len(split))
        level = level * jnp.repeat(jnp.exp(heights), extent[axis_at] // parts).reshape((-1,) + (1,) * (len(extent) - 1 - axis_at))
    return level


def noise(own_key, dims, width, bound, cuts=(), kind=jnp.bfloat16):
    gain = block_levels(own_key, dims, cuts, -0.22, 0.18) if cuts else 1.0
    array = jax.random.normal(own_key, dims, jnp.float32) * width * gain
    return jnp.minimum(jnp.maximum(array, -bound), bound).astype(kind)


def setup_inputs(seed: int = 0) -> dict:
    splits = jax.random.split(jax.random.key(seed), 21)
    tokens = noise(splits[0], (GROUPS, MEMBERS, TOK_DEV, D), 1.0, 6.0, ((0, 8), (1, 4)))
    cotangent = noise(splits[1], (GROUPS, MEMBERS, TOK_DEV, D), 1.0, 6.0, ((0, 8), (1, 4)))
    teacher = draw_teacher(jax.random.fold_in(splits[20], 71), 0)
    valid_mask = touch_ends((jax.random.randint(splits[3], (GROUPS, MEMBERS, TOK_DEV), 0, 4) < 3).astype(jnp.int32), jax.random.fold_in(splits[3], 1), 0, 1)
    valid_count = jax.random.randint(splits[4], (), TOKENS // 2, TOKENS).astype(jnp.int32)
    query_weight = noise(splits[5], (D, D), (D // 2) ** -0.5, 0.3125, ((0, 8),))
    query_bias = noise(splits[6], (D,), 0.15, 0.8984375, ((0, 8),))
    key_weight = noise(splits[7], (D, D), D ** -0.5, 0.21875, ((0, 8),))
    value_weight = noise(splits[8], (D, D), D ** -0.5, 0.21875, ((0, 8),))
    value_bias = noise(splits[9], (D,), 0.05, 0.29882812, ((0, 8),))
    attn_weight = noise(splits[10], (D, D), (max(D // 128, 2)) ** -0.5, 2.5, ((0, 8),))
    attn_bias = noise(splits[11], (D,), 0.1, 0.59765625, ((0, 8),))
    first_gain = jnp.clip(1.0 + 0.1 * jax.random.normal(splits[12], (D,), jnp.float32), 0.5, 1.5).astype(jnp.bfloat16)
    first_shift = noise(splits[13], (D,), 0.1, 0.59765625, ((0, 8),))
    up_weight = noise(splits[14], (D, FF), D ** -0.5, 0.21875, ((0, 8),))
    up_bias = noise(splits[15], (FF,), 0.1, 0.59765625, ((0, 8),))
    down_weight = noise(splits[16], (FF, D), FF ** -0.5, 0.109375, ((0, 8),))
    down_bias = noise(splits[17], (D,), 0.1, 0.59765625, ((0, 8),))
    second_gain = jnp.clip(1.0 + 0.1 * jax.random.normal(splits[18], (D,), jnp.float32), 0.5, 1.5).astype(jnp.bfloat16)
    second_shift = noise(splits[19], (D,), 0.1, 0.59765625, ((0, 8),))
    return {"tokens": tokens, "cotangent": cotangent, "teacher": teacher, "valid_mask": valid_mask, "valid_count": valid_count, "query_weight": query_weight, "query_bias": query_bias, "key_weight": key_weight, "value_weight": value_weight, "value_bias": value_bias, "attn_weight": attn_weight, "attn_bias": attn_bias, "first_gain": first_gain, "first_shift": first_shift, "up_weight": up_weight, "up_bias": up_bias, "down_weight": down_weight, "down_bias": down_bias, "second_gain": second_gain, "second_shift": second_shift}


@jax.custom_vjp
def low(v):
    return lax.optimization_barrier(v.astype(jnp.bfloat16)).astype(jnp.float32)

@jax.custom_vjp
def low_back(v):
    return v

def low_keep(v):
    return (low(v), None)

def low_pass(kept, grad):
    return (grad,)

def back_keep(v):
    return (v, None)

def back_low(kept, grad):
    return (low(grad),)
low.defvjp(low_keep, low_pass)
low_back.defvjp(back_keep, back_low)
HIGHEST = lax.Precision.HIGHEST
EPSILON = 1e-05
NEGATIVE = -1e+30

def matmul(left_matrix, right_matrix):
    return jnp.dot(left_matrix, right_matrix, precision=HIGHEST, preferred_element_type=jnp.float32)

def both_ways(values):
    return low(low_back(values))

def layer_norm(values, norm_gain, norm_shift):
    centered = values - lax.optimization_barrier(jnp.mean(values, axis=-1, keepdims=True))
    variance = lax.optimization_barrier(jnp.mean(centered * centered, axis=-1, keepdims=True))
    return centered * lax.rsqrt(variance + EPSILON) * norm_gain + norm_shift

def allowed_table(member_index, keep_rows, prompt_keep):
    row_index = jnp.arange(TOK_DEV, dtype=jnp.int32)
    key_index = jnp.arange(KEYS, dtype=jnp.int32)
    in_prompt = row_index < PPIECE
    row_cont = jnp.maximum(row_index - PPIECE, 0) // CLEN
    row_group = jnp.where(in_prompt, -1, row_cont)
    row_self = jnp.where(in_prompt, member_index * PPIECE + row_index, MEMBERS * PPIECE + row_index - PPIECE)
    key_is_prompt = key_index < MEMBERS * PPIECE
    key_group = jnp.where(key_is_prompt, -2, (key_index - MEMBERS * PPIECE) // CLEN)
    key_keep = jnp.concatenate([prompt_keep, keep_rows[PPIECE:]]) > 0
    sees = key_is_prompt[None, :] | (row_group[:, None] == key_group[None, :])
    return sees & (key_keep[None, :] | (row_self[:, None] == key_index[None, :]))

def attend(member_queries, all_keys, all_values, allowed):
    heads_query = member_queries.reshape(TOK_DEV, HEADS, HDIM)
    heads_key = all_keys.reshape(KEYS, HEADS, HDIM)
    heads_value = all_values.reshape(KEYS, HEADS, HDIM)
    scores = low_back(jnp.einsum('qhd,khd->hqk', heads_query, heads_key, precision=HIGHEST) * (1.0 / math.sqrt(HDIM)))
    scores = jnp.where(allowed[None], scores, NEGATIVE)
    row_max = lax.optimization_barrier(jnp.max(scores, axis=-1, keepdims=True))
    exponent = jnp.exp(scores - row_max)
    attn_probs = low(exponent / lax.optimization_barrier(jnp.sum(exponent, axis=-1, keepdims=True)))
    attn_mixed = jnp.einsum('hqk,khd->qhd', attn_probs, heads_value, precision=HIGHEST)
    return attn_mixed.reshape(TOK_DEV, D)

def one_member(prompt_key, prompt_value, prompt_keep, member_item):
    member_index, member_queries, cont_keys, cont_values, keep_rows = member_item
    allowed = allowed_table(member_index, keep_rows, prompt_keep)
    all_keys = jnp.concatenate([prompt_key, cont_keys], axis=0)
    all_values = jnp.concatenate([prompt_value, cont_values], axis=0)
    return attend(member_queries, all_keys, all_values, allowed)

def forward(params, tokens32, valid_rows):
    query_weight, query_bias, key_weight, value_weight, value_bias, attn_weight, attn_bias, first_gain, first_shift, up_weight, up_bias, down_weight, down_bias, second_gain, second_shift = params
    flat_tokens = tokens32.reshape(MEMBERS * TOK_DEV, D)
    queries = both_ways(matmul(flat_tokens, query_weight) + query_bias).reshape(MEMBERS, TOK_DEV, D)
    key_rows = both_ways(matmul(flat_tokens, key_weight)).reshape(MEMBERS, TOK_DEV, D)
    value_rows = both_ways(matmul(flat_tokens, value_weight) + value_bias).reshape(MEMBERS, TOK_DEV, D)
    prompt_key = key_rows[:, :PPIECE].reshape(MEMBERS * PPIECE, D)
    prompt_value = value_rows[:, :PPIECE].reshape(MEMBERS * PPIECE, D)
    prompt_keep = valid_rows[:, :PPIECE].reshape(MEMBERS * PPIECE)
    member_step = jax.checkpoint(one_member)

    def run_member(member_item):
        return member_step(prompt_key, prompt_value, prompt_keep, member_item)
    member_items = (jnp.arange(MEMBERS, dtype=jnp.int32), queries, key_rows[:, PPIECE:], value_rows[:, PPIECE:], valid_rows)
    attn_mixed = both_ways(lax.map(run_member, member_items).reshape(MEMBERS * TOK_DEV, D))
    branch = low_back(matmul(attn_mixed, attn_weight) + attn_bias)
    hidden = layer_norm(flat_tokens + branch, first_gain, first_shift)
    up_input = low_back(matmul(low(hidden), up_weight) + up_bias)
    activation = low(jax.nn.gelu(up_input, approximate=False))
    second_sum = hidden + low_back(matmul(activation, down_weight) + down_bias)
    return layer_norm(second_sum, second_gain, second_shift).reshape(MEMBERS, TOK_DEV, D)

def reference(tokens, cotangent, teacher, valid_mask, valid_count, query_weight, query_bias, key_weight, value_weight, value_bias, attn_weight, attn_bias, first_gain, first_shift, up_weight, up_bias, down_weight, down_bias, second_gain, second_shift):
    params = (query_weight.astype(jnp.float32), query_bias.astype(jnp.float32), key_weight.astype(jnp.float32), value_weight.astype(jnp.float32), value_bias.astype(jnp.float32), attn_weight.astype(jnp.float32), attn_bias.astype(jnp.float32), first_gain.astype(jnp.float32), first_shift.astype(jnp.float32), up_weight.astype(jnp.float32), up_bias.astype(jnp.float32), down_weight.astype(jnp.float32), down_bias.astype(jnp.float32), second_gain.astype(jnp.float32), second_shift.astype(jnp.float32))
    loss_denom = valid_count.astype(jnp.float32)

    def group_step(carried, group_item):
        grad_sums, loss_sum = carried
        group_tokens, group_cot, group_teacher, group_valid = group_item
        tokens32 = group_tokens.astype(jnp.float32)
        cot32 = group_cot.astype(jnp.float32)
        teacher32 = group_teacher.astype(jnp.float32)
        valid32 = group_valid.astype(jnp.float32)[..., None]

        def objective(weights, inputs):
            result = forward(weights, inputs, group_valid)
            errors = result - teacher32
            loss_part = jnp.sum(valid32 * errors * errors) / loss_denom
            return (jnp.sum(cot32 * result) + loss_part, (result, loss_part))
        objective_value, pullback, (result, loss_part) = jax.vjp(objective, params, tokens32, has_aux=True)
        weight_grads, input_grad = pullback(jnp.ones_like(objective_value))
        grad_sums = jax.tree.map(jnp.add, grad_sums, weight_grads)
        return ((grad_sums, loss_sum + loss_part), (result.astype(jnp.bfloat16), input_grad.astype(jnp.bfloat16)))
    initial = (jax.tree.map(jnp.zeros_like, params), jnp.zeros((), jnp.float32))
    (grad_sums, total_loss), (layer_out, tokens_grad) = lax.scan(group_step, initial, (tokens, cotangent, teacher, valid_mask))
    return (layer_out, total_loss, tokens_grad, grad_sums[0], grad_sums[1], grad_sums[2], grad_sums[3], grad_sums[4], grad_sums[5], grad_sums[6], grad_sums[7], grad_sums[8], grad_sums[9], grad_sums[10], grad_sums[11], grad_sums[12], grad_sums[13], grad_sums[14])
```

```python
import functools

import jax
import jax.numpy as jnp
from jax import lax
from jax.experimental import pallas as pl
from jax.experimental.pallas import tpu as pltpu
from jax.sharding import PartitionSpec as P

HDIM = 64
PPIECE = 512
CLEN = 256
EPSILON = 1e-05
NEGATIVE = -1e30
LOG2E = 1.4426950408889634
SCALE = 1.0 / 8.0
LIMIT = 100.0

f32 = jnp.float32
bf16 = jnp.bfloat16
NT = (((1,), (1,)), ((), ()))
NN = (((1,), (0,)), ((), ()))
TN = (((0,), (0,)), ((), ()))
ANY = pl.BlockSpec(memory_space=pl.ANY)
MESH = pl.DeviceIdType.MESH


def dot(left, right, dims):
    return lax.dot_general(left, right, dims, preferred_element_type=f32)


def params(mib=56, **more):
    return pltpu.CompilerParams(vmem_limit_bytes=mib * 2**20, **more)


def cost(gflop, mbytes):
    return pl.CostEstimate(
        flops=int(gflop * 1e9), bytes_accessed=int(mbytes * 1e6), transcendentals=0
    )


def lane_of(rows):
    return lax.broadcasted_iota(jnp.int32, (rows, 128), 1)


def split3(values):
    hi = values.astype(bf16).astype(f32)
    mid = (values - hi).astype(bf16).astype(f32)
    low = values - hi - mid
    return hi, mid, low


def side_lanes(first, values):
    lane = lane_of(values.shape[0])
    hi, mid, low = split3(values)
    out = jnp.where(lane == 1, -hi, jnp.where(lane == 2, -mid, jnp.where(lane == 3, -low, 0.0)))
    return jnp.where(lane == 0, first, out).astype(bf16)


def gather_kernel(
    wq, wk, wv, vec, tok, keep,
    fq, fk, fv, fvec, ptok, pkeep,
    local_sem, zrecv, yrecv, crecv, usend, dsend, ysend, csend, tsend, trecv,
):
    depth = 4
    rep = lax.axis_index("rep")
    shard = lax.axis_index("shard")
    core = rep % 2
    z = shard // 2
    y = shard % 2
    other_core = {"rep": rep + 1 - 2 * core}
    other_x = {"rep": (rep + 2) % 4}
    other_y = {"shard": z * 2 + 1 - y}
    up = {"shard": (shard + 2) % 8}
    down = {"shard": (shard + 6) % 8}

    barrier = pltpu.get_barrier_semaphore()
    for place in (other_core, other_x, other_y):
        pl.semaphore_signal(barrier, inc=1, device_id=place, device_id_type=MESH)

    @pl.when(z < depth - 1)
    def _():
        pl.semaphore_signal(barrier, inc=1, device_id=up, device_id_type=MESH)

    @pl.when(z > 0)
    def _():
        pl.semaphore_signal(barrier, inc=1, device_id=down, device_id_type=MESH)

    inner = jnp.where((z > 0) & (z < depth - 1), 5, 4)
    pl.semaphore_wait(barrier, inner)

    sources = (wq, wk, wv, vec)
    targets = (fq, fk, fv, fvec)

    def place_of(u, zz, yy, cc):
        if u == 3:
            return targets[u].at[zz * 2 + yy]
        return targets[u].at[(zz * 2 + yy) * 2 + cc]

    def own_of(u):
        return sources[u] if u == 3 else sources[u].at[core]

    def move(src, dst, send, recv, where):
        return pltpu.make_async_remote_copy(
            src_ref=src, dst_ref=dst, send_sem=send, recv_sem=recv,
            device_id=where, device_id_type=MESH,
        )

    def to_up(u, zz, src):
        return move(src, place_of(u, zz, y, core), usend.at[u, zz], zrecv.at[u, zz], up)

    def to_down(u, zz, src):
        return move(src, place_of(u, zz, y, core), dsend.at[u, zz], zrecv.at[u, zz], down)

    def to_y(u, zz, src):
        return move(src, place_of(u, zz, y, core), ysend.at[u, zz], yrecv.at[u, zz], other_y)

    def to_core(u, zz, yy):
        at = place_of(u, zz, yy, core)
        index = zz * 2 + yy
        return move(at, at, csend.at[u, index], crecv.at[u, index], other_core)

    for u in range(4):
        @pl.when(z < depth - 1)
        def _():
            to_up(u, z, own_of(u)).start()

        @pl.when(z > 0)
        def _():
            to_down(u, z, own_of(u)).start()

        to_y(u, z, own_of(u)).start()

    prompt = tok.at[pl.ds(0, PPIECE)]
    copies = [
        move(prompt, ptok.at[1], tsend.at[0], trecv.at[0], other_x),
        move(keep, pkeep.at[1], tsend.at[1], trecv.at[1], other_x),
        move(prompt, ptok.at[0], tsend.at[2], trecv.at[2], other_core),
        move(keep, pkeep.at[0], tsend.at[3], trecv.at[3], other_core),
    ]
    for copy in copies:
        copy.start()
    locals_ = []
    for u in range(4):
        if u == 3:
            dst = fvec.at[shard]
        else:
            dst = targets[u].at[pl.ds(shard * 2, 2)]
        locals_.append(pltpu.make_async_copy(sources[u], dst, local_sem.at[u]))
        locals_[-1].start()

    for step in range(1, depth + 1):
        for u in range(4):
            if step < depth:
                @pl.when(z - step >= 0)
                def _():
                    zz = z - step
                    at = place_of(u, zz, y, core)
                    to_up(u, zz, at).wait_recv()

                    @pl.when(z < depth - 1)
                    def _():
                        to_up(u, zz, at).start()

                    to_y(u, zz, at).start()
                    if u < 3:
                        to_core(u, zz, y).start()

                @pl.when(z + step < depth)
                def _():
                    zz = z + step
                    at = place_of(u, zz, y, core)
                    to_down(u, zz, at).wait_recv()

                    @pl.when(z > 0)
                    def _():
                        to_down(u, zz, at).start()

                    to_y(u, zz, at).start()
                    if u < 3:
                        to_core(u, zz, y).start()

        for u in range(4):
            def from_y(zz):
                at = targets[u].at[zz * 2 + 1 - y] if u == 3 else place_of(u, zz, 1 - y, core)
                move(at, at, ysend.at[u, zz], yrecv.at[u, zz], other_y).wait_recv()
                if u < 3:
                    to_core(u, zz, 1 - y).start()

            if step == 1:
                from_y(z)
            else:
                @pl.when(z - (step - 1) >= 0)
                def _():
                    from_y(z - (step - 1))

                @pl.when(z + (step - 1) < depth)
                def _():
                    from_y(z + (step - 1))

    copies[0].wait_recv()
    copies[1].wait_recv()
    forward = [
        move(ptok.at[1], ptok.at[2], tsend.at[4], trecv.at[4], other_core),
        move(pkeep.at[1], pkeep.at[2], tsend.at[5], trecv.at[5], other_core),
    ]
    for copy in forward:
        copy.start()

    def others(act):
        for zz in range(depth):
            for yy in range(2):
                @pl.when((zz != z) | (yy != y))
                def _():
                    act(zz, yy)

    for u in range(3):
        def arrived(zz, yy):
            at = place_of(u, zz, yy, 1 - core)
            index = zz * 2 + yy
            move(at, at, csend.at[u, index], crecv.at[u, index], other_core).wait_recv()

        others(arrived)
    copies[2].wait_recv()
    copies[3].wait_recv()
    for copy in forward:
        copy.wait_recv()

    for copy in copies + forward:
        copy.wait_send()
    for copy in locals_:
        copy.wait()
    for u in range(4):
        for zz in range(depth):
            at = place_of(u, zz, y, core)
            to_y(u, zz, at).wait_send()

            @pl.when((zz <= z) & (z < depth - 1))
            def _():
                to_up(u, zz, at).wait_send()

            @pl.when((zz >= z) & (z > 0))
            def _():
                to_down(u, zz, at).wait_send()

        if u < 3:
            others(lambda zz, yy: to_core(u, zz, yy).wait_send())


def first_gather(wq, wk, wv, vec, tok, keep):
    width = wq.shape[1]
    sem = pltpu.SemaphoreType.DMA
    halves = [w.reshape(2, 48, width) for w in (wq, wk, wv)]
    full = jax.ShapeDtypeStruct((16, 48, width), bf16)
    outs = pl.pallas_call(
        gather_kernel,
        in_specs=[ANY] * 6,
        out_specs=[ANY] * 6,
        out_shape=[
            full, full, full,
            jax.ShapeDtypeStruct((8, 16, 128), bf16),
            jax.ShapeDtypeStruct((3, PPIECE, width), bf16),
            jax.ShapeDtypeStruct((3, 8, 128), f32),
        ],
        scratch_shapes=[
            sem((4,)), sem((4, 4)), sem((4, 4)), sem((3, 8)), sem((4, 4)), sem((4, 4)),
            sem((4, 4)), sem((3, 8)), sem((6,)), sem((6,)),
        ],
        compiler_params=params(8, collective_id=1, has_side_effects=True),
        cost_estimate=cost(0, 20),
    )(*halves, vec, tok, keep)
    fq, fk, fv, fvec, ptok, pkeep = outs
    return (
        fq.reshape(width, width), fk.reshape(width, width), fv.reshape(width, width),
        fvec, ptok.reshape(3 * PPIECE, width), pkeep,
    )


def project_kernel(tok, oth, wq, wk, wv, qb, vb, q, k, v, qn, kn):
    step = pl.program_id(0)
    own = (step == 0) | (step == 4)
    width = wq.shape[0]
    row = lax.broadcasted_iota(jnp.int32, (width, 128), 0)
    lane = lax.broadcasted_iota(jnp.int32, (width, 128), 1)
    heads = jnp.where(row // HDIM == lane, 1.0, 0.0).astype(bf16)

    @pl.when(step == 0)
    def _():
        qn[...] = jnp.zeros_like(qn)
        kn[...] = jnp.zeros_like(kn)

    def norms(values):
        wide = values.astype(f32)
        sums = dot((wide * wide).astype(bf16), heads, NN)
        return jnp.broadcast_to(jnp.max(sums, axis=0, keepdims=True), (8, 128))

    def keys(rows):
        keys_low = dot(rows, wk[...], NN).astype(bf16)
        k[...] = keys_low
        kn[...] = jnp.maximum(kn[...], norms(keys_low))
        v[...] = (dot(rows, wv[...], NN) + vb[...].astype(f32)).astype(bf16)

    @pl.when(own)
    def _():
        rows = tok[...]
        keys(rows)
        low = (dot(rows, wq[...], NN) + qb[...].astype(f32)).astype(bf16)
        q[...] = low
        qn[...] = jnp.maximum(qn[...], norms(low))

    @pl.when(jnp.logical_not(own))
    def _():
        keys(oth[...])


def project(tok, oth, wq, wk, wv, qb, vb):
    width = tok.shape[1]
    block = (PPIECE, width)
    whole = pl.BlockSpec((width, width), lambda i: (0, 0))
    row = pl.BlockSpec((1, width), lambda i: (0, 0))
    small = pl.BlockSpec((8, 128), lambda i: (0, 0))
    return pl.pallas_call(
        project_kernel,
        grid=(5,),
        in_specs=[
            pl.BlockSpec(block, lambda i: (i // 4, 0)),
            pl.BlockSpec(block, lambda i: (jnp.clip(i - 1, 0, 2), 0)),
            whole, whole, whole, row, row,
        ],
        out_specs=[
            pl.BlockSpec(block, lambda i: (i // 4, 0)),
            pl.BlockSpec(block, lambda i: (i, 0)),
            pl.BlockSpec(block, lambda i: (i, 0)),
            small, small,
        ],
        out_shape=[
            jax.ShapeDtypeStruct((1024, width), bf16),
            jax.ShapeDtypeStruct((2560, width), bf16),
            jax.ShapeDtypeStruct((2560, width), bf16),
            jax.ShapeDtypeStruct((8, 128), f32),
            jax.ShapeDtypeStruct((8, 128), f32),
        ],
        compiler_params=params(),
        cost_estimate=cost(7.5, 20),
    )(tok, oth, wq, wk, wv, qb, vb)


def head_twice(values, head):
    wide = values.astype(f32)
    turned = pltpu.roll(wide, 64, 1)
    first = lane_of(values.shape[0]) < 64
    if head == 0:
        return jnp.where(first, wide, turned).astype(bf16)
    return jnp.where(first, turned, wide).astype(bf16)


def head_parts(values, head):
    wide = values.astype(f32) * (SCALE * LOG2E)
    hi = wide.astype(bf16).astype(f32)
    low = wide - hi
    first = lane_of(values.shape[0]) < 64
    if head == 0:
        return jnp.where(first, hi, pltpu.roll(low, 64, 1)).astype(bf16)
    return jnp.where(first, pltpu.roll(hi, 64, 1), low).astype(bf16)


def head_only(values, head):
    first = lane_of(values.shape[0]) < 64
    keep = first if head == 0 else jnp.logical_not(first)
    return jnp.where(keep, values, jnp.zeros_like(values))


def off_diagonal(size, bias):
    row = lax.broadcasted_iota(jnp.int32, (size, size), 0)
    col = lax.broadcasted_iota(jnp.int32, (size, size), 1)
    return jnp.where(row == col, 0.0, bias)


def attend_kernel(q, k, v, kb, brow, qn, kn, o, side, qx, qd, kx, vx, pm, pc, bown, bcont, top):
    @pl.when(pl.program_id(0) == 0)
    def _():
        for head in range(2):
            kx[head, :, 128:] = kb[...]
        vx[:, 128:] = jnp.ones((2560, 128), bf16)
        bown[...] = off_diagonal(512, brow[0:1, 0:512])
        for c in range(2):
            bcont[c] = off_diagonal(256, brow[0:1, 2048 + 256 * c : 2304 + 256 * c])

    far = jnp.max(qn[...] * kn[...]) * (SCALE * LOG2E) ** 2 * 1.1 > LIMIT * LIMIT
    near = jnp.logical_not(far)
    lane = lane_of(1024)
    vx[:, :128] = v[...]
    for head in range(2):
        parts = head_parts(q[...], head)
        qx[head, :, :128] = parts
        qd[head, :, :128] = parts
        kx[head, :, :128] = head_twice(k[...], head)
        qx[head, :, 128:] = jnp.where(lane == 0, 1.0, 0.0).astype(bf16)
        qd[head, :, 128:] = jnp.zeros((1024, 128), bf16)

    def own_scores(head):
        return dot(qd[head, :512], kx[head, :512], NT) + bown[...]

    def cont_scores(head, c):
        rows = slice(512 + 256 * c, 768 + 256 * c)
        keys = slice(2048 + 256 * c, 2304 + 256 * c)
        return dot(qd[head, rows], kx[head, keys], NT) + bcont[c]

    @pl.when(near)
    def _():
        top[...] = jnp.zeros_like(top)

    @pl.when(far)
    def _():
        def widest(scores):
            return jnp.broadcast_to(
                jnp.max(scores, axis=1, keepdims=True), (scores.shape[0], 128)
            )

        for head in range(2):
            def more(c, carry):
                found = widest(dot(qx[head], kx[head, pl.ds(512 + c * 256, 256)], NT))
                top[head] = jnp.maximum(top[head], found)
                return carry

            top[head] = jnp.full((1024, 128), -3e38, f32)
            lax.fori_loop(0, 6, more, 0)
            top[head, 0:512] = jnp.maximum(top[head, 0:512], widest(own_scores(head)))
            top[head, 512:1024] = jnp.maximum(
                top[head, 512:1024], widest(dot(qx[head, 512:], kx[head, :512], NT))
            )
            for c in range(2):
                rows = slice(512 + 256 * c, 768 + 256 * c)
                top[head, rows] = jnp.maximum(top[head, rows], widest(cont_scores(head, c)))
            qx[head, :, 128:] = side_lanes(1.0, top[head])
            qd[head, :, 128:] = side_lanes(0.0, top[head])

    outs = []
    for head in range(2):
        for c in range(3):
            keys = slice(512 + 512 * c, 1024 + 512 * c)
            pm[head, :, keys] = jnp.exp2(dot(qx[head], kx[head, keys], NT)).astype(bf16)
        pm[head, 512:, :512] = jnp.exp2(dot(qx[head, 512:], kx[head, :512], NT)).astype(bf16)
        pm[head, :512, :512] = jnp.exp2(own_scores(head)).astype(bf16)
        for c in range(2):
            pc[head, c] = jnp.exp2(cont_scores(head, c)).astype(bf16)
        total = dot(pm[head], vx[:2048], NN)
        extra = [dot(pc[head, c], vx[2048 + 256 * c : 2304 + 256 * c], NN) for c in range(2)]
        total = jnp.concatenate(
            [total[:512], total[512:768] + extra[0], total[768:] + extra[1]], axis=0
        )
        mass = total[:, 128:]
        outs.append(total[:, :128] / mass)
        side[head] = side_lanes(1.0, top[head] + jnp.log2(mass))
    o[...] = jnp.where(lane < 64, outs[0], outs[1]).astype(bf16)


def attend(q, k, v, kb, brow, qn, kn, first, count):
    def pair(rows):
        return pl.BlockSpec((rows, 128), lambda i: (0, i + first))

    def fixed(*shape):
        return pl.BlockSpec(shape, lambda i: (0,) * len(shape))

    return pl.pallas_call(
        attend_kernel,
        grid=(count,),
        in_specs=[
            pair(1024), pair(2560), pair(2560), fixed(2560, 128), fixed(8, 2560),
            fixed(8, 128), fixed(8, 128),
        ],
        out_specs=[
            pl.BlockSpec((1024, 128), lambda i: (0, i)),
            pl.BlockSpec((2, 1024, 128), lambda i: (i, 0, 0)),
        ],
        out_shape=[
            jax.ShapeDtypeStruct((1024, 128 * count), bf16),
            jax.ShapeDtypeStruct((2 * count, 1024, 128), bf16),
        ],
        scratch_shapes=[
            pltpu.VMEM((2, 1024, 256), bf16),
            pltpu.VMEM((2, 1024, 256), bf16),
            pltpu.VMEM((2, 2560, 256), bf16),
            pltpu.VMEM((2560, 256), bf16),
            pltpu.VMEM((2, 1024, 2048), bf16),
            pltpu.VMEM((2, 2, 256, 256), bf16),
            pltpu.VMEM((512, 512), f32),
            pltpu.VMEM((2, 256, 256), f32),
            pltpu.VMEM((2, 1024, 128), f32),
        ],
        compiler_params=params(),
        cost_estimate=cost(7.0 * count, 3 * count),
    )(q, k, v, kb, brow, qn, kn)


def attend_back_kernel(
    q, k, v, d, o, side, kb, dq, dkv, qx, qd, kx, vx, dx, qm, kt, pt, st, pc, sc, bown, bcont
):
    @pl.when(pl.program_id(0) == 0)
    def _():
        for head in range(2):
            kx[head, :, 128:] = kb[...]
        vx[:, 128:] = kb[...]
        column = kb[:, 0:1].astype(f32)
        bown[...] = off_diagonal(512, column[:512])
        for c in range(2):
            bcont[c] = off_diagonal(256, column[2048 + 256 * c : 2304 + 256 * c])

    lane = lane_of(1024)
    vx[:, :128] = v[...]
    kt[...] = jnp.transpose(k[...].astype(f32)).astype(bf16)
    product = d[...].astype(f32) * o[...].astype(f32)
    for head in range(2):
        parts = head_parts(q[...], head)
        qx[head, :, :128] = parts
        qd[head, :, :128] = parts
        tail = side[head]
        qx[head, :, 128:] = tail
        qd[head, :, 128:] = jnp.where(lane == 0, jnp.zeros_like(tail), tail)
        kx[head, :, :128] = head_twice(k[...], head)
        qm[head] = head_only(q[...], head)
        dx[head, :, :128] = head_only(d[...], head)
        inner = jnp.sum(head_only(product, head), axis=1, keepdims=True)
        dx[head, :, 128:] = side_lanes(0.0, jnp.broadcast_to(inner, (1024, 128)))

    dq_rows = []
    for head in range(2):
        def tile(keys, rows, queries, bias=None):
            scores = dot(kx[head, keys], queries[head, rows], NT)
            if bias is not None:
                scores = scores + bias
            probs = jnp.exp2(scores)
            return probs, probs * dot(vx[keys], dx[head, rows], NT)

        for c in range(3):
            keys = slice(512 + 512 * c, 1024 + 512 * c)
            probs, delta = tile(keys, slice(0, 1024), qx)
            pt[head, keys] = probs.astype(bf16)
            st[head, keys] = delta.astype(bf16)
        probs, delta = tile(slice(0, 512), slice(512, 1024), qx)
        pt[head, :512, 512:] = probs.astype(bf16)
        st[head, :512, 512:] = delta.astype(bf16)
        probs, delta = tile(slice(0, 512), slice(0, 512), qd, bown[...])
        pt[head, :512, :512] = probs.astype(bf16)
        st[head, :512, :512] = delta.astype(bf16)
        for c in range(2):
            keys = slice(2048 + 256 * c, 2304 + 256 * c)
            rows = slice(512 + 256 * c, 768 + 256 * c)
            probs, delta = tile(keys, rows, qd, bcont[c])
            pc[head, c] = probs.astype(bf16)
            sc[head, c] = delta.astype(bf16)
        kth = kt[64 * head : 64 * head + 64]
        main = dot(kth[:, :2048], st[head], NN)
        extra = [dot(kth[:, 2048 + 256 * c : 2304 + 256 * c], sc[head, c], NN) for c in range(2)]
        dq_rows.append(
            jnp.concatenate(
                [main[:, :512], main[:, 512:768] + extra[0], main[:, 768:] + extra[1]], axis=1
            )
        )
    dq[...] = jnp.transpose(jnp.concatenate(dq_rows, axis=0) * SCALE).astype(bf16)
    dkv[1, :2048] = (dot(pt[0], dx[0, :, :128], NN) + dot(pt[1], dx[1, :, :128], NN)).astype(bf16)
    dkv[0, :2048] = ((dot(st[0], qm[0], NN) + dot(st[1], qm[1], NN)) * SCALE).astype(bf16)
    for c in range(2):
        keys = slice(2048 + 256 * c, 2304 + 256 * c)
        rows = slice(512 + 256 * c, 768 + 256 * c)
        dkv[1, keys] = (
            dot(pc[0, c], dx[0, rows, :128], NN) + dot(pc[1, c], dx[1, rows, :128], NN)
        ).astype(bf16)
        dkv[0, keys] = (
            (dot(sc[0, c], qm[0, rows], NN) + dot(sc[1, c], qm[1, rows], NN)) * SCALE
        ).astype(bf16)


def attend_back(q, k, v, d, o, side, kb, first, count):
    def pair(rows):
        return pl.BlockSpec((rows, 128), lambda i: (0, i + first))

    return pl.pallas_call(
        attend_back_kernel,
        grid=(count,),
        in_specs=[
            pair(1024), pair(2560), pair(2560), pair(1024),
            pl.BlockSpec((1024, 128), lambda i: (0, i)),
            pl.BlockSpec((2, 1024, 128), lambda i: (i, 0, 0)),
            pl.BlockSpec((2560, 128), lambda i: (0, 0)),
        ],
        out_specs=[
            pl.BlockSpec((1024, 128), lambda i: (0, i)),
            pl.BlockSpec((2, 2560, 128), lambda i: (0, 0, i)),
        ],
        out_shape=[
            jax.ShapeDtypeStruct((1024, 128 * count), bf16),
            jax.ShapeDtypeStruct((2, 2560, 128 * count), bf16),
        ],
        scratch_shapes=[
            pltpu.VMEM((2, 1024, 256), bf16),
            pltpu.VMEM((2, 1024, 256), bf16),
            pltpu.VMEM((2, 2560, 256), bf16),
            pltpu.VMEM((2560, 256), bf16),
            pltpu.VMEM((2, 1024, 256), bf16),
            pltpu.VMEM((2, 1024, 128), bf16),
            pltpu.VMEM((128, 2560), bf16),
            pltpu.VMEM((2, 2048, 1024), bf16),
            pltpu.VMEM((2, 2048, 1024), bf16),
            pltpu.VMEM((2, 2, 256, 256), bf16),
            pltpu.VMEM((2, 2, 256, 256), bf16),
            pltpu.VMEM((512, 512), f32),
            pltpu.VMEM((2, 256, 256), f32),
        ],
        compiler_params=params(),
        cost_estimate=cost(14.0 * count, 5 * count),
    )(q, k, v, d, o, side, kb)


def gelu_parts(x):
    bell = jnp.exp2(x * x * (-0.5 * LOG2E))
    t = 1.0 / (1.0 + (0.3275911 * 0.7071067811865476) * jnp.abs(x))
    poly = 0.5 * 1.061405429
    for term in (-1.453152027, 1.421413741, -0.284496736, 0.254829592):
        poly = poly * t + 0.5 * term
    below = poly * t * bell
    phi = jnp.where(x >= 0.0, 1.0 - below, below)
    return x * phi, phi + x * bell * 0.3989422804014327


def normed_of(values):
    centered = values - jnp.mean(values, axis=-1, keepdims=True)
    spread = lax.rsqrt(jnp.mean(centered * centered, axis=-1, keepdims=True) + EPSILON)
    return centered * spread, spread


def norm_back(incoming, normed, spread, gain):
    scaled = incoming * gain
    centered = scaled - jnp.mean(scaled, axis=-1, keepdims=True)
    return (centered - normed * jnp.mean(scaled * normed, axis=-1, keepdims=True)) * spread


FCH = 768


def forward_back_kernel(
    order, m0, m1, m2, tok, cot, teach, keep, scale, vecs, upb,
    ua, ub, uc, ud, da, db, dc, dd,
    result, hid_o, act_o, ddel_o, udel_o, adel_o, mdel_o, sums,
    wa, wu, wd, slope, sems,
):
    step = pl.program_id(0)
    width = tok.shape[1]
    hidden_units = upb.shape[1]

    def arrivals(wait):
        for group, (up_part, down_part) in enumerate(((ua, da), (ub, db), (uc, dc), (ud, dd))):
            for j in range(4):
                place = order[group * 4 + j]
                at = pl.ds(pl.multiple_of(place * 48, 16), 48)
                far = pl.ds(pl.multiple_of(place * 192, 64), 192)
                for copy in (
                    pltpu.make_async_copy(
                        up_part.at[j, :, pl.ds(0, width)], wa.at[at], sems.at[0, group, j]
                    ),
                    pltpu.make_async_copy(
                        up_part.at[j, :, pl.ds(width, hidden_units)], wu.at[at],
                        sems.at[1, group, j],
                    ),
                    pltpu.make_async_copy(down_part.at[j], wd.at[far], sems.at[2, group, j]),
                ):
                    if wait:
                        copy.wait()
                    else:
                        copy.start()

    @pl.when(step == 0)
    def _():
        arrivals(False)
        sums[...] = jnp.zeros_like(sums)
        arrivals(True)

    def vector(index):
        return vecs[index : index + 1].astype(f32)

    attn_b, gain1, shift1, down_b, gain2, shift2 = [vector(i) for i in range(2, 8)]

    def add_sum(index, values):
        sums[index : index + 1] += jnp.sum(values, axis=0, keepdims=True)

    x = tok[...].astype(f32)
    branch = attn_b + x
    for g, part in enumerate((m0, m1, m2)):
        branch = branch + dot(part[...], wa[256 * g : 256 * g + 256], NN)
    normed1, inv1 = normed_of(branch)
    hidden = normed1 * gain1 + shift1
    hid_low = hidden.astype(bf16)
    hid_o[...] = hid_low
    for c in range(hidden_units // FCH):
        cols = slice(c * FCH, c * FCH + FCH)
        value, rise = gelu_parts(dot(hid_low, wu[:, cols], NN) + upb[:, cols].astype(f32))
        act_o[:, cols] = value.astype(bf16)
        slope[:, cols] = rise.astype(bf16)
    second = hidden + dot(act_o[...], wd[...], NN) + down_b
    normed2, inv2 = normed_of(second)
    final = normed2 * gain2 + shift2
    result[...] = final.astype(bf16)
    errors = final - teach[...].astype(f32)
    kept = errors * jnp.concatenate([keep[...]] * (width // 128), axis=1)
    add_sum(6, kept * errors)
    grad = cot[...].astype(f32) + kept * (2.0 * scale[...])
    add_sum(1, grad * normed2)
    add_sum(2, grad)
    grad2 = norm_back(grad, normed2, inv2, gain2)
    ddel = grad2.astype(bf16)
    ddel_o[...] = ddel
    add_sum(0, ddel.astype(f32))
    for c in range(hidden_units // FCH):
        cols = slice(c * FCH, c * FCH + FCH)
        delta = dot(ddel, wd[cols], NT) * slope[:, cols].astype(f32)
        low = delta.astype(bf16)
        udel_o[:, cols] = low
        add_sum(8 + c, low.astype(f32))
    hgrad = grad2 + dot(udel_o[...], wu[...], NT)
    add_sum(4, hgrad * normed1)
    add_sum(5, hgrad)
    grad1 = norm_back(hgrad, normed1, inv1, gain1)
    adel = grad1.astype(bf16)
    adel_o[...] = adel
    add_sum(3, adel.astype(f32))
    mdel_o[...] = dot(adel, wa[...], NT).astype(bf16)


def forward_back(order, mixed, tok, cot, teach, keep, scale, vecs, upb, ups, downs):
    rows, width = tok.shape
    hidden_units = upb.shape[1]
    half = 512

    def block(columns):
        return pl.BlockSpec((half, columns), lambda i, *_: (i, 0))

    def fixed(*shape):
        return pl.BlockSpec(shape, lambda i, *_: (0,) * len(shape))

    def out(columns):
        return jax.ShapeDtypeStruct((rows, columns), bf16)

    return pl.pallas_call(
        forward_back_kernel,
        grid_spec=pltpu.PrefetchScalarGridSpec(
            num_scalar_prefetch=1,
            grid=(rows // half,),
            in_specs=[
                block(256), block(256), block(256), block(width), block(width), block(width),
                block(128), fixed(1, 1), fixed(8, width), fixed(1, hidden_units),
            ] + [ANY] * 8,
            out_specs=[
                block(width), block(width), block(hidden_units), block(width),
                block(hidden_units), block(width), block(width), fixed(16, width),
            ],
            scratch_shapes=[
                pltpu.VMEM((width, width), bf16),
                pltpu.VMEM((width, hidden_units), bf16),
                pltpu.VMEM((hidden_units, width), bf16),
                pltpu.VMEM((half, hidden_units), bf16),
                pltpu.SemaphoreType.DMA((3, 4, 4)),
            ],
        ),
        out_shape=[
            out(width), out(width), out(hidden_units), out(width), out(hidden_units),
            out(width), out(width), jax.ShapeDtypeStruct((16, width), f32),
        ],
        compiler_params=params(60),
        cost_estimate=cost(32.6, 30),
    )(order, *mixed, tok, cot, teach, keep, scale, vecs, upb, *ups, *downs)


def store_pieces(order, source, mine, other, piece):
    for i in range(8):
        at = pl.multiple_of(order[i] * piece, 16)
        mine[i] = source[pl.ds(at, piece)]
        at = pl.multiple_of(order[i + 8] * piece, 16)
        other[i] = source[pl.ds(at, piece)]


def weight_grad_kernel(order, *refs, count, piece):
    lefts, right = refs[:count], refs[count]
    mine, other, whole = refs[count + 1 :]
    at = 0
    for left in lefts:
        size = left.shape[1]
        whole[at : at + size] = dot(left[...], right[...], TN).astype(bf16)
        at += size
    store_pieces(order, whole, mine, other, piece)


def weight_grad(order, lefts, right, chunk):
    rows, columns = right.shape
    total = sum(left.shape[1] for left in lefts)
    piece = total // 16
    shape = jax.ShapeDtypeStruct((8, piece, columns), bf16)
    out = pl.BlockSpec((8, piece, chunk), lambda i, *_: (0, 0, i))
    return pl.pallas_call(
        functools.partial(weight_grad_kernel, count=len(lefts), piece=piece),
        grid_spec=pltpu.PrefetchScalarGridSpec(
            num_scalar_prefetch=1,
            grid=(columns // chunk,),
            in_specs=[pl.BlockSpec(left.shape, lambda i, *_: (0, 0)) for left in lefts]
            + [pl.BlockSpec((rows, chunk), lambda i, *_: (0, i))],
            out_specs=[out, out],
            scratch_shapes=[pltpu.VMEM((total, chunk), bf16)],
        ),
        out_shape=[shape, shape],
        compiler_params=params(),
        cost_estimate=cost(2e-9 * rows * total * columns, 10),
    )(order, *lefts, right)


def project_grad_kernel(order, tok, oth, dq, dkv, mine, other, sums, whole):
    cols = dq.shape[1]
    whole[:, :cols] = dot(tok[...], dq[...], TN).astype(bf16)
    for j in range(2):
        total = dot(oth[...], dkv[j, 512:2048], TN)
        total = total + dot(tok[:512], dkv[j, :512], TN)
        total = total + dot(tok[512:], dkv[j, 2048:], TN)
        whole[:, cols * (j + 1) : cols * (j + 2)] = total.astype(bf16)
    store_pieces(order, whole, mine, other, 48)
    sums[...] = jnp.zeros_like(sums)
    sums[0:1] = jnp.sum(dq[...].astype(f32), axis=0, keepdims=True)
    sums[1:2] = jnp.sum(dkv[1].astype(f32), axis=0, keepdims=True)


def project_grad(order, tok, oth, dq, dkv):
    width = tok.shape[1]
    cols = dq.shape[1]

    def fixed(shape):
        return pl.BlockSpec(shape, lambda i, *_: (0,) * len(shape))

    piece = (8, 48, 3 * cols)
    return pl.pallas_call(
        project_grad_kernel,
        grid_spec=pltpu.PrefetchScalarGridSpec(
            num_scalar_prefetch=1,
            grid=(1,),
            in_specs=[fixed(tok.shape), fixed(oth.shape), fixed(dq.shape), fixed(dkv.shape)],
            out_specs=[fixed(piece), fixed(piece), fixed((8, cols))],
            scratch_shapes=[pltpu.VMEM((width, 3 * cols), bf16)],
        ),
        out_shape=[
            jax.ShapeDtypeStruct(piece, bf16), jax.ShapeDtypeStruct(piece, bf16),
            jax.ShapeDtypeStruct((8, cols), f32),
        ],
        compiler_params=params(),
        cost_estimate=cost(2.5, 12),
    )(order, tok, oth, dq, dkv)


def tokens_grad_kernel(adel, *refs):
    parts, (wq, wk, wv, out) = refs[:-4], refs[-4:]
    for half in range(2):
        rows = slice(512 * half, 512 * half + 512)
        total = adel[rows].astype(f32)
        for g in range(3):
            dq, own, cont = parts[3 * g : 3 * g + 3]
            cols = slice(256 * g, 256 * g + 256)
            low = own if half == 0 else cont
            total = total + dot(dq[rows], wq[:, cols], NT)
            total = total + dot(low[0], wk[:, cols], NT)
            total = total + dot(low[1], wv[:, cols], NT)
        out[rows] = total.astype(bf16)


def tokens_grad(adel, parts, wq, wk, wv):
    def fixed(shape):
        return pl.BlockSpec(shape, lambda i: (0,) * len(shape))

    specs, flat = [], []
    for dq, own, dkv in parts:
        specs += [
            fixed(dq.shape), fixed(own.shape),
            pl.BlockSpec((2, 512, dkv.shape[2]), lambda i: (0, 4, 0)),
        ]
        flat += [dq, own, dkv]
    return pl.pallas_call(
        tokens_grad_kernel,
        grid=(1,),
        in_specs=[fixed(adel.shape)] + specs + [fixed(wq.shape)] * 3,
        out_specs=fixed(adel.shape),
        out_shape=jax.ShapeDtypeStruct(adel.shape, bf16),
        compiler_params=params(),
        cost_estimate=cost(3.6, 12),
    )(adel, *flat, wq, wk, wv)


def swap(values, axis, bit):
    size = lax.axis_size(axis)
    return lax.ppermute(values, axis, [(i, i ^ bit) for i in range(size)])


def sum_all(values):
    for axis in ("rep", "shard"):
        bit = 1
        while bit < lax.axis_size(axis):
            values = values + swap(values, axis, bit)
            bit *= 2
    return values


def local(
    tokens, cotangent, teacher, valid_mask, valid_count,
    query_weight, query_bias, key_weight, value_weight, value_bias,
    attn_weight, attn_bias, first_gain, first_shift,
    up_weight, up_bias, down_weight, down_bias, second_gain, second_shift,
):
    rows, width = tokens.shape[2:]
    shards = lax.axis_size("shard")
    split = shards == 8
    rep = lax.axis_index("rep")
    shard = lax.axis_index("shard")
    core = rep % 2
    z, y = shard // 2, shard % 2
    tok = tokens.reshape(rows, width)
    keep = valid_mask.reshape(rows)
    if split:
        i = jnp.arange(16, dtype=jnp.int32)
        order = (((z ^ (i % 4)) * 2 + (y ^ (i // 4 % 2))) * 2 + (core ^ (i // 8))).astype(jnp.int32)
    else:
        order = jnp.arange(16, dtype=jnp.int32)

    small = [
        query_bias, value_bias, attn_bias, first_gain, first_shift, down_bias, second_gain,
        second_shift, up_bias,
    ]
    part = query_bias.shape[0]
    vec = jnp.concatenate(small)
    keep_low = keep[:PPIECE].astype(f32).reshape(4, 128)
    if split:
        keep_low = jnp.concatenate([keep_low, keep_low])
        vec = jnp.pad(vec, (0, 2048 - vec.shape[0])).reshape(16, 128)
        wq, wk, wv, vecs, oth, others_keep = first_gather(
            query_weight, key_weight, value_weight, vec, tok, keep_low
        )
        vecs = vecs.reshape(8, 2048)
    else:
        wq, wk, wv, vecs = [
            lax.all_gather(w, "shard", axis=0, tiled=True)
            for w in (query_weight, key_weight, value_weight, vec[None])
        ]
        prompt = tok[:PPIECE]
        oth = jnp.concatenate([swap(prompt, "rep", bit) for bit in (1, 2, 3)])
        others_keep = jnp.stack([swap(keep_low, "rep", bit) for bit in (1, 2, 3)])
    others_keep = others_keep[:, :4].reshape(3 * PPIECE)
    upb = vecs[:, 8 * part : 8 * part + up_bias.shape[0]].reshape(1, -1)
    vecs = vecs[:, : 8 * part].reshape(shards, 8, part).transpose(1, 0, 2).reshape(8, width)

    if split:
        up_half = jnp.concatenate(
            [attn_weight.reshape(2, 48, width), up_weight.reshape(2, 48, -1)], axis=2
        )
        down_half = down_weight.reshape(2, 192, width)
        up_half, down_half, wq = lax.optimization_barrier((up_half, down_half, wq))

        def gather(half):
            half = lax.dynamic_index_in_dim(half, core, 0, keepdims=False)
            near = jnp.stack([half] + [swap(half, "shard", 2 * d) for d in (1, 2, 3)])
            far = swap(near, "shard", 1)
            return near, far, swap(near, "rep", 1), swap(far, "rep", 1)

        ups, downs = gather(up_half), gather(down_half)
    else:
        full = jnp.concatenate(
            [
                lax.all_gather(w, "shard", axis=0, tiled=True)
                for w in (attn_weight, up_weight)
            ],
            axis=1,
        ).reshape(4, 4, 48, -1)
        ups = [full[j] for j in range(4)]
        full = lax.all_gather(down_weight, "shard", axis=0, tiled=True).reshape(4, 4, 192, width)
        downs = [full[j] for j in range(4)]

    q, k, v, qn, kn = project(tok, oth, wq, wk, wv, vecs[0:1], vecs[1:2])
    all_keep = jnp.concatenate(
        [keep[:PPIECE].astype(f32), others_keep, keep[PPIECE:].astype(f32)]
    )
    bias = jnp.where(all_keep > 0.5, 0.0, NEGATIVE)
    brow = jnp.broadcast_to(bias[None], (8, bias.shape[0]))
    lane = jnp.arange(128)[None]
    kb = jnp.where(lane == 0, bias[:, None], jnp.where(lane < 4, 1.0, 0.0)).astype(bf16)
    groups = 3
    pairs = width // 128 // groups
    mixed, sides = zip(
        *[attend(q, k, v, kb, brow, qn, kn, g * pairs, pairs) for g in range(groups)]
    )

    keep_wide = jnp.broadcast_to(keep.astype(f32)[:, None], (rows, 128))
    scale = (1.0 / valid_count.astype(f32)).reshape(1, 1)
    result, hid, act, ddel, udel, adel, mdel, sums = forward_back(
        order, mixed, tok, cotangent.reshape(rows, width), teacher.reshape(rows, width),
        keep_wide, scale, vecs, upb, ups, downs,
    )
    down_pieces = weight_grad(order, [act], ddel, 256)
    up_pieces = weight_grad(order, [hid], udel, 512)
    attn_pieces = weight_grad(order, mixed, adel, 256)

    def scatter(mine, other):
        if not split:
            piece, columns = mine.shape[1:]
            full = jnp.concatenate([mine, other]).reshape(16 * piece, columns)
            part = lax.psum_scatter(full, "shard", scatter_dimension=0, tiled=True)
            return lax.psum(part, "rep").astype(f32)
        got = mine.astype(f32) + swap(other, "rep", 1).astype(f32)
        got = got.astype(bf16)
        got = got[:4].astype(f32) + swap(got[4:], "shard", 1).astype(f32)
        got = got.astype(bf16)
        total = got[0].astype(f32)
        for d in (1, 2, 3):
            total = total + swap(got[d], "shard", 2 * d).astype(f32)
        total = total.astype(bf16)
        first, second, third = [swap(total, "rep", bit).astype(f32) for bit in (1, 2, 3)]
        own, twin = total.astype(f32) + second, first + third
        return jnp.where(
            core == 0, jnp.concatenate([own, twin]), jnp.concatenate([twin, own])
        )

    down_grad = scatter(*down_pieces)
    up_grad = scatter(*up_pieces)
    attn_grad = scatter(*attn_pieces)
    sums = sum_all(sums)

    parts, pieces, tails = [], [], []
    for g in range(groups):
        dq, dkv = attend_back(q, k, v, mdel, mixed[g], sides[g], kb, g * pairs, pairs)
        pieces_mine, pieces_other, tail = project_grad(order, tok, oth, dq, dkv)
        pieces.append(scatter(pieces_mine, pieces_other))
        tails.append(tail)
        near = swap(dkv[:, 512:1024], "rep", 1).astype(f32)
        turn = swap(dkv[:, 1536:2048], "rep", 1).astype(f32)
        turn = (turn + dkv[:, 1024:1536].astype(f32)).astype(bf16)
        turn = swap(turn, "rep", 2).astype(f32)
        own = (dkv[:, :512].astype(f32) + near + turn).astype(bf16)
        parts.append((dq, own, dkv))
    tails = sum_all(jnp.concatenate(tails, axis=1))
    token_grad = tokens_grad(adel, parts, wq, wk, wv)

    cols = width // groups
    query_grad, key_grad, value_grad = [
        jnp.concatenate([p[:, cols * j : cols * (j + 1)] for p in pieces], axis=1)
        for j in range(3)
    ]

    def owned(row):
        return lax.dynamic_slice(row, (shard * part,), (part,))

    up_part = up_bias.shape[0]
    loss = jnp.sum(sums[6]) / valid_count.astype(f32)
    return (
        result.reshape(tokens.shape),
        loss,
        token_grad.reshape(tokens.shape),
        query_grad,
        owned(tails[0]),
        key_grad,
        value_grad,
        owned(tails[1]),
        attn_grad,
        owned(sums[3]),
        owned(sums[4]),
        owned(sums[5]),
        up_grad,
        lax.dynamic_slice(sums[8:12].reshape(-1), (shard * up_part,), (up_part,)),
        down_grad,
        owned(sums[0]),
        owned(sums[1]),
        owned(sums[2]),
    )


def solution(mesh):
    wide = P("shard", "rep", None, None)
    matrix, vector = P("shard", None), P("shard")
    return jax.shard_map(
        local,
        mesh=mesh,
        in_specs=(
            wide, wide, wide, P("shard", "rep", None), P(),
            matrix, vector, matrix, matrix, vector, matrix, vector, vector, vector,
            matrix, vector, matrix, vector, vector, vector,
        ),
        out_specs=(
            wide, P(), wide,
            matrix, vector, matrix, matrix, vector, matrix, vector, vector, vector,
            matrix, vector, matrix, vector, vector, vector,
        ),
        check_vma=False,
    )
```

```python
import functools

import jax
import jax.numpy as jnp
from jax import lax
from jax.experimental import pallas as pl
from jax.experimental.pallas import tpu as pltpu
from jax.sharding import PartitionSpec as P

HDIM = 64
PPIECE = 512
CLEN = 256
EPSILON = 1e-05
NEGATIVE = -1e30
LOG2E = 1.4426950408889634
SCALE = 1.0 / 8.0
LIMIT = 100.0

f32 = jnp.float32
bf16 = jnp.bfloat16
NT = (((1,), (1,)), ((), ()))
NN = (((1,), (0,)), ((), ()))
TN = (((0,), (0,)), ((), ()))
ANY = pl.BlockSpec(memory_space=pl.ANY)
MESH = pl.DeviceIdType.MESH


def dot(left, right, dims):
    return lax.dot_general(left, right, dims, preferred_element_type=f32)


def params(mib=56, **more):
    return pltpu.CompilerParams(vmem_limit_bytes=mib * 2**20, **more)


def cost(gflop, mbytes):
    return pl.CostEstimate(
        flops=int(gflop * 1e9), bytes_accessed=int(mbytes * 1e6), transcendentals=0
    )


def lane_of(rows):
    return lax.broadcasted_iota(jnp.int32, (rows, 128), 1)


def split3(values):
    hi = values.astype(bf16).astype(f32)
    mid = (values - hi).astype(bf16).astype(f32)
    low = values - hi - mid
    return hi, mid, low


def side_lanes(first, values):
    lane = lane_of(values.shape[0])
    hi, mid, low = split3(values)
    out = jnp.where(lane == 1, -hi, jnp.where(lane == 2, -mid, jnp.where(lane == 3, -low, 0.0)))
    return jnp.where(lane == 0, first, out).astype(bf16)


def gather_kernel(
    wq, wk, wv, vec, tok, keep,
    fq, fk, fv, fvec, ptok, pkeep,
    local_sem, zrecv, yrecv, crecv, usend, dsend, ysend, csend, tsend, trecv,
):
    depth = 4
    rep = lax.axis_index("rep")
    shard = lax.axis_index("shard")
    core = rep % 2
    z = shard // 2
    y = shard % 2
    other_core = {"rep": rep + 1 - 2 * core}
    other_x = {"rep": (rep + 2) % 4}
    other_y = {"shard": z * 2 + 1 - y}
    up = {"shard": (shard + 2) % 8}
    down = {"shard": (shard + 6) % 8}

    barrier = pltpu.get_barrier_semaphore()
    for place in (other_core, other_x, other_y):
        pl.semaphore_signal(barrier, inc=1, device_id=place, device_id_type=MESH)

    @pl.when(z < depth - 1)
    def _():
        pl.semaphore_signal(barrier, inc=1, device_id=up, device_id_type=MESH)

    @pl.when(z > 0)
    def _():
        pl.semaphore_signal(barrier, inc=1, device_id=down, device_id_type=MESH)

    inner = jnp.where((z > 0) & (z < depth - 1), 5, 4)
    pl.semaphore_wait(barrier, inner)

    sources = (wq, wk, wv, vec)
    targets = (fq, fk, fv, fvec)

    def place_of(u, zz, yy, cc):
        if u == 3:
            return targets[u].at[zz * 2 + yy]
        return targets[u].at[(zz * 2 + yy) * 2 + cc]

    def own_of(u):
        return sources[u] if u == 3 else sources[u].at[core]

    def move(src, dst, send, recv, where):
        return pltpu.make_async_remote_copy(
            src_ref=src, dst_ref=dst, send_sem=send, recv_sem=recv,
            device_id=where, device_id_type=MESH,
        )

    def to_up(u, zz, src):
        return move(src, place_of(u, zz, y, core), usend.at[u, zz], zrecv.at[u, zz], up)

    def to_down(u, zz, src):
        return move(src, place_of(u, zz, y, core), dsend.at[u, zz], zrecv.at[u, zz], down)

    def to_y(u, zz, src):
        return move(src, place_of(u, zz, y, core), ysend.at[u, zz], yrecv.at[u, zz], other_y)

    def to_core(u, zz, yy):
        at = place_of(u, zz, yy, core)
        index = zz * 2 + yy
        return move(at, at, csend.at[u, index], crecv.at[u, index], other_core)

    for u in range(4):
        @pl.when(z < depth - 1)
        def _():
            to_up(u, z, own_of(u)).start()

        @pl.when(z > 0)
        def _():
            to_down(u, z, own_of(u)).start()

        to_y(u, z, own_of(u)).start()

    prompt = tok.at[pl.ds(0, PPIECE)]
    copies = [
        move(prompt, ptok.at[1], tsend.at[0], trecv.at[0], other_x),
        move(keep, pkeep.at[1], tsend.at[1], trecv.at[1], other_x),
        move(prompt, ptok.at[0], tsend.at[2], trecv.at[2], other_core),
        move(keep, pkeep.at[0], tsend.at[3], trecv.at[3], other_core),
    ]
    for copy in copies:
        copy.start()
    locals_ = []
    for u in range(4):
        if u == 3:
            dst = fvec.at[shard]
        else:
            dst = targets[u].at[pl.ds(shard * 2, 2)]
        locals_.append(pltpu.make_async_copy(sources[u], dst, local_sem.at[u]))
        locals_[-1].start()

    for step in range(1, depth + 1):
        for u in range(4):
            if step < depth:
                @pl.when(z - step >= 0)
                def _():
                    zz = z - step
                    at = place_of(u, zz, y, core)
                    to_up(u, zz, at).wait_recv()

                    @pl.when(z < depth - 1)
                    def _():
                        to_up(u, zz, at).start()

                    to_y(u, zz, at).start()
                    if u < 3:
                        to_core(u, zz, y).start()

                @pl.when(z + step < depth)
                def _():
                    zz = z + step
                    at = place_of(u, zz, y, core)
                    to_down(u, zz, at).wait_recv()

                    @pl.when(z > 0)
                    def _():
                        to_down(u, zz, at).start()

                    to_y(u, zz, at).start()
                    if u < 3:
                        to_core(u, zz, y).start()

        for u in range(4):
            def from_y(zz):
                at = targets[u].at[zz * 2 + 1 - y] if u == 3 else place_of(u, zz, 1 - y, core)
                move(at, at, ysend.at[u, zz], yrecv.at[u, zz], other_y).wait_recv()
                if u < 3:
                    to_core(u, zz, 1 - y).start()

            if step == 1:
                from_y(z)
            else:
                @pl.when(z - (step - 1) >= 0)
                def _():
                    from_y(z - (step - 1))

                @pl.when(z + (step - 1) < depth)
                def _():
                    from_y(z + (step - 1))

    copies[0].wait_recv()
    copies[1].wait_recv()
    forward = [
        move(ptok.at[1], ptok.at[2], tsend.at[4], trecv.at[4], other_core),
        move(pkeep.at[1], pkeep.at[2], tsend.at[5], trecv.at[5], other_core),
    ]
    for copy in forward:
        copy.start()

    def others(act):
        for zz in range(depth):
            for yy in range(2):
                @pl.when((zz != z) | (yy != y))
                def _():
                    act(zz, yy)

    for u in range(3):
        def arrived(zz, yy):
            at = place_of(u, zz, yy, 1 - core)
            index = zz * 2 + yy
            move(at, at, csend.at[u, index], crecv.at[u, index], other_core).wait_recv()

        others(arrived)
    copies[2].wait_recv()
    copies[3].wait_recv()
    for copy in forward:
        copy.wait_recv()

    for copy in copies + forward:
        copy.wait_send()
    for copy in locals_:
        copy.wait()
    for u in range(4):
        for zz in range(depth):
            at = place_of(u, zz, y, core)
            to_y(u, zz, at).wait_send()

            @pl.when((zz <= z) & (z < depth - 1))
            def _():
                to_up(u, zz, at).wait_send()

            @pl.when((zz >= z) & (z > 0))
            def _():
                to_down(u, zz, at).wait_send()

        if u < 3:
            others(lambda zz, yy: to_core(u, zz, yy).wait_send())


def first_gather(wq, wk, wv, vec, tok, keep):
    width = wq.shape[1]
    sem = pltpu.SemaphoreType.DMA
    halves = [w.reshape(2, 48, width) for w in (wq, wk, wv)]
    full = jax.ShapeDtypeStruct((16, 48, width), bf16)
    outs = pl.pallas_call(
        gather_kernel,
        in_specs=[ANY] * 6,
        out_specs=[ANY] * 6,
        out_shape=[
            full, full, full,
            jax.ShapeDtypeStruct((8, 16, 128), bf16),
            jax.ShapeDtypeStruct((3, PPIECE, width), bf16),
            jax.ShapeDtypeStruct((3, 8, 128), f32),
        ],
        scratch_shapes=[
            sem((4,)), sem((4, 4)), sem((4, 4)), sem((3, 8)), sem((4, 4)), sem((4, 4)),
            sem((4, 4)), sem((3, 8)), sem((6,)), sem((6,)),
        ],
        compiler_params=params(8, collective_id=1, has_side_effects=True),
        cost_estimate=cost(0, 20),
    )(*halves, vec, tok, keep)
    fq, fk, fv, fvec, ptok, pkeep = outs
    return (
        fq.reshape(width, width), fk.reshape(width, width), fv.reshape(width, width),
        fvec, ptok.reshape(3 * PPIECE, width), pkeep,
    )


def project_kernel(tok, oth, wq, wk, wv, qb, vb, q, k, v, xt, qn, kn):
    step = pl.program_id(0)
    own = (step == 0) | (step == 4)
    width = wq.shape[0]
    row = lax.broadcasted_iota(jnp.int32, (width, 128), 0)
    lane = lax.broadcasted_iota(jnp.int32, (width, 128), 1)
    heads = jnp.where(row // HDIM == lane, 1.0, 0.0).astype(bf16)

    @pl.when(step == 0)
    def _():
        qn[...] = jnp.zeros_like(qn)
        kn[...] = jnp.zeros_like(kn)

    def norms(values):
        wide = values.astype(f32)
        sums = dot((wide * wide).astype(bf16), heads, NN)
        return jnp.broadcast_to(jnp.max(sums, axis=0, keepdims=True), (8, 128))

    def keys(rows):
        keys_low = dot(rows, wk[...], NN).astype(bf16)
        k[...] = keys_low
        kn[...] = jnp.maximum(kn[...], norms(keys_low))
        v[...] = (dot(rows, wv[...], NN) + vb[...].astype(f32)).astype(bf16)
        xt[...] = jnp.transpose(rows)

    @pl.when(own)
    def _():
        rows = tok[...]
        keys(rows)
        low = (dot(rows, wq[...], NN) + qb[...].astype(f32)).astype(bf16)
        q[...] = low
        qn[...] = jnp.maximum(qn[...], norms(low))

    @pl.when(jnp.logical_not(own))
    def _():
        keys(oth[...])


def project(tok, oth, wq, wk, wv, qb, vb):
    width = tok.shape[1]
    block = (PPIECE, width)
    whole = pl.BlockSpec((width, width), lambda i: (0, 0))
    row = pl.BlockSpec((1, width), lambda i: (0, 0))
    small = pl.BlockSpec((8, 128), lambda i: (0, 0))
    return pl.pallas_call(
        project_kernel,
        grid=(5,),
        in_specs=[
            pl.BlockSpec(block, lambda i: (i // 4, 0)),
            pl.BlockSpec(block, lambda i: (jnp.clip(i - 1, 0, 2), 0)),
            whole, whole, whole, row, row,
        ],
        out_specs=[
            pl.BlockSpec(block, lambda i: (i // 4, 0)),
            pl.BlockSpec(block, lambda i: (i, 0)),
            pl.BlockSpec(block, lambda i: (i, 0)),
            pl.BlockSpec((width, PPIECE), lambda i: (0, i)),
            small, small,
        ],
        out_shape=[
            jax.ShapeDtypeStruct((1024, width), bf16),
            jax.ShapeDtypeStruct((2560, width), bf16),
            jax.ShapeDtypeStruct((2560, width), bf16),
            jax.ShapeDtypeStruct((width, 2560), bf16),
            jax.ShapeDtypeStruct((8, 128), f32),
            jax.ShapeDtypeStruct((8, 128), f32),
        ],
        compiler_params=params(),
        cost_estimate=cost(7.5, 20),
    )(tok, oth, wq, wk, wv, qb, vb)


def head_twice(values, head):
    wide = values.astype(f32)
    turned = pltpu.roll(wide, 64, 1)
    first = lane_of(values.shape[0]) < 64
    if head == 0:
        return jnp.where(first, wide, turned).astype(bf16)
    return jnp.where(first, turned, wide).astype(bf16)


def head_parts(values, head):
    wide = values.astype(f32) * (SCALE * LOG2E)
    hi = wide.astype(bf16).astype(f32)
    low = wide - hi
    first = lane_of(values.shape[0]) < 64
    if head == 0:
        return jnp.where(first, hi, pltpu.roll(low, 64, 1)).astype(bf16)
    return jnp.where(first, pltpu.roll(hi, 64, 1), low).astype(bf16)


def head_only(values, head):
    first = lane_of(values.shape[0]) < 64
    keep = first if head == 0 else jnp.logical_not(first)
    return jnp.where(keep, values, jnp.zeros_like(values))


def off_diagonal(size, bias):
    row = lax.broadcasted_iota(jnp.int32, (size, size), 0)
    col = lax.broadcasted_iota(jnp.int32, (size, size), 1)
    return jnp.where(row == col, 0.0, bias)


def attend_kernel(q, k, v, kb, brow, qn, kn, o_in, side_in, o, side, qx, qd, kx, vx, pm, pc, bown, bcont, top):
    @pl.when(pl.program_id(0) == 0)
    def _():
        for head in range(2):
            kx[head, :, 128:] = kb[...]
        vx[:, 128:] = jnp.ones((2560, 128), bf16)
        bown[...] = off_diagonal(512, brow[0:1, 0:512])
        for c in range(2):
            bcont[c] = off_diagonal(256, brow[0:1, 2048 + 256 * c : 2304 + 256 * c])

    far = jnp.max(qn[...] * kn[...]) * (SCALE * LOG2E) ** 2 * 1.1 > LIMIT * LIMIT
    near = jnp.logical_not(far)
    lane = lane_of(1024)
    vx[:, :128] = v[...]
    for head in range(2):
        parts = head_parts(q[...], head)
        qx[head, :, :128] = parts
        qd[head, :, :128] = parts
        kx[head, :, :128] = head_twice(k[...], head)
        qx[head, :, 128:] = jnp.where(lane == 0, 1.0, 0.0).astype(bf16)
        qd[head, :, 128:] = jnp.zeros((1024, 128), bf16)

    def own_scores(head):
        return dot(qd[head, :512], kx[head, :512], NT) + bown[...]

    def cont_scores(head, c):
        rows = slice(512 + 256 * c, 768 + 256 * c)
        keys = slice(2048 + 256 * c, 2304 + 256 * c)
        return dot(qd[head, rows], kx[head, keys], NT) + bcont[c]

    @pl.when(near)
    def _():
        top[...] = jnp.zeros_like(top)

    @pl.when(far)
    def _():
        def widest(scores):
            return jnp.broadcast_to(
                jnp.max(scores, axis=1, keepdims=True), (scores.shape[0], 128)
            )

        for head in range(2):
            def more(c, carry):
                found = widest(dot(qx[head], kx[head, pl.ds(512 + c * 256, 256)], NT))
                top[head] = jnp.maximum(top[head], found)
                return carry

            top[head] = jnp.full((1024, 128), -3e38, f32)
            lax.fori_loop(0, 6, more, 0)
            top[head, 0:512] = jnp.maximum(top[head, 0:512], widest(own_scores(head)))
            top[head, 512:1024] = jnp.maximum(
                top[head, 512:1024], widest(dot(qx[head, 512:], kx[head, :512], NT))
            )
            for c in range(2):
                rows = slice(512 + 256 * c, 768 + 256 * c)
                top[head, rows] = jnp.maximum(top[head, rows], widest(cont_scores(head, c)))
            qx[head, :, 128:] = side_lanes(1.0, top[head])
            qd[head, :, 128:] = side_lanes(0.0, top[head])

    outs = []
    for head in range(2):
        for c in range(3):
            keys = slice(512 + 512 * c, 1024 + 512 * c)
            pm[head, :, keys] = jnp.exp2(dot(qx[head], kx[head, keys], NT)).astype(bf16)
        pm[head, 512:, :512] = jnp.exp2(dot(qx[head, 512:], kx[head, :512], NT)).astype(bf16)
        pm[head, :512, :512] = jnp.exp2(own_scores(head)).astype(bf16)
        for c in range(2):
            pc[head, c] = jnp.exp2(cont_scores(head, c)).astype(bf16)
        total = dot(pm[head], vx[:2048], NN)
        extra = [dot(pc[head, c], vx[2048 + 256 * c : 2304 + 256 * c], NN) for c in range(2)]
        total = jnp.concatenate(
            [total[:512], total[512:768] + extra[0], total[768:] + extra[1]], axis=0
        )
        mass = total[:, 128:]
        outs.append(total[:, :128] / mass)
        side[head] = side_lanes(1.0, top[head] + jnp.log2(mass))
    o[...] = jnp.where(lane < 64, outs[0], outs[1]).astype(bf16)


def attend(q, k, v, kb, brow, qn, kn, outs, first, count):
    def pair(rows):
        return pl.BlockSpec((rows, 128), lambda i: (0, i + first))

    def fixed(*shape):
        return pl.BlockSpec(shape, lambda i: (0,) * len(shape))

    kernel = attend_kernel if outs else functools.partial(fresh, attend_kernel)
    width = q.shape[1]
    return pl.pallas_call(
        kernel,
        grid=(count,),
        in_specs=[
            pair(1024), pair(2560), pair(2560), fixed(2560, 128), fixed(8, 2560),
            fixed(8, 128), fixed(8, 128),
        ] + [ANY] * len(outs),
        out_specs=[
            pair(1024),
            pl.BlockSpec((2, 1024, 128), lambda i: (i + first, 0, 0)),
        ],
        out_shape=[
            jax.ShapeDtypeStruct((1024, width), bf16),
            jax.ShapeDtypeStruct((width // HDIM, 1024, 128), bf16),
        ],
        scratch_shapes=[
            pltpu.VMEM((2, 1024, 256), bf16),
            pltpu.VMEM((2, 1024, 256), bf16),
            pltpu.VMEM((2, 2560, 256), bf16),
            pltpu.VMEM((2560, 256), bf16),
            pltpu.VMEM((2, 1024, 2048), bf16),
            pltpu.VMEM((2, 2, 256, 256), bf16),
            pltpu.VMEM((512, 512), f32),
            pltpu.VMEM((2, 256, 256), f32),
            pltpu.VMEM((2, 1024, 128), f32),
        ],
        input_output_aliases={7: 0, 8: 1} if outs else {},
        compiler_params=params(),
        cost_estimate=cost(7.0 * count, 3 * count),
    )(q, k, v, kb, brow, qn, kn, *outs)


def fresh(kernel, *refs):
    return kernel(*refs[:7], None, None, *refs[7:])


def back_fill(q, k, v, d, o, side, kb, qx, qd, kx, vx, dx, qm, kt, bown, bcont):
    @pl.when(pl.program_id(0) == 0)
    def _():
        for head in range(2):
            kx[head, :, 128:] = kb[...]
        vx[:, 128:] = kb[...]
        column = kb[:, 0:1].astype(f32)
        bown[...] = off_diagonal(512, column[:512]).astype(bf16)
        for c in range(2):
            keys = slice(2048 + 256 * c, 2304 + 256 * c)
            bcont[c] = off_diagonal(256, column[keys]).astype(bf16)

    lane = lane_of(1024)
    vx[:, :128] = v[...]
    kt[...] = jnp.transpose(k[...].astype(f32)).astype(bf16)
    product = d[...].astype(f32) * o[...].astype(f32)
    for head in range(2):
        parts = head_parts(q[...], head)
        qx[head, :, :128] = parts
        qd[head, :, :128] = parts
        tail = side[head]
        qx[head, :, 128:] = tail
        qd[head, :, 128:] = jnp.where(lane == 0, jnp.zeros_like(tail), tail)
        kx[head, :, :128] = head_twice(k[...], head)
        qm[head] = head_only(q[...], head)
        dx[head, :, :128] = head_only(d[...], head)
        inner = jnp.sum(head_only(product, head), axis=1, keepdims=True)
        dx[head, :, 128:] = side_lanes(0.0, jnp.broadcast_to(inner, (1024, 128)))


def back_head(head, qx, qd, kx, vx, dx, qm, kt, pt, st, pc, sc, bown, bcont):
    def tile(keys, rows, queries, bias=None):
        scores = dot(kx[head, keys], queries[head, rows], NT)
        if bias is not None:
            scores = scores + bias.astype(f32)
        probs = jnp.exp2(scores)
        return probs.astype(bf16), (probs * dot(vx[keys], dx[head, rows], NT)).astype(bf16)

    for c in range(3):
        keys = slice(512 + 512 * c, 1024 + 512 * c)
        pt[keys], st[keys] = tile(keys, slice(0, 1024), qx)
    pt[:512, 512:], st[:512, 512:] = tile(slice(0, 512), slice(512, 1024), qx)
    pt[:512, :512], st[:512, :512] = tile(slice(0, 512), slice(0, 512), qd, bown[...])
    for c in range(2):
        keys = slice(2048 + 256 * c, 2304 + 256 * c)
        pc[c], sc[c] = tile(keys, slice(512 + 256 * c, 768 + 256 * c), qd, bcont[c])
    kth = kt[64 * head : 64 * head + 64]
    main = dot(kth[:, :2048], st[...], NN)
    extra = [dot(kth[:, 2048 + 256 * c : 2304 + 256 * c], sc[c], NN) for c in range(2)]
    rows = jnp.concatenate(
        [main[:, :512], main[:, 512:768] + extra[0], main[:, 768:] + extra[1]], axis=1
    )
    return rows


def back_keys(head, dx, qm, pt, st, pc, sc, acc):
    def put(keys, cols, value):
        if head == 0:
            acc[keys, cols] = value
        else:
            acc[keys, cols] += value

    left, right = slice(0, 128), slice(128, 256)
    put(slice(0, 2048), left, dot(st[...], qm[head], NN) * SCALE)
    put(slice(0, 2048), right, dot(pt[...], dx[head, :, :128], NN))
    for c in range(2):
        keys = slice(2048 + 256 * c, 2304 + 256 * c)
        rows = slice(512 + 256 * c, 768 + 256 * c)
        put(keys, left, dot(sc[c], qm[head, rows], NN) * SCALE)
        put(keys, right, dot(pc[c], dx[head, rows, :128], NN))


BACK_SCRATCH = [
    pltpu.VMEM((2, 1024, 256), bf16),
    pltpu.VMEM((2, 1024, 256), bf16),
    pltpu.VMEM((2, 2560, 256), bf16),
    pltpu.VMEM((2560, 256), bf16),
    pltpu.VMEM((2, 1024, 256), bf16),
    pltpu.VMEM((2, 1024, 128), bf16),
    pltpu.VMEM((128, 2560), bf16),
    pltpu.VMEM((2048, 1024), bf16),
    pltpu.VMEM((2048, 1024), bf16),
    pltpu.VMEM((2, 256, 256), bf16),
    pltpu.VMEM((2, 256, 256), bf16),
    pltpu.VMEM((512, 512), bf16),
    pltpu.VMEM((2, 256, 256), bf16),
    pltpu.VMEM((2560, 256), f32),
]


def back_specs():
    def pair(rows):
        return pl.BlockSpec((rows, 128), lambda i: (0, i))

    def once(*shape):
        return pl.BlockSpec(shape, lambda i: (0,) * len(shape), pipeline_mode=pl.Buffered(1))

    return [
        pair(1024), pair(2560), pair(2560), pair(1024), pair(1024),
        pl.BlockSpec((2, 1024, 128), lambda i: (i, 0, 0)),
        once(2560, 128), once(768, 2560),
    ]


def back_alone_kernel(q, k, v, d, o, side, kb, xt, dq, cont, partial_rows, whole, *scratch):
    (qx, qd, kx, vx, dx, qm, kt, pt, st, pc, sc, bown, bcont, acc) = scratch
    back_fill(q, k, v, d, o, side, kb, qx, qd, kx, vx, dx, qm, kt, bown, bcont)
    rows = []
    for head in range(2):
        rows.append(back_head(head, qx, qd, kx, vx, dx, qm, kt, pt, st, pc, sc, bown, bcont))
        back_keys(head, dx, qm, pt, st, pc, sc, acc)
    delta = jnp.transpose(jnp.concatenate(rows, axis=0) * SCALE).astype(bf16)
    dq[...] = delta
    low = acc[...].astype(bf16)
    partial_rows[...] = low[:2048]
    cont[...] = low[2048:]
    grad = dot(xt[:, :512], delta[:512], NN) + dot(xt[:, 2048:], delta[512:], NN)
    whole[:, :128] = grad.astype(bf16)
    whole[:, 128:] = dot(xt[...], low, NN).astype(bf16)


def attend_back_alone(q, k, v, d, o, side, kb, xt):
    width = q.shape[1]
    count = width // 128
    return pl.pallas_call(
        back_alone_kernel,
        grid=(count,),
        in_specs=back_specs(),
        out_specs=[
            pl.BlockSpec((1024, 128), lambda i: (0, i)),
            pl.BlockSpec((512, 256), lambda i: (0, i)),
            pl.BlockSpec((2048, 256), lambda i: (0, i)),
            pl.BlockSpec((width, 384), lambda i: (0, i)),
        ],
        out_shape=[
            jax.ShapeDtypeStruct((1024, width), bf16),
            jax.ShapeDtypeStruct((512, 2 * width), bf16),
            jax.ShapeDtypeStruct((2048, 2 * width), bf16),
            jax.ShapeDtypeStruct((width, 3 * width), bf16),
        ],
        scratch_shapes=BACK_SCRATCH,
        compiler_params=params(60),
        cost_estimate=cost(100, 40),
    )(q, k, v, d, o, side, kb, xt)


PAIRS = 6
HALF_UP = 1920
AB_COPIES = 15
PAIR_COPIES = 11


def back_linked_kernel(
    q, k, v, d, o, side, kb, xt, xa, xb,
    dq, cont, own, gq, gk, gv, qrow, ga, gb,
    qx, qd, kx, vx, dx, qm, kt, pt, st, pc, sc, bown, bcont, acc,
    a_mine, a_x, a_y, a_z, a_q, b_mine, b_y, b_z, b_r,
    p_mine, p_other, c_in, y_in, z_in, r_in, keys_low, k_in, k_far, k_x, dw,
    lsem, ab_send, ab_recv, p_send, p_recv,
):
    step = pl.program_id(0)
    rep = lax.axis_index("rep")
    shard = lax.axis_index("shard")
    core = rep % 2
    x = rep // 2
    z = shard // 2
    y = shard % 2
    rep1 = rep + 1 - 2 * core
    to_rep = [None, {"rep": rep1}, {"rep": (rep + 2) % 4}, {"rep": (rep1 + 2) % 4}]
    to_y = {"shard": z * 2 + 1 - y}
    zs = [z, z + 1 - 2 * (z % 2), (z + 2) % 4, 3 - z]
    to_z = [None] + [{"shard": zs[j] * 2 + y} for j in range(1, 4)]

    def move(src, dst, send, recv, where):
        return pltpu.make_async_remote_copy(
            src_ref=src, dst_ref=dst, send_sem=send, recv_sem=recv,
            device_id=where, device_id_type=MESH,
        )

    def ab(index, src, dst, where):
        return move(src, dst, ab_send.at[index], ab_recv.at[index], where)

    def columns(which):
        return pl.ds(pl.multiple_of(which * HALF_UP, 128), HALF_UP)

    def copy_ax():
        return ab(0, xa.at[:, :, columns(1 - x)], a_x, to_rep[2])

    def copy_ay():
        return ab(1, a_mine.at[pl.ds(4, 4)], a_y, to_y)

    def copy_az(j):
        return ab(1 + j, a_mine.at[j], a_z.at[j - 1], to_z[j])

    def copy_aq(j):
        return ab(4 + j, a_q.at[0], a_q.at[j], to_rep[j])

    def copy_by():
        return ab(8, xb.at[pl.ds(4, 4)], b_y, to_y)

    def copy_bz(j):
        return ab(8 + j, b_mine.at[j], b_z.at[j - 1], to_z[j])

    def copy_br(j):
        return ab(11 + j, b_r.at[0], b_r.at[j], to_rep[j])

    def pair_copy(p, index, src, dst, where):
        return move(src, dst, p_send.at[p, index], p_recv.at[p, index], where)

    def copy_core(p):
        return pair_copy(p, 0, p_other, c_in.at[p], to_rep[1])

    def copy_y(p):
        return pair_copy(p, 1, p_mine.at[p % 2, pl.ds(4, 4)], y_in.at[p], to_y)

    def copy_z(p, j):
        return pair_copy(p, 1 + j, p_mine.at[p % 2, j], z_in.at[p, j - 1], to_z[j])

    def copy_rep(p, j):
        return pair_copy(p, 4 + j, r_in.at[p, 0], r_in.at[p, j], to_rep[j])

    def copy_near(p):
        return pair_copy(p, 8, keys_low.at[p % 2, pl.ds(512, 512)], k_in.at[p], to_rep[1])

    def copy_far(p):
        return pair_copy(p, 9, keys_low.at[p % 2, pl.ds(1536, 512)], k_far.at[p], to_rep[1])

    def copy_turn(p):
        return pair_copy(p, 10, keys_low.at[p % 2, pl.ds(1024, 512)], k_x.at[p], to_rep[2])

    def add(left, right):
        return (left.astype(f32) + right.astype(f32)).astype(bf16)

    def after_core(p):
        slot = p % 2
        copy_core(p).wait()
        for i in range(8):
            p_mine[slot, i] = add(p_mine[slot, i], c_in[p, i])
        copy_y(p).start()
        copy_near(p).wait()
        copy_far(p).wait()
        keys_low[slot, 1024:1536] = add(keys_low[slot, 1024:1536], k_far[p])
        copy_turn(p).start()

    def after_y(p):
        slot = p % 2
        copy_y(p).wait()
        for i in range(4):
            p_mine[slot, i] = add(p_mine[slot, i], y_in[p, i])
        for j in range(1, 4):
            copy_z(p, j).start()
        copy_turn(p).wait()
        total = keys_low[slot, :512].astype(f32) + k_in[p].astype(f32) + k_x[p].astype(f32)
        own[:, pl.ds(pl.multiple_of(p * 256, 256), 256)] = total.astype(bf16)

    def after_z(p):
        slot = p % 2
        for j in range(1, 4):
            copy_z(p, j).wait()
        total = p_mine[slot, 0].astype(f32)
        for j in range(3):
            total = total + z_in[p, j].astype(f32)
        r_in[p, 0] = total.astype(bf16)
        for j in range(1, 4):
            copy_rep(p, j).start()

    def after_rep(p):
        for j in range(1, 4):
            copy_rep(p, j).wait()
        at = pl.ds(pl.multiple_of(p * 128, 128), 128)
        for half, (one, two) in enumerate(((0, 2), (1, 3))):
            total = add(r_in[p, one], r_in[p, two])
            rows = core if half == 0 else 1 - core
            rows = pl.ds(pl.multiple_of(rows * 48, 16), 48)
            for j, out in enumerate((gq, gk, gv)):
                out[rows, at] = total[:48, 128 * j : 128 * j + 128]
            if half == 0:
                qrow[:, at] = total[48:64, :128]

    @pl.when(step == 0)
    def _():
        barrier = pltpu.get_barrier_semaphore()
        for place in to_rep[1:] + [to_y] + to_z[1:]:
            pl.semaphore_signal(barrier, inc=1, device_id=place, device_id_type=MESH)
        pl.semaphore_wait(barrier, 7)
        copy_by().start()
        copy_ax().start()
        for copy in (
            pltpu.make_async_copy(xa.at[:, :, columns(x)], a_mine, lsem.at[0]),
            pltpu.make_async_copy(xb.at[pl.ds(0, 4)], b_mine, lsem.at[1]),
        ):
            copy.start()

    back_fill(q, k, v, d, o, side, kb, qx, qd, kx, vx, dx, qm, kt, bown, bcont)
    turned = []
    turned.append(back_head(0, qx, qd, kx, vx, dx, qm, kt, pt, st, pc, sc, bown, bcont))
    back_keys(0, dx, qm, pt, st, pc, sc, acc)

    @pl.when(step > 0)
    def _():
        after_core(step - 1)

    @pl.when(step > 1)
    def _():
        after_z(step - 2)

    @pl.when(step == 2)
    def _():
        copy_ax().wait()
        pltpu.make_async_copy(xa.at[:, :, columns(x)], a_mine, lsem.at[0]).wait()

        def sum_piece(i, carry):
            a_mine[i] = add(a_mine[i], a_x[i])
            return carry

        lax.fori_loop(0, 8, sum_piece, 0)
        copy_ay().start()

    @pl.when(step == 3)
    def _():
        copy_ay().wait()

        def sum_piece(i, carry):
            a_mine[i] = add(a_mine[i], a_y[i])
            return carry

        lax.fori_loop(0, 4, sum_piece, 0)
        for j in range(1, 4):
            copy_az(j).start()

    turned.append(back_head(1, qx, qd, kx, vx, dx, qm, kt, pt, st, pc, sc, bown, bcont))
    back_keys(1, dx, qm, pt, st, pc, sc, acc)

    @pl.when(step > 0)
    def _():
        after_y(step - 1)

    @pl.when(step > 1)
    def _():
        after_rep(step - 2)

    @pl.when(step == 1)
    def _():
        copy_by().wait()
        pltpu.make_async_copy(xb.at[pl.ds(0, 4)], b_mine, lsem.at[1]).wait()

        def sum_piece(i, carry):
            b_mine[i] = add(b_mine[i], b_y[i])
            return carry

        lax.fori_loop(0, 4, sum_piece, 0)
        for j in range(1, 4):
            copy_bz(j).start()

    @pl.when(step == 3)
    def _():
        for j in range(1, 4):
            copy_bz(j).wait()
        total = b_mine[0].astype(f32)
        for j in range(3):
            total = total + b_z[j].astype(f32)
        b_r[0] = total.astype(bf16)
        for j in range(1, 4):
            copy_br(j).start()

    @pl.when(step == 4)
    def _():
        for j in range(1, 4):
            copy_br(j).wait()
        gb[core] = add(b_r[0], b_r[2])
        gb[1 - core] = add(b_r[1], b_r[3])
        for j in range(1, 4):
            copy_az(j).wait()
        total = a_mine[0].astype(f32)
        for j in range(3):
            total = total + a_z[j].astype(f32)
        a_q[0] = total.astype(bf16)
        for j in range(1, 4):
            copy_aq(j).start()

    delta = jnp.transpose(jnp.concatenate(turned, axis=0) * SCALE)
    low = delta.astype(bf16)
    dq[...] = low
    slot = step % 2
    keys_low[slot] = acc[:2048].astype(bf16)
    tail = acc[2048:].astype(bf16)
    cont[...] = tail
    copy_near(step).start()
    copy_far(step).start()
    grad = dot(xt[:, :512], low[:512], NN) + dot(xt[:, 2048:], low[512:], NN)
    dw[:, :128] = grad.astype(bf16)
    dw[:, 128:] = (dot(xt[:, :2048], keys_low[slot], NN) + dot(xt[:, 2048:], tail, NN)).astype(bf16)
    extra = jnp.sum(low.astype(f32), axis=0, keepdims=True)
    extra = jnp.concatenate([jnp.broadcast_to(extra, (16, 128)), jnp.zeros((16, 256), f32)], axis=1)
    extra = extra.astype(bf16)
    for i in range(8):
        place = (zs[i % 4] * 2 + (y if i < 4 else 1 - y)) * 2
        at = pl.multiple_of((place + core) * 48, 16)
        p_mine[slot, i, :48] = dw[pl.ds(at, 48)]
        p_mine[slot, i, 48:] = extra
        at = pl.multiple_of((place + 1 - core) * 48, 16)
        p_other[i, :48] = dw[pl.ds(at, 48)]
        p_other[i, 48:] = extra
    copy_core(step).start()

    @pl.when(step == PAIRS - 1)
    def _():
        after_z(PAIRS - 2)
        after_core(PAIRS - 1)
        for j in range(1, 4):
            copy_aq(j).wait()
        for j, (rows, which) in enumerate(
            ((core, x), (1 - core, x), (core, 1 - x), (1 - core, 1 - x))
        ):
            rows = pl.ds(pl.multiple_of(rows * 48, 16), 48)
            ga[rows, columns(which)] = a_q[j]
        after_y(PAIRS - 1)
        after_rep(PAIRS - 2)
        after_z(PAIRS - 1)
        after_rep(PAIRS - 1)


def attend_back(q, k, v, d, o, side, kb, xt, xa, xb):
    width = q.shape[1]
    count = width // 128
    full = xa.shape[2]

    def held(*shape):
        return pl.BlockSpec(shape, lambda i: (0,) * len(shape), pipeline_mode=pl.Buffered(1))

    def vm(*shape):
        return pltpu.VMEM(shape, bf16)

    def out(*shape):
        return jax.ShapeDtypeStruct(shape, bf16)

    sem = pltpu.SemaphoreType.DMA
    piece = (64, 384)
    return pl.pallas_call(
        back_linked_kernel,
        grid=(count,),
        in_specs=back_specs() + [ANY, ANY],
        out_specs=[
            pl.BlockSpec((1024, 128), lambda i: (0, i)),
            pl.BlockSpec((512, 256), lambda i: (0, i)),
            held(512, 2 * width), held(96, width), held(96, width), held(96, width),
            held(16, width), held(96, full), held(2, 208, width),
        ],
        out_shape=[
            out(1024, width), out(512, 2 * width), out(512, 2 * width), out(96, width),
            out(96, width), out(96, width), out(16, width), out(96, full), out(2, 208, width),
        ],
        scratch_shapes=BACK_SCRATCH
        + [
            vm(8, 48, HALF_UP), vm(8, 48, HALF_UP), vm(4, 48, HALF_UP), vm(3, 48, HALF_UP),
            vm(4, 48, HALF_UP), vm(4, 208, width), vm(4, 208, width), vm(3, 208, width),
            vm(4, 208, width),
            vm(2, 8, *piece), vm(8, *piece), vm(PAIRS, 8, *piece), vm(PAIRS, 4, *piece),
            vm(PAIRS, 3, *piece), vm(PAIRS, 4, *piece), vm(2, 2048, 256), vm(PAIRS, 512, 256),
            vm(PAIRS, 512, 256), vm(PAIRS, 512, 256), vm(width, 384),
            sem((2,)), sem((AB_COPIES,)), sem((AB_COPIES,)), sem((PAIRS, PAIR_COPIES)),
            sem((PAIRS, PAIR_COPIES)),
        ],
        compiler_params=params(62, collective_id=2, has_side_effects=True),
        cost_estimate=cost(100, 40),
    )(q, k, v, d, o, side, kb, xt, xa, xb)


def gelu_parts(x):
    bell = jnp.exp2(x * x * (-0.5 * LOG2E))
    t = 1.0 / (1.0 + (0.3275911 * 0.7071067811865476) * jnp.abs(x))
    poly = 0.5 * 1.061405429
    for term in (-1.453152027, 1.421413741, -0.284496736, 0.254829592):
        poly = poly * t + 0.5 * term
    below = poly * t * bell
    phi = jnp.where(x >= 0.0, 1.0 - below, below)
    return x * phi, phi + x * bell * 0.3989422804014327


def normed_of(values):
    centered = values - jnp.mean(values, axis=-1, keepdims=True)
    spread = lax.rsqrt(jnp.mean(centered * centered, axis=-1, keepdims=True) + EPSILON)
    return centered * spread, spread


def norm_back(incoming, normed, spread, gain):
    scaled = incoming * gain
    centered = scaled - jnp.mean(scaled, axis=-1, keepdims=True)
    return (centered - normed * jnp.mean(scaled * normed, axis=-1, keepdims=True)) * spread


FCH = 768


def forward_back_kernel(
    order, mixed, tok, cot, teach, keep, scale, vecs, upb,
    ua, ub, uc, ud, da, db, dc, dd,
    result, hid_o, act_o, ddel_o, udel_o, adel_o, mdel_o, sums,
    wa, wu, wd, slope, sems,
):
    step = pl.program_id(0)
    width = tok.shape[1]
    hidden_units = upb.shape[1]

    def arrivals(wait):
        for group, (up_part, down_part) in enumerate(((ua, da), (ub, db), (uc, dc), (ud, dd))):
            for j in range(4):
                place = order[group * 4 + j]
                at = pl.ds(pl.multiple_of(place * 48, 16), 48)
                far = pl.ds(pl.multiple_of(place * 192, 64), 192)
                for copy in (
                    pltpu.make_async_copy(
                        up_part.at[j, :, pl.ds(0, width)], wa.at[at], sems.at[0, group, j]
                    ),
                    pltpu.make_async_copy(
                        up_part.at[j, :, pl.ds(width, hidden_units)], wu.at[at],
                        sems.at[1, group, j],
                    ),
                    pltpu.make_async_copy(down_part.at[j], wd.at[far], sems.at[2, group, j]),
                ):
                    if wait:
                        copy.wait()
                    else:
                        copy.start()

    @pl.when(step == 0)
    def _():
        arrivals(False)
        sums[...] = jnp.zeros_like(sums)
        arrivals(True)

    def vector(index):
        return vecs[index : index + 1].astype(f32)

    attn_b, gain1, shift1, down_b, gain2, shift2 = [vector(i) for i in range(2, 8)]

    def add_sum(index, values):
        sums[index : index + 1] += jnp.sum(values, axis=0, keepdims=True)

    x = tok[...].astype(f32)
    branch = attn_b + x + dot(mixed[...], wa[...], NN)
    normed1, inv1 = normed_of(branch)
    hidden = normed1 * gain1 + shift1
    hid_low = hidden.astype(bf16)
    hid_o[...] = hid_low
    for c in range(hidden_units // FCH):
        cols = slice(c * FCH, c * FCH + FCH)
        value, rise = gelu_parts(dot(hid_low, wu[:, cols], NN) + upb[:, cols].astype(f32))
        act_o[:, cols] = value.astype(bf16)
        slope[:, cols] = rise.astype(bf16)
    second = hidden + dot(act_o[...], wd[...], NN) + down_b
    normed2, inv2 = normed_of(second)
    final = normed2 * gain2 + shift2
    result[...] = final.astype(bf16)
    errors = final - teach[...].astype(f32)
    kept = errors * jnp.concatenate([keep[...]] * (width // 128), axis=1)
    add_sum(6, kept * errors)
    grad = cot[...].astype(f32) + kept * (2.0 * scale[...])
    add_sum(1, grad * normed2)
    add_sum(2, grad)
    grad2 = norm_back(grad, normed2, inv2, gain2)
    ddel = grad2.astype(bf16)
    ddel_o[...] = ddel
    add_sum(0, ddel.astype(f32))
    for c in range(hidden_units // FCH):
        cols = slice(c * FCH, c * FCH + FCH)
        delta = dot(ddel, wd[cols], NT) * slope[:, cols].astype(f32)
        low = delta.astype(bf16)
        udel_o[:, cols] = low
        add_sum(8 + c, low.astype(f32))
    hgrad = grad2 + dot(udel_o[...], wu[...], NT)
    add_sum(4, hgrad * normed1)
    add_sum(5, hgrad)
    grad1 = norm_back(hgrad, normed1, inv1, gain1)
    adel = grad1.astype(bf16)
    adel_o[...] = adel
    add_sum(3, adel.astype(f32))
    mdel = dot(adel, wa[...], NT).astype(bf16)
    mdel_o[...] = mdel
    add_sum(7, mdel.astype(f32))


def forward_back(order, mixed, tok, cot, teach, keep, scale, vecs, upb, ups, downs):
    rows, width = tok.shape
    hidden_units = upb.shape[1]
    half = 512

    def block(columns):
        return pl.BlockSpec((half, columns), lambda i, *_: (i, 0))

    def fixed(*shape):
        return pl.BlockSpec(shape, lambda i, *_: (0,) * len(shape))

    def out(columns):
        return jax.ShapeDtypeStruct((rows, columns), bf16)

    return pl.pallas_call(
        forward_back_kernel,
        grid_spec=pltpu.PrefetchScalarGridSpec(
            num_scalar_prefetch=1,
            grid=(rows // half,),
            in_specs=[
                block(width), block(width), block(width), block(width),
                block(128), fixed(1, 1), fixed(8, width), fixed(1, hidden_units),
            ] + [ANY] * 8,
            out_specs=[
                block(width), block(width), block(hidden_units), block(width),
                block(hidden_units), block(width), block(width), fixed(16, width),
            ],
            scratch_shapes=[
                pltpu.VMEM((width, width), bf16),
                pltpu.VMEM((width, hidden_units), bf16),
                pltpu.VMEM((hidden_units, width), bf16),
                pltpu.VMEM((half, hidden_units), bf16),
                pltpu.SemaphoreType.DMA((3, 4, 4)),
            ],
        ),
        out_shape=[
            out(width), out(width), out(hidden_units), out(width), out(hidden_units),
            out(width), out(width), jax.ShapeDtypeStruct((16, width), f32),
        ],
        compiler_params=params(60),
        cost_estimate=cost(32.6, 30),
    )(order, mixed, tok, cot, teach, keep, scale, vecs, upb, *ups, *downs)


def up_grad_kernel(order, mixed, adel, hid, udel, mine, other, whole):
    step = pl.program_id(0)

    @pl.when(step == 0)
    def _():
        whole[...] = dot(mixed[...], adel[...], TN).astype(bf16)

    @pl.when(step > 0)
    def _():
        whole[...] = dot(hid[...], udel[...], TN).astype(bf16)

    store_pieces(order, whole, mine, other, 48)


def store_pieces(order, source, mine, other, piece):
    for i in range(8):
        at = pl.multiple_of(order[i] * piece, 16)
        mine[i, :piece] = source[pl.ds(at, piece)]
        at = pl.multiple_of(order[i + 8] * piece, 16)
        other[i, :piece] = source[pl.ds(at, piece)]


def up_grad(order, mixed, adel, hid, udel):
    rows, width = adel.shape
    columns = udel.shape[1]
    shape = jax.ShapeDtypeStruct((8, 48, width + columns), bf16)
    out = pl.BlockSpec((8, 48, width), lambda i, *_: (0, 0, i))
    full = pl.BlockSpec((rows, width), lambda i, *_: (0, 0))
    return pl.pallas_call(
        up_grad_kernel,
        grid_spec=pltpu.PrefetchScalarGridSpec(
            num_scalar_prefetch=1,
            grid=(1 + columns // width,),
            in_specs=[
                full, full, full,
                pl.BlockSpec((rows, width), lambda i, *_: (0, jnp.maximum(i - 1, 0))),
            ],
            out_specs=[out, out],
            scratch_shapes=[pltpu.VMEM((width, width), bf16)],
        ),
        out_shape=[shape, shape],
        compiler_params=params(),
        cost_estimate=cost(6, 20),
    )(order, mixed, adel, hid, udel)


def down_grad_kernel(order, act, ddel, sums, mine, other, whole):
    whole[...] = dot(act[...], ddel[...], TN).astype(bf16)
    store_pieces(order, whole, mine, other, 192)
    low = sums[...].astype(bf16)
    for i in range(8):
        mine[i, 192:] = low
        other[i, 192:] = low


def down_grad(order, act, ddel, sums):
    rows, columns = ddel.shape
    total = act.shape[1]
    chunk = 256
    shape = jax.ShapeDtypeStruct((8, 208, columns), bf16)
    out = pl.BlockSpec((8, 208, chunk), lambda i, *_: (0, 0, i))
    return pl.pallas_call(
        down_grad_kernel,
        grid_spec=pltpu.PrefetchScalarGridSpec(
            num_scalar_prefetch=1,
            grid=(columns // chunk,),
            in_specs=[
                pl.BlockSpec(act.shape, lambda i, *_: (0, 0)),
                pl.BlockSpec((rows, chunk), lambda i, *_: (0, i)),
                pl.BlockSpec((16, chunk), lambda i, *_: (0, i)),
            ],
            out_specs=[out, out],
            scratch_shapes=[pltpu.VMEM((total, chunk), bf16)],
        ),
        out_shape=[shape, shape],
        compiler_params=params(),
        cost_estimate=cost(5, 20),
    )(order, act, ddel, sums)


def tokens_grad_kernel(adel, dq, own, cont, wq, wk, wv, out):
    for half, low in enumerate((own, cont)):
        rows = slice(512 * half, 512 * half + 512)
        total = adel[rows].astype(f32) + dot(dq[rows], wq[...], NT)
        for p in range(wq.shape[1] // 128):
            cols = slice(128 * p, 128 * p + 128)
            both = jnp.concatenate([wk[:, cols], wv[:, cols]], axis=1)
            total = total + dot(low[:, 256 * p : 256 * p + 256], both, NT)
        out[rows] = total.astype(bf16)


def tokens_grad(adel, dq, own, cont, wq, wk, wv):
    args = (adel, dq, own, cont, wq, wk, wv)
    return pl.pallas_call(
        tokens_grad_kernel,
        grid=(1,),
        in_specs=[pl.BlockSpec(a.shape, lambda i: (0, 0)) for a in args],
        out_specs=pl.BlockSpec(adel.shape, lambda i: (0, 0)),
        out_shape=jax.ShapeDtypeStruct(adel.shape, bf16),
        compiler_params=params(),
        cost_estimate=cost(3.6, 12),
    )(*args)


def swap(values, axis, bit):
    size = lax.axis_size(axis)
    return lax.ppermute(values, axis, [(i, i ^ bit) for i in range(size)])


def local(
    tokens, cotangent, teacher, valid_mask, valid_count,
    query_weight, query_bias, key_weight, value_weight, value_bias,
    attn_weight, attn_bias, first_gain, first_shift,
    up_weight, up_bias, down_weight, down_bias, second_gain, second_shift,
):
    rows, width = tokens.shape[2:]
    shards = lax.axis_size("shard")
    split = shards == 8
    rep = lax.axis_index("rep")
    shard = lax.axis_index("shard")
    core = rep % 2
    z, y = shard // 2, shard % 2
    tok = tokens.reshape(rows, width)
    keep = valid_mask.reshape(rows)
    if split:
        i = jnp.arange(16, dtype=jnp.int32)
        order = (((z ^ (i % 4)) * 2 + (y ^ (i // 4 % 2))) * 2 + (core ^ (i // 8))).astype(jnp.int32)
    else:
        order = jnp.arange(16, dtype=jnp.int32)

    small = [
        query_bias, value_bias, attn_bias, first_gain, first_shift, down_bias, second_gain,
        second_shift, up_bias,
    ]
    part = query_bias.shape[0]
    vec = jnp.concatenate([v[None] for v in small], axis=1)[0]
    keep_low = keep[:PPIECE].astype(f32).reshape(4, 128)
    if split:
        keep_low = jnp.concatenate([keep_low, keep_low])
        vec = jnp.pad(vec, (0, 2048 - vec.shape[0])).reshape(16, 128)
        wq, wk, wv, vecs, oth, others_keep = first_gather(
            query_weight, key_weight, value_weight, vec, tok, keep_low
        )
        vecs = vecs.reshape(8, 2048)
    else:
        wq, wk, wv, vecs = [
            lax.all_gather(w, "shard", axis=0, tiled=True)
            for w in (query_weight, key_weight, value_weight, vec[None])
        ]
        prompt = tok[:PPIECE]
        oth = jnp.concatenate([swap(prompt, "rep", bit) for bit in (1, 2, 3)])
        others_keep = jnp.stack([swap(keep_low, "rep", bit) for bit in (1, 2, 3)])
    others_keep = others_keep[:, :4].reshape(3 * PPIECE)
    upb = vecs[:, 8 * part : 8 * part + up_bias.shape[0]].reshape(1, -1)
    vecs = vecs[:, : 8 * part].reshape(shards, 8, part).transpose(1, 0, 2).reshape(8, width)

    if split:
        up_half = jnp.concatenate(
            [attn_weight.reshape(2, 48, width), up_weight.reshape(2, 48, -1)], axis=2
        )
        down_half = down_weight.reshape(2, 192, width)
        up_half, down_half, wq = lax.optimization_barrier((up_half, down_half, wq))

        def gather(half):
            half = lax.dynamic_index_in_dim(half, core, 0, keepdims=False)
            near = jnp.stack([half] + [swap(half, "shard", 2 * d) for d in (1, 2, 3)])
            far = swap(near, "shard", 1)
            return near, far, swap(near, "rep", 1), swap(far, "rep", 1)

        ups, downs = gather(up_half), gather(down_half)
    else:
        full = jnp.concatenate(
            [
                lax.all_gather(w, "shard", axis=0, tiled=True)
                for w in (attn_weight, up_weight)
            ],
            axis=1,
        ).reshape(4, 4, 48, -1)
        ups = [full[j] for j in range(4)]
        full = lax.all_gather(down_weight, "shard", axis=0, tiled=True).reshape(4, 4, 192, width)
        downs = [full[j] for j in range(4)]

    q, k, v, xt, qn, kn = project(tok, oth, wq, wk, wv, vecs[0:1], vecs[1:2])
    all_keep = jnp.concatenate(
        [keep[:PPIECE].astype(f32), others_keep, keep[PPIECE:].astype(f32)]
    )
    bias = jnp.where(all_keep > 0.5, 0.0, NEGATIVE)
    brow = jnp.broadcast_to(bias[None], (8, bias.shape[0]))
    lane = jnp.arange(128)[None]
    kb = jnp.where(lane == 0, bias[:, None], jnp.where(lane < 4, 1.0, 0.0)).astype(bf16)
    groups = 3
    pairs = width // 128 // groups
    outs = ()
    for g in range(groups):
        outs = attend(q, k, v, kb, brow, qn, kn, outs, g * pairs, pairs)
    mixed, sides = outs

    keep_wide = jnp.broadcast_to(keep.astype(f32)[:, None], (rows, 128))
    scale = (1.0 / valid_count.astype(f32)).reshape(1, 1)
    result, hid, act, ddel, udel, adel, mdel, sums = forward_back(
        order, mixed, tok, cotangent.reshape(rows, width), teacher.reshape(rows, width),
        keep_wide, scale, vecs, upb, ups, downs,
    )
    down_mine, down_other = down_grad(order, act, ddel, sums)
    up_mine, up_other = up_grad(order, mixed, adel, hid, udel)
    if split:
        down_sum = (down_mine.astype(f32) + swap(down_other, "rep", 1).astype(f32)).astype(bf16)
        up_sum = (up_mine.astype(f32) + swap(up_other, "rep", 1).astype(f32)).astype(bf16)
        dq, cont, own, query_low, key_low, value_low, qrow, up_low, down_low = attend_back(
            q, k, v, mdel, mixed, sides, kb, xt, up_sum, down_sum
        )
        query_grad, key_grad, value_grad = [g.astype(f32) for g in (query_low, key_low, value_low)]
        up_all = up_low.astype(f32)
        down_all = down_low[:, :192].astype(f32).reshape(-1, width)
        sums = down_low[0, 192:].astype(f32)
        query_row = qrow[0].astype(f32)
    else:
        dq, cont, partial_rows, whole = attend_back_alone(q, k, v, mdel, mixed, sides, kb, xt)

        def scatter(part):
            part = lax.psum_scatter(part, "shard", scatter_dimension=0, tiled=True)
            return lax.psum(part, "rep").astype(f32)

        def joined(mine, other, piece):
            return jnp.concatenate([mine, other])[:, :piece].reshape(16 * piece, -1)

        turned = partial_rows.reshape(2, 2, PPIECE, -1)
        turned = jnp.where(core == 1, turned[:, ::-1], turned)
        turned = jnp.where(rep // 2 == 1, turned[::-1], turned)
        own = lax.psum_scatter(
            turned.reshape(4 * PPIECE, -1), "rep", scatter_dimension=0, tiled=True
        )
        whole = scatter(whole).reshape(part, width // 128, 3, 128)
        query_grad, key_grad, value_grad = [whole[:, :, j].reshape(part, width) for j in range(3)]
        up_all = scatter(joined(up_mine, up_other, 48))
        down_all = scatter(joined(down_mine, down_other, 192))
        sums = lax.psum(sums, ("rep", "shard"))
        query_row = lax.psum(jnp.sum(dq.astype(f32), axis=0), ("rep", "shard"))
    token_grad = tokens_grad(adel, dq, own, cont, wq, wk, wv)

    def owned(row):
        return lax.dynamic_slice(row, (shard * part,), (part,))

    up_part = up_bias.shape[0]
    loss = jnp.sum(sums[6]) / valid_count.astype(f32)
    return (
        result.reshape(tokens.shape),
        loss,
        token_grad.reshape(tokens.shape),
        query_grad,
        owned(query_row),
        key_grad,
        value_grad,
        owned(sums[7]),
        up_all[:, :width],
        owned(sums[3]),
        owned(sums[4]),
        owned(sums[5]),
        up_all[:, width:],
        lax.dynamic_slice(sums[8:12].reshape(-1), (shard * up_part,), (up_part,)),
        down_all,
        owned(sums[0]),
        owned(sums[1]),
        owned(sums[2]),
    )


def solution(mesh):
    wide = P("shard", "rep", None, None)
    matrix, vector = P("shard", None), P("shard")
    return jax.shard_map(
        local,
        mesh=mesh,
        in_specs=(
            wide, wide, wide, P("shard", "rep", None), P(),
            matrix, vector, matrix, matrix, vector, matrix, vector, vector, vector,
            matrix, vector, matrix, vector, vector, vector,
        ),
        out_specs=(
            wide, P(), wide,
            matrix, vector, matrix, matrix, vector, matrix, vector, vector, vector,
            matrix, vector, matrix, vector, vector, vector,
        ),
        check_vma=False,
    )
```

```python
import functools

import jax
import jax.numpy as jnp
from jax import lax
from jax.experimental import pallas as pl
from jax.experimental.pallas import tpu as pltpu
from jax.sharding import PartitionSpec as P

HDIM = 64
PPIECE = 512
CLEN = 256
EPSILON = 1e-05
NEGATIVE = -1e30
LOG2E = 1.4426950408889634
SCALE = 1.0 / 8.0
LIMIT = 100.0

f32 = jnp.float32
bf16 = jnp.bfloat16
NT = (((1,), (1,)), ((), ()))
NN = (((1,), (0,)), ((), ()))
TN = (((0,), (0,)), ((), ()))
ANY = pl.BlockSpec(memory_space=pl.ANY)
MESH = pl.DeviceIdType.MESH


def dot(left, right, dims):
    return lax.dot_general(left, right, dims, preferred_element_type=f32)


def params(mib=56, **more):
    return pltpu.CompilerParams(vmem_limit_bytes=mib * 2**20, **more)


def cost(gflop, mbytes):
    return pl.CostEstimate(
        flops=int(gflop * 1e9), bytes_accessed=int(mbytes * 1e6), transcendentals=0
    )


def lane_of(rows):
    return lax.broadcasted_iota(jnp.int32, (rows, 128), 1)


def split3(values):
    hi = values.astype(bf16).astype(f32)
    mid = (values - hi).astype(bf16).astype(f32)
    low = values - hi - mid
    return hi, mid, low


def side_lanes(first, values):
    lane = lane_of(values.shape[0])
    hi, mid, low = split3(values)
    out = jnp.where(lane == 1, -hi, jnp.where(lane == 2, -mid, jnp.where(lane == 3, -low, 0.0)))
    return jnp.where(lane == 0, first, out).astype(bf16)


def gather_kernel(
    wq, wk, wv, vec, tok, keep, up_own,
    fq, fk, fv, fvec, ptok, pkeep, up_full,
    asend, arecv, local_sem, zrecv, yrecv, crecv, usend, dsend, ysend, csend, tsend, trecv,
):
    depth = 4
    rep = lax.axis_index("rep")
    shard = lax.axis_index("shard")
    core = rep % 2
    z = shard // 2
    y = shard % 2
    other_core = {"rep": rep + 1 - 2 * core}
    other_x = {"rep": (rep + 2) % 4}
    other_y = {"shard": z * 2 + 1 - y}
    up = {"shard": (shard + 2) % 8}
    down = {"shard": (shard + 6) % 8}

    barrier = pltpu.get_barrier_semaphore()
    for place in (other_core, other_x, other_y):
        pl.semaphore_signal(barrier, inc=1, device_id=place, device_id_type=MESH)

    @pl.when(z < depth - 1)
    def _():
        pl.semaphore_signal(barrier, inc=1, device_id=up, device_id_type=MESH)

    @pl.when(z > 0)
    def _():
        pl.semaphore_signal(barrier, inc=1, device_id=down, device_id_type=MESH)

    inner = jnp.where((z > 0) & (z < depth - 1), 5, 4)
    pl.semaphore_wait(barrier, inner)

    sources = (wq, wk, wv, vec)
    targets = (fq, fk, fv, fvec)

    def place_of(u, zz, yy, cc):
        if u == 3:
            return targets[u].at[zz * 2 + yy]
        return targets[u].at[(zz * 2 + yy) * 2 + cc]

    def own_of(u):
        return sources[u] if u == 3 else sources[u].at[core]

    def move(src, dst, send, recv, where):
        return pltpu.make_async_remote_copy(
            src_ref=src, dst_ref=dst, send_sem=send, recv_sem=recv,
            device_id=where, device_id_type=MESH,
        )

    def to_up(u, zz, src):
        return move(src, place_of(u, zz, y, core), usend.at[u, zz], zrecv.at[u, zz], up)

    def to_down(u, zz, src):
        return move(src, place_of(u, zz, y, core), dsend.at[u, zz], zrecv.at[u, zz], down)

    def to_y(u, zz, src):
        return move(src, place_of(u, zz, y, core), ysend.at[u, zz], yrecv.at[u, zz], other_y)

    def to_core(u, zz, yy):
        at = place_of(u, zz, yy, core)
        index = zz * 2 + yy
        return move(at, at, csend.at[u, index], crecv.at[u, index], other_core)

    for u in range(4):
        @pl.when(z < depth - 1)
        def _():
            to_up(u, z, own_of(u)).start()

        @pl.when(z > 0)
        def _():
            to_down(u, z, own_of(u)).start()

        to_y(u, z, own_of(u)).start()

    prompt = tok.at[pl.ds(0, PPIECE)]
    copies = [
        move(prompt, ptok.at[1], tsend.at[0], trecv.at[0], other_x),
        move(keep, pkeep.at[1], tsend.at[1], trecv.at[1], other_x),
        move(prompt, ptok.at[0], tsend.at[2], trecv.at[2], other_core),
        move(keep, pkeep.at[0], tsend.at[3], trecv.at[3], other_core),
    ]
    for copy in copies:
        copy.start()
    locals_ = []
    for u in range(4):
        if u == 3:
            dst = fvec.at[shard]
        else:
            dst = targets[u].at[pl.ds(shard * 2, 2)]
        locals_.append(pltpu.make_async_copy(sources[u], dst, local_sem.at[u]))
        locals_[-1].start()

    columns = pl.ds(pl.multiple_of(rep // 2 * HALF_UP, 128), HALF_UP)

    def up_place(zz):
        return up_full.at[(zz * 2 + y) * 2 + core, :, columns]

    def up_up(zz, src):
        return move(src, up_place(zz), asend.at[0, zz], arecv.at[zz], up)

    def up_down(zz, src):
        return move(src, up_place(zz), asend.at[1, zz], arecv.at[zz], down)

    def up_start():
        src = up_own.at[core, :, columns]

        @pl.when(z < depth - 1)
        def _():
            up_up(z, src).start()

        @pl.when(z > 0)
        def _():
            up_down(z, src).start()

    def up_hop(step):
        @pl.when(z - step >= 0)
        def _():
            at = up_place(z - step)
            up_up(z - step, at).wait_recv()
            if step == 1:
                @pl.when(z < depth - 1)
                def _():
                    up_up(z - step, at).start()

        @pl.when(z + step < depth)
        def _():
            at = up_place(z + step)
            up_down(z + step, at).wait_recv()
            if step == 1:
                @pl.when(z > 0)
                def _():
                    up_down(z + step, at).start()

    for step in range(1, depth + 1):
        if step == 2:
            up_start()
        if step == 4:
            up_hop(1)
        for u in range(4):
            if step < depth:
                @pl.when(z - step >= 0)
                def _():
                    zz = z - step
                    at = place_of(u, zz, y, core)
                    to_up(u, zz, at).wait_recv()

                    @pl.when(z < depth - 1)
                    def _():
                        to_up(u, zz, at).start()

                    to_y(u, zz, at).start()
                    if u < 3:
                        to_core(u, zz, y).start()

                @pl.when(z + step < depth)
                def _():
                    zz = z + step
                    at = place_of(u, zz, y, core)
                    to_down(u, zz, at).wait_recv()

                    @pl.when(z > 0)
                    def _():
                        to_down(u, zz, at).start()

                    to_y(u, zz, at).start()
                    if u < 3:
                        to_core(u, zz, y).start()

        for u in range(4):
            def from_y(zz):
                at = targets[u].at[zz * 2 + 1 - y] if u == 3 else place_of(u, zz, 1 - y, core)
                move(at, at, ysend.at[u, zz], yrecv.at[u, zz], other_y).wait_recv()
                if u < 3:
                    to_core(u, zz, 1 - y).start()

            if step == 1:
                from_y(z)
            else:
                @pl.when(z - (step - 1) >= 0)
                def _():
                    from_y(z - (step - 1))

                @pl.when(z + (step - 1) < depth)
                def _():
                    from_y(z + (step - 1))

    up_hop(2)
    copies[0].wait_recv()
    copies[1].wait_recv()
    forward = [
        move(ptok.at[1], ptok.at[2], tsend.at[4], trecv.at[4], other_core),
        move(pkeep.at[1], pkeep.at[2], tsend.at[5], trecv.at[5], other_core),
    ]
    for copy in forward:
        copy.start()

    def others(act):
        for zz in range(depth):
            for yy in range(2):
                @pl.when((zz != z) | (yy != y))
                def _():
                    act(zz, yy)

    for u in range(3):
        def arrived(zz, yy):
            at = place_of(u, zz, yy, 1 - core)
            index = zz * 2 + yy
            move(at, at, csend.at[u, index], crecv.at[u, index], other_core).wait_recv()

        others(arrived)
    copies[2].wait_recv()
    copies[3].wait_recv()
    for copy in forward:
        copy.wait_recv()

    for copy in copies + forward:
        copy.wait_send()
    for zz in range(depth):
        at = up_place(zz)

        @pl.when((zz <= z) & (zz >= z - 1) & (z < depth - 1))
        def _():
            up_up(zz, at).wait_send()

        @pl.when((zz >= z) & (zz <= z + 1) & (z > 0))
        def _():
            up_down(zz, at).wait_send()

    for copy in locals_:
        copy.wait()
    for u in range(4):
        for zz in range(depth):
            at = place_of(u, zz, y, core)
            to_y(u, zz, at).wait_send()

            @pl.when((zz <= z) & (z < depth - 1))
            def _():
                to_up(u, zz, at).wait_send()

            @pl.when((zz >= z) & (z > 0))
            def _():
                to_down(u, zz, at).wait_send()

        if u < 3:
            others(lambda zz, yy: to_core(u, zz, yy).wait_send())


def first_gather(wq, wk, wv, vec, tok, keep, up_own):
    width = wq.shape[1]
    sem = pltpu.SemaphoreType.DMA
    halves = [w.reshape(2, 48, width) for w in (wq, wk, wv)]
    full = jax.ShapeDtypeStruct((16, 48, width), bf16)
    outs = pl.pallas_call(
        gather_kernel,
        in_specs=[ANY] * 7,
        out_specs=[ANY] * 7,
        out_shape=[
            full, full, full,
            jax.ShapeDtypeStruct((8, 16, 128), bf16),
            jax.ShapeDtypeStruct((3, PPIECE, width), bf16),
            jax.ShapeDtypeStruct((3, 8, 128), f32),
            jax.ShapeDtypeStruct((16, 48, up_own.shape[2]), bf16),
        ],
        scratch_shapes=[
            sem((2, 4)), sem((4,)), sem((4,)), sem((4, 4)), sem((4, 4)), sem((3, 8)), sem((4, 4)), sem((4, 4)),
            sem((4, 4)), sem((3, 8)), sem((6,)), sem((6,)),
        ],
        compiler_params=params(60, collective_id=1, has_side_effects=True),
        cost_estimate=cost(0, 20),
    )(*halves, vec, tok, keep, up_own)
    fq, fk, fv, fvec, ptok, pkeep, up_full = outs
    return (
        fq.reshape(width, width), fk.reshape(width, width), fv.reshape(width, width),
        fvec, ptok.reshape(3 * PPIECE, width), pkeep, up_full,
    )


class Link:
    def __init__(self):
        rep = lax.axis_index("rep")
        shard = lax.axis_index("shard")
        self.core = rep % 2
        self.x = rep // 2
        self.z = shard // 2
        self.y = shard % 2
        self.shard = shard
        self.to_core = {"rep": rep + 1 - 2 * self.core}
        self.to_x = {"rep": (rep + 2) % 4}
        self.to_y = {"shard": self.z * 2 + 1 - self.y}
        self.to_up = {"shard": (shard + 2) % 8}
        self.to_down = {"shard": (shard + 6) % 8}

    def greet(self):
        barrier = pltpu.get_barrier_semaphore()
        for place in (self.to_core, self.to_x, self.to_y):
            pl.semaphore_signal(barrier, inc=1, device_id=place, device_id_type=MESH)

        @pl.when(self.z < 3)
        def _():
            pl.semaphore_signal(barrier, inc=1, device_id=self.to_up, device_id_type=MESH)

        @pl.when(self.z > 0)
        def _():
            pl.semaphore_signal(barrier, inc=1, device_id=self.to_down, device_id_type=MESH)

        count = jnp.where((self.z > 0) & (self.z < 3), 5, 4)
        pl.semaphore_wait(barrier, count)


def move(src, dst, send, recv, where):
    return pltpu.make_async_remote_copy(
        src_ref=src, dst_ref=dst, send_sem=send, recv_sem=recv,
        device_id=where, device_id_type=MESH,
    )


class Spread:
    def __init__(self, own, full, sems):
        self.at = Link()
        self.own, self.full = own, full
        (
            self.local, self.zrecv, self.yrecv, self.usend, self.dsend, self.ysend,
            self.xrecv, self.xsend, self.crecv, self.csend,
        ) = sems

    def columns(self, xx):
        return pl.ds(pl.multiple_of(xx * HALF_UP, 128), HALF_UP)

    def place(self, u, zz, yy, cc, xx):
        index = (zz * 2 + yy) * 2 + cc
        if u == 0:
            return self.full[0].at[index, :, self.columns(xx)]
        return self.full[1].at[index]

    def mine(self, u, zz, yy):
        return self.place(u, zz, yy, self.at.core, self.at.x)

    def source(self, u):
        if u == 0:
            return self.own[0].at[self.at.core, :, self.columns(self.at.x)]
        return self.own[1].at[self.at.core]

    def up(self, u, zz, src):
        return move(
            src, self.mine(u, zz, self.at.y), self.usend.at[u, zz], self.zrecv.at[u, zz],
            self.at.to_up,
        )

    def down(self, u, zz, src):
        return move(
            src, self.mine(u, zz, self.at.y), self.dsend.at[u, zz], self.zrecv.at[u, zz],
            self.at.to_down,
        )

    def side(self, u, zz, src):
        return move(
            src, self.mine(u, zz, self.at.y), self.ysend.at[u, zz], self.yrecv.at[u, zz],
            self.at.to_y,
        )

    def across(self, zz, yy):
        at = self.mine(0, zz, yy)
        index = zz * 2 + yy
        return move(at, at, self.xsend.at[index], self.xrecv.at[index], self.at.to_x)

    def twin(self, kind, zz, yy):
        if kind == 1:
            at = self.place(0, zz, yy, self.at.core, 1 - self.at.x)
        else:
            at = self.mine(0 if kind == 0 else 1, zz, yy)
        index = zz * 2 + yy
        return move(
            at, at, self.csend.at[kind, index], self.crecv.at[kind, index], self.at.to_core
        )

    def twin_in(self, kind, zz, yy):
        cc = 1 - self.at.core
        xx = 1 - self.at.x if kind == 1 else self.at.x
        at = self.place(1 if kind == 2 else 0, zz, yy, cc, xx)
        index = zz * 2 + yy
        return move(
            at, at, self.csend.at[kind, index], self.crecv.at[kind, index], self.at.to_core
        )

    def locals_(self):
        return [
            pltpu.make_async_copy(
                self.own[u], self.full[u].at[pl.ds(self.at.shard * 2, 2)], self.local.at[u]
            )
            for u in range(2)
        ]

    def begin(self):
        z, y = self.at.z, self.at.y
        self.at.greet()

        @pl.when(z < 3)
        def _():
            self.up(1, z, self.source(1)).start()

        @pl.when(z > 0)
        def _():
            self.down(1, z, self.source(1)).start()

        @pl.when((z >= 2) & (z < 3))
        def _():
            self.up(0, z - 2, self.mine(0, z - 2, y)).start()

        @pl.when((z <= 1) & (z > 0))
        def _():
            self.down(0, z + 2, self.mine(0, z + 2, y)).start()

        self.side(0, z, self.source(0)).start()
        for step in (1, 2):
            @pl.when(z - step >= 0)
            def _():
                self.side(0, z - step, self.mine(0, z - step, y)).start()
                self.got(0, z - step, y)

            @pl.when(z + step < 4)
            def _():
                self.side(0, z + step, self.mine(0, z + step, y)).start()
                self.got(0, z + step, y)

        self.side(1, z, self.source(1)).start()
        for copy in self.locals_():
            copy.start()

    def got(self, u, zz, yy):
        if u == 0:
            self.across(zz, yy).start()
            self.twin(0, zz, yy).start()
        else:
            self.twin(2, zz, yy).start()

    def hop(self, u, step):
        z, y = self.at.z, self.at.y

        @pl.when(z - step >= 0)
        def _():
            zz = z - step
            at = self.mine(u, zz, y)
            self.up(u, zz, at).wait_recv()
            if step < 3:
                @pl.when(z < 3)
                def _():
                    self.up(u, zz, at).start()

            self.side(u, zz, at).start()
            self.got(u, zz, y)

        @pl.when(z + step < 4)
        def _():
            zz = z + step
            at = self.mine(u, zz, y)
            self.down(u, zz, at).wait_recv()
            if step < 3:
                @pl.when(z > 0)
                def _():
                    self.down(u, zz, at).start()

            self.side(u, zz, at).start()
            self.got(u, zz, y)

    def from_side(self, u, step):
        z, yy = self.at.z, 1 - self.at.y

        def take(zz):
            at = self.mine(u, zz, yy)
            move(at, at, self.ysend.at[u, zz], self.yrecv.at[u, zz], self.at.to_y).wait_recv()
            self.got(u, zz, yy)

        if step == 0:
            take(z)
        else:
            @pl.when(z - step >= 0)
            def _():
                take(z - step)

            @pl.when(z + step < 4)
            def _():
                take(z + step)

    def others(self, act):
        for zz in range(4):
            for yy in range(2):
                @pl.when((zz != self.at.z) | (yy != self.at.y))
                def _():
                    act(zz, yy)

    def from_across(self):
        def take(zz, yy):
            at = self.place(0, zz, yy, self.at.core, 1 - self.at.x)
            index = zz * 2 + yy
            move(at, at, self.xsend.at[index], self.xrecv.at[index], self.at.to_x).wait_recv()
            self.twin(1, zz, yy).start()

        self.others(take)

    def end(self):
        z, y = self.at.z, self.at.y

        def take(zz, yy):
            for kind in range(3):
                self.twin_in(kind, zz, yy).wait_recv()
                self.twin(kind, zz, yy).wait_send()
            self.across(zz, yy).wait_send()

        self.others(take)
        for copy in self.locals_():
            copy.wait()
        for u in range(2):
            for zz in range(4):
                at = self.mine(u, zz, y)
                self.side(u, zz, at).wait_send()

                rising = (zz <= z) & (z < 3)
                falling = (zz >= z) & (z > 0)
                if u == 0:
                    rising = (zz == z - 2) & (z < 3)
                    falling = (zz == z + 2) & (z > 0)

                @pl.when(rising)
                def _():
                    self.up(u, zz, at).wait_send()

                @pl.when(falling)
                def _():
                    self.down(u, zz, at).wait_send()


HALF_UP = 1920


def head_twice(values, head):
    wide = values.astype(f32)
    turned = pltpu.roll(wide, 64, 1)
    first = lane_of(values.shape[0]) < 64
    if head == 0:
        return jnp.where(first, wide, turned).astype(bf16)
    return jnp.where(first, turned, wide).astype(bf16)


def head_parts(values, head):
    wide = values.astype(f32) * (SCALE * LOG2E)
    hi = wide.astype(bf16).astype(f32)
    low = wide - hi
    first = lane_of(values.shape[0]) < 64
    if head == 0:
        return jnp.where(first, hi, pltpu.roll(low, 64, 1)).astype(bf16)
    return jnp.where(first, pltpu.roll(hi, 64, 1), low).astype(bf16)


def head_only(values, head):
    first = lane_of(values.shape[0]) < 64
    keep = first if head == 0 else jnp.logical_not(first)
    return jnp.where(keep, values, jnp.zeros_like(values))


def off_diagonal(size, bias):
    row = lax.broadcasted_iota(jnp.int32, (size, size), 0)
    col = lax.broadcasted_iota(jnp.int32, (size, size), 1)
    return jnp.where(row == col, 0.0, bias)


def attend_setup(kb, brow, kx, vx, bown, bcont):
    for head in range(2):
        kx[head, :, 128:] = kb[...]
    vx[:, 128:] = jnp.ones((2560, 128), bf16)
    bown[...] = off_diagonal(512, brow[0:1, 0:512])
    for c in range(2):
        bcont[c] = off_diagonal(256, brow[0:1, 2048 + 256 * c : 2304 + 256 * c])


def attend_fill(q, k, v, qx, kx, vx):
    ones = jnp.where(lane_of(1024) == 0, 1.0, 0.0).astype(bf16)
    vx[:, :128] = v
    for head in range(2):
        qx[head, :, :128] = head_parts(q, head)
        kx[head, :, :128] = head_twice(k, head)
        qx[head, :, 128:] = ones


def own_scores(head, qx, kx, bown):
    return dot(qx[head, :512, :128], kx[head, :512, :128], NT) + bown[...]


def cont_scores(head, c, qx, kx, bcont):
    rows = slice(512 + 256 * c, 768 + 256 * c)
    keys = slice(2048 + 256 * c, 2304 + 256 * c)
    return dot(qx[head, rows, :128], kx[head, keys, :128], NT) + bcont[c]


def attend_head(head, o, side, qx, kx, vx, pm, pc, bown, bcont, top=None):
    def below(scores, rows):
        if top is None:
            return jnp.exp2(scores).astype(bf16)
        return jnp.exp2(scores - top[head, rows, 0:1]).astype(bf16)

    lane = lane_of(256)
    for c in range(3):
        keys = slice(512 + 512 * c, 1024 + 512 * c)
        pm[head, :, keys] = jnp.exp2(dot(qx[head], kx[head, keys], NT)).astype(bf16)
    pm[head, 512:, :512] = jnp.exp2(dot(qx[head, 512:], kx[head, :512], NT)).astype(bf16)
    pm[head, :512, :512] = below(own_scores(head, qx, kx, bown), slice(0, 512))
    for c in range(2):
        rows = slice(512 + 256 * c, 768 + 256 * c)
        pc[head, c] = below(cont_scores(head, c, qx, kx, bcont), rows)
    for r in range(4):
        rows = slice(256 * r, 256 * r + 256)
        total = dot(pm[head, rows], vx[:2048], NN)
        if r >= 2:
            total = total + dot(pc[head, r - 2], vx[1536 + 256 * r : 1792 + 256 * r], NN)
        mass = total[:, 128:]
        value = total[:, :128] / mass
        if head == 0:
            o[rows] = value.astype(bf16)
        else:
            o[rows] = jnp.where(lane < 64, o[rows].astype(f32), value).astype(bf16)
        logs = jnp.log2(mass)
        if top is not None:
            logs = logs + top[head, rows]
        side[head, rows] = side_lanes(1.0, logs)


ROW_STEPS = 5


def near_kernel(
    tok, oth, wq, wk, wv, qb, vb, kb, brow, *refs, linked
):
    if linked:
        own_parts, refs = refs[:2], refs[3:]
    q, k, v, xt, qn, kn, o, side = refs[:8]
    refs = refs[8:]
    if linked:
        full, refs = refs[:2], refs[2:]
    qs, ks, vs, qx, kx, vx, pm, pc, bown, bcont = refs[:10]
    step = pl.program_id(0)
    spread = Spread(own_parts, full, refs[10:]) if linked else None

    def comm(at, act):
        if linked:
            @pl.when(step == at)
            def _():
                act()

    comm(0, lambda: spread.begin())
    width = wq.shape[0]

    @pl.when(step < ROW_STEPS)
    def _():
        own = (step == 0) | (step == 4)
        row = lax.broadcasted_iota(jnp.int32, (width, 128), 0)
        lane = lax.broadcasted_iota(jnp.int32, (width, 128), 1)
        heads = jnp.where(row // HDIM == lane, 1.0, 0.0).astype(bf16)
        at = pl.ds(pl.multiple_of(step * PPIECE, PPIECE), PPIECE)

        @pl.when(step == 0)
        def _():
            qn[...] = jnp.zeros_like(qn)
            kn[...] = jnp.zeros_like(kn)
            attend_setup(kb, brow, kx, vx, bown, bcont)

        def norms(values):
            wide = values.astype(f32)
            sums = dot((wide * wide).astype(bf16), heads, NN)
            return jnp.broadcast_to(jnp.max(sums, axis=0, keepdims=True), (8, 128))

        def keep(low, out, held, where):
            out[...] = low
            for p in range(width // 128):
                held[p, where] = low[:, 128 * p : 128 * p + 128]

        def keys(rows):
            low = dot(rows, wk[...], NN).astype(bf16)
            keep(low, k, ks, at)
            kn[...] = jnp.maximum(kn[...], norms(low))
            keep((dot(rows, wv[...], NN) + vb[...].astype(f32)).astype(bf16), v, vs, at)
            xt[...] = jnp.transpose(rows)

        @pl.when(own)
        def _():
            rows = tok[...]
            keys(rows)
            low = (dot(rows, wq[...], NN) + qb[...].astype(f32)).astype(bf16)
            keep(low, q, qs, pl.ds(pl.multiple_of(step // 4 * PPIECE, PPIECE), PPIECE))
            qn[...] = jnp.maximum(qn[...], norms(low))

        @pl.when(jnp.logical_not(own))
        def _():
            keys(oth[...])

    comm(4, lambda: (spread.hop(0, 3), spread.hop(1, 1)))

    @pl.when(step >= ROW_STEPS)
    def _():
        p = step - ROW_STEPS
        attend_fill(qs[p], ks[p], vs[p], qx, kx, vx)
        attend_head(0, o, side, qx, kx, vx, pm, pc, bown, bcont)

    comm(5, lambda: [spread.from_side(0, j) for j in range(3)])
    comm(6, lambda: spread.hop(1, 2))
    comm(7, lambda: (spread.from_side(1, 0), spread.from_side(0, 3)))
    comm(9, lambda: spread.from_side(1, 1))
    comm(10, lambda: spread.from_side(1, 2))

    @pl.when(step >= ROW_STEPS)
    def _():
        attend_head(1, o, side, qx, kx, vx, pm, pc, bown, bcont)

    comm(7, lambda: spread.hop(1, 3))
    comm(8, lambda: spread.from_across())
    comm(10, lambda: (spread.from_side(1, 3), spread.end()))


def attend_near(tok, oth, wq, wk, wv, qb, vb, kb, brow, own_parts):
    width = tok.shape[1]
    linked = bool(own_parts)
    pairs = width // 128
    block = (PPIECE, width)

    def once(*shape):
        return pl.BlockSpec(shape, lambda i: (0,) * len(shape), pipeline_mode=pl.Buffered(1))

    def rows_at(i):
        return jnp.minimum(i, ROW_STEPS - 1)

    def pair_at(i):
        return jnp.maximum(i - ROW_STEPS, 0)

    small = pl.BlockSpec((8, 128), lambda i: (0, 0))
    extra_shape, extra_sems, more = [], [], {}
    if linked:
        sem = pltpu.SemaphoreType.DMA
        extra_shape = [
            jax.ShapeDtypeStruct((16, 48, own_parts[0].shape[2]), bf16),
            jax.ShapeDtypeStruct((16, 192, width), bf16),
        ]
        extra_sems = [
            sem((2,)), sem((2, 4)), sem((2, 4)), sem((2, 4)), sem((2, 4)), sem((2, 4)),
            sem((8,)), sem((8,)), sem((3, 8)), sem((3, 8)),
        ]
        more = {"collective_id": 3, "has_side_effects": True}
    return pl.pallas_call(
        functools.partial(near_kernel, linked=linked),
        grid=(ROW_STEPS + pairs,),
        in_specs=[
            pl.BlockSpec(block, lambda i: (rows_at(i) // 4, 0)),
            pl.BlockSpec(block, lambda i: (jnp.clip(i - 1, 0, 2), 0)),
            once(width, width), once(width, width), once(width, width),
            once(1, width), once(1, width), once(2560, 128), once(8, 2560),
        ] + [ANY] * len(own_parts),
        out_specs=[
            pl.BlockSpec(block, lambda i: (rows_at(i) // 4, 0)),
            pl.BlockSpec(block, lambda i: (rows_at(i), 0)),
            pl.BlockSpec(block, lambda i: (rows_at(i), 0)),
            pl.BlockSpec((width, PPIECE), lambda i: (0, rows_at(i))),
            small, small,
            pl.BlockSpec((1024, 128), lambda i: (0, pair_at(i))),
            pl.BlockSpec((2, 1024, 128), lambda i: (pair_at(i), 0, 0)),
        ] + [ANY] * len(extra_shape),
        out_shape=[
            jax.ShapeDtypeStruct((1024, width), bf16),
            jax.ShapeDtypeStruct((2560, width), bf16),
            jax.ShapeDtypeStruct((2560, width), bf16),
            jax.ShapeDtypeStruct((width, 2560), bf16),
            jax.ShapeDtypeStruct((8, 128), f32),
            jax.ShapeDtypeStruct((8, 128), f32),
            jax.ShapeDtypeStruct((1024, width), bf16),
            jax.ShapeDtypeStruct((2 * pairs, 1024, 128), bf16),
        ] + extra_shape,
        scratch_shapes=[
            pltpu.VMEM((pairs, 1024, 128), bf16),
            pltpu.VMEM((pairs, 2560, 128), bf16),
            pltpu.VMEM((pairs, 2560, 128), bf16),
            pltpu.VMEM((2, 1024, 256), bf16),
            pltpu.VMEM((2, 2560, 256), bf16),
            pltpu.VMEM((2560, 256), bf16),
            pltpu.VMEM((2, 1024, 2048), bf16),
            pltpu.VMEM((2, 2, 256, 256), bf16),
            pltpu.VMEM((512, 512), f32),
            pltpu.VMEM((2, 256, 256), f32),
        ] + extra_sems,
        input_output_aliases={11: 8} if linked else {},
        compiler_params=params(60, **more),
        cost_estimate=cost(50, 50),
    )(tok, oth, wq, wk, wv, qb, vb, kb, brow, *own_parts)


def far_kernel(
    q, k, v, kb, brow, qn, kn, o_in, side_in, o_out, side_out,
    qs, ks, vs, o, side, qx, kx, vx, pm, pc, bown, bcont, top, sems,
):
    pair = pl.program_id(0)
    widest_product = jnp.max(qn[...] * kn[...]) * ((SCALE * LOG2E) ** 2 * 1.1)

    @pl.when(widest_product > LIMIT * LIMIT)
    def _():
        at = pl.ds(pl.multiple_of(pair * 128, 128), 128)
        copies = [
            pltpu.make_async_copy(ref.at[:, at], held, sems.at[i])
            for i, (ref, held) in enumerate(((q, qs), (k, ks), (v, vs)))
        ]
        for copy in copies:
            copy.start()
        for copy in copies:
            copy.wait()
        attend_setup(kb, brow, kx, vx, bown, bcont)
        attend_fill(qs[...], ks[...], vs[...], qx, kx, vx)

        def widest(scores):
            return jnp.broadcast_to(
                jnp.max(scores, axis=1, keepdims=True), (scores.shape[0], 128)
            )

        for head in range(2):
            def more(c, carry):
                found = widest(dot(qx[head], kx[head, pl.ds(512 + c * 256, 256)], NT))
                top[head] = jnp.maximum(top[head], found)
                return carry

            top[head] = jnp.full((1024, 128), -3e38, f32)
            lax.fori_loop(0, 6, more, 0)
            top[head, 0:512] = jnp.maximum(
                top[head, 0:512], widest(own_scores(head, qx, kx, bown))
            )
            top[head, 512:1024] = jnp.maximum(
                top[head, 512:1024], widest(dot(qx[head, 512:], kx[head, :512], NT))
            )
            for c in range(2):
                rows = slice(512 + 256 * c, 768 + 256 * c)
                top[head, rows] = jnp.maximum(
                    top[head, rows], widest(cont_scores(head, c, qx, kx, bcont))
                )
            qx[head, :, 128:] = side_lanes(1.0, top[head])
            attend_head(head, o, side, qx, kx, vx, pm, pc, bown, bcont, top)
        copies = [
            pltpu.make_async_copy(o, o_out.at[:, at], sems.at[0]),
            pltpu.make_async_copy(side, side_out.at[pl.ds(pair * 2, 2)], sems.at[1]),
        ]
        for copy in copies:
            copy.start()
        for copy in copies:
            copy.wait()


def attend_far(q, k, v, kb, brow, qn, kn, o, side):
    def fixed(*shape):
        return pl.BlockSpec(shape, lambda i: (0,) * len(shape), pipeline_mode=pl.Buffered(1))

    return pl.pallas_call(
        far_kernel,
        grid=(q.shape[1] // 128,),
        in_specs=[
            ANY, ANY, ANY, fixed(2560, 128), fixed(8, 2560), fixed(8, 128), fixed(8, 128),
            ANY, ANY,
        ],
        out_specs=[ANY, ANY],
        out_shape=[
            jax.ShapeDtypeStruct(o.shape, bf16), jax.ShapeDtypeStruct(side.shape, bf16),
        ],
        scratch_shapes=[
            pltpu.VMEM((1024, 128), bf16),
            pltpu.VMEM((2560, 128), bf16),
            pltpu.VMEM((2560, 128), bf16),
            pltpu.VMEM((1024, 128), bf16),
            pltpu.VMEM((2, 1024, 128), bf16),
            pltpu.VMEM((2, 1024, 256), bf16),
            pltpu.VMEM((2, 2560, 256), bf16),
            pltpu.VMEM((2560, 256), bf16),
            pltpu.VMEM((2, 1024, 2048), bf16),
            pltpu.VMEM((2, 2, 256, 256), bf16),
            pltpu.VMEM((512, 512), f32),
            pltpu.VMEM((2, 256, 256), f32),
            pltpu.VMEM((2, 1024, 128), f32),
            pltpu.SemaphoreType.DMA((3,)),
        ],
        input_output_aliases={7: 0, 8: 1},
        compiler_params=params(),
        cost_estimate=cost(0.1, 1),
    )(q, k, v, kb, brow, qn, kn, o, side)


def back_fill(q, k, v, d, o, side, kb, qx, qd, kx, vx, dx, qm, kt, bown, bcont):
    @pl.when(pl.program_id(0) == 0)
    def _():
        for head in range(2):
            kx[head, :, 128:] = kb[...]
        vx[:, 128:] = kb[...]
        column = kb[:, 0:1].astype(f32)
        bown[...] = off_diagonal(512, column[:512]).astype(bf16)
        for c in range(2):
            keys = slice(2048 + 256 * c, 2304 + 256 * c)
            bcont[c] = off_diagonal(256, column[keys]).astype(bf16)

    lane = lane_of(1024)
    vx[:, :128] = v[...]
    kt[...] = jnp.transpose(k[...].astype(f32)).astype(bf16)
    product = d[...].astype(f32) * o[...].astype(f32)
    for head in range(2):
        parts = head_parts(q[...], head)
        qx[head, :, :128] = parts
        qd[head, :, :128] = parts
        tail = side[head]
        qx[head, :, 128:] = tail
        qd[head, :, 128:] = jnp.where(lane == 0, jnp.zeros_like(tail), tail)
        kx[head, :, :128] = head_twice(k[...], head)
        qm[head] = head_only(q[...], head)
        dx[head, :, :128] = head_only(d[...], head)
        inner = jnp.sum(head_only(product, head), axis=1, keepdims=True)
        dx[head, :, 128:] = side_lanes(0.0, jnp.broadcast_to(inner, (1024, 128)))


def back_head(head, qx, qd, kx, vx, dx, qm, kt, pt, st, pc, sc, bown, bcont):
    def tile(keys, rows, queries, bias=None):
        scores = dot(kx[head, keys], queries[head, rows], NT)
        if bias is not None:
            scores = scores + bias.astype(f32)
        probs = jnp.exp2(scores)
        return probs.astype(bf16), (probs * dot(vx[keys], dx[head, rows], NT)).astype(bf16)

    for c in range(3):
        keys = slice(512 + 512 * c, 1024 + 512 * c)
        pt[keys], st[keys] = tile(keys, slice(0, 1024), qx)
    pt[:512, 512:], st[:512, 512:] = tile(slice(0, 512), slice(512, 1024), qx)
    pt[:512, :512], st[:512, :512] = tile(slice(0, 512), slice(0, 512), qd, bown[...])
    for c in range(2):
        keys = slice(2048 + 256 * c, 2304 + 256 * c)
        pc[c], sc[c] = tile(keys, slice(512 + 256 * c, 768 + 256 * c), qd, bcont[c])
    kth = kt[64 * head : 64 * head + 64]
    main = dot(kth[:, :2048], st[...], NN)
    extra = [dot(kth[:, 2048 + 256 * c : 2304 + 256 * c], sc[c], NN) for c in range(2)]
    rows = jnp.concatenate(
        [main[:, :512], main[:, 512:768] + extra[0], main[:, 768:] + extra[1]], axis=1
    )
    return rows


def back_keys(head, dx, qm, pt, st, pc, sc, acc):
    def put(keys, cols, value):
        if head == 0:
            acc[keys, cols] = value
        else:
            acc[keys, cols] += value

    left, right = slice(0, 128), slice(128, 256)
    for c in range(4):
        keys = slice(512 * c, 512 * c + 512)
        put(keys, left, dot(st[keys], qm[head], NN) * SCALE)
        put(keys, right, dot(pt[keys], dx[head, :, :128], NN))
    for c in range(2):
        keys = slice(2048 + 256 * c, 2304 + 256 * c)
        rows = slice(512 + 256 * c, 768 + 256 * c)
        put(keys, left, dot(sc[c], qm[head, rows], NN) * SCALE)
        put(keys, right, dot(pc[c], dx[head, rows, :128], NN))


BACK_SCRATCH = [
    pltpu.VMEM((2, 1024, 256), bf16),
    pltpu.VMEM((2, 1024, 256), bf16),
    pltpu.VMEM((2, 2560, 256), bf16),
    pltpu.VMEM((2560, 256), bf16),
    pltpu.VMEM((2, 1024, 256), bf16),
    pltpu.VMEM((2, 1024, 128), bf16),
    pltpu.VMEM((128, 2560), bf16),
    pltpu.VMEM((2048, 1024), bf16),
    pltpu.VMEM((2048, 1024), bf16),
    pltpu.VMEM((2, 256, 256), bf16),
    pltpu.VMEM((2, 256, 256), bf16),
    pltpu.VMEM((512, 512), bf16),
    pltpu.VMEM((2, 256, 256), bf16),
    pltpu.VMEM((2560, 256), f32),
]


def back_specs():
    def pair(rows):
        return pl.BlockSpec((rows, 128), lambda i: (0, i))

    def once(*shape):
        return pl.BlockSpec(shape, lambda i: (0,) * len(shape), pipeline_mode=pl.Buffered(1))

    return [
        pair(1024), pair(2560), pair(2560), pair(1024), pair(1024),
        pl.BlockSpec((2, 1024, 128), lambda i: (i, 0, 0)),
        once(2560, 128), once(768, 2560),
    ]


def back_alone_kernel(q, k, v, d, o, side, kb, xt, dq, cont, partial_rows, whole, *scratch):
    (qx, qd, kx, vx, dx, qm, kt, pt, st, pc, sc, bown, bcont, acc) = scratch
    back_fill(q, k, v, d, o, side, kb, qx, qd, kx, vx, dx, qm, kt, bown, bcont)
    rows = []
    for head in range(2):
        rows.append(back_head(head, qx, qd, kx, vx, dx, qm, kt, pt, st, pc, sc, bown, bcont))
        back_keys(head, dx, qm, pt, st, pc, sc, acc)
    delta = jnp.transpose(jnp.concatenate(rows, axis=0) * SCALE).astype(bf16)
    dq[...] = delta
    low = acc[...].astype(bf16)
    partial_rows[...] = low[:2048]
    cont[...] = low[2048:]
    grad = dot(xt[:, :512], delta[:512], NN) + dot(xt[:, 2048:], delta[512:], NN)
    whole[:, :128] = grad.astype(bf16)
    whole[:, 128:] = dot(xt[...], low, NN).astype(bf16)


def attend_back_alone(q, k, v, d, o, side, kb, xt):
    width = q.shape[1]
    count = width // 128
    return pl.pallas_call(
        back_alone_kernel,
        grid=(count,),
        in_specs=back_specs(),
        out_specs=[
            pl.BlockSpec((1024, 128), lambda i: (0, i)),
            pl.BlockSpec((512, 256), lambda i: (0, i)),
            pl.BlockSpec((2048, 256), lambda i: (0, i)),
            pl.BlockSpec((width, 384), lambda i: (0, i)),
        ],
        out_shape=[
            jax.ShapeDtypeStruct((1024, width), bf16),
            jax.ShapeDtypeStruct((512, 2 * width), bf16),
            jax.ShapeDtypeStruct((2048, 2 * width), bf16),
            jax.ShapeDtypeStruct((width, 3 * width), bf16),
        ],
        scratch_shapes=BACK_SCRATCH,
        compiler_params=params(60),
        cost_estimate=cost(100, 40),
    )(q, k, v, d, o, side, kb, xt)


PAIRS = 6
AB_COPIES = 15
PAIR_COPIES = 11


def back_linked_kernel(
    q, k, v, d, o, side, kb, xt, xa, xb, wq, wk, wv, adel,
    token_grad, gq, gk, gv, qrow, ga, gb,
    qx, qd, kx, vx, dx, qm, kt, pt, st, pc, sc, bown, bcont, acc,
    a_mine, a_x, a_y, a_z, a_q, b_mine, b_y, b_z, b_r,
    p_mine, p_other, c_in, y_in, z_in, r_in, keys_low, k_in, k_far, k_x, dw,
    dq, cont_k, cont_v, own_k, own_v, wsem, lsem, ab_send, ab_recv, p_send, p_recv,
):
    step = pl.program_id(0)
    rep = lax.axis_index("rep")
    shard = lax.axis_index("shard")
    core = rep % 2
    x = rep // 2
    z = shard // 2
    y = shard % 2
    rep1 = rep + 1 - 2 * core
    to_rep = [None, {"rep": rep1}, {"rep": (rep + 2) % 4}, {"rep": (rep1 + 2) % 4}]
    to_y = {"shard": z * 2 + 1 - y}
    zs = [z, z + 1 - 2 * (z % 2), (z + 2) % 4, 3 - z]
    to_z = [None] + [{"shard": zs[j] * 2 + y} for j in range(1, 4)]

    def move(src, dst, send, recv, where):
        return pltpu.make_async_remote_copy(
            src_ref=src, dst_ref=dst, send_sem=send, recv_sem=recv,
            device_id=where, device_id_type=MESH,
        )

    def ab(index, src, dst, where):
        return move(src, dst, ab_send.at[index], ab_recv.at[index], where)

    def columns(which):
        return pl.ds(pl.multiple_of(which * HALF_UP, 128), HALF_UP)

    def copy_ax():
        return ab(0, xa.at[:, :, columns(1 - x)], a_x, to_rep[2])

    def copy_ay():
        return ab(1, a_mine.at[pl.ds(4, 4)], a_y, to_y)

    def copy_az(j):
        return ab(1 + j, a_mine.at[j], a_z.at[j - 1], to_z[j])

    def copy_aq(j):
        return ab(4 + j, a_q.at[0], a_q.at[j], to_rep[j])

    def copy_by():
        return ab(8, xb.at[pl.ds(4, 4)], b_y, to_y)

    def copy_bz(j):
        return ab(8 + j, b_mine.at[j], b_z.at[j - 1], to_z[j])

    def copy_br(j):
        return ab(11 + j, b_r.at[0], b_r.at[j], to_rep[j])

    def pair_copy(p, index, src, dst, where):
        return move(src, dst, p_send.at[p, index], p_recv.at[p, index], where)

    def copy_core(p):
        return pair_copy(p, 0, p_other, c_in.at[p % 2], to_rep[1])

    def copy_y(p):
        return pair_copy(p, 1, p_mine.at[p % 2, pl.ds(4, 4)], y_in.at[p % 2], to_y)

    def copy_z(p, j):
        return pair_copy(p, 1 + j, p_mine.at[p % 2, j], z_in.at[p % 2, j - 1], to_z[j])

    def copy_rep(p, j):
        return pair_copy(p, 4 + j, r_in.at[p % 2, 0], r_in.at[p % 2, j], to_rep[j])

    def copy_near(p):
        return pair_copy(p, 8, keys_low.at[p % 2, pl.ds(512, 512)], k_in.at[p % 2], to_rep[1])

    def copy_far(p):
        return pair_copy(p, 9, keys_low.at[p % 2, pl.ds(1536, 512)], k_far.at[p % 2], to_rep[1])

    def copy_turn(p):
        return pair_copy(p, 10, keys_low.at[p % 2, pl.ds(1024, 512)], k_x.at[p % 2], to_rep[2])

    def add(left, right):
        return left + right

    def after_core(p):
        slot = p % 2
        copy_core(p).wait()
        for i in range(8):
            p_mine[slot, i] = add(p_mine[slot, i], c_in[slot, i])
        copy_y(p).start()
        copy_near(p).wait()
        copy_far(p).wait()
        keys_low[slot, 1024:1536] = add(keys_low[slot, 1024:1536], k_far[slot])
        copy_turn(p).start()
        keys_low[slot, :512] = add(keys_low[slot, :512], k_in[slot])

    def after_y(p):
        slot = p % 2
        copy_y(p).wait()
        for i in range(4):
            p_mine[slot, i] = add(p_mine[slot, i], y_in[slot, i])
        for j in range(1, 4):
            copy_z(p, j).start()

    def own_keys(p):
        slot = p % 2
        copy_turn(p).wait()
        total = add(keys_low[slot, :512], k_x[slot])
        at = pl.ds(pl.multiple_of(p * 128, 128), 128)
        own_k[:, at] = total[:, :128]
        own_v[:, at] = total[:, 128:]

    def after_z(p):
        slot = p % 2
        for j in range(1, 4):
            copy_z(p, j).wait()
        total = p_mine[slot, 0].astype(f32)
        for j in range(3):
            total = total + z_in[slot, j].astype(f32)
        r_in[slot, 0] = total.astype(bf16)
        for j in range(1, 4):
            copy_rep(p, j).start()

    def after_rep(p):
        slot = p % 2
        for j in range(1, 4):
            copy_rep(p, j).wait()
        at = pl.ds(pl.multiple_of(p * 128, 128), 128)
        for half, (one, two) in enumerate(((0, 2), (1, 3))):
            total = add(r_in[slot, one], r_in[slot, two])
            rows = core if half == 0 else 1 - core
            rows = pl.ds(pl.multiple_of(rows * 48, 16), 48)
            for j, out in enumerate((gq, gk, gv)):
                out[rows, at] = total[:48, 128 * j : 128 * j + 128]
            if half == 0:
                qrow[:, at] = total[48:64, :128]

    @pl.when(step == 0)
    def _():
        barrier = pltpu.get_barrier_semaphore()
        for place in to_rep[1:] + [to_y] + to_z[1:]:
            pl.semaphore_signal(barrier, inc=1, device_id=place, device_id_type=MESH)
        pl.semaphore_wait(barrier, 7)
        copy_by().start()
        copy_ax().start()
        for copy in (
            pltpu.make_async_copy(xa.at[:, :, columns(x)], a_mine, lsem.at[0]),
            pltpu.make_async_copy(xb.at[pl.ds(0, 4)], b_mine, lsem.at[1]),
        ):
            copy.start()

    back_fill(q, k, v, d, o, side, kb, qx, qd, kx, vx, dx, qm, kt, bown, bcont)
    turned = []
    turned.append(back_head(0, qx, qd, kx, vx, dx, qm, kt, pt, st, pc, sc, bown, bcont))
    back_keys(0, dx, qm, pt, st, pc, sc, acc)

    @pl.when(step > 1)
    def _():
        after_z(step - 2)
        own_keys(step - 2)

    @pl.when(step > 0)
    def _():
        after_core(step - 1)

    @pl.when(step == 2)
    def _():
        copy_ax().wait()
        pltpu.make_async_copy(xa.at[:, :, columns(x)], a_mine, lsem.at[0]).wait()

        def sum_piece(i, carry):
            a_mine[i] = add(a_mine[i], a_x[i])
            return carry

        lax.fori_loop(0, 8, sum_piece, 0)
        copy_ay().start()

    @pl.when(step == 3)
    def _():
        copy_ay().wait()

        def sum_piece(i, carry):
            a_mine[i] = add(a_mine[i], a_y[i])
            return carry

        lax.fori_loop(0, 4, sum_piece, 0)
        for j in range(1, 4):
            copy_az(j).start()

    turned.append(back_head(1, qx, qd, kx, vx, dx, qm, kt, pt, st, pc, sc, bown, bcont))
    back_keys(1, dx, qm, pt, st, pc, sc, acc)

    @pl.when(step > 0)
    def _():
        after_y(step - 1)

    @pl.when(step > 1)
    def _():
        after_rep(step - 2)

    @pl.when(step == 1)
    def _():
        copy_by().wait()
        pltpu.make_async_copy(xb.at[pl.ds(0, 4)], b_mine, lsem.at[1]).wait()

        def sum_piece(i, carry):
            b_mine[i] = add(b_mine[i], b_y[i])
            return carry

        lax.fori_loop(0, 4, sum_piece, 0)
        for j in range(1, 4):
            copy_bz(j).start()

    @pl.when(step == 3)
    def _():
        for j in range(1, 4):
            copy_bz(j).wait()
        total = b_mine[0].astype(f32)
        for j in range(3):
            total = total + b_z[j].astype(f32)
        b_r[0] = total.astype(bf16)
        for j in range(1, 4):
            copy_br(j).start()

    @pl.when(step == 4)
    def _():
        for j in range(1, 4):
            copy_br(j).wait()
        gb[core] = add(b_r[0], b_r[2])
        gb[1 - core] = add(b_r[1], b_r[3])
        for j in range(1, 4):
            copy_az(j).wait()
        total = a_mine[0].astype(f32)
        for j in range(3):
            total = total + a_z[j].astype(f32)
        a_q[0] = total.astype(bf16)
        for j in range(1, 4):
            copy_aq(j).start()

    def loads():
        wide = pl.ds(0, 768)
        return [
            pltpu.make_async_copy(wq, pt.at[pl.ds(0, 768), wide], wsem.at[0]),
            pltpu.make_async_copy(wk, pt.at[pl.ds(1024, 768), wide], wsem.at[1]),
            pltpu.make_async_copy(wv, st.at[pl.ds(0, 768), wide], wsem.at[2]),
            pltpu.make_async_copy(adel, st.at[pl.ds(1024, 1024), wide], wsem.at[3]),
        ]

    def results(half):
        rows = pl.ds(512 * half, 512)
        return pltpu.make_async_copy(dq.at[rows], token_grad.at[rows], wsem.at[4 + half])

    def tokens_half(half):
        rows = slice(512 * half, 512 * half + 512)
        far_rows = slice(1024 + 512 * half, 1536 + 512 * half)
        total = st[far_rows, :768].astype(f32) + dot(dq[rows], pt[:768, :768], NT)
        total = total + dot((own_k if half == 0 else cont_k)[...], pt[1024:1792, :768], NT)
        total = total + dot((own_v if half == 0 else cont_v)[...], st[:768, :768], NT)
        dq[rows] = total.astype(bf16)
        results(half).start()

    @pl.when(step == PAIRS - 1)
    def _():
        for load in loads():
            load.start()

    delta = jnp.transpose(jnp.concatenate(turned, axis=0) * SCALE)
    low = delta.astype(bf16)
    pair_at = pl.ds(pl.multiple_of(step * 128, 128), 128)
    dq[:, pair_at] = low
    slot = step % 2
    keys_low[slot] = acc[:2048].astype(bf16)
    tail = acc[2048:].astype(bf16)
    cont_k[:, pair_at] = tail[:, :128]
    cont_v[:, pair_at] = tail[:, 128:]
    copy_near(step).start()
    copy_far(step).start()
    grad = dot(xt[:, :512], low[:512], NN) + dot(xt[:, 2048:], low[512:], NN)
    dw[:, :128] = grad.astype(bf16)
    dw[:, 128:] = (dot(xt[:, :2048], keys_low[slot], NN) + dot(xt[:, 2048:], tail, NN)).astype(bf16)
    extra = jnp.sum(low.astype(f32), axis=0, keepdims=True)
    extra = jnp.concatenate([jnp.broadcast_to(extra, (16, 128)), jnp.zeros((16, 256), f32)], axis=1)
    extra = extra.astype(bf16)
    for i in range(8):
        place = (zs[i % 4] * 2 + (y if i < 4 else 1 - y)) * 2
        at = pl.multiple_of((place + core) * 48, 16)
        p_mine[slot, i, :48] = dw[pl.ds(at, 48)]
        p_mine[slot, i, 48:] = extra
        at = pl.multiple_of((place + 1 - core) * 48, 16)
        p_other[i, :48] = dw[pl.ds(at, 48)]
        p_other[i, 48:] = extra
    copy_core(step).start()

    @pl.when(step == PAIRS - 1)
    def _():
        after_z(PAIRS - 2)
        own_keys(PAIRS - 2)
        after_core(PAIRS - 1)
        for load in loads():
            load.wait()
        tokens_half(1)
        after_y(PAIRS - 1)
        for j in range(1, 4):
            copy_aq(j).wait()
        for j, (rows, which) in enumerate(
            ((core, x), (1 - core, x), (core, 1 - x), (1 - core, 1 - x))
        ):
            rows = pl.ds(pl.multiple_of(rows * 48, 16), 48)
            ga[rows, columns(which)] = a_q[j]
        after_rep(PAIRS - 2)
        own_keys(PAIRS - 1)
        after_z(PAIRS - 1)
        tokens_half(0)
        after_rep(PAIRS - 1)
        for half in range(2):
            results(half).wait()


def attend_back(q, k, v, d, o, side, kb, xt, xa, xb, wq, wk, wv, adel):
    width = q.shape[1]
    count = width // 128
    full = xa.shape[2]

    def held(*shape):
        return pl.BlockSpec(shape, lambda i: (0,) * len(shape), pipeline_mode=pl.Buffered(1))

    def vm(*shape):
        return pltpu.VMEM(shape, bf16)

    def out(*shape):
        return jax.ShapeDtypeStruct(shape, bf16)

    sem = pltpu.SemaphoreType.DMA
    piece = (64, 384)
    return pl.pallas_call(
        back_linked_kernel,
        grid=(count,),
        in_specs=back_specs() + [ANY] * 6,
        out_specs=[
            ANY, held(96, width), held(96, width), held(96, width),
            held(16, width), held(96, full), held(2, 208, width),
        ],
        out_shape=[
            out(1024, width), out(96, width), out(96, width), out(96, width),
            out(16, width), out(96, full), out(2, 208, width),
        ],
        scratch_shapes=BACK_SCRATCH
        + [
            vm(8, 48, HALF_UP), vm(8, 48, HALF_UP), vm(4, 48, HALF_UP), vm(3, 48, HALF_UP),
            vm(4, 48, HALF_UP), vm(4, 208, width), vm(4, 208, width), vm(3, 208, width),
            vm(4, 208, width),
            vm(2, 8, *piece), vm(8, *piece), vm(2, 8, *piece), vm(2, 4, *piece),
            vm(2, 3, *piece), vm(2, 4, *piece), vm(2, 2048, 256), vm(2, 512, 256),
            vm(2, 512, 256), vm(2, 512, 256), vm(width, 384),
            vm(1024, width), vm(512, width), vm(512, width), vm(512, width), vm(512, width),
            sem((6,)), sem((2,)), sem((AB_COPIES,)), sem((AB_COPIES,)), sem((PAIRS, PAIR_COPIES)),
            sem((PAIRS, PAIR_COPIES)),
        ],
        compiler_params=params(62, collective_id=2, has_side_effects=True),
        cost_estimate=cost(100, 40),
    )(q, k, v, d, o, side, kb, xt, xa, xb, wq, wk, wv, adel)


def gelu_parts(x):
    bell = jnp.exp2(x * x * (-0.5 * LOG2E))
    t = 1.0 / (1.0 + (0.3275911 * 0.7071067811865476) * jnp.abs(x))
    poly = 0.5 * 1.061405429
    for term in (-1.453152027, 1.421413741, -0.284496736, 0.254829592):
        poly = poly * t + 0.5 * term
    below = poly * t * bell
    phi = jnp.where(x >= 0.0, 1.0 - below, below)
    return x * phi, phi + x * bell * 0.3989422804014327


def normed_of(values):
    centered = values - jnp.mean(values, axis=-1, keepdims=True)
    spread = lax.rsqrt(jnp.mean(centered * centered, axis=-1, keepdims=True) + EPSILON)
    return centered * spread, spread


def norm_back(incoming, normed, spread, gain):
    scaled = incoming * gain
    centered = scaled - jnp.mean(scaled, axis=-1, keepdims=True)
    return (centered - normed * jnp.mean(scaled * normed, axis=-1, keepdims=True)) * spread


FCH = 768


def forward_back_kernel(
    mixed, tok, cot, teach, keep, scale, vecs, upb, up_full, down_full,
    result, hid_o, act_o, ddel_o, udel_o, adel_o, mdel_o, sums,
    wa_pieces, wu_pieces, wd_pieces, slope, sems,
):
    step = pl.program_id(0)
    width = tok.shape[1]
    hidden_units = upb.shape[1]

    loads = [
        pltpu.make_async_copy(up_full.at[:, :, pl.ds(0, width)], wa_pieces, sems.at[0]),
        pltpu.make_async_copy(up_full.at[:, :, pl.ds(width, hidden_units)], wu_pieces, sems.at[1]),
        pltpu.make_async_copy(down_full, wd_pieces, sems.at[2]),
    ]

    @pl.when(step == 0)
    def _():
        for load in loads:
            load.start()
        sums[...] = jnp.zeros_like(sums)
        for load in loads:
            load.wait()

    wa = wa_pieces.reshape(width, width)
    wu = wu_pieces.reshape(width, hidden_units)
    wd = wd_pieces.reshape(hidden_units, width)

    def vector(index):
        return vecs[index : index + 1].astype(f32)

    attn_b, gain1, shift1, down_b, gain2, shift2 = [vector(i) for i in range(2, 8)]

    def add_sum(index, values):
        sums[index : index + 1] += jnp.sum(values, axis=0, keepdims=True)

    x = tok[...].astype(f32)
    branch = attn_b + x + dot(mixed[...], wa[...], NN)
    normed1, inv1 = normed_of(branch)
    hidden = normed1 * gain1 + shift1
    hid_low = hidden.astype(bf16)
    hid_o[...] = hid_low
    for c in range(hidden_units // FCH):
        cols = slice(c * FCH, c * FCH + FCH)
        value, rise = gelu_parts(dot(hid_low, wu[:, cols], NN) + upb[:, cols].astype(f32))
        act_o[:, cols] = value.astype(bf16)
        slope[:, cols] = rise.astype(bf16)
    second = hidden + dot(act_o[...], wd[...], NN) + down_b
    normed2, inv2 = normed_of(second)
    final = normed2 * gain2 + shift2
    result[...] = final.astype(bf16)
    errors = final - teach[...].astype(f32)
    kept = errors * jnp.concatenate([keep[...]] * (width // 128), axis=1)
    add_sum(6, kept * errors)
    grad = cot[...].astype(f32) + kept * (2.0 * scale[...])
    add_sum(1, grad * normed2)
    add_sum(2, grad)
    grad2 = norm_back(grad, normed2, inv2, gain2)
    ddel = grad2.astype(bf16)
    ddel_o[...] = ddel
    add_sum(0, ddel.astype(f32))
    for c in range(hidden_units // FCH):
        cols = slice(c * FCH, c * FCH + FCH)
        delta = dot(ddel, wd[cols], NT) * slope[:, cols].astype(f32)
        low = delta.astype(bf16)
        udel_o[:, cols] = low
        add_sum(8 + c, low.astype(f32))
    hgrad = grad2 + dot(udel_o[...], wu[...], NT)
    add_sum(4, hgrad * normed1)
    add_sum(5, hgrad)
    grad1 = norm_back(hgrad, normed1, inv1, gain1)
    adel = grad1.astype(bf16)
    adel_o[...] = adel
    add_sum(3, adel.astype(f32))
    mdel = dot(adel, wa[...], NT).astype(bf16)
    mdel_o[...] = mdel
    add_sum(7, mdel.astype(f32))


def forward_back(mixed, tok, cot, teach, keep, scale, vecs, upb, up_full, down_full):
    rows, width = tok.shape
    hidden_units = upb.shape[1]
    half = 512

    def block(columns):
        return pl.BlockSpec((half, columns), lambda i, *_: (i, 0))

    def fixed(*shape):
        return pl.BlockSpec(shape, lambda i, *_: (0,) * len(shape))

    def out(columns):
        return jax.ShapeDtypeStruct((rows, columns), bf16)

    return pl.pallas_call(
        forward_back_kernel,
        grid=(rows // half,),
        in_specs=[
            block(width), block(width), block(width), block(width),
            block(128), fixed(1, 1), fixed(8, width), fixed(1, hidden_units), ANY, ANY,
        ],
        out_specs=[
            block(width), block(width), block(hidden_units), block(width),
            block(hidden_units), block(width), block(width), fixed(16, width),
        ],
        scratch_shapes=[
            pltpu.VMEM((16, width // 16, width), bf16),
            pltpu.VMEM((16, width // 16, hidden_units), bf16),
            pltpu.VMEM((16, hidden_units // 16, width), bf16),
            pltpu.VMEM((half, hidden_units), bf16),
            pltpu.SemaphoreType.DMA((3,)),
        ],
        out_shape=[
            out(width), out(width), out(hidden_units), out(width), out(hidden_units),
            out(width), out(width), jax.ShapeDtypeStruct((16, width), f32),
        ],
        compiler_params=params(60),
        cost_estimate=cost(32.6, 30),
    )(mixed, tok, cot, teach, keep, scale, vecs, upb, up_full, down_full)


def up_grad_kernel(order, mixed, adel, hid, udel, mine, other, whole):
    step = pl.program_id(0)

    @pl.when(step == 0)
    def _():
        whole[...] = dot(mixed[...], adel[...], TN).astype(bf16)

    @pl.when(step > 0)
    def _():
        whole[...] = dot(hid[...], udel[...], TN).astype(bf16)

    store_pieces(order, whole, mine, other, 48)


def store_pieces(order, source, mine, other, piece):
    for i in range(8):
        at = pl.multiple_of(order[i] * piece, 16)
        mine[i, :piece] = source[pl.ds(at, piece)]
        at = pl.multiple_of(order[i + 8] * piece, 16)
        other[i, :piece] = source[pl.ds(at, piece)]


def up_grad(order, mixed, adel, hid, udel):
    rows, width = adel.shape
    columns = udel.shape[1]
    shape = jax.ShapeDtypeStruct((8, 48, width + columns), bf16)
    out = pl.BlockSpec((8, 48, width), lambda i, *_: (0, 0, i))
    full = pl.BlockSpec((rows, width), lambda i, *_: (0, 0))
    return pl.pallas_call(
        up_grad_kernel,
        grid_spec=pltpu.PrefetchScalarGridSpec(
            num_scalar_prefetch=1,
            grid=(1 + columns // width,),
            in_specs=[
                full, full, full,
                pl.BlockSpec((rows, width), lambda i, *_: (0, jnp.maximum(i - 1, 0))),
            ],
            out_specs=[out, out],
            scratch_shapes=[pltpu.VMEM((width, width), bf16)],
        ),
        out_shape=[shape, shape],
        compiler_params=params(),
        cost_estimate=cost(6, 20),
    )(order, mixed, adel, hid, udel)


def down_grad_kernel(order, act, ddel, sums, mine, other, whole):
    whole[...] = dot(act[...], ddel[...], TN).astype(bf16)
    store_pieces(order, whole, mine, other, 192)
    low = sums[...].astype(bf16)
    for i in range(8):
        mine[i, 192:] = low
        other[i, 192:] = low


def down_grad(order, act, ddel, sums):
    rows, columns = ddel.shape
    total = act.shape[1]
    chunk = 256
    shape = jax.ShapeDtypeStruct((8, 208, columns), bf16)
    out = pl.BlockSpec((8, 208, chunk), lambda i, *_: (0, 0, i))
    return pl.pallas_call(
        down_grad_kernel,
        grid_spec=pltpu.PrefetchScalarGridSpec(
            num_scalar_prefetch=1,
            grid=(columns // chunk,),
            in_specs=[
                pl.BlockSpec(act.shape, lambda i, *_: (0, 0)),
                pl.BlockSpec((rows, chunk), lambda i, *_: (0, i)),
                pl.BlockSpec((16, chunk), lambda i, *_: (0, i)),
            ],
            out_specs=[out, out],
            scratch_shapes=[pltpu.VMEM((total, chunk), bf16)],
        ),
        out_shape=[shape, shape],
        compiler_params=params(),
        cost_estimate=cost(5, 20),
    )(order, act, ddel, sums)


def tokens_grad_kernel(adel, dq, own, cont, wq, wk, wv, out):
    for half, low in enumerate((own, cont)):
        rows = slice(512 * half, 512 * half + 512)
        total = adel[rows].astype(f32) + dot(dq[rows], wq[...], NT)
        for p in range(wq.shape[1] // 128):
            cols = slice(128 * p, 128 * p + 128)
            both = jnp.concatenate([wk[:, cols], wv[:, cols]], axis=1)
            total = total + dot(low[:, 256 * p : 256 * p + 256], both, NT)
        out[rows] = total.astype(bf16)


def tokens_grad(adel, dq, own, cont, wq, wk, wv):
    args = (adel, dq, own, cont, wq, wk, wv)
    return pl.pallas_call(
        tokens_grad_kernel,
        grid=(1,),
        in_specs=[pl.BlockSpec(a.shape, lambda i: (0, 0)) for a in args],
        out_specs=pl.BlockSpec(adel.shape, lambda i: (0, 0)),
        out_shape=jax.ShapeDtypeStruct(adel.shape, bf16),
        compiler_params=params(),
        cost_estimate=cost(3.6, 12),
    )(*args)


def swap(values, axis, bit):
    size = lax.axis_size(axis)
    return lax.ppermute(values, axis, [(i, i ^ bit) for i in range(size)])


def local(
    tokens, cotangent, teacher, valid_mask, valid_count,
    query_weight, query_bias, key_weight, value_weight, value_bias,
    attn_weight, attn_bias, first_gain, first_shift,
    up_weight, up_bias, down_weight, down_bias, second_gain, second_shift,
):
    rows, width = tokens.shape[2:]
    shards = lax.axis_size("shard")
    split = shards == 8
    rep = lax.axis_index("rep")
    shard = lax.axis_index("shard")
    core = rep % 2
    z, y = shard // 2, shard % 2
    tok = tokens.reshape(rows, width)
    keep = valid_mask.reshape(rows)
    if split:
        i = jnp.arange(16, dtype=jnp.int32)
        order = (((z ^ (i % 4)) * 2 + (y ^ (i // 4 % 2))) * 2 + (core ^ (i // 8))).astype(jnp.int32)
    else:
        order = jnp.arange(16, dtype=jnp.int32)

    small = [
        query_bias, value_bias, attn_bias, first_gain, first_shift, down_bias, second_gain,
        second_shift, up_bias,
    ]
    part = query_bias.shape[0]
    vec = jnp.concatenate([v[None] for v in small], axis=1)[0]
    keep_low = keep[:PPIECE].astype(f32).reshape(4, 128)
    if split:
        keep_low = jnp.concatenate([keep_low, keep_low])
        vec = jnp.pad(vec, (0, 2048 - vec.shape[0])).reshape(16, 128)
        up_own = jnp.concatenate([attn_weight, up_weight], axis=1).reshape(2, 48, -1)
        wq, wk, wv, vecs, oth, others_keep, up_full = first_gather(
            query_weight, key_weight, value_weight, vec, tok, keep_low, up_own
        )
        vecs = vecs.reshape(8, 2048)
    else:
        wq, wk, wv, vecs = [
            lax.all_gather(w, "shard", axis=0, tiled=True)
            for w in (query_weight, key_weight, value_weight, vec[None])
        ]
        prompt = tok[:PPIECE]
        oth = jnp.concatenate([swap(prompt, "rep", bit) for bit in (1, 2, 3)])
        others_keep = jnp.stack([swap(keep_low, "rep", bit) for bit in (1, 2, 3)])
    others_keep = others_keep[:, :4].reshape(3 * PPIECE)
    upb = vecs[:, 8 * part : 8 * part + up_bias.shape[0]].reshape(1, -1)
    vecs = vecs[:, : 8 * part].reshape(shards, 8, part).transpose(1, 0, 2).reshape(8, width)

    all_keep = jnp.concatenate(
        [keep[:PPIECE].astype(f32), others_keep, keep[PPIECE:].astype(f32)]
    )
    bias = jnp.where(all_keep > 0.5, 0.0, NEGATIVE)
    brow = jnp.broadcast_to(bias[None], (8, bias.shape[0]))
    lane = jnp.arange(128)[None]
    kb = jnp.where(lane == 0, bias[:, None], jnp.where(lane < 4, 1.0, 0.0)).astype(bf16)

    own_parts = ()
    if split:
        own_parts = (up_own, down_weight.reshape(2, 192, width), up_full)
    outs = attend_near(tok, oth, wq, wk, wv, vecs[0:1], vecs[1:2], kb, brow, own_parts)
    q, k, v, xt, qn, kn, mixed, sides = outs[:8]
    if split:
        up_full, down_full = outs[8:]
    else:
        up_full = jnp.concatenate(
            [
                lax.all_gather(w, "shard", axis=0, tiled=True)
                for w in (attn_weight, up_weight)
            ],
            axis=1,
        ).reshape(16, 48, -1)
        down_full = lax.all_gather(down_weight, "shard", axis=0, tiled=True)
        down_full = down_full.reshape(16, 192, width)
    mixed, sides = attend_far(q, k, v, kb, brow, qn, kn, mixed, sides)

    keep_wide = jnp.broadcast_to(keep.astype(f32)[:, None], (rows, 128))
    scale = (1.0 / valid_count.astype(f32)).reshape(1, 1)
    result, hid, act, ddel, udel, adel, mdel, sums = forward_back(
        mixed, tok, cotangent.reshape(rows, width), teacher.reshape(rows, width),
        keep_wide, scale, vecs, upb, up_full, down_full,
    )
    down_mine, down_other = down_grad(order, act, ddel, sums)
    up_mine, up_other = up_grad(order, mixed, adel, hid, udel)
    if split:
        down_sum = (down_mine.astype(f32) + swap(down_other, "rep", 1).astype(f32)).astype(bf16)
        up_sum = (up_mine.astype(f32) + swap(up_other, "rep", 1).astype(f32)).astype(bf16)
        token_grad, query_low, key_low, value_low, qrow, up_low, down_low = attend_back(
            q, k, v, mdel, mixed, sides, kb, xt, up_sum, down_sum, wq, wk, wv, adel
        )
        query_grad, key_grad, value_grad = [g.astype(f32) for g in (query_low, key_low, value_low)]
        up_all = up_low.astype(f32)
        down_all = down_low[:, :192].astype(f32).reshape(-1, width)
        sums = down_low[0, 192:].astype(f32)
        query_row = qrow[0].astype(f32)
    else:
        dq, cont, partial_rows, whole = attend_back_alone(q, k, v, mdel, mixed, sides, kb, xt)

        def scatter(part):
            part = lax.psum_scatter(part, "shard", scatter_dimension=0, tiled=True)
            return lax.psum(part, "rep").astype(f32)

        def joined(mine, other, piece):
            return jnp.concatenate([mine, other])[:, :piece].reshape(16 * piece, -1)

        turned = partial_rows.reshape(2, 2, PPIECE, -1)
        turned = jnp.where(core == 1, turned[:, ::-1], turned)
        turned = jnp.where(rep // 2 == 1, turned[::-1], turned)
        own = lax.psum_scatter(
            turned.reshape(4 * PPIECE, -1), "rep", scatter_dimension=0, tiled=True
        )
        whole = scatter(whole).reshape(part, width // 128, 3, 128)
        query_grad, key_grad, value_grad = [whole[:, :, j].reshape(part, width) for j in range(3)]
        up_all = scatter(joined(up_mine, up_other, 48))
        down_all = scatter(joined(down_mine, down_other, 192))
        sums = lax.psum(sums, ("rep", "shard"))
        query_row = lax.psum(jnp.sum(dq.astype(f32), axis=0), ("rep", "shard"))
        token_grad = tokens_grad(adel, dq, own, cont, wq, wk, wv)

    def owned(row):
        return lax.dynamic_slice(row, (shard * part,), (part,))

    up_part = up_bias.shape[0]
    loss = jnp.sum(sums[6]) / valid_count.astype(f32)
    return (
        result.reshape(tokens.shape),
        loss,
        token_grad.reshape(tokens.shape),
        query_grad,
        owned(query_row),
        key_grad,
        value_grad,
        owned(sums[7]),
        up_all[:, :width],
        owned(sums[3]),
        owned(sums[4]),
        owned(sums[5]),
        up_all[:, width:],
        lax.dynamic_slice(sums[8:12].reshape(-1), (shard * up_part,), (up_part,)),
        down_all,
        owned(sums[0]),
        owned(sums[1]),
        owned(sums[2]),
    )


def solution(mesh):
    wide = P("shard", "rep", None, None)
    matrix, vector = P("shard", None), P("shard")
    return jax.shard_map(
        local,
        mesh=mesh,
        in_specs=(
            wide, wide, wide, P("shard", "rep", None), P(),
            matrix, vector, matrix, matrix, vector, matrix, vector, vector, vector,
            matrix, vector, matrix, vector, vector, vector,
        ),
        out_specs=(
            wide, P(), wide,
            matrix, vector, matrix, matrix, vector, matrix, vector, vector, vector,
            matrix, vector, matrix, vector, vector, vector,
        ),
        check_vma=False,
    )
```

```python
import functools

import jax
import jax.numpy as jnp
from jax import lax
from jax.experimental import pallas as pl
from jax.experimental.pallas import tpu as pltpu
from jax.sharding import PartitionSpec as P

HDIM = 64
PPIECE = 512
CLEN = 256
EPSILON = 1e-05
NEGATIVE = -1e30
LOG2E = 1.4426950408889634
SCALE = 1.0 / 8.0
LIMIT = 100.0

f32 = jnp.float32
bf16 = jnp.bfloat16
NT = (((1,), (1,)), ((), ()))
NN = (((1,), (0,)), ((), ()))
TN = (((0,), (0,)), ((), ()))
ANY = pl.BlockSpec(memory_space=pl.ANY)
MESH = pl.DeviceIdType.MESH


def dot(left, right, dims):
    return lax.dot_general(left, right, dims, preferred_element_type=f32)


def params(mib=56, **more):
    return pltpu.CompilerParams(vmem_limit_bytes=mib * 2**20, **more)


def cost(gflop, mbytes):
    return pl.CostEstimate(
        flops=int(gflop * 1e9), bytes_accessed=int(mbytes * 1e6), transcendentals=0
    )


def lane_of(rows):
    return lax.broadcasted_iota(jnp.int32, (rows, 128), 1)


def split3(values):
    hi = values.astype(bf16).astype(f32)
    mid = (values - hi).astype(bf16).astype(f32)
    low = values - hi - mid
    return hi, mid, low


def side_lanes(first, values):
    lane = lane_of(values.shape[0])
    hi, mid, low = split3(values)
    out = jnp.where(lane == 1, -hi, jnp.where(lane == 2, -mid, jnp.where(lane == 3, -low, 0.0)))
    return jnp.where(lane == 0, first, out).astype(bf16)


def gather_kernel(
    wq, wk, wv, vec, tok, keep, up_own,
    fq, fk, fv, fvec, ptok, pkeep, up_full,
    asend, arecv, local_sem, zrecv, yrecv, crecv, usend, dsend, ysend, csend, tsend, trecv,
):
    depth = 4
    rep = lax.axis_index("rep")
    shard = lax.axis_index("shard")
    core = rep % 2
    z = shard // 2
    y = shard % 2
    other_core = {"rep": rep + 1 - 2 * core}
    other_x = {"rep": (rep + 2) % 4}
    other_y = {"shard": z * 2 + 1 - y}
    up = {"shard": (shard + 2) % 8}
    down = {"shard": (shard + 6) % 8}

    barrier = pltpu.get_barrier_semaphore()
    for place in (other_core, other_x, other_y):
        pl.semaphore_signal(barrier, inc=1, device_id=place, device_id_type=MESH)

    @pl.when(z < depth - 1)
    def _():
        pl.semaphore_signal(barrier, inc=1, device_id=up, device_id_type=MESH)

    @pl.when(z > 0)
    def _():
        pl.semaphore_signal(barrier, inc=1, device_id=down, device_id_type=MESH)

    inner = jnp.where((z > 0) & (z < depth - 1), 5, 4)
    pl.semaphore_wait(barrier, inner)

    sources = (wq, wk, wv, vec)
    targets = (fq, fk, fv, fvec)

    def place_of(u, zz, yy, cc):
        if u == 3:
            return targets[u].at[zz * 2 + yy]
        return targets[u].at[(zz * 2 + yy) * 2 + cc]

    def own_of(u):
        return sources[u] if u == 3 else sources[u].at[core]

    def move(src, dst, send, recv, where):
        return pltpu.make_async_remote_copy(
            src_ref=src, dst_ref=dst, send_sem=send, recv_sem=recv,
            device_id=where, device_id_type=MESH,
        )

    def to_up(u, zz, src):
        return move(src, place_of(u, zz, y, core), usend.at[u, zz], zrecv.at[u, zz], up)

    def to_down(u, zz, src):
        return move(src, place_of(u, zz, y, core), dsend.at[u, zz], zrecv.at[u, zz], down)

    def to_y(u, zz, src):
        return move(src, place_of(u, zz, y, core), ysend.at[u, zz], yrecv.at[u, zz], other_y)

    def to_core(u, zz, yy):
        at = place_of(u, zz, yy, core)
        index = zz * 2 + yy
        return move(at, at, csend.at[u, index], crecv.at[u, index], other_core)

    for u in range(4):
        @pl.when(z < depth - 1)
        def _():
            to_up(u, z, own_of(u)).start()

        @pl.when(z > 0)
        def _():
            to_down(u, z, own_of(u)).start()

        to_y(u, z, own_of(u)).start()

    prompt = tok.at[pl.ds(0, PPIECE)]
    copies = [
        move(prompt, ptok.at[1], tsend.at[0], trecv.at[0], other_x),
        move(keep, pkeep.at[1], tsend.at[1], trecv.at[1], other_x),
        move(prompt, ptok.at[0], tsend.at[2], trecv.at[2], other_core),
        move(keep, pkeep.at[0], tsend.at[3], trecv.at[3], other_core),
    ]
    for copy in copies:
        copy.start()
    locals_ = []
    for u in range(4):
        if u == 3:
            dst = fvec.at[shard]
        else:
            dst = targets[u].at[pl.ds(shard * 2, 2)]
        locals_.append(pltpu.make_async_copy(sources[u], dst, local_sem.at[u]))
        locals_[-1].start()

    columns = pl.ds(pl.multiple_of(rep // 2 * HALF_UP, 128), HALF_UP)

    def up_place(zz):
        return up_full.at[(zz * 2 + y) * 2 + core, :, columns]

    def up_up(zz, src):
        return move(src, up_place(zz), asend.at[0, zz], arecv.at[zz], up)

    def up_down(zz, src):
        return move(src, up_place(zz), asend.at[1, zz], arecv.at[zz], down)

    def up_start():
        src = up_own.at[core, :, columns]

        @pl.when(z < depth - 1)
        def _():
            up_up(z, src).start()

        @pl.when(z > 0)
        def _():
            up_down(z, src).start()

    def up_hop(step):
        @pl.when(z - step >= 0)
        def _():
            at = up_place(z - step)
            up_up(z - step, at).wait_recv()
            if step == 1:
                @pl.when(z < depth - 1)
                def _():
                    up_up(z - step, at).start()

        @pl.when(z + step < depth)
        def _():
            at = up_place(z + step)
            up_down(z + step, at).wait_recv()
            if step == 1:
                @pl.when(z > 0)
                def _():
                    up_down(z + step, at).start()

    for step in range(1, depth + 1):
        if step == 2:
            up_start()
        if step == 4:
            up_hop(1)
        for u in range(4):
            if step < depth:
                @pl.when(z - step >= 0)
                def _():
                    zz = z - step
                    at = place_of(u, zz, y, core)
                    to_up(u, zz, at).wait_recv()

                    @pl.when(z < depth - 1)
                    def _():
                        to_up(u, zz, at).start()

                    to_y(u, zz, at).start()
                    if u < 3:
                        to_core(u, zz, y).start()

                @pl.when(z + step < depth)
                def _():
                    zz = z + step
                    at = place_of(u, zz, y, core)
                    to_down(u, zz, at).wait_recv()

                    @pl.when(z > 0)
                    def _():
                        to_down(u, zz, at).start()

                    to_y(u, zz, at).start()
                    if u < 3:
                        to_core(u, zz, y).start()

        for u in range(4):
            def from_y(zz):
                at = targets[u].at[zz * 2 + 1 - y] if u == 3 else place_of(u, zz, 1 - y, core)
                move(at, at, ysend.at[u, zz], yrecv.at[u, zz], other_y).wait_recv()
                if u < 3:
                    to_core(u, zz, 1 - y).start()

            if step == 1:
                from_y(z)
            else:
                @pl.when(z - (step - 1) >= 0)
                def _():
                    from_y(z - (step - 1))

                @pl.when(z + (step - 1) < depth)
                def _():
                    from_y(z + (step - 1))

    up_hop(2)
    copies[0].wait_recv()
    copies[1].wait_recv()
    forward = [
        move(ptok.at[1], ptok.at[2], tsend.at[4], trecv.at[4], other_core),
        move(pkeep.at[1], pkeep.at[2], tsend.at[5], trecv.at[5], other_core),
    ]
    for copy in forward:
        copy.start()

    def others(act):
        for zz in range(depth):
            for yy in range(2):
                @pl.when((zz != z) | (yy != y))
                def _():
                    act(zz, yy)

    for u in range(3):
        def arrived(zz, yy):
            at = place_of(u, zz, yy, 1 - core)
            index = zz * 2 + yy
            move(at, at, csend.at[u, index], crecv.at[u, index], other_core).wait_recv()

        others(arrived)
    copies[2].wait_recv()
    copies[3].wait_recv()
    for copy in forward:
        copy.wait_recv()

    for copy in copies + forward:
        copy.wait_send()
    for zz in range(depth):
        at = up_place(zz)

        @pl.when((zz <= z) & (zz >= z - 1) & (z < depth - 1))
        def _():
            up_up(zz, at).wait_send()

        @pl.when((zz >= z) & (zz <= z + 1) & (z > 0))
        def _():
            up_down(zz, at).wait_send()

    for copy in locals_:
        copy.wait()
    for u in range(4):
        for zz in range(depth):
            at = place_of(u, zz, y, core)
            to_y(u, zz, at).wait_send()

            @pl.when((zz <= z) & (z < depth - 1))
            def _():
                to_up(u, zz, at).wait_send()

            @pl.when((zz >= z) & (z > 0))
            def _():
                to_down(u, zz, at).wait_send()

        if u < 3:
            others(lambda zz, yy: to_core(u, zz, yy).wait_send())


def first_gather(wq, wk, wv, vec, tok, keep, up_own):
    width = wq.shape[1]
    sem = pltpu.SemaphoreType.DMA
    halves = [w.reshape(2, 48, width) for w in (wq, wk, wv)]
    full = jax.ShapeDtypeStruct((16, 48, width), bf16)
    outs = pl.pallas_call(
        gather_kernel,
        in_specs=[ANY] * 7,
        out_specs=[ANY] * 7,
        out_shape=[
            full, full, full,
            jax.ShapeDtypeStruct((8, 16, 128), bf16),
            jax.ShapeDtypeStruct((3, PPIECE, width), bf16),
            jax.ShapeDtypeStruct((3, 8, 128), f32),
            jax.ShapeDtypeStruct((16, 48, up_own.shape[2]), bf16),
        ],
        scratch_shapes=[
            sem((2, 4)), sem((4,)), sem((4,)), sem((4, 4)), sem((4, 4)), sem((3, 8)), sem((4, 4)), sem((4, 4)),
            sem((4, 4)), sem((3, 8)), sem((6,)), sem((6,)),
        ],
        compiler_params=params(60, collective_id=1, has_side_effects=True),
        cost_estimate=cost(0, 20),
    )(*halves, vec, tok, keep, up_own)
    fq, fk, fv, fvec, ptok, pkeep, up_full = outs
    return (
        fq.reshape(width, width), fk.reshape(width, width), fv.reshape(width, width),
        fvec, ptok.reshape(3 * PPIECE, width), pkeep, up_full,
    )


class Link:
    def __init__(self):
        rep = lax.axis_index("rep")
        shard = lax.axis_index("shard")
        self.core = rep % 2
        self.x = rep // 2
        self.z = shard // 2
        self.y = shard % 2
        self.shard = shard
        self.to_core = {"rep": rep + 1 - 2 * self.core}
        self.to_x = {"rep": (rep + 2) % 4}
        self.to_y = {"shard": self.z * 2 + 1 - self.y}
        self.to_up = {"shard": (shard + 2) % 8}
        self.to_down = {"shard": (shard + 6) % 8}

    def greet(self):
        barrier = pltpu.get_barrier_semaphore()
        for place in (self.to_core, self.to_x, self.to_y):
            pl.semaphore_signal(barrier, inc=1, device_id=place, device_id_type=MESH)

        @pl.when(self.z < 3)
        def _():
            pl.semaphore_signal(barrier, inc=1, device_id=self.to_up, device_id_type=MESH)

        @pl.when(self.z > 0)
        def _():
            pl.semaphore_signal(barrier, inc=1, device_id=self.to_down, device_id_type=MESH)

        count = jnp.where((self.z > 0) & (self.z < 3), 5, 4)
        pl.semaphore_wait(barrier, count)


def move(src, dst, send, recv, where):
    return pltpu.make_async_remote_copy(
        src_ref=src, dst_ref=dst, send_sem=send, recv_sem=recv,
        device_id=where, device_id_type=MESH,
    )


class Spread:
    def __init__(self, own, full, sems):
        self.at = Link()
        self.own, self.full = own, full
        (
            self.local, self.zrecv, self.yrecv, self.usend, self.dsend, self.ysend,
            self.xrecv, self.xsend, self.crecv, self.csend,
        ) = sems

    def columns(self, xx):
        return pl.ds(pl.multiple_of(xx * HALF_UP, 128), HALF_UP)

    def place(self, u, zz, yy, cc, xx):
        index = (zz * 2 + yy) * 2 + cc
        if u == 0:
            return self.full[0].at[index, :, self.columns(xx)]
        return self.full[1].at[index]

    def mine(self, u, zz, yy):
        return self.place(u, zz, yy, self.at.core, self.at.x)

    def source(self, u):
        if u == 0:
            return self.own[0].at[self.at.core, :, self.columns(self.at.x)]
        return self.own[1].at[self.at.core]

    def up(self, u, zz, src):
        return move(
            src, self.mine(u, zz, self.at.y), self.usend.at[u, zz], self.zrecv.at[u, zz],
            self.at.to_up,
        )

    def down(self, u, zz, src):
        return move(
            src, self.mine(u, zz, self.at.y), self.dsend.at[u, zz], self.zrecv.at[u, zz],
            self.at.to_down,
        )

    def side(self, u, zz, src):
        return move(
            src, self.mine(u, zz, self.at.y), self.ysend.at[u, zz], self.yrecv.at[u, zz],
            self.at.to_y,
        )

    def across(self, zz, yy):
        at = self.mine(0, zz, yy)
        index = zz * 2 + yy
        return move(at, at, self.xsend.at[index], self.xrecv.at[index], self.at.to_x)

    def twin(self, kind, zz, yy):
        if kind == 1:
            at = self.place(0, zz, yy, self.at.core, 1 - self.at.x)
        else:
            at = self.mine(0 if kind == 0 else 1, zz, yy)
        index = zz * 2 + yy
        return move(
            at, at, self.csend.at[kind, index], self.crecv.at[kind, index], self.at.to_core
        )

    def twin_in(self, kind, zz, yy):
        cc = 1 - self.at.core
        xx = 1 - self.at.x if kind == 1 else self.at.x
        at = self.place(1 if kind == 2 else 0, zz, yy, cc, xx)
        index = zz * 2 + yy
        return move(
            at, at, self.csend.at[kind, index], self.crecv.at[kind, index], self.at.to_core
        )

    def locals_(self):
        return [
            pltpu.make_async_copy(
                self.own[u], self.full[u].at[pl.ds(self.at.shard * 2, 2)], self.local.at[u]
            )
            for u in range(2)
        ]

    def begin(self):
        z, y = self.at.z, self.at.y
        self.at.greet()

        @pl.when(z < 3)
        def _():
            self.up(1, z, self.source(1)).start()

        @pl.when(z > 0)
        def _():
            self.down(1, z, self.source(1)).start()

        @pl.when((z >= 2) & (z < 3))
        def _():
            self.up(0, z - 2, self.mine(0, z - 2, y)).start()

        @pl.when((z <= 1) & (z > 0))
        def _():
            self.down(0, z + 2, self.mine(0, z + 2, y)).start()

        self.side(0, z, self.source(0)).start()
        for step in (1, 2):
            @pl.when(z - step >= 0)
            def _():
                self.side(0, z - step, self.mine(0, z - step, y)).start()
                self.got(0, z - step, y)

            @pl.when(z + step < 4)
            def _():
                self.side(0, z + step, self.mine(0, z + step, y)).start()
                self.got(0, z + step, y)

        self.side(1, z, self.source(1)).start()
        for copy in self.locals_():
            copy.start()

    def got(self, u, zz, yy):
        if u == 0:
            self.across(zz, yy).start()
            self.twin(0, zz, yy).start()
        else:
            self.twin(2, zz, yy).start()

    def hop(self, u, step):
        z, y = self.at.z, self.at.y

        @pl.when(z - step >= 0)
        def _():
            zz = z - step
            at = self.mine(u, zz, y)
            self.up(u, zz, at).wait_recv()
            if step < 3:
                @pl.when(z < 3)
                def _():
                    self.up(u, zz, at).start()

            self.side(u, zz, at).start()
            self.got(u, zz, y)

        @pl.when(z + step < 4)
        def _():
            zz = z + step
            at = self.mine(u, zz, y)
            self.down(u, zz, at).wait_recv()
            if step < 3:
                @pl.when(z > 0)
                def _():
                    self.down(u, zz, at).start()

            self.side(u, zz, at).start()
            self.got(u, zz, y)

    def from_side(self, u, step):
        z, yy = self.at.z, 1 - self.at.y

        def take(zz):
            at = self.mine(u, zz, yy)
            move(at, at, self.ysend.at[u, zz], self.yrecv.at[u, zz], self.at.to_y).wait_recv()
            self.got(u, zz, yy)

        if step == 0:
            take(z)
        else:
            @pl.when(z - step >= 0)
            def _():
                take(z - step)

            @pl.when(z + step < 4)
            def _():
                take(z + step)

    def others(self, act):
        for zz in range(4):
            for yy in range(2):
                @pl.when((zz != self.at.z) | (yy != self.at.y))
                def _():
                    act(zz, yy)

    def from_across(self):
        def take(zz, yy):
            at = self.place(0, zz, yy, self.at.core, 1 - self.at.x)
            index = zz * 2 + yy
            move(at, at, self.xsend.at[index], self.xrecv.at[index], self.at.to_x).wait_recv()
            self.twin(1, zz, yy).start()

        self.others(take)

    def end(self):
        z, y = self.at.z, self.at.y

        def take(zz, yy):
            for kind in range(3):
                self.twin_in(kind, zz, yy).wait_recv()
                self.twin(kind, zz, yy).wait_send()
            self.across(zz, yy).wait_send()

        self.others(take)
        for copy in self.locals_():
            copy.wait()
        for u in range(2):
            for zz in range(4):
                at = self.mine(u, zz, y)
                self.side(u, zz, at).wait_send()

                rising = (zz <= z) & (z < 3)
                falling = (zz >= z) & (z > 0)
                if u == 0:
                    rising = (zz == z - 2) & (z < 3)
                    falling = (zz == z + 2) & (z > 0)

                @pl.when(rising)
                def _():
                    self.up(u, zz, at).wait_send()

                @pl.when(falling)
                def _():
                    self.down(u, zz, at).wait_send()


HALF_UP = 1920


def head_twice(values, head):
    wide = values.astype(f32)
    turned = pltpu.roll(wide, 64, 1)
    first = lane_of(values.shape[0]) < 64
    if head == 0:
        return jnp.where(first, wide, turned).astype(bf16)
    return jnp.where(first, turned, wide).astype(bf16)


def head_parts(values, head):
    wide = values.astype(f32) * (SCALE * LOG2E)
    hi = wide.astype(bf16).astype(f32)
    low = wide - hi
    first = lane_of(values.shape[0]) < 64
    if head == 0:
        return jnp.where(first, hi, pltpu.roll(low, 64, 1)).astype(bf16)
    return jnp.where(first, pltpu.roll(hi, 64, 1), low).astype(bf16)


def head_only(values, head):
    first = lane_of(values.shape[0]) < 64
    keep = first if head == 0 else jnp.logical_not(first)
    return jnp.where(keep, values, jnp.zeros_like(values))


def off_diagonal(size, bias):
    row = lax.broadcasted_iota(jnp.int32, (size, size), 0)
    col = lax.broadcasted_iota(jnp.int32, (size, size), 1)
    return jnp.where(row == col, 0.0, bias)


def attend_setup(kb, brow, kx, vx, bown, bcont):
    for head in range(2):
        kx[head, :, 128:] = kb[...]
    vx[:, 128:] = jnp.ones((2560, 128), bf16)
    bown[...] = off_diagonal(512, brow[0:1, 0:512])
    for c in range(2):
        bcont[c] = off_diagonal(256, brow[0:1, 2048 + 256 * c : 2304 + 256 * c])


def attend_fill(q, k, v, qx, kx, vx):
    ones = jnp.where(lane_of(1024) == 0, 1.0, 0.0).astype(bf16)
    vx[:, :128] = v
    for head in range(2):
        qx[head, :, :128] = head_parts(q, head)
        kx[head, :, :128] = head_twice(k, head)
        qx[head, :, 128:] = ones


def own_scores(head, qx, kx, bown):
    return dot(qx[head, :512, :128], kx[head, :512, :128], NT) + bown[...]


def cont_scores(head, c, qx, kx, bcont):
    rows = slice(512 + 256 * c, 768 + 256 * c)
    keys = slice(2048 + 256 * c, 2304 + 256 * c)
    return dot(qx[head, rows, :128], kx[head, keys, :128], NT) + bcont[c]


def attend_head(head, o, side, qx, kx, vx, pm, pc, bown, bcont, top=None):
    def below(scores, rows):
        if top is None:
            return jnp.exp2(scores).astype(bf16)
        return jnp.exp2(scores - top[head, rows, 0:1]).astype(bf16)

    lane = lane_of(256)
    for c in range(3):
        keys = slice(512 + 512 * c, 1024 + 512 * c)
        pm[head, :, keys] = jnp.exp2(dot(qx[head], kx[head, keys], NT)).astype(bf16)
    pm[head, 512:, :512] = jnp.exp2(dot(qx[head, 512:], kx[head, :512], NT)).astype(bf16)
    pm[head, :512, :512] = below(own_scores(head, qx, kx, bown), slice(0, 512))
    for c in range(2):
        rows = slice(512 + 256 * c, 768 + 256 * c)
        pc[head, c] = below(cont_scores(head, c, qx, kx, bcont), rows)
    for r in range(4):
        rows = slice(256 * r, 256 * r + 256)
        total = dot(pm[head, rows], vx[:2048], NN)
        if r >= 2:
            total = total + dot(pc[head, r - 2], vx[1536 + 256 * r : 1792 + 256 * r], NN)
        mass = total[:, 128:]
        value = total[:, :128] / mass
        if head == 0:
            o[rows] = value.astype(bf16)
        else:
            o[rows] = jnp.where(lane < 64, o[rows].astype(f32), value).astype(bf16)
        logs = jnp.log2(mass)
        if top is not None:
            logs = logs + top[head, rows]
        side[head, rows] = side_lanes(1.0, logs)


ROW_STEPS = 5


def near_kernel(
    tok, oth, wq, wk, wv, qb, vb, kb, brow, *refs, linked
):
    if linked:
        own_parts, refs = refs[:2], refs[3:]
    q, k, v, xt, qn, kn, o, side = refs[:8]
    refs = refs[8:]
    if linked:
        full, refs = refs[:2], refs[2:]
    qs, ks, vs, qx, kx, vx, pm, pc, bown, bcont = refs[:10]
    step = pl.program_id(0)
    spread = Spread(own_parts, full, refs[10:]) if linked else None

    def comm(at, act):
        if linked:
            @pl.when(step == at)
            def _():
                act()

    comm(0, lambda: spread.begin())
    width = wq.shape[0]

    @pl.when(step < ROW_STEPS)
    def _():
        own = (step == 0) | (step == 4)
        row = lax.broadcasted_iota(jnp.int32, (width, 128), 0)
        lane = lax.broadcasted_iota(jnp.int32, (width, 128), 1)
        heads = jnp.where(row // HDIM == lane, 1.0, 0.0).astype(bf16)
        at = pl.ds(pl.multiple_of(step * PPIECE, PPIECE), PPIECE)

        @pl.when(step == 0)
        def _():
            qn[...] = jnp.zeros_like(qn)
            kn[...] = jnp.zeros_like(kn)
            attend_setup(kb, brow, kx, vx, bown, bcont)

        def norms(values):
            wide = values.astype(f32)
            sums = dot((wide * wide).astype(bf16), heads, NN)
            return jnp.broadcast_to(jnp.max(sums, axis=0, keepdims=True), (8, 128))

        def keep(low, out, held, where):
            out[...] = low
            for p in range(width // 128):
                held[p, where] = low[:, 128 * p : 128 * p + 128]

        def keys(rows):
            low = dot(rows, wk[...], NN).astype(bf16)
            keep(low, k, ks, at)
            kn[...] = jnp.maximum(kn[...], norms(low))
            keep((dot(rows, wv[...], NN) + vb[...].astype(f32)).astype(bf16), v, vs, at)
            xt[...] = jnp.transpose(rows)

        @pl.when(own)
        def _():
            rows = tok[...]
            keys(rows)
            low = (dot(rows, wq[...], NN) + qb[...].astype(f32)).astype(bf16)
            keep(low, q, qs, pl.ds(pl.multiple_of(step // 4 * PPIECE, PPIECE), PPIECE))
            qn[...] = jnp.maximum(qn[...], norms(low))

        @pl.when(jnp.logical_not(own))
        def _():
            keys(oth[...])

    comm(4, lambda: (spread.hop(0, 3), spread.hop(1, 1)))

    @pl.when(step >= ROW_STEPS)
    def _():
        p = step - ROW_STEPS
        attend_fill(qs[p], ks[p], vs[p], qx, kx, vx)
        attend_head(0, o, side, qx, kx, vx, pm, pc, bown, bcont)

    comm(5, lambda: [spread.from_side(0, j) for j in range(3)])
    comm(6, lambda: spread.hop(1, 2))
    comm(7, lambda: (spread.from_side(1, 0), spread.from_side(0, 3)))
    comm(9, lambda: spread.from_side(1, 1))
    comm(10, lambda: spread.from_side(1, 2))

    @pl.when(step >= ROW_STEPS)
    def _():
        attend_head(1, o, side, qx, kx, vx, pm, pc, bown, bcont)

    comm(7, lambda: spread.hop(1, 3))
    comm(8, lambda: spread.from_across())
    comm(10, lambda: (spread.from_side(1, 3), spread.end()))


def attend_near(tok, oth, wq, wk, wv, qb, vb, kb, brow, own_parts):
    width = tok.shape[1]
    linked = bool(own_parts)
    pairs = width // 128
    block = (PPIECE, width)

    def once(*shape):
        return pl.BlockSpec(shape, lambda i: (0,) * len(shape), pipeline_mode=pl.Buffered(1))

    def rows_at(i):
        return jnp.minimum(i, ROW_STEPS - 1)

    def pair_at(i):
        return jnp.maximum(i - ROW_STEPS, 0)

    small = pl.BlockSpec((8, 128), lambda i: (0, 0))
    extra_shape, extra_sems, more = [], [], {}
    if linked:
        sem = pltpu.SemaphoreType.DMA
        extra_shape = [
            jax.ShapeDtypeStruct((16, 48, own_parts[0].shape[2]), bf16),
            jax.ShapeDtypeStruct((16, 192, width), bf16),
        ]
        extra_sems = [
            sem((2,)), sem((2, 4)), sem((2, 4)), sem((2, 4)), sem((2, 4)), sem((2, 4)),
            sem((8,)), sem((8,)), sem((3, 8)), sem((3, 8)),
        ]
        more = {"collective_id": 3, "has_side_effects": True}
    return pl.pallas_call(
        functools.partial(near_kernel, linked=linked),
        grid=(ROW_STEPS + pairs,),
        in_specs=[
            pl.BlockSpec(block, lambda i: (rows_at(i) // 4, 0)),
            pl.BlockSpec(block, lambda i: (jnp.clip(i - 1, 0, 2), 0)),
            once(width, width), once(width, width), once(width, width),
            once(1, width), once(1, width), once(2560, 128), once(8, 2560),
        ] + [ANY] * len(own_parts),
        out_specs=[
            pl.BlockSpec(block, lambda i: (rows_at(i) // 4, 0)),
            pl.BlockSpec(block, lambda i: (rows_at(i), 0)),
            pl.BlockSpec(block, lambda i: (rows_at(i), 0)),
            pl.BlockSpec((width, PPIECE), lambda i: (0, rows_at(i))),
            small, small,
            pl.BlockSpec((1024, 128), lambda i: (0, pair_at(i))),
            pl.BlockSpec((2, 1024, 128), lambda i: (pair_at(i), 0, 0)),
        ] + [ANY] * len(extra_shape),
        out_shape=[
            jax.ShapeDtypeStruct((1024, width), bf16),
            jax.ShapeDtypeStruct((2560, width), bf16),
            jax.ShapeDtypeStruct((2560, width), bf16),
            jax.ShapeDtypeStruct((width, 2560), bf16),
            jax.ShapeDtypeStruct((8, 128), f32),
            jax.ShapeDtypeStruct((8, 128), f32),
            jax.ShapeDtypeStruct((1024, width), bf16),
            jax.ShapeDtypeStruct((2 * pairs, 1024, 128), bf16),
        ] + extra_shape,
        scratch_shapes=[
            pltpu.VMEM((pairs, 1024, 128), bf16),
            pltpu.VMEM((pairs, 2560, 128), bf16),
            pltpu.VMEM((pairs, 2560, 128), bf16),
            pltpu.VMEM((2, 1024, 256), bf16),
            pltpu.VMEM((2, 2560, 256), bf16),
            pltpu.VMEM((2560, 256), bf16),
            pltpu.VMEM((2, 1024, 2048), bf16),
            pltpu.VMEM((2, 2, 256, 256), bf16),
            pltpu.VMEM((512, 512), f32),
            pltpu.VMEM((2, 256, 256), f32),
        ] + extra_sems,
        input_output_aliases={11: 8} if linked else {},
        compiler_params=params(60, **more),
        cost_estimate=cost(50, 50),
    )(tok, oth, wq, wk, wv, qb, vb, kb, brow, *own_parts)


def far_kernel(
    q, k, v, kb, brow, qn, kn, o_in, side_in, o_out, side_out,
    qs, ks, vs, o, side, qx, kx, vx, pm, pc, bown, bcont, top, sems,
):
    pair = pl.program_id(0)
    widest_product = jnp.max(qn[...] * kn[...]) * ((SCALE * LOG2E) ** 2 * 1.1)

    @pl.when(widest_product > LIMIT * LIMIT)
    def _():
        at = pl.ds(pl.multiple_of(pair * 128, 128), 128)
        copies = [
            pltpu.make_async_copy(ref.at[:, at], held, sems.at[i])
            for i, (ref, held) in enumerate(((q, qs), (k, ks), (v, vs)))
        ]
        for copy in copies:
            copy.start()
        for copy in copies:
            copy.wait()
        attend_setup(kb, brow, kx, vx, bown, bcont)
        attend_fill(qs[...], ks[...], vs[...], qx, kx, vx)

        def widest(scores):
            return jnp.broadcast_to(
                jnp.max(scores, axis=1, keepdims=True), (scores.shape[0], 128)
            )

        for head in range(2):
            def more(c, carry):
                found = widest(dot(qx[head], kx[head, pl.ds(512 + c * 256, 256)], NT))
                top[head] = jnp.maximum(top[head], found)
                return carry

            top[head] = jnp.full((1024, 128), -3e38, f32)
            lax.fori_loop(0, 6, more, 0)
            top[head, 0:512] = jnp.maximum(
                top[head, 0:512], widest(own_scores(head, qx, kx, bown))
            )
            top[head, 512:1024] = jnp.maximum(
                top[head, 512:1024], widest(dot(qx[head, 512:], kx[head, :512], NT))
            )
            for c in range(2):
                rows = slice(512 + 256 * c, 768 + 256 * c)
                top[head, rows] = jnp.maximum(
                    top[head, rows], widest(cont_scores(head, c, qx, kx, bcont))
                )
            qx[head, :, 128:] = side_lanes(1.0, top[head])
            attend_head(head, o, side, qx, kx, vx, pm, pc, bown, bcont, top)
        copies = [
            pltpu.make_async_copy(o, o_out.at[:, at], sems.at[0]),
            pltpu.make_async_copy(side, side_out.at[pl.ds(pair * 2, 2)], sems.at[1]),
        ]
        for copy in copies:
            copy.start()
        for copy in copies:
            copy.wait()


def attend_far(q, k, v, kb, brow, qn, kn, o, side):
    def fixed(*shape):
        return pl.BlockSpec(shape, lambda i: (0,) * len(shape), pipeline_mode=pl.Buffered(1))

    return pl.pallas_call(
        far_kernel,
        grid=(q.shape[1] // 128,),
        in_specs=[
            ANY, ANY, ANY, fixed(2560, 128), fixed(8, 2560), fixed(8, 128), fixed(8, 128),
            ANY, ANY,
        ],
        out_specs=[ANY, ANY],
        out_shape=[
            jax.ShapeDtypeStruct(o.shape, bf16), jax.ShapeDtypeStruct(side.shape, bf16),
        ],
        scratch_shapes=[
            pltpu.VMEM((1024, 128), bf16),
            pltpu.VMEM((2560, 128), bf16),
            pltpu.VMEM((2560, 128), bf16),
            pltpu.VMEM((1024, 128), bf16),
            pltpu.VMEM((2, 1024, 128), bf16),
            pltpu.VMEM((2, 1024, 256), bf16),
            pltpu.VMEM((2, 2560, 256), bf16),
            pltpu.VMEM((2560, 256), bf16),
            pltpu.VMEM((2, 1024, 2048), bf16),
            pltpu.VMEM((2, 2, 256, 256), bf16),
            pltpu.VMEM((512, 512), f32),
            pltpu.VMEM((2, 256, 256), f32),
            pltpu.VMEM((2, 1024, 128), f32),
            pltpu.SemaphoreType.DMA((3,)),
        ],
        input_output_aliases={7: 0, 8: 1},
        compiler_params=params(),
        cost_estimate=cost(0.1, 1),
    )(q, k, v, kb, brow, qn, kn, o, side)


def back_fill(q, k, v, d, o, side, kb, qx, qd, kx, vx, dx, qm, kt, bown, bcont):
    @pl.when(pl.program_id(0) == 0)
    def _():
        for head in range(2):
            kx[head, :, 128:] = kb[...]
        vx[:, 128:] = kb[...]
        column = kb[:, 0:1].astype(f32)
        bown[...] = off_diagonal(512, column[:512]).astype(bf16)
        for c in range(2):
            keys = slice(2048 + 256 * c, 2304 + 256 * c)
            bcont[c] = off_diagonal(256, column[keys]).astype(bf16)

    lane = lane_of(1024)
    vx[:, :128] = v[...]
    kt[...] = jnp.transpose(k[...].astype(f32)).astype(bf16)
    product = d[...].astype(f32) * o[...].astype(f32)
    for head in range(2):
        parts = head_parts(q[...], head)
        qx[head, :, :128] = parts
        qd[head, :, :128] = parts
        tail = side[head]
        qx[head, :, 128:] = tail
        qd[head, :, 128:] = jnp.where(lane == 0, jnp.zeros_like(tail), tail)
        kx[head, :, :128] = head_twice(k[...], head)
        qm[head] = head_only(q[...], head)
        dx[head, :, :128] = head_only(d[...], head)
        inner = jnp.sum(head_only(product, head), axis=1, keepdims=True)
        dx[head, :, 128:] = side_lanes(0.0, jnp.broadcast_to(inner, (1024, 128)))


def back_head(head, qx, qd, kx, vx, dx, qm, kt, pt, st, pc, sc, bown, bcont):
    def tile(keys, rows, queries, bias=None):
        scores = dot(kx[head, keys], queries[head, rows], NT)
        if bias is not None:
            scores = scores + bias.astype(f32)
        probs = jnp.exp2(scores)
        return probs.astype(bf16), (probs * dot(vx[keys], dx[head, rows], NT)).astype(bf16)

    for c in range(3):
        keys = slice(512 + 512 * c, 1024 + 512 * c)
        pt[keys], st[keys] = tile(keys, slice(0, 1024), qx)
    pt[:512, 512:], st[:512, 512:] = tile(slice(0, 512), slice(512, 1024), qx)
    pt[:512, :512], st[:512, :512] = tile(slice(0, 512), slice(0, 512), qd, bown[...])
    for c in range(2):
        keys = slice(2048 + 256 * c, 2304 + 256 * c)
        pc[c], sc[c] = tile(keys, slice(512 + 256 * c, 768 + 256 * c), qd, bcont[c])
    kth = kt[64 * head : 64 * head + 64]
    main = dot(kth[:, :2048], st[...], NN)
    extra = [dot(kth[:, 2048 + 256 * c : 2304 + 256 * c], sc[c], NN) for c in range(2)]
    rows = jnp.concatenate(
        [main[:, :512], main[:, 512:768] + extra[0], main[:, 768:] + extra[1]], axis=1
    )
    return rows


def back_keys(head, dx, qm, pt, st, pc, sc, acc):
    def put(keys, cols, value):
        if head == 0:
            acc[keys, cols] = value
        else:
            acc[keys, cols] += value

    left, right = slice(0, 128), slice(128, 256)
    for c in range(4):
        keys = slice(512 * c, 512 * c + 512)
        put(keys, left, dot(st[keys], qm[head], NN) * SCALE)
        put(keys, right, dot(pt[keys], dx[head, :, :128], NN))
    for c in range(2):
        keys = slice(2048 + 256 * c, 2304 + 256 * c)
        rows = slice(512 + 256 * c, 768 + 256 * c)
        put(keys, left, dot(sc[c], qm[head, rows], NN) * SCALE)
        put(keys, right, dot(pc[c], dx[head, rows, :128], NN))


BACK_SCRATCH = [
    pltpu.VMEM((2, 1024, 256), bf16),
    pltpu.VMEM((2, 1024, 256), bf16),
    pltpu.VMEM((2, 2560, 256), bf16),
    pltpu.VMEM((2560, 256), bf16),
    pltpu.VMEM((2, 1024, 256), bf16),
    pltpu.VMEM((2, 1024, 128), bf16),
    pltpu.VMEM((128, 2560), bf16),
    pltpu.VMEM((2048, 1024), bf16),
    pltpu.VMEM((2048, 1024), bf16),
    pltpu.VMEM((2, 256, 256), bf16),
    pltpu.VMEM((2, 256, 256), bf16),
    pltpu.VMEM((512, 512), bf16),
    pltpu.VMEM((2, 256, 256), bf16),
    pltpu.VMEM((2560, 256), f32),
]


def back_specs():
    def pair(rows):
        return pl.BlockSpec((rows, 128), lambda i: (0, i))

    def once(*shape):
        return pl.BlockSpec(shape, lambda i: (0,) * len(shape), pipeline_mode=pl.Buffered(1))

    return [
        pair(1024), pair(2560), pair(2560), pair(1024), pair(1024),
        pl.BlockSpec((2, 1024, 128), lambda i: (i, 0, 0)),
        once(2560, 128), once(768, 2560),
    ]


def back_alone_kernel(q, k, v, d, o, side, kb, xt, dq, cont, partial_rows, whole, *scratch):
    (qx, qd, kx, vx, dx, qm, kt, pt, st, pc, sc, bown, bcont, acc) = scratch
    back_fill(q, k, v, d, o, side, kb, qx, qd, kx, vx, dx, qm, kt, bown, bcont)
    rows = []
    for head in range(2):
        rows.append(back_head(head, qx, qd, kx, vx, dx, qm, kt, pt, st, pc, sc, bown, bcont))
        back_keys(head, dx, qm, pt, st, pc, sc, acc)
    delta = jnp.transpose(jnp.concatenate(rows, axis=0) * SCALE).astype(bf16)
    dq[...] = delta
    low = acc[...].astype(bf16)
    partial_rows[...] = low[:2048]
    cont[...] = low[2048:]
    grad = dot(xt[:, :512], delta[:512], NN) + dot(xt[:, 2048:], delta[512:], NN)
    whole[:, :128] = grad.astype(bf16)
    whole[:, 128:] = dot(xt[...], low, NN).astype(bf16)


def attend_back_alone(q, k, v, d, o, side, kb, xt):
    width = q.shape[1]
    count = width // 128
    return pl.pallas_call(
        back_alone_kernel,
        grid=(count,),
        in_specs=back_specs(),
        out_specs=[
            pl.BlockSpec((1024, 128), lambda i: (0, i)),
            pl.BlockSpec((512, 256), lambda i: (0, i)),
            pl.BlockSpec((2048, 256), lambda i: (0, i)),
            pl.BlockSpec((width, 384), lambda i: (0, i)),
        ],
        out_shape=[
            jax.ShapeDtypeStruct((1024, width), bf16),
            jax.ShapeDtypeStruct((512, 2 * width), bf16),
            jax.ShapeDtypeStruct((2048, 2 * width), bf16),
            jax.ShapeDtypeStruct((width, 3 * width), bf16),
        ],
        scratch_shapes=BACK_SCRATCH,
        compiler_params=params(60),
        cost_estimate=cost(100, 40),
    )(q, k, v, d, o, side, kb, xt)


PAIRS = 6
A_X = 2
B_Y = 2
AB_COPIES = 15
PAIR_COPIES = 11


def back_linked_kernel(
    q, k, v, d, o, side, kb, xt, xa, xb, wq, wk, wv, adel,
    token_grad, gq, gk, gv, qrow, ga, gb,
    qx, qd, kx, vx, dx, qm, kt, pt, st, pc, sc, bown, bcont, acc,
    a_mine, a_x, a_y, a_z, a_q, b_mine, b_y, b_z, b_r,
    p_mine, p_other, c_in, y_in, z_in, r_in, keys_low, k_in, k_far, k_x, dw,
    dq, cont_k, cont_v, own_k, own_v, wsem, lsem, ab_send, ab_recv, p_send, p_recv,
):
    step = pl.program_id(0)
    rep = lax.axis_index("rep")
    shard = lax.axis_index("shard")
    core = rep % 2
    x = rep // 2
    z = shard // 2
    y = shard % 2
    rep1 = rep + 1 - 2 * core
    to_rep = [None, {"rep": rep1}, {"rep": (rep + 2) % 4}, {"rep": (rep1 + 2) % 4}]
    to_y = {"shard": z * 2 + 1 - y}
    zs = [z, z + 1 - 2 * (z % 2), (z + 2) % 4, 3 - z]
    to_z = [None] + [{"shard": zs[j] * 2 + y} for j in range(1, 4)]

    def move(src, dst, send, recv, where):
        return pltpu.make_async_remote_copy(
            src_ref=src, dst_ref=dst, send_sem=send, recv_sem=recv,
            device_id=where, device_id_type=MESH,
        )

    def ab(index, src, dst, where):
        return move(src, dst, ab_send.at[index], ab_recv.at[index], where)

    def columns(which):
        return pl.ds(pl.multiple_of(which * HALF_UP, 128), HALF_UP)

    def copy_ax():
        return ab(0, xa.at[:, :, columns(1 - x)], a_x, to_rep[2])

    def copy_ay():
        return ab(1, a_mine.at[pl.ds(4, 4)], a_y, to_y)

    def copy_az(j):
        return ab(1 + j, a_mine.at[j], a_z.at[j - 1], to_z[j])

    def copy_aq(j):
        src = a_q.at[1] if j == 3 else a_q.at[0]
        return ab(4 + j, src, a_q.at[j], to_rep[2 if j == 1 else 1])

    def copy_by():
        return ab(8, xb.at[pl.ds(4, 4)], b_y, to_y)

    def copy_bz(j):
        return ab(8 + j, b_mine.at[j], b_z.at[j - 1], to_z[j])

    def copy_br(j):
        return ab(12 + j, b_r.at[2 * j], b_r.at[2 * j + 1], to_rep[2 - j])

    def pair_copy(p, index, src, dst, where):
        return move(src, dst, p_send.at[p, index], p_recv.at[p, index], where)

    def copy_core(p):
        return pair_copy(p, 0, p_other, c_in.at[p % 2], to_rep[1])

    def copy_y(p):
        return pair_copy(p, 1, p_mine.at[p % 3, pl.ds(4, 4)], y_in.at[p % 2], to_y)

    def copy_z(p, j):
        return pair_copy(p, 1 + j, p_mine.at[p % 3, j], z_in.at[p % 2, j - 1], to_z[j])

    def copy_rep(p, j):
        return pair_copy(
            p, 5 + j, r_in.at[p % 2, 2 * j], r_in.at[p % 2, 2 * j + 1], to_rep[2 - j]
        )

    def copy_near(p):
        return pair_copy(p, 8, keys_low.at[p % 2, pl.ds(512, 512)], k_in.at[p % 2], to_rep[1])

    def copy_far(p):
        return pair_copy(p, 9, keys_low.at[p % 2, pl.ds(1536, 512)], k_far.at[p % 2], to_rep[1])

    def copy_turn(p):
        return pair_copy(p, 10, keys_low.at[p % 2, pl.ds(1024, 512)], k_x.at[p % 2], to_rep[2])

    def after_core(p):
        slot = p % 2
        copy_core(p).wait()
        for i in range(8):
            p_mine[p % 3, i] = p_mine[p % 3, i] + c_in[slot, i]
        copy_y(p).start()
        copy_near(p).wait()
        copy_far(p).wait()
        keys_low[slot, 1024:1536] = keys_low[slot, 1024:1536] + k_far[slot]
        copy_turn(p).start()
        keys_low[slot, :512] = keys_low[slot, :512] + k_in[slot]

    def after_y(p):
        copy_y(p).wait()
        for i in range(4):
            p_mine[p % 3, i] = p_mine[p % 3, i] + y_in[p % 2, i]
        for j in range(1, 4):
            copy_z(p, j).start()

    def own_keys(p):
        slot = p % 2
        copy_turn(p).wait()
        total = keys_low[slot, :512] + k_x[slot]
        at = pl.ds(pl.multiple_of(p * 128, 128), 128)
        own_k[:, at] = total[:, :128]
        own_v[:, at] = total[:, 128:]

    def after_z(p):
        slot = p % 2
        for j in range(1, 4):
            copy_z(p, j).wait()
        total = p_mine[p % 3, 0].astype(f32)
        for j in range(3):
            total = total + z_in[slot, j].astype(f32)
        r_in[slot, 0] = total.astype(bf16)
        copy_rep(p, 0).start()

    def after_x(p):
        slot = p % 2
        copy_rep(p, 0).wait()
        r_in[slot, 2] = r_in[slot, 0] + r_in[slot, 1]
        copy_rep(p, 1).start()

    def after_twin(p):
        slot = p % 2
        copy_rep(p, 1).wait()
        at = pl.ds(pl.multiple_of(p * 128, 128), 128)
        for half in range(2):
            total = r_in[slot, 2 + half]
            rows = core if half == 0 else 1 - core
            rows = pl.ds(pl.multiple_of(rows * 48, 16), 48)
            for j, out in enumerate((gq, gk, gv)):
                out[rows, at] = total[:48, 128 * j : 128 * j + 128]
            if half == 0:
                qrow[:, at] = total[48:64, :128]

    stages = (
        (5, after_twin), (4, after_x), (3, after_z), (2, after_y), (2, own_keys), (1, after_core),
    )

    def sum_pieces(total, more, count):
        def sum_piece(i, carry):
            total[i] = total[i] + more[i]
            return carry

        lax.fori_loop(0, count, sum_piece, 0)

    def sum_four(first, rest, out):
        total = first[0].astype(f32)
        for j in range(3):
            total = total + rest[j].astype(f32)
        out[0] = total.astype(bf16)

    @pl.when(step == 0)
    def _():
        barrier = pltpu.get_barrier_semaphore()
        for place in to_rep[1:] + [to_y] + to_z[1:]:
            pl.semaphore_signal(barrier, inc=1, device_id=place, device_id_type=MESH)
        pl.semaphore_wait(barrier, 7)
        copy_by().start()
        copy_ax().start()
        for copy in (
            pltpu.make_async_copy(xa.at[:, :, columns(x)], a_mine, lsem.at[0]),
            pltpu.make_async_copy(xb.at[pl.ds(0, 4)], b_mine, lsem.at[1]),
        ):
            copy.start()

    back_fill(q, k, v, d, o, side, kb, qx, qd, kx, vx, dx, qm, kt, bown, bcont)
    turned = []
    turned.append(back_head(0, qx, qd, kx, vx, dx, qm, kt, pt, st, pc, sc, bown, bcont))
    back_keys(0, dx, qm, pt, st, pc, sc, acc)

    for back, stage in stages:
        @pl.when(step >= back)
        def _():
            stage(step - back)

    @pl.when(step == 4)
    def _():
        copy_ay().wait()
        sum_pieces(a_mine, a_y, 4)
        for j in range(1, 4):
            copy_az(j).start()

    turned.append(back_head(1, qx, qd, kx, vx, dx, qm, kt, pt, st, pc, sc, bown, bcont))
    back_keys(1, dx, qm, pt, st, pc, sc, acc)

    @pl.when(step == A_X)
    def _():
        copy_ax().wait()
        pltpu.make_async_copy(xa.at[:, :, columns(x)], a_mine, lsem.at[0]).wait()
        sum_pieces(a_mine, a_x, 8)
        copy_ay().start()

    @pl.when(step == B_Y)
    def _():
        copy_by().wait()
        pltpu.make_async_copy(xb.at[pl.ds(0, 4)], b_mine, lsem.at[1]).wait()
        sum_pieces(b_mine, b_y, 4)
        for j in range(1, 4):
            copy_bz(j).start()

    @pl.when(step == 4)
    def _():
        for j in range(1, 4):
            copy_bz(j).wait()
        sum_four(b_mine, b_z, b_r)
        copy_br(0).start()

    def loads():
        wide = pl.ds(0, 768)
        return [
            pltpu.make_async_copy(wq, pt.at[pl.ds(0, 768), wide], wsem.at[0]),
            pltpu.make_async_copy(wk, pt.at[pl.ds(1024, 768), wide], wsem.at[1]),
            pltpu.make_async_copy(wv, st.at[pl.ds(0, 768), wide], wsem.at[2]),
            pltpu.make_async_copy(adel, st.at[pl.ds(1024, 1024), wide], wsem.at[3]),
        ]

    def results(half):
        rows = pl.ds(512 * half, 512)
        return pltpu.make_async_copy(dq.at[rows], token_grad.at[rows], wsem.at[4 + half])

    def tokens_half(half):
        rows = slice(512 * half, 512 * half + 512)
        far_rows = slice(1024 + 512 * half, 1536 + 512 * half)
        total = st[far_rows, :768].astype(f32) + dot(dq[rows], pt[:768, :768], NT)
        total = total + dot((own_k if half == 0 else cont_k)[...], pt[1024:1792, :768], NT)
        total = total + dot((own_v if half == 0 else cont_v)[...], st[:768, :768], NT)
        dq[rows] = total.astype(bf16)
        results(half).start()

    @pl.when(step == PAIRS - 1)
    def _():
        for load in loads():
            load.start()

    delta = jnp.transpose(jnp.concatenate(turned, axis=0) * SCALE)
    low = delta.astype(bf16)
    pair_at = pl.ds(pl.multiple_of(step * 128, 128), 128)
    dq[:, pair_at] = low
    slot = step % 2
    keys_low[slot] = acc[:2048].astype(bf16)
    tail = acc[2048:].astype(bf16)
    cont_k[:, pair_at] = tail[:, :128]
    cont_v[:, pair_at] = tail[:, 128:]
    copy_near(step).start()
    copy_far(step).start()
    grad = dot(xt[:, :512], low[:512], NN) + dot(xt[:, 2048:], low[512:], NN)
    dw[:, :128] = grad.astype(bf16)
    dw[:, 128:] = (dot(xt[:, :2048], keys_low[slot], NN) + dot(xt[:, 2048:], tail, NN)).astype(bf16)
    extra = jnp.sum(low.astype(f32), axis=0, keepdims=True)
    extra = jnp.concatenate([jnp.broadcast_to(extra, (16, 128)), jnp.zeros((16, 256), f32)], axis=1)
    extra = extra.astype(bf16)
    for i in range(8):
        place = (zs[i % 4] * 2 + (y if i < 4 else 1 - y)) * 2
        at = pl.multiple_of((place + core) * 48, 16)
        p_mine[step % 3, i, :48] = dw[pl.ds(at, 48)]
        p_mine[step % 3, i, 48:] = extra
        at = pl.multiple_of((place + 1 - core) * 48, 16)
        p_other[i, :48] = dw[pl.ds(at, 48)]
        p_other[i, 48:] = extra
    copy_core(step).start()

    @pl.when(step == PAIRS - 1)
    def _():
        def late(at):
            for back, stage in stages:
                if 0 <= at - back < PAIRS:
                    stage(at - back)

        late(PAIRS)
        for load in loads():
            load.wait()
        tokens_half(1)
        copy_br(0).wait()
        b_r[2] = b_r[0] + b_r[1]
        copy_br(1).start()
        late(PAIRS + 1)
        for j in range(1, 4):
            copy_az(j).wait()
        sum_four(a_mine, a_z, a_q)
        copy_aq(1).start()
        copy_aq(2).start()
        tokens_half(0)
        late(PAIRS + 2)
        copy_aq(1).wait()
        copy_aq(3).start()
        copy_br(1).wait()
        gb[core] = b_r[2]
        gb[1 - core] = b_r[3]
        late(PAIRS + 3)
        copy_aq(2).wait()
        copy_aq(3).wait()
        for j, (rows, which) in enumerate(
            ((core, x), (core, 1 - x), (1 - core, x), (1 - core, 1 - x))
        ):
            rows = pl.ds(pl.multiple_of(rows * 48, 16), 48)
            ga[rows, columns(which)] = a_q[j]
        late(PAIRS + 4)
        for half in range(2):
            results(half).wait()


def attend_back(q, k, v, d, o, side, kb, xt, xa, xb, wq, wk, wv, adel):
    width = q.shape[1]
    count = width // 128
    full = xa.shape[2]

    def held(*shape):
        return pl.BlockSpec(shape, lambda i: (0,) * len(shape), pipeline_mode=pl.Buffered(1))

    def vm(*shape):
        return pltpu.VMEM(shape, bf16)

    def out(*shape):
        return jax.ShapeDtypeStruct(shape, bf16)

    sem = pltpu.SemaphoreType.DMA
    piece = (64, 384)
    return pl.pallas_call(
        back_linked_kernel,
        grid=(count,),
        in_specs=back_specs() + [ANY] * 6,
        out_specs=[
            ANY, held(96, width), held(96, width), held(96, width),
            held(16, width), held(96, full), held(2, 208, width),
        ],
        out_shape=[
            out(1024, width), out(96, width), out(96, width), out(96, width),
            out(16, width), out(96, full), out(2, 208, width),
        ],
        scratch_shapes=BACK_SCRATCH
        + [
            vm(8, 48, HALF_UP), vm(8, 48, HALF_UP), vm(4, 48, HALF_UP), vm(3, 48, HALF_UP),
            vm(4, 48, HALF_UP), vm(4, 208, width), vm(4, 208, width), vm(3, 208, width),
            vm(4, 208, width),
            vm(3, 8, *piece), vm(8, *piece), vm(2, 8, *piece), vm(2, 4, *piece),
            vm(2, 3, *piece), vm(2, 4, *piece), vm(2, 2048, 256), vm(2, 512, 256),
            vm(2, 512, 256), vm(2, 512, 256), vm(width, 384),
            vm(1024, width), vm(512, width), vm(512, width), vm(512, width), vm(512, width),
            sem((6,)), sem((2,)), sem((AB_COPIES,)), sem((AB_COPIES,)), sem((PAIRS, PAIR_COPIES)),
            sem((PAIRS, PAIR_COPIES)),
        ],
        compiler_params=params(62, collective_id=2, has_side_effects=True),
        cost_estimate=cost(100, 40),
    )(q, k, v, d, o, side, kb, xt, xa, xb, wq, wk, wv, adel)


def gelu_parts(x):
    bell = jnp.exp2(x * x * (-0.5 * LOG2E))
    t = 1.0 / (1.0 + (0.3275911 * 0.7071067811865476) * jnp.abs(x))
    poly = 0.5 * 1.061405429
    for term in (-1.453152027, 1.421413741, -0.284496736, 0.254829592):
        poly = poly * t + 0.5 * term
    below = poly * t * bell
    phi = jnp.where(x >= 0.0, 1.0 - below, below)
    return x * phi, phi + x * bell * 0.3989422804014327


def normed_of(values):
    centered = values - jnp.mean(values, axis=-1, keepdims=True)
    spread = lax.rsqrt(jnp.mean(centered * centered, axis=-1, keepdims=True) + EPSILON)
    return centered * spread, spread


def norm_back(incoming, normed, spread, gain):
    scaled = incoming * gain
    centered = scaled - jnp.mean(scaled, axis=-1, keepdims=True)
    return (centered - normed * jnp.mean(scaled * normed, axis=-1, keepdims=True)) * spread


FCH = 768


def forward_back_kernel(
    mixed, tok, cot, teach, keep, scale, vecs, upb, up_full, down_full,
    result, hid_o, act_o, ddel_o, udel_o, adel_o, mdel_o, sums,
    wa_pieces, wu_pieces, wd_pieces, slope, sems,
):
    step = pl.program_id(0)
    width = tok.shape[1]
    hidden_units = upb.shape[1]

    loads = [
        pltpu.make_async_copy(up_full.at[:, :, pl.ds(0, width)], wa_pieces, sems.at[0]),
        pltpu.make_async_copy(up_full.at[:, :, pl.ds(width, hidden_units)], wu_pieces, sems.at[1]),
        pltpu.make_async_copy(down_full, wd_pieces, sems.at[2]),
    ]

    @pl.when(step == 0)
    def _():
        for load in loads:
            load.start()
        sums[...] = jnp.zeros_like(sums)
        for load in loads:
            load.wait()

    wa = wa_pieces.reshape(width, width)
    wu = wu_pieces.reshape(width, hidden_units)
    wd = wd_pieces.reshape(hidden_units, width)

    def vector(index):
        return vecs[index : index + 1].astype(f32)

    attn_b, gain1, shift1, down_b, gain2, shift2 = [vector(i) for i in range(2, 8)]

    def add_sum(index, values):
        sums[index : index + 1] += jnp.sum(values, axis=0, keepdims=True)

    x = tok[...].astype(f32)
    branch = attn_b + x + dot(mixed[...], wa[...], NN)
    normed1, inv1 = normed_of(branch)
    hidden = normed1 * gain1 + shift1
    hid_low = hidden.astype(bf16)
    hid_o[...] = hid_low
    for c in range(hidden_units // FCH):
        cols = slice(c * FCH, c * FCH + FCH)
        value, rise = gelu_parts(dot(hid_low, wu[:, cols], NN) + upb[:, cols].astype(f32))
        act_o[:, cols] = value.astype(bf16)
        slope[:, cols] = rise.astype(bf16)
    second = hidden + dot(act_o[...], wd[...], NN) + down_b
    normed2, inv2 = normed_of(second)
    final = normed2 * gain2 + shift2
    result[...] = final.astype(bf16)
    errors = final - teach[...].astype(f32)
    kept = errors * jnp.concatenate([keep[...]] * (width // 128), axis=1)
    add_sum(6, kept * errors)
    grad = cot[...].astype(f32) + kept * (2.0 * scale[...])
    add_sum(1, grad * normed2)
    add_sum(2, grad)
    grad2 = norm_back(grad, normed2, inv2, gain2)
    ddel = grad2.astype(bf16)
    ddel_o[...] = ddel
    add_sum(0, ddel.astype(f32))
    for c in range(hidden_units // FCH):
        cols = slice(c * FCH, c * FCH + FCH)
        delta = dot(ddel, wd[cols], NT) * slope[:, cols].astype(f32)
        low = delta.astype(bf16)
        udel_o[:, cols] = low
        add_sum(8 + c, low.astype(f32))
    hgrad = grad2 + dot(udel_o[...], wu[...], NT)
    add_sum(4, hgrad * normed1)
    add_sum(5, hgrad)
    grad1 = norm_back(hgrad, normed1, inv1, gain1)
    adel = grad1.astype(bf16)
    adel_o[...] = adel
    add_sum(3, adel.astype(f32))
    mdel = dot(adel, wa[...], NT).astype(bf16)
    mdel_o[...] = mdel
    add_sum(7, mdel.astype(f32))


def forward_back(mixed, tok, cot, teach, keep, scale, vecs, upb, up_full, down_full):
    rows, width = tok.shape
    hidden_units = upb.shape[1]
    half = 512

    def block(columns):
        return pl.BlockSpec((half, columns), lambda i, *_: (i, 0))

    def fixed(*shape):
        return pl.BlockSpec(shape, lambda i, *_: (0,) * len(shape))

    def out(columns):
        return jax.ShapeDtypeStruct((rows, columns), bf16)

    return pl.pallas_call(
        forward_back_kernel,
        grid=(rows // half,),
        in_specs=[
            block(width), block(width), block(width), block(width),
            block(128), fixed(1, 1), fixed(8, width), fixed(1, hidden_units), ANY, ANY,
        ],
        out_specs=[
            block(width), block(width), block(hidden_units), block(width),
            block(hidden_units), block(width), block(width), fixed(16, width),
        ],
        scratch_shapes=[
            pltpu.VMEM((16, width // 16, width), bf16),
            pltpu.VMEM((16, width // 16, hidden_units), bf16),
            pltpu.VMEM((16, hidden_units // 16, width), bf16),
            pltpu.VMEM((half, hidden_units), bf16),
            pltpu.SemaphoreType.DMA((3,)),
        ],
        out_shape=[
            out(width), out(width), out(hidden_units), out(width), out(hidden_units),
            out(width), out(width), jax.ShapeDtypeStruct((16, width), f32),
        ],
        compiler_params=params(60),
        cost_estimate=cost(32.6, 30),
    )(mixed, tok, cot, teach, keep, scale, vecs, upb, up_full, down_full)


def up_grad_kernel(order, mixed, adel, hid, udel, mine, other, whole):
    step = pl.program_id(0)

    @pl.when(step == 0)
    def _():
        whole[...] = dot(mixed[...], adel[...], TN).astype(bf16)

    @pl.when(step > 0)
    def _():
        whole[...] = dot(hid[...], udel[...], TN).astype(bf16)

    store_pieces(order, whole, mine, other, 48)


def store_pieces(order, source, mine, other, piece):
    for i in range(8):
        at = pl.multiple_of(order[i] * piece, 16)
        mine[i, :piece] = source[pl.ds(at, piece)]
        at = pl.multiple_of(order[i + 8] * piece, 16)
        other[i, :piece] = source[pl.ds(at, piece)]


def up_grad(order, mixed, adel, hid, udel):
    rows, width = adel.shape
    columns = udel.shape[1]
    shape = jax.ShapeDtypeStruct((8, 48, width + columns), bf16)
    out = pl.BlockSpec((8, 48, width), lambda i, *_: (0, 0, i))
    full = pl.BlockSpec((rows, width), lambda i, *_: (0, 0))
    return pl.pallas_call(
        up_grad_kernel,
        grid_spec=pltpu.PrefetchScalarGridSpec(
            num_scalar_prefetch=1,
            grid=(1 + columns // width,),
            in_specs=[
                full, full, full,
                pl.BlockSpec((rows, width), lambda i, *_: (0, jnp.maximum(i - 1, 0))),
            ],
            out_specs=[out, out],
            scratch_shapes=[pltpu.VMEM((width, width), bf16)],
        ),
        out_shape=[shape, shape],
        compiler_params=params(),
        cost_estimate=cost(6, 20),
    )(order, mixed, adel, hid, udel)


def down_grad_kernel(order, act, ddel, sums, mine, other, whole):
    whole[...] = dot(act[...], ddel[...], TN).astype(bf16)
    store_pieces(order, whole, mine, other, 192)
    low = sums[...].astype(bf16)
    for i in range(8):
        mine[i, 192:] = low
        other[i, 192:] = low


def down_grad(order, act, ddel, sums):
    rows, columns = ddel.shape
    total = act.shape[1]
    chunk = 256
    shape = jax.ShapeDtypeStruct((8, 208, columns), bf16)
    out = pl.BlockSpec((8, 208, chunk), lambda i, *_: (0, 0, i))
    return pl.pallas_call(
        down_grad_kernel,
        grid_spec=pltpu.PrefetchScalarGridSpec(
            num_scalar_prefetch=1,
            grid=(columns // chunk,),
            in_specs=[
                pl.BlockSpec(act.shape, lambda i, *_: (0, 0)),
                pl.BlockSpec((rows, chunk), lambda i, *_: (0, i)),
                pl.BlockSpec((16, chunk), lambda i, *_: (0, i)),
            ],
            out_specs=[out, out],
            scratch_shapes=[pltpu.VMEM((total, chunk), bf16)],
        ),
        out_shape=[shape, shape],
        compiler_params=params(),
        cost_estimate=cost(5, 20),
    )(order, act, ddel, sums)


def tokens_grad_kernel(adel, dq, own, cont, wq, wk, wv, out):
    for half, low in enumerate((own, cont)):
        rows = slice(512 * half, 512 * half + 512)
        total = adel[rows].astype(f32) + dot(dq[rows], wq[...], NT)
        for p in range(wq.shape[1] // 128):
            cols = slice(128 * p, 128 * p + 128)
            both = jnp.concatenate([wk[:, cols], wv[:, cols]], axis=1)
            total = total + dot(low[:, 256 * p : 256 * p + 256], both, NT)
        out[rows] = total.astype(bf16)


def tokens_grad(adel, dq, own, cont, wq, wk, wv):
    args = (adel, dq, own, cont, wq, wk, wv)
    return pl.pallas_call(
        tokens_grad_kernel,
        grid=(1,),
        in_specs=[pl.BlockSpec(a.shape, lambda i: (0, 0)) for a in args],
        out_specs=pl.BlockSpec(adel.shape, lambda i: (0, 0)),
        out_shape=jax.ShapeDtypeStruct(adel.shape, bf16),
        compiler_params=params(),
        cost_estimate=cost(3.6, 12),
    )(*args)


def swap(values, axis, bit):
    size = lax.axis_size(axis)
    return lax.ppermute(values, axis, [(i, i ^ bit) for i in range(size)])


def local(
    tokens, cotangent, teacher, valid_mask, valid_count,
    query_weight, query_bias, key_weight, value_weight, value_bias,
    attn_weight, attn_bias, first_gain, first_shift,
    up_weight, up_bias, down_weight, down_bias, second_gain, second_shift,
):
    rows, width = tokens.shape[2:]
    shards = lax.axis_size("shard")
    split = shards == 8
    rep = lax.axis_index("rep")
    shard = lax.axis_index("shard")
    core = rep % 2
    z, y = shard // 2, shard % 2
    tok = tokens.reshape(rows, width)
    keep = valid_mask.reshape(rows)
    if split:
        i = jnp.arange(16, dtype=jnp.int32)
        order = (((z ^ (i % 4)) * 2 + (y ^ (i // 4 % 2))) * 2 + (core ^ (i // 8))).astype(jnp.int32)
    else:
        order = jnp.arange(16, dtype=jnp.int32)

    small = [
        query_bias, value_bias, attn_bias, first_gain, first_shift, down_bias, second_gain,
        second_shift, up_bias,
    ]
    part = query_bias.shape[0]
    vec = jnp.concatenate([v[None] for v in small], axis=1)[0]
    keep_low = keep[:PPIECE].astype(f32).reshape(4, 128)
    if split:
        keep_low = jnp.concatenate([keep_low, keep_low])
        vec = jnp.pad(vec, (0, 2048 - vec.shape[0])).reshape(16, 128)
        up_own = jnp.concatenate([attn_weight, up_weight], axis=1).reshape(2, 48, -1)
        wq, wk, wv, vecs, oth, others_keep, up_full = first_gather(
            query_weight, key_weight, value_weight, vec, tok, keep_low, up_own
        )
        vecs = vecs.reshape(8, 2048)
    else:
        wq, wk, wv, vecs = [
            lax.all_gather(w, "shard", axis=0, tiled=True)
            for w in (query_weight, key_weight, value_weight, vec[None])
        ]
        prompt = tok[:PPIECE]
        oth = jnp.concatenate([swap(prompt, "rep", bit) for bit in (1, 2, 3)])
        others_keep = jnp.stack([swap(keep_low, "rep", bit) for bit in (1, 2, 3)])
    others_keep = others_keep[:, :4].reshape(3 * PPIECE)
    upb = vecs[:, 8 * part : 8 * part + up_bias.shape[0]].reshape(1, -1)
    vecs = vecs[:, : 8 * part].reshape(shards, 8, part).transpose(1, 0, 2).reshape(8, width)

    all_keep = jnp.concatenate(
        [keep[:PPIECE].astype(f32), others_keep, keep[PPIECE:].astype(f32)]
    )
    bias = jnp.where(all_keep > 0.5, 0.0, NEGATIVE)
    brow = jnp.broadcast_to(bias[None], (8, bias.shape[0]))
    lane = jnp.arange(128)[None]
    kb = jnp.where(lane == 0, bias[:, None], jnp.where(lane < 4, 1.0, 0.0)).astype(bf16)

    own_parts = ()
    if split:
        own_parts = (up_own, down_weight.reshape(2, 192, width), up_full)
    outs = attend_near(tok, oth, wq, wk, wv, vecs[0:1], vecs[1:2], kb, brow, own_parts)
    q, k, v, xt, qn, kn, mixed, sides = outs[:8]
    if split:
        up_full, down_full = outs[8:]
    else:
        up_full = jnp.concatenate(
            [
                lax.all_gather(w, "shard", axis=0, tiled=True)
                for w in (attn_weight, up_weight)
            ],
            axis=1,
        ).reshape(16, 48, -1)
        down_full = lax.all_gather(down_weight, "shard", axis=0, tiled=True)
        down_full = down_full.reshape(16, 192, width)
    mixed, sides = attend_far(q, k, v, kb, brow, qn, kn, mixed, sides)

    keep_wide = jnp.broadcast_to(keep.astype(f32)[:, None], (rows, 128))
    scale = (1.0 / valid_count.astype(f32)).reshape(1, 1)
    result, hid, act, ddel, udel, adel, mdel, sums = forward_back(
        mixed, tok, cotangent.reshape(rows, width), teacher.reshape(rows, width),
        keep_wide, scale, vecs, upb, up_full, down_full,
    )
    down_mine, down_other = down_grad(order, act, ddel, sums)
    up_mine, up_other = up_grad(order, mixed, adel, hid, udel)
    if split:
        down_sum = (down_mine.astype(f32) + swap(down_other, "rep", 1).astype(f32)).astype(bf16)
        up_sum = (up_mine.astype(f32) + swap(up_other, "rep", 1).astype(f32)).astype(bf16)
        token_grad, query_low, key_low, value_low, qrow, up_low, down_low = attend_back(
            q, k, v, mdel, mixed, sides, kb, xt, up_sum, down_sum, wq, wk, wv, adel
        )
        query_grad, key_grad, value_grad = [g.astype(f32) for g in (query_low, key_low, value_low)]
        up_all = up_low.astype(f32)
        down_all = down_low[:, :192].astype(f32).reshape(-1, width)
        sums = down_low[0, 192:].astype(f32)
        query_row = qrow[0].astype(f32)
    else:
        dq, cont, partial_rows, whole = attend_back_alone(q, k, v, mdel, mixed, sides, kb, xt)

        def scatter(part):
            part = lax.psum_scatter(part, "shard", scatter_dimension=0, tiled=True)
            return lax.psum(part, "rep").astype(f32)

        def joined(mine, other, piece):
            return jnp.concatenate([mine, other])[:, :piece].reshape(16 * piece, -1)

        turned = partial_rows.reshape(2, 2, PPIECE, -1)
        turned = jnp.where(core == 1, turned[:, ::-1], turned)
        turned = jnp.where(rep // 2 == 1, turned[::-1], turned)
        own = lax.psum_scatter(
            turned.reshape(4 * PPIECE, -1), "rep", scatter_dimension=0, tiled=True
        )
        whole = scatter(whole).reshape(part, width // 128, 3, 128)
        query_grad, key_grad, value_grad = [whole[:, :, j].reshape(part, width) for j in range(3)]
        up_all = scatter(joined(up_mine, up_other, 48))
        down_all = scatter(joined(down_mine, down_other, 192))
        sums = lax.psum(sums, ("rep", "shard"))
        query_row = lax.psum(jnp.sum(dq.astype(f32), axis=0), ("rep", "shard"))
        token_grad = tokens_grad(adel, dq, own, cont, wq, wk, wv)

    def owned(row):
        return lax.dynamic_slice(row, (shard * part,), (part,))

    up_part = up_bias.shape[0]
    loss = jnp.sum(sums[6]) / valid_count.astype(f32)
    return (
        result.reshape(tokens.shape),
        loss,
        token_grad.reshape(tokens.shape),
        query_grad,
        owned(query_row),
        key_grad,
        value_grad,
        owned(sums[7]),
        up_all[:, :width],
        owned(sums[3]),
        owned(sums[4]),
        owned(sums[5]),
        up_all[:, width:],
        lax.dynamic_slice(sums[8:12].reshape(-1), (shard * up_part,), (up_part,)),
        down_all,
        owned(sums[0]),
        owned(sums[1]),
        owned(sums[2]),
    )


def solution(mesh):
    wide = P("shard", "rep", None, None)
    matrix, vector = P("shard", None), P("shard")
    return jax.shard_map(
        local,
        mesh=mesh,
        in_specs=(
            wide, wide, wide, P("shard", "rep", None), P(),
            matrix, vector, matrix, matrix, vector, matrix, vector, vector, vector,
            matrix, vector, matrix, vector, vector, vector,
        ),
        out_specs=(
            wide, P(), wide,
            matrix, vector, matrix, matrix, vector, matrix, vector, vector, vector,
            matrix, vector, matrix, vector, vector, vector,
        ),
        check_vma=False,
    )
```

```python
import functools

import jax
import jax.numpy as jnp
from jax import lax
from jax.experimental import pallas as pl
from jax.experimental.pallas import tpu as pltpu
from jax.sharding import PartitionSpec as P

HDIM = 64
PPIECE = 512
CLEN = 256
EPSILON = 1e-05
NEGATIVE = -1e30
LOG2E = 1.4426950408889634
SCALE = 1.0 / 8.0
LIMIT = 100.0

f32 = jnp.float32
bf16 = jnp.bfloat16
NT = (((1,), (1,)), ((), ()))
NN = (((1,), (0,)), ((), ()))
TN = (((0,), (0,)), ((), ()))
ANY = pl.BlockSpec(memory_space=pl.ANY)
MESH = pl.DeviceIdType.MESH


def dot(left, right, dims):
    return lax.dot_general(left, right, dims, preferred_element_type=f32)


def params(mib=56, **more):
    return pltpu.CompilerParams(vmem_limit_bytes=mib * 2**20, **more)


def cost(gflop, mbytes):
    return pl.CostEstimate(
        flops=int(gflop * 1e9), bytes_accessed=int(mbytes * 1e6), transcendentals=0
    )


def lane_of(rows):
    return lax.broadcasted_iota(jnp.int32, (rows, 128), 1)


def split3(values):
    hi = values.astype(bf16).astype(f32)
    mid = (values - hi).astype(bf16).astype(f32)
    low = values - hi - mid
    return hi, mid, low


def side_lanes(first, values):
    lane = lane_of(values.shape[0])
    hi, mid, low = split3(values)
    out = jnp.where(lane == 1, -hi, jnp.where(lane == 2, -mid, jnp.where(lane == 3, -low, 0.0)))
    return jnp.where(lane == 0, first, out).astype(bf16)


def gather_kernel(
    wq, wk, wv, vec, tok, keep, up_own,
    fq, fk, fv, fvec, ptok, pkeep, up_full,
    asend, arecv, local_sem, zrecv, yrecv, crecv, usend, dsend, ysend, csend, tsend, trecv,
):
    depth = 4
    rep = lax.axis_index("rep")
    shard = lax.axis_index("shard")
    core = rep % 2
    z = shard // 2
    y = shard % 2
    other_core = {"rep": rep + 1 - 2 * core}
    other_x = {"rep": (rep + 2) % 4}
    other_y = {"shard": z * 2 + 1 - y}
    up = {"shard": (shard + 2) % 8}
    down = {"shard": (shard + 6) % 8}

    barrier = pltpu.get_barrier_semaphore()
    for place in (other_core, other_x, other_y):
        pl.semaphore_signal(barrier, inc=1, device_id=place, device_id_type=MESH)

    @pl.when(z < depth - 1)
    def _():
        pl.semaphore_signal(barrier, inc=1, device_id=up, device_id_type=MESH)

    @pl.when(z > 0)
    def _():
        pl.semaphore_signal(barrier, inc=1, device_id=down, device_id_type=MESH)

    inner = jnp.where((z > 0) & (z < depth - 1), 5, 4)
    pl.semaphore_wait(barrier, inner)

    sources = (wq, wk, wv, vec)
    targets = (fq, fk, fv, fvec)

    def place_of(u, zz, yy, cc):
        if u == 3:
            return targets[u].at[zz * 2 + yy]
        return targets[u].at[(zz * 2 + yy) * 2 + cc]

    def own_of(u):
        return sources[u] if u == 3 else sources[u].at[core]

    def move(src, dst, send, recv, where):
        return pltpu.make_async_remote_copy(
            src_ref=src, dst_ref=dst, send_sem=send, recv_sem=recv,
            device_id=where, device_id_type=MESH,
        )

    def to_up(u, zz, src):
        return move(src, place_of(u, zz, y, core), usend.at[u, zz], zrecv.at[u, zz], up)

    def to_down(u, zz, src):
        return move(src, place_of(u, zz, y, core), dsend.at[u, zz], zrecv.at[u, zz], down)

    def to_y(u, zz, src):
        return move(src, place_of(u, zz, y, core), ysend.at[u, zz], yrecv.at[u, zz], other_y)

    def to_core(u, zz, yy):
        at = place_of(u, zz, yy, core)
        index = zz * 2 + yy
        return move(at, at, csend.at[u, index], crecv.at[u, index], other_core)

    for u in range(4):
        @pl.when(z < depth - 1)
        def _():
            to_up(u, z, own_of(u)).start()

        @pl.when(z > 0)
        def _():
            to_down(u, z, own_of(u)).start()

        to_y(u, z, own_of(u)).start()

    prompt = tok.at[pl.ds(0, PPIECE)]
    copies = [
        move(prompt, ptok.at[1], tsend.at[0], trecv.at[0], other_x),
        move(keep, pkeep.at[1], tsend.at[1], trecv.at[1], other_x),
        move(prompt, ptok.at[0], tsend.at[2], trecv.at[2], other_core),
        move(keep, pkeep.at[0], tsend.at[3], trecv.at[3], other_core),
    ]
    for copy in copies:
        copy.start()
    locals_ = []
    for u in range(4):
        if u == 3:
            dst = fvec.at[shard]
        else:
            dst = targets[u].at[pl.ds(shard * 2, 2)]
        locals_.append(pltpu.make_async_copy(sources[u], dst, local_sem.at[u]))
        locals_[-1].start()

    columns = pl.ds(pl.multiple_of(rep // 2 * HALF_UP, 128), HALF_UP)

    def up_place(zz):
        return up_full.at[(zz * 2 + y) * 2 + core, :, columns]

    def up_up(zz, src):
        return move(src, up_place(zz), asend.at[0, zz], arecv.at[zz], up)

    def up_down(zz, src):
        return move(src, up_place(zz), asend.at[1, zz], arecv.at[zz], down)

    def up_start():
        src = up_own.at[core, :, columns]

        @pl.when(z < depth - 1)
        def _():
            up_up(z, src).start()

        @pl.when(z > 0)
        def _():
            up_down(z, src).start()

    def up_hop(step):
        @pl.when(z - step >= 0)
        def _():
            at = up_place(z - step)
            up_up(z - step, at).wait_recv()
            if step == 1:
                @pl.when(z < depth - 1)
                def _():
                    up_up(z - step, at).start()

        @pl.when(z + step < depth)
        def _():
            at = up_place(z + step)
            up_down(z + step, at).wait_recv()
            if step == 1:
                @pl.when(z > 0)
                def _():
                    up_down(z + step, at).start()

    for step in range(1, depth + 1):
        if step == 2:
            up_start()
        if step == 4:
            up_hop(1)
        for u in range(4):
            if step < depth:
                @pl.when(z - step >= 0)
                def _():
                    zz = z - step
                    at = place_of(u, zz, y, core)
                    to_up(u, zz, at).wait_recv()

                    @pl.when(z < depth - 1)
                    def _():
                        to_up(u, zz, at).start()

                    to_y(u, zz, at).start()
                    if u < 3:
                        to_core(u, zz, y).start()

                @pl.when(z + step < depth)
                def _():
                    zz = z + step
                    at = place_of(u, zz, y, core)
                    to_down(u, zz, at).wait_recv()

                    @pl.when(z > 0)
                    def _():
                        to_down(u, zz, at).start()

                    to_y(u, zz, at).start()
                    if u < 3:
                        to_core(u, zz, y).start()

        for u in range(4):
            def from_y(zz):
                at = targets[u].at[zz * 2 + 1 - y] if u == 3 else place_of(u, zz, 1 - y, core)
                move(at, at, ysend.at[u, zz], yrecv.at[u, zz], other_y).wait_recv()
                if u < 3:
                    to_core(u, zz, 1 - y).start()

            if step == 1:
                from_y(z)
            else:
                @pl.when(z - (step - 1) >= 0)
                def _():
                    from_y(z - (step - 1))

                @pl.when(z + (step - 1) < depth)
                def _():
                    from_y(z + (step - 1))

    up_hop(2)
    copies[0].wait_recv()
    copies[1].wait_recv()
    forward = [
        move(ptok.at[1], ptok.at[2], tsend.at[4], trecv.at[4], other_core),
        move(pkeep.at[1], pkeep.at[2], tsend.at[5], trecv.at[5], other_core),
    ]
    for copy in forward:
        copy.start()

    def others(act):
        for zz in range(depth):
            for yy in range(2):
                @pl.when((zz != z) | (yy != y))
                def _():
                    act(zz, yy)

    for u in range(3):
        def arrived(zz, yy):
            at = place_of(u, zz, yy, 1 - core)
            index = zz * 2 + yy
            move(at, at, csend.at[u, index], crecv.at[u, index], other_core).wait_recv()

        others(arrived)
    copies[2].wait_recv()
    copies[3].wait_recv()
    for copy in forward:
        copy.wait_recv()

    for copy in copies + forward:
        copy.wait_send()
    for zz in range(depth):
        at = up_place(zz)

        @pl.when((zz <= z) & (zz >= z - 1) & (z < depth - 1))
        def _():
            up_up(zz, at).wait_send()

        @pl.when((zz >= z) & (zz <= z + 1) & (z > 0))
        def _():
            up_down(zz, at).wait_send()

    for copy in locals_:
        copy.wait()
    for u in range(4):
        for zz in range(depth):
            at = place_of(u, zz, y, core)
            to_y(u, zz, at).wait_send()

            @pl.when((zz <= z) & (z < depth - 1))
            def _():
                to_up(u, zz, at).wait_send()

            @pl.when((zz >= z) & (z > 0))
            def _():
                to_down(u, zz, at).wait_send()

        if u < 3:
            others(lambda zz, yy: to_core(u, zz, yy).wait_send())


def first_gather(wq, wk, wv, vec, tok, keep, up_own):
    width = wq.shape[1]
    sem = pltpu.SemaphoreType.DMA
    halves = [w.reshape(2, 48, width) for w in (wq, wk, wv)]
    full = jax.ShapeDtypeStruct((16, 48, width), bf16)
    outs = pl.pallas_call(
        gather_kernel,
        in_specs=[ANY] * 7,
        out_specs=[ANY] * 7,
        out_shape=[
            full, full, full,
            jax.ShapeDtypeStruct((8, 16, 128), bf16),
            jax.ShapeDtypeStruct((3, PPIECE, width), bf16),
            jax.ShapeDtypeStruct((3, 8, 128), f32),
            jax.ShapeDtypeStruct((16, 48, up_own.shape[2]), bf16),
        ],
        scratch_shapes=[
            sem((2, 4)), sem((4,)), sem((4,)), sem((4, 4)), sem((4, 4)), sem((3, 8)), sem((4, 4)), sem((4, 4)),
            sem((4, 4)), sem((3, 8)), sem((6,)), sem((6,)),
        ],
        compiler_params=params(60, collective_id=1, has_side_effects=True),
        cost_estimate=cost(0, 20),
    )(*halves, vec, tok, keep, up_own)
    fq, fk, fv, fvec, ptok, pkeep, up_full = outs
    return (
        fq.reshape(width, width), fk.reshape(width, width), fv.reshape(width, width),
        fvec, ptok.reshape(3 * PPIECE, width), pkeep, up_full,
    )


class Link:
    def __init__(self):
        rep = lax.axis_index("rep")
        shard = lax.axis_index("shard")
        self.core = rep % 2
        self.x = rep // 2
        self.z = shard // 2
        self.y = shard % 2
        self.shard = shard
        self.to_core = {"rep": rep + 1 - 2 * self.core}
        self.to_x = {"rep": (rep + 2) % 4}
        self.to_y = {"shard": self.z * 2 + 1 - self.y}
        self.to_up = {"shard": (shard + 2) % 8}
        self.to_down = {"shard": (shard + 6) % 8}

    def greet(self):
        barrier = pltpu.get_barrier_semaphore()
        for place in (self.to_core, self.to_x, self.to_y):
            pl.semaphore_signal(barrier, inc=1, device_id=place, device_id_type=MESH)

        @pl.when(self.z < 3)
        def _():
            pl.semaphore_signal(barrier, inc=1, device_id=self.to_up, device_id_type=MESH)

        @pl.when(self.z > 0)
        def _():
            pl.semaphore_signal(barrier, inc=1, device_id=self.to_down, device_id_type=MESH)

        count = jnp.where((self.z > 0) & (self.z < 3), 5, 4)
        pl.semaphore_wait(barrier, count)


def move(src, dst, send, recv, where):
    return pltpu.make_async_remote_copy(
        src_ref=src, dst_ref=dst, send_sem=send, recv_sem=recv,
        device_id=where, device_id_type=MESH,
    )


class Spread:
    def __init__(self, own, full, sems):
        self.at = Link()
        self.own, self.full = own, full
        (
            self.local, self.zrecv, self.yrecv, self.usend, self.dsend, self.ysend,
            self.xrecv, self.xsend, self.crecv, self.csend,
        ) = sems

    def columns(self, xx):
        return pl.ds(pl.multiple_of(xx * HALF_UP, 128), HALF_UP)

    def place(self, u, zz, yy, cc, xx):
        index = (zz * 2 + yy) * 2 + cc
        if u == 0:
            return self.full[0].at[index, :, self.columns(xx)]
        return self.full[1].at[index]

    def mine(self, u, zz, yy):
        return self.place(u, zz, yy, self.at.core, self.at.x)

    def source(self, u):
        if u == 0:
            return self.own[0].at[self.at.core, :, self.columns(self.at.x)]
        return self.own[1].at[self.at.core]

    def up(self, u, zz, src):
        return move(
            src, self.mine(u, zz, self.at.y), self.usend.at[u, zz], self.zrecv.at[u, zz],
            self.at.to_up,
        )

    def down(self, u, zz, src):
        return move(
            src, self.mine(u, zz, self.at.y), self.dsend.at[u, zz], self.zrecv.at[u, zz],
            self.at.to_down,
        )

    def side(self, u, zz, src):
        return move(
            src, self.mine(u, zz, self.at.y), self.ysend.at[u, zz], self.yrecv.at[u, zz],
            self.at.to_y,
        )

    def across(self, zz, yy):
        at = self.mine(0, zz, yy)
        index = zz * 2 + yy
        return move(at, at, self.xsend.at[index], self.xrecv.at[index], self.at.to_x)

    def twin(self, kind, zz, yy):
        if kind == 1:
            at = self.place(0, zz, yy, self.at.core, 1 - self.at.x)
        else:
            at = self.mine(0 if kind == 0 else 1, zz, yy)
        index = zz * 2 + yy
        return move(
            at, at, self.csend.at[kind, index], self.crecv.at[kind, index], self.at.to_core
        )

    def twin_in(self, kind, zz, yy):
        cc = 1 - self.at.core
        xx = 1 - self.at.x if kind == 1 else self.at.x
        at = self.place(1 if kind == 2 else 0, zz, yy, cc, xx)
        index = zz * 2 + yy
        return move(
            at, at, self.csend.at[kind, index], self.crecv.at[kind, index], self.at.to_core
        )

    def locals_(self):
        return [
            pltpu.make_async_copy(
                self.own[u], self.full[u].at[pl.ds(self.at.shard * 2, 2)], self.local.at[u]
            )
            for u in range(2)
        ]

    def begin(self):
        z, y = self.at.z, self.at.y
        self.at.greet()

        @pl.when(z < 3)
        def _():
            self.up(1, z, self.source(1)).start()

        @pl.when(z > 0)
        def _():
            self.down(1, z, self.source(1)).start()

        @pl.when((z >= 2) & (z < 3))
        def _():
            self.up(0, z - 2, self.mine(0, z - 2, y)).start()

        @pl.when((z <= 1) & (z > 0))
        def _():
            self.down(0, z + 2, self.mine(0, z + 2, y)).start()

        self.side(0, z, self.source(0)).start()
        for step in (1, 2):
            @pl.when(z - step >= 0)
            def _():
                self.side(0, z - step, self.mine(0, z - step, y)).start()
                self.got(0, z - step, y)

            @pl.when(z + step < 4)
            def _():
                self.side(0, z + step, self.mine(0, z + step, y)).start()
                self.got(0, z + step, y)

        self.side(1, z, self.source(1)).start()
        for copy in self.locals_():
            copy.start()

    def got(self, u, zz, yy):
        if u == 0:
            self.across(zz, yy).start()
            self.twin(0, zz, yy).start()
        else:
            self.twin(2, zz, yy).start()

    def hop(self, u, step):
        z, y = self.at.z, self.at.y

        @pl.when(z - step >= 0)
        def _():
            zz = z - step
            at = self.mine(u, zz, y)
            self.up(u, zz, at).wait_recv()
            if step < 3:
                @pl.when(z < 3)
                def _():
                    self.up(u, zz, at).start()

            self.side(u, zz, at).start()
            self.got(u, zz, y)

        @pl.when(z + step < 4)
        def _():
            zz = z + step
            at = self.mine(u, zz, y)
            self.down(u, zz, at).wait_recv()
            if step < 3:
                @pl.when(z > 0)
                def _():
                    self.down(u, zz, at).start()

            self.side(u, zz, at).start()
            self.got(u, zz, y)

    def from_side(self, u, step):
        z, yy = self.at.z, 1 - self.at.y

        def take(zz):
            at = self.mine(u, zz, yy)
            move(at, at, self.ysend.at[u, zz], self.yrecv.at[u, zz], self.at.to_y).wait_recv()
            self.got(u, zz, yy)

        if step == 0:
            take(z)
        else:
            @pl.when(z - step >= 0)
            def _():
                take(z - step)

            @pl.when(z + step < 4)
            def _():
                take(z + step)

    def others(self, act):
        for zz in range(4):
            for yy in range(2):
                @pl.when((zz != self.at.z) | (yy != self.at.y))
                def _():
                    act(zz, yy)

    def from_across(self):
        def take(zz, yy):
            at = self.place(0, zz, yy, self.at.core, 1 - self.at.x)
            index = zz * 2 + yy
            move(at, at, self.xsend.at[index], self.xrecv.at[index], self.at.to_x).wait_recv()
            self.twin(1, zz, yy).start()

        self.others(take)

    def end(self):
        z, y = self.at.z, self.at.y

        def take(zz, yy):
            for kind in range(3):
                self.twin_in(kind, zz, yy).wait_recv()
                self.twin(kind, zz, yy).wait_send()
            self.across(zz, yy).wait_send()

        self.others(take)
        for copy in self.locals_():
            copy.wait()
        for u in range(2):
            for zz in range(4):
                at = self.mine(u, zz, y)
                self.side(u, zz, at).wait_send()

                rising = (zz <= z) & (z < 3)
                falling = (zz >= z) & (z > 0)
                if u == 0:
                    rising = (zz == z - 2) & (z < 3)
                    falling = (zz == z + 2) & (z > 0)

                @pl.when(rising)
                def _():
                    self.up(u, zz, at).wait_send()

                @pl.when(falling)
                def _():
                    self.down(u, zz, at).wait_send()


HALF_UP = 1920


def head_twice(values, head):
    wide = values.astype(f32)
    turned = pltpu.roll(wide, 64, 1)
    first = lane_of(values.shape[0]) < 64
    if head == 0:
        return jnp.where(first, wide, turned).astype(bf16)
    return jnp.where(first, turned, wide).astype(bf16)


def head_parts(values, head):
    wide = values.astype(f32) * (SCALE * LOG2E)
    hi = wide.astype(bf16).astype(f32)
    low = wide - hi
    first = lane_of(values.shape[0]) < 64
    if head == 0:
        return jnp.where(first, hi, pltpu.roll(low, 64, 1)).astype(bf16)
    return jnp.where(first, pltpu.roll(hi, 64, 1), low).astype(bf16)


def head_only(values, head):
    first = lane_of(values.shape[0]) < 64
    keep = first if head == 0 else jnp.logical_not(first)
    return jnp.where(keep, values, jnp.zeros_like(values))


def off_diagonal(size, bias):
    row = lax.broadcasted_iota(jnp.int32, (size, size), 0)
    col = lax.broadcasted_iota(jnp.int32, (size, size), 1)
    return jnp.where(row == col, 0.0, bias)


def attend_setup(kb, brow, kx, vx, bown, bcont):
    for head in range(2):
        kx[head, :, 128:] = kb[...]
    vx[:, 128:] = jnp.ones((2560, 128), bf16)
    bown[...] = off_diagonal(512, brow[0:1, 0:512])
    for c in range(2):
        bcont[c] = off_diagonal(256, brow[0:1, 2048 + 256 * c : 2304 + 256 * c])


def attend_fill(q, k, v, qx, kx, vx):
    ones = jnp.where(lane_of(1024) == 0, 1.0, 0.0).astype(bf16)
    vx[:, :128] = v
    for head in range(2):
        qx[head, :, :128] = head_parts(q, head)
        kx[head, :, :128] = head_twice(k, head)
        qx[head, :, 128:] = ones


def own_scores(head, qx, kx, bown):
    return dot(qx[head, :512, :128], kx[head, :512, :128], NT) + bown[...]


def cont_scores(head, c, qx, kx, bcont):
    rows = slice(512 + 256 * c, 768 + 256 * c)
    keys = slice(2048 + 256 * c, 2304 + 256 * c)
    return dot(qx[head, rows, :128], kx[head, keys, :128], NT) + bcont[c]


def attend_head(head, o, side, qx, kx, vx, pm, pc, bown, bcont, top=None):
    def below(scores, rows):
        if top is None:
            return jnp.exp2(scores).astype(bf16)
        return jnp.exp2(scores - top[head, rows, 0:1]).astype(bf16)

    lane = lane_of(256)
    for c in range(3):
        keys = slice(512 + 512 * c, 1024 + 512 * c)
        pm[head, :, keys] = jnp.exp2(dot(qx[head], kx[head, keys], NT)).astype(bf16)
    pm[head, 512:, :512] = jnp.exp2(dot(qx[head, 512:], kx[head, :512], NT)).astype(bf16)
    pm[head, :512, :512] = below(own_scores(head, qx, kx, bown), slice(0, 512))
    for c in range(2):
        rows = slice(512 + 256 * c, 768 + 256 * c)
        pc[head, c] = below(cont_scores(head, c, qx, kx, bcont), rows)
    for r in range(4):
        rows = slice(256 * r, 256 * r + 256)
        total = dot(pm[head, rows], vx[:2048], NN)
        if r >= 2:
            total = total + dot(pc[head, r - 2], vx[1536 + 256 * r : 1792 + 256 * r], NN)
        mass = total[:, 128:]
        value = total[:, :128] / mass
        if head == 0:
            o[rows] = value.astype(bf16)
        else:
            o[rows] = jnp.where(lane < 64, o[rows].astype(f32), value).astype(bf16)
        logs = jnp.log2(mass)
        if top is not None:
            logs = logs + top[head, rows]
        side[head, rows] = side_lanes(1.0, logs)


ROW_STEPS = 5


def near_kernel(
    tok, oth, wq, wk, wv, qb, vb, kb, brow, *refs, linked
):
    if linked:
        own_parts, refs = refs[:2], refs[3:]
    q, k, v, xt, qn, kn, o, side = refs[:8]
    refs = refs[8:]
    if linked:
        full, refs = refs[:2], refs[2:]
    qs, ks, vs, qx, kx, vx, pm, pc, bown, bcont = refs[:10]
    step = pl.program_id(0)
    spread = Spread(own_parts, full, refs[10:]) if linked else None

    def comm(at, act):
        if linked:
            @pl.when(step == at)
            def _():
                act()

    comm(0, lambda: spread.begin())
    width = wq.shape[0]

    @pl.when(step < ROW_STEPS)
    def _():
        own = (step == 0) | (step == 4)
        row = lax.broadcasted_iota(jnp.int32, (width, 128), 0)
        lane = lax.broadcasted_iota(jnp.int32, (width, 128), 1)
        heads = jnp.where(row // HDIM == lane, 1.0, 0.0).astype(bf16)
        at = pl.ds(pl.multiple_of(step * PPIECE, PPIECE), PPIECE)

        @pl.when(step == 0)
        def _():
            qn[...] = jnp.zeros_like(qn)
            kn[...] = jnp.zeros_like(kn)
            attend_setup(kb, brow, kx, vx, bown, bcont)

        def norms(values):
            wide = values.astype(f32)
            sums = dot((wide * wide).astype(bf16), heads, NN)
            return jnp.broadcast_to(jnp.max(sums, axis=0, keepdims=True), (8, 128))

        def keep(low, out, held, where):
            out[...] = low
            for p in range(width // 128):
                held[p, where] = low[:, 128 * p : 128 * p + 128]

        def keys(rows):
            low = dot(rows, wk[...], NN).astype(bf16)
            keep(low, k, ks, at)
            kn[...] = jnp.maximum(kn[...], norms(low))
            keep((dot(rows, wv[...], NN) + vb[...].astype(f32)).astype(bf16), v, vs, at)
            xt[...] = jnp.transpose(rows)

        @pl.when(own)
        def _():
            rows = tok[...]
            keys(rows)
            low = (dot(rows, wq[...], NN) + qb[...].astype(f32)).astype(bf16)
            keep(low, q, qs, pl.ds(pl.multiple_of(step // 4 * PPIECE, PPIECE), PPIECE))
            qn[...] = jnp.maximum(qn[...], norms(low))

        @pl.when(jnp.logical_not(own))
        def _():
            keys(oth[...])

    comm(4, lambda: (spread.hop(0, 3), spread.hop(1, 1)))

    @pl.when(step >= ROW_STEPS)
    def _():
        p = step - ROW_STEPS
        attend_fill(qs[p], ks[p], vs[p], qx, kx, vx)
        attend_head(0, o, side, qx, kx, vx, pm, pc, bown, bcont)

    comm(5, lambda: [spread.from_side(0, j) for j in range(3)])
    comm(6, lambda: spread.hop(1, 2))
    comm(7, lambda: (spread.from_side(1, 0), spread.from_side(0, 3)))
    comm(9, lambda: spread.from_side(1, 1))
    comm(10, lambda: spread.from_side(1, 2))

    @pl.when(step >= ROW_STEPS)
    def _():
        attend_head(1, o, side, qx, kx, vx, pm, pc, bown, bcont)

    comm(7, lambda: spread.hop(1, 3))
    comm(8, lambda: spread.from_across())
    comm(10, lambda: (spread.from_side(1, 3), spread.end()))


def attend_near(tok, oth, wq, wk, wv, qb, vb, kb, brow, own_parts):
    width = tok.shape[1]
    linked = bool(own_parts)
    pairs = width // 128
    block = (PPIECE, width)

    def once(*shape):
        return pl.BlockSpec(shape, lambda i: (0,) * len(shape), pipeline_mode=pl.Buffered(1))

    def rows_at(i):
        return jnp.minimum(i, ROW_STEPS - 1)

    def pair_at(i):
        return jnp.maximum(i - ROW_STEPS, 0)

    small = pl.BlockSpec((8, 128), lambda i: (0, 0))
    extra_shape, extra_sems, more = [], [], {}
    if linked:
        sem = pltpu.SemaphoreType.DMA
        extra_shape = [
            jax.ShapeDtypeStruct((16, 48, own_parts[0].shape[2]), bf16),
            jax.ShapeDtypeStruct((16, 192, width), bf16),
        ]
        extra_sems = [
            sem((2,)), sem((2, 4)), sem((2, 4)), sem((2, 4)), sem((2, 4)), sem((2, 4)),
            sem((8,)), sem((8,)), sem((3, 8)), sem((3, 8)),
        ]
        more = {"collective_id": 3, "has_side_effects": True}
    return pl.pallas_call(
        functools.partial(near_kernel, linked=linked),
        grid=(ROW_STEPS + pairs,),
        in_specs=[
            pl.BlockSpec(block, lambda i: (rows_at(i) // 4, 0)),
            pl.BlockSpec(block, lambda i: (jnp.clip(i - 1, 0, 2), 0)),
            once(width, width), once(width, width), once(width, width),
            once(1, width), once(1, width), once(2560, 128), once(8, 2560),
        ] + [ANY] * len(own_parts),
        out_specs=[
            pl.BlockSpec(block, lambda i: (rows_at(i) // 4, 0)),
            pl.BlockSpec(block, lambda i: (rows_at(i), 0)),
            pl.BlockSpec(block, lambda i: (rows_at(i), 0)),
            pl.BlockSpec((width, PPIECE), lambda i: (0, rows_at(i))),
            small, small,
            pl.BlockSpec((1024, 128), lambda i: (0, pair_at(i))),
            pl.BlockSpec((2, 1024, 128), lambda i: (pair_at(i), 0, 0)),
        ] + [ANY] * len(extra_shape),
        out_shape=[
            jax.ShapeDtypeStruct((1024, width), bf16),
            jax.ShapeDtypeStruct((2560, width), bf16),
            jax.ShapeDtypeStruct((2560, width), bf16),
            jax.ShapeDtypeStruct((width, 2560), bf16),
            jax.ShapeDtypeStruct((8, 128), f32),
            jax.ShapeDtypeStruct((8, 128), f32),
            jax.ShapeDtypeStruct((1024, width), bf16),
            jax.ShapeDtypeStruct((2 * pairs, 1024, 128), bf16),
        ] + extra_shape,
        scratch_shapes=[
            pltpu.VMEM((pairs, 1024, 128), bf16),
            pltpu.VMEM((pairs, 2560, 128), bf16),
            pltpu.VMEM((pairs, 2560, 128), bf16),
            pltpu.VMEM((2, 1024, 256), bf16),
            pltpu.VMEM((2, 2560, 256), bf16),
            pltpu.VMEM((2560, 256), bf16),
            pltpu.VMEM((2, 1024, 2048), bf16),
            pltpu.VMEM((2, 2, 256, 256), bf16),
            pltpu.VMEM((512, 512), f32),
            pltpu.VMEM((2, 256, 256), f32),
        ] + extra_sems,
        input_output_aliases={11: 8} if linked else {},
        compiler_params=params(60, **more),
        cost_estimate=cost(50, 50),
    )(tok, oth, wq, wk, wv, qb, vb, kb, brow, *own_parts)


def far_kernel(
    q, k, v, kb, brow, qn, kn, o_in, side_in, o_out, side_out,
    qs, ks, vs, o, side, qx, kx, vx, pm, pc, bown, bcont, top, sems,
):
    pair = pl.program_id(0)
    widest_product = jnp.max(qn[...] * kn[...]) * ((SCALE * LOG2E) ** 2 * 1.1)

    @pl.when(widest_product > LIMIT * LIMIT)
    def _():
        at = pl.ds(pl.multiple_of(pair * 128, 128), 128)
        copies = [
            pltpu.make_async_copy(ref.at[:, at], held, sems.at[i])
            for i, (ref, held) in enumerate(((q, qs), (k, ks), (v, vs)))
        ]
        for copy in copies:
            copy.start()
        for copy in copies:
            copy.wait()
        attend_setup(kb, brow, kx, vx, bown, bcont)
        attend_fill(qs[...], ks[...], vs[...], qx, kx, vx)

        def widest(scores):
            return jnp.broadcast_to(
                jnp.max(scores, axis=1, keepdims=True), (scores.shape[0], 128)
            )

        for head in range(2):
            def more(c, carry):
                found = widest(dot(qx[head], kx[head, pl.ds(512 + c * 256, 256)], NT))
                top[head] = jnp.maximum(top[head], found)
                return carry

            top[head] = jnp.full((1024, 128), -3e38, f32)
            lax.fori_loop(0, 6, more, 0)
            top[head, 0:512] = jnp.maximum(
                top[head, 0:512], widest(own_scores(head, qx, kx, bown))
            )
            top[head, 512:1024] = jnp.maximum(
                top[head, 512:1024], widest(dot(qx[head, 512:], kx[head, :512], NT))
            )
            for c in range(2):
                rows = slice(512 + 256 * c, 768 + 256 * c)
                top[head, rows] = jnp.maximum(
                    top[head, rows], widest(cont_scores(head, c, qx, kx, bcont))
                )
            qx[head, :, 128:] = side_lanes(1.0, top[head])
            attend_head(head, o, side, qx, kx, vx, pm, pc, bown, bcont, top)
        copies = [
            pltpu.make_async_copy(o, o_out.at[:, at], sems.at[0]),
            pltpu.make_async_copy(side, side_out.at[pl.ds(pair * 2, 2)], sems.at[1]),
        ]
        for copy in copies:
            copy.start()
        for copy in copies:
            copy.wait()


def attend_far(q, k, v, kb, brow, qn, kn, o, side):
    def fixed(*shape):
        return pl.BlockSpec(shape, lambda i: (0,) * len(shape), pipeline_mode=pl.Buffered(1))

    return pl.pallas_call(
        far_kernel,
        grid=(q.shape[1] // 128,),
        in_specs=[
            ANY, ANY, ANY, fixed(2560, 128), fixed(8, 2560), fixed(8, 128), fixed(8, 128),
            ANY, ANY,
        ],
        out_specs=[ANY, ANY],
        out_shape=[
            jax.ShapeDtypeStruct(o.shape, bf16), jax.ShapeDtypeStruct(side.shape, bf16),
        ],
        scratch_shapes=[
            pltpu.VMEM((1024, 128), bf16),
            pltpu.VMEM((2560, 128), bf16),
            pltpu.VMEM((2560, 128), bf16),
            pltpu.VMEM((1024, 128), bf16),
            pltpu.VMEM((2, 1024, 128), bf16),
            pltpu.VMEM((2, 1024, 256), bf16),
            pltpu.VMEM((2, 2560, 256), bf16),
            pltpu.VMEM((2560, 256), bf16),
            pltpu.VMEM((2, 1024, 2048), bf16),
            pltpu.VMEM((2, 2, 256, 256), bf16),
            pltpu.VMEM((512, 512), f32),
            pltpu.VMEM((2, 256, 256), f32),
            pltpu.VMEM((2, 1024, 128), f32),
            pltpu.SemaphoreType.DMA((3,)),
        ],
        input_output_aliases={7: 0, 8: 1},
        compiler_params=params(),
        cost_estimate=cost(0.1, 1),
    )(q, k, v, kb, brow, qn, kn, o, side)


def back_fill(q, k, v, d, o, side, kb, qx, qd, kx, vx, dx, qm, kt, bown, bcont):
    @pl.when(pl.program_id(0) == 0)
    def _():
        for head in range(2):
            kx[head, :, 128:] = kb[...]
        vx[:, 128:] = kb[...]
        column = kb[:, 0:1].astype(f32)
        bown[...] = off_diagonal(512, column[:512]).astype(bf16)
        for c in range(2):
            keys = slice(2048 + 256 * c, 2304 + 256 * c)
            bcont[c] = off_diagonal(256, column[keys]).astype(bf16)

    lane = lane_of(1024)
    vx[:, :128] = v[...]
    kt[...] = jnp.transpose(k[...].astype(f32)).astype(bf16)
    product = d[...].astype(f32) * o[...].astype(f32)
    for head in range(2):
        parts = head_parts(q[...], head)
        qx[head, :, :128] = parts
        qd[head, :, :128] = parts
        tail = side[head]
        qx[head, :, 128:] = tail
        qd[head, :, 128:] = jnp.where(lane == 0, jnp.zeros_like(tail), tail)
        kx[head, :, :128] = head_twice(k[...], head)
        qm[head] = head_only(q[...], head)
        dx[head, :, :128] = head_only(d[...], head)
        inner = jnp.sum(head_only(product, head), axis=1, keepdims=True)
        dx[head, :, 128:] = side_lanes(0.0, jnp.broadcast_to(inner, (1024, 128)))


def back_head(head, qx, qd, kx, vx, dx, qm, kt, pt, st, pc, sc, bown, bcont):
    def tile(keys, rows, queries, bias=None):
        scores = dot(kx[head, keys], queries[head, rows], NT)
        if bias is not None:
            scores = scores + bias.astype(f32)
        probs = jnp.exp2(scores)
        return probs.astype(bf16), (probs * dot(vx[keys], dx[head, rows], NT)).astype(bf16)

    for c in range(3):
        keys = slice(512 + 512 * c, 1024 + 512 * c)
        pt[keys], st[keys] = tile(keys, slice(0, 1024), qx)
    pt[:512, 512:], st[:512, 512:] = tile(slice(0, 512), slice(512, 1024), qx)
    pt[:512, :512], st[:512, :512] = tile(slice(0, 512), slice(0, 512), qd, bown[...])
    for c in range(2):
        keys = slice(2048 + 256 * c, 2304 + 256 * c)
        pc[c], sc[c] = tile(keys, slice(512 + 256 * c, 768 + 256 * c), qd, bcont[c])
    kth = kt[64 * head : 64 * head + 64]
    main = dot(kth[:, :2048], st[...], NN)
    extra = [dot(kth[:, 2048 + 256 * c : 2304 + 256 * c], sc[c], NN) for c in range(2)]
    rows = jnp.concatenate(
        [main[:, :512], main[:, 512:768] + extra[0], main[:, 768:] + extra[1]], axis=1
    )
    return rows


def back_keys(head, dx, qm, pt, st, pc, sc, acc):
    def put(keys, cols, value):
        if head == 0:
            acc[keys, cols] = value
        else:
            acc[keys, cols] += value

    left, right = slice(0, 128), slice(128, 256)
    for c in range(4):
        keys = slice(512 * c, 512 * c + 512)
        put(keys, left, dot(st[keys], qm[head], NN) * SCALE)
        put(keys, right, dot(pt[keys], dx[head, :, :128], NN))
    for c in range(2):
        keys = slice(2048 + 256 * c, 2304 + 256 * c)
        rows = slice(512 + 256 * c, 768 + 256 * c)
        put(keys, left, dot(sc[c], qm[head, rows], NN) * SCALE)
        put(keys, right, dot(pc[c], dx[head, rows, :128], NN))


BACK_SCRATCH = [
    pltpu.VMEM((2, 1024, 256), bf16),
    pltpu.VMEM((2, 1024, 256), bf16),
    pltpu.VMEM((2, 2560, 256), bf16),
    pltpu.VMEM((2560, 256), bf16),
    pltpu.VMEM((2, 1024, 256), bf16),
    pltpu.VMEM((2, 1024, 128), bf16),
    pltpu.VMEM((128, 2560), bf16),
    pltpu.VMEM((2048, 1024), bf16),
    pltpu.VMEM((2048, 1024), bf16),
    pltpu.VMEM((2, 256, 256), bf16),
    pltpu.VMEM((2, 256, 256), bf16),
    pltpu.VMEM((512, 512), bf16),
    pltpu.VMEM((2, 256, 256), bf16),
    pltpu.VMEM((2560, 256), f32),
]


def back_specs():
    def pair(rows):
        return pl.BlockSpec((rows, 128), lambda i: (0, i))

    def once(*shape):
        return pl.BlockSpec(shape, lambda i: (0,) * len(shape), pipeline_mode=pl.Buffered(1))

    return [
        pair(1024), pair(2560), pair(2560), pair(1024), pair(1024),
        pl.BlockSpec((2, 1024, 128), lambda i: (i, 0, 0)),
        once(2560, 128), once(768, 2560),
    ]


def back_alone_kernel(q, k, v, d, o, side, kb, xt, dq, cont, partial_rows, whole, *scratch):
    (qx, qd, kx, vx, dx, qm, kt, pt, st, pc, sc, bown, bcont, acc) = scratch
    back_fill(q, k, v, d, o, side, kb, qx, qd, kx, vx, dx, qm, kt, bown, bcont)
    rows = []
    for head in range(2):
        rows.append(back_head(head, qx, qd, kx, vx, dx, qm, kt, pt, st, pc, sc, bown, bcont))
        back_keys(head, dx, qm, pt, st, pc, sc, acc)
    delta = jnp.transpose(jnp.concatenate(rows, axis=0) * SCALE).astype(bf16)
    dq[...] = delta
    low = acc[...].astype(bf16)
    partial_rows[...] = low[:2048]
    cont[...] = low[2048:]
    grad = dot(xt[:, :512], delta[:512], NN) + dot(xt[:, 2048:], delta[512:], NN)
    whole[:, :128] = grad.astype(bf16)
    whole[:, 128:] = dot(xt[...], low, NN).astype(bf16)


def attend_back_alone(q, k, v, d, o, side, kb, xt):
    width = q.shape[1]
    count = width // 128
    return pl.pallas_call(
        back_alone_kernel,
        grid=(count,),
        in_specs=back_specs(),
        out_specs=[
            pl.BlockSpec((1024, 128), lambda i: (0, i)),
            pl.BlockSpec((512, 256), lambda i: (0, i)),
            pl.BlockSpec((2048, 256), lambda i: (0, i)),
            pl.BlockSpec((width, 384), lambda i: (0, i)),
        ],
        out_shape=[
            jax.ShapeDtypeStruct((1024, width), bf16),
            jax.ShapeDtypeStruct((512, 2 * width), bf16),
            jax.ShapeDtypeStruct((2048, 2 * width), bf16),
            jax.ShapeDtypeStruct((width, 3 * width), bf16),
        ],
        scratch_shapes=BACK_SCRATCH,
        compiler_params=params(60),
        cost_estimate=cost(100, 40),
    )(q, k, v, d, o, side, kb, xt)


PAIRS = 6
A_X = 2
B_Y = 2
AB_COPIES = 15
PAIR_COPIES = 11


def back_linked_kernel(
    q, k, v, d, o, side, kb, xt, xa, xb, wq, wk, wv, adel,
    token_grad, gq, gk, gv, qrow, ga, gb,
    qx, qd, kx, vx, dx, qm, kt, pt, st, pc, sc, bown, bcont, acc,
    a_mine, a_x, a_y, a_z, a_q, b_mine, b_y, b_z, b_r,
    p_mine, p_other, c_in, y_in, z_in, r_in, keys_low, k_in, k_far, k_x, dw,
    dq, cont_k, cont_v, own_k, own_v, wsem, lsem, ab_send, ab_recv, p_send, p_recv,
):
    step = pl.program_id(0)
    rep = lax.axis_index("rep")
    shard = lax.axis_index("shard")
    core = rep % 2
    x = rep // 2
    z = shard // 2
    y = shard % 2
    rep1 = rep + 1 - 2 * core
    to_rep = [None, {"rep": rep1}, {"rep": (rep + 2) % 4}, {"rep": (rep1 + 2) % 4}]
    to_y = {"shard": z * 2 + 1 - y}
    zs = [z, z + 1 - 2 * (z % 2), (z + 2) % 4, 3 - z]
    to_z = [None] + [{"shard": zs[j] * 2 + y} for j in range(1, 4)]

    def move(src, dst, send, recv, where):
        return pltpu.make_async_remote_copy(
            src_ref=src, dst_ref=dst, send_sem=send, recv_sem=recv,
            device_id=where, device_id_type=MESH,
        )

    def ab(index, src, dst, where):
        return move(src, dst, ab_send.at[index], ab_recv.at[index], where)

    def columns(which):
        return pl.ds(pl.multiple_of(which * HALF_UP, 128), HALF_UP)

    def copy_ax():
        return ab(0, xa.at[:, :, columns(1 - x)], a_x, to_rep[2])

    def copy_ay():
        return ab(1, a_mine.at[pl.ds(4, 4)], a_y, to_y)

    def copy_az(j):
        return ab(1 + j, a_mine.at[j], a_z.at[j - 1], to_z[j])

    def copy_aq(j):
        src = a_q.at[1] if j == 3 else a_q.at[0]
        return ab(4 + j, src, a_q.at[j], to_rep[2 if j == 1 else 1])

    def copy_by():
        return ab(8, xb.at[pl.ds(4, 4)], b_y, to_y)

    def copy_bz(j):
        return ab(8 + j, b_mine.at[j], b_z.at[j - 1], to_z[j])

    def copy_br(j):
        return ab(12 + j, b_r.at[2 * j], b_r.at[2 * j + 1], to_rep[2 - j])

    def pair_copy(p, index, src, dst, where):
        return move(src, dst, p_send.at[p, index], p_recv.at[p, index], where)

    def copy_core(p):
        return pair_copy(p, 0, p_other, c_in.at[p % 2], to_rep[1])

    def copy_y(p):
        return pair_copy(p, 1, p_mine.at[p % 3, pl.ds(4, 4)], y_in.at[p % 2], to_y)

    def copy_z(p, j):
        return pair_copy(p, 1 + j, p_mine.at[p % 3, j], z_in.at[p % 2, j - 1], to_z[j])

    def copy_rep(p, j):
        return pair_copy(
            p, 5 + j, r_in.at[p % 2, 2 * j], r_in.at[p % 2, 2 * j + 1], to_rep[2 - j]
        )

    def copy_near(p):
        return pair_copy(p, 8, keys_low.at[p % 2, pl.ds(512, 512)], k_in.at[p % 2], to_rep[1])

    def copy_far(p):
        return pair_copy(p, 9, keys_low.at[p % 2, pl.ds(1536, 512)], k_far.at[p % 2], to_rep[1])

    def copy_turn(p):
        return pair_copy(p, 10, keys_low.at[p % 2, pl.ds(1024, 512)], k_x.at[p % 2], to_rep[2])

    def after_core(p):
        slot = p % 2
        copy_core(p).wait()
        for i in range(8):
            p_mine[p % 3, i] = p_mine[p % 3, i] + c_in[slot, i]
        copy_y(p).start()
        copy_near(p).wait()
        copy_far(p).wait()
        keys_low[slot, 1024:1536] = keys_low[slot, 1024:1536] + k_far[slot]
        copy_turn(p).start()
        keys_low[slot, :512] = keys_low[slot, :512] + k_in[slot]

    def after_y(p):
        copy_y(p).wait()
        for i in range(4):
            p_mine[p % 3, i] = p_mine[p % 3, i] + y_in[p % 2, i]
        for j in range(1, 4):
            copy_z(p, j).start()

    def own_keys(p):
        slot = p % 2
        copy_turn(p).wait()
        total = keys_low[slot, :512] + k_x[slot]
        at = pl.ds(pl.multiple_of(p * 128, 128), 128)
        own_k[:, at] = total[:, :128]
        own_v[:, at] = total[:, 128:]

    def after_z(p):
        slot = p % 2
        for j in range(1, 4):
            copy_z(p, j).wait()
        total = p_mine[p % 3, 0].astype(f32)
        for j in range(3):
            total = total + z_in[slot, j].astype(f32)
        r_in[slot, 0] = total.astype(bf16)
        copy_rep(p, 0).start()

    def after_x(p):
        slot = p % 2
        copy_rep(p, 0).wait()
        r_in[slot, 2] = r_in[slot, 0] + r_in[slot, 1]
        copy_rep(p, 1).start()

    def after_twin(p):
        slot = p % 2
        copy_rep(p, 1).wait()
        at = pl.ds(pl.multiple_of(p * 128, 128), 128)
        for half in range(2):
            total = r_in[slot, 2 + half]
            rows = core if half == 0 else 1 - core
            rows = pl.ds(pl.multiple_of(rows * 48, 16), 48)
            for j, out in enumerate((gq, gk, gv)):
                out[rows, at] = total[:48, 128 * j : 128 * j + 128]
            if half == 0:
                qrow[:, at] = total[48:64, :128]

    stages = (
        (5, after_twin), (4, after_x), (3, after_z), (2, after_y), (2, own_keys), (1, after_core),
    )

    def sum_pieces(total, more, count):
        def sum_piece(i, carry):
            total[i] = total[i] + more[i]
            return carry

        lax.fori_loop(0, count, sum_piece, 0)

    def sum_four(first, rest, out):
        total = first[0].astype(f32)
        for j in range(3):
            total = total + rest[j].astype(f32)
        out[0] = total.astype(bf16)

    @pl.when(step == 0)
    def _():
        barrier = pltpu.get_barrier_semaphore()
        for place in to_rep[1:] + [to_y] + to_z[1:]:
            pl.semaphore_signal(barrier, inc=1, device_id=place, device_id_type=MESH)
        pl.semaphore_wait(barrier, 7)
        copy_by().start()
        copy_ax().start()
        for copy in (
            pltpu.make_async_copy(xa.at[:, :, columns(x)], a_mine, lsem.at[0]),
            pltpu.make_async_copy(xb.at[pl.ds(0, 4)], b_mine, lsem.at[1]),
        ):
            copy.start()

    back_fill(q, k, v, d, o, side, kb, qx, qd, kx, vx, dx, qm, kt, bown, bcont)
    turned = []
    turned.append(back_head(0, qx, qd, kx, vx, dx, qm, kt, pt, st, pc, sc, bown, bcont))
    back_keys(0, dx, qm, pt, st, pc, sc, acc)

    for back, stage in stages:
        @pl.when(step >= back)
        def _():
            stage(step - back)

    @pl.when(step == 4)
    def _():
        copy_ay().wait()
        sum_pieces(a_mine, a_y, 4)
        for j in range(1, 4):
            copy_az(j).start()

    turned.append(back_head(1, qx, qd, kx, vx, dx, qm, kt, pt, st, pc, sc, bown, bcont))
    back_keys(1, dx, qm, pt, st, pc, sc, acc)

    @pl.when(step == A_X)
    def _():
        copy_ax().wait()
        pltpu.make_async_copy(xa.at[:, :, columns(x)], a_mine, lsem.at[0]).wait()
        sum_pieces(a_mine, a_x, 8)
        copy_ay().start()

    @pl.when(step == B_Y)
    def _():
        copy_by().wait()
        pltpu.make_async_copy(xb.at[pl.ds(0, 4)], b_mine, lsem.at[1]).wait()
        sum_pieces(b_mine, b_y, 4)
        for j in range(1, 4):
            copy_bz(j).start()

    @pl.when(step == 4)
    def _():
        for j in range(1, 4):
            copy_bz(j).wait()
        sum_four(b_mine, b_z, b_r)
        copy_br(0).start()

    def loads():
        wide = pl.ds(0, 768)
        return [
            pltpu.make_async_copy(wq, pt.at[pl.ds(0, 768), wide], wsem.at[0]),
            pltpu.make_async_copy(wk, pt.at[pl.ds(1024, 768), wide], wsem.at[1]),
            pltpu.make_async_copy(wv, st.at[pl.ds(0, 768), wide], wsem.at[2]),
            pltpu.make_async_copy(adel, st.at[pl.ds(1024, 1024), wide], wsem.at[3]),
        ]

    def results(half):
        rows = pl.ds(512 * half, 512)
        return pltpu.make_async_copy(dq.at[rows], token_grad.at[rows], wsem.at[4 + half])

    def tokens_half(half):
        rows = slice(512 * half, 512 * half + 512)
        far_rows = slice(1024 + 512 * half, 1536 + 512 * half)
        total = st[far_rows, :768].astype(f32) + dot(dq[rows], pt[:768, :768], NT)
        total = total + dot((own_k if half == 0 else cont_k)[...], pt[1024:1792, :768], NT)
        total = total + dot((own_v if half == 0 else cont_v)[...], st[:768, :768], NT)
        dq[rows] = total.astype(bf16)
        results(half).start()

    @pl.when(step == PAIRS - 1)
    def _():
        for load in loads():
            load.start()

    delta = jnp.transpose(jnp.concatenate(turned, axis=0) * SCALE)
    low = delta.astype(bf16)
    pair_at = pl.ds(pl.multiple_of(step * 128, 128), 128)
    dq[:, pair_at] = low
    slot = step % 2
    keys_low[slot] = acc[:2048].astype(bf16)
    tail = acc[2048:].astype(bf16)
    cont_k[:, pair_at] = tail[:, :128]
    cont_v[:, pair_at] = tail[:, 128:]
    copy_near(step).start()
    copy_far(step).start()
    grad = dot(xt[:, :512], low[:512], NN) + dot(xt[:, 2048:], low[512:], NN)
    dw[:, :128] = grad.astype(bf16)
    dw[:, 128:] = (dot(xt[:, :2048], keys_low[slot], NN) + dot(xt[:, 2048:], tail, NN)).astype(bf16)
    extra = jnp.sum(low.astype(f32), axis=0, keepdims=True)
    extra = jnp.concatenate([jnp.broadcast_to(extra, (16, 128)), jnp.zeros((16, 256), f32)], axis=1)
    extra = extra.astype(bf16)
    for i in range(8):
        place = (zs[i % 4] * 2 + (y if i < 4 else 1 - y)) * 2
        at = pl.multiple_of((place + core) * 48, 16)
        p_mine[step % 3, i, :48] = dw[pl.ds(at, 48)]
        p_mine[step % 3, i, 48:] = extra
        at = pl.multiple_of((place + 1 - core) * 48, 16)
        p_other[i, :48] = dw[pl.ds(at, 48)]
        p_other[i, 48:] = extra
    copy_core(step).start()

    @pl.when(step == PAIRS - 1)
    def _():
        def late(at):
            for back, stage in stages:
                if 0 <= at - back < PAIRS:
                    stage(at - back)

        late(PAIRS)
        for load in loads():
            load.wait()
        tokens_half(1)
        copy_br(0).wait()
        b_r[2] = b_r[0] + b_r[1]
        copy_br(1).start()
        late(PAIRS + 1)
        for j in range(1, 4):
            copy_az(j).wait()
        sum_four(a_mine, a_z, a_q)
        copy_aq(1).start()
        copy_aq(2).start()
        tokens_half(0)
        late(PAIRS + 2)
        copy_aq(1).wait()
        copy_aq(3).start()
        copy_br(1).wait()
        gb[core] = b_r[2]
        gb[1 - core] = b_r[3]
        late(PAIRS + 3)
        copy_aq(2).wait()
        copy_aq(3).wait()
        for j, (rows, which) in enumerate(
            ((core, x), (core, 1 - x), (1 - core, x), (1 - core, 1 - x))
        ):
            rows = pl.ds(pl.multiple_of(rows * 48, 16), 48)
            ga[rows, columns(which)] = a_q[j]
        late(PAIRS + 4)
        for half in range(2):
            results(half).wait()


def attend_back(q, k, v, d, o, side, kb, xt, xa, xb, wq, wk, wv, adel):
    width = q.shape[1]
    count = width // 128
    full = xa.shape[2]

    def held(*shape):
        return pl.BlockSpec(shape, lambda i: (0,) * len(shape), pipeline_mode=pl.Buffered(1))

    def vm(*shape):
        return pltpu.VMEM(shape, bf16)

    def out(*shape):
        return jax.ShapeDtypeStruct(shape, bf16)

    sem = pltpu.SemaphoreType.DMA
    piece = (64, 384)
    return pl.pallas_call(
        back_linked_kernel,
        grid=(count,),
        in_specs=back_specs() + [ANY] * 6,
        out_specs=[
            ANY, held(96, width), held(96, width), held(96, width),
            held(16, width), held(96, full), held(2, 208, width),
        ],
        out_shape=[
            out(1024, width), out(96, width), out(96, width), out(96, width),
            out(16, width), out(96, full), out(2, 208, width),
        ],
        scratch_shapes=BACK_SCRATCH
        + [
            vm(8, 48, HALF_UP), vm(8, 48, HALF_UP), vm(4, 48, HALF_UP), vm(3, 48, HALF_UP),
            vm(4, 48, HALF_UP), vm(4, 208, width), vm(4, 208, width), vm(3, 208, width),
            vm(4, 208, width),
            vm(3, 8, *piece), vm(8, *piece), vm(2, 8, *piece), vm(2, 4, *piece),
            vm(2, 3, *piece), vm(2, 4, *piece), vm(2, 2048, 256), vm(2, 512, 256),
            vm(2, 512, 256), vm(2, 512, 256), vm(width, 384),
            vm(1024, width), vm(512, width), vm(512, width), vm(512, width), vm(512, width),
            sem((6,)), sem((2,)), sem((AB_COPIES,)), sem((AB_COPIES,)), sem((PAIRS, PAIR_COPIES)),
            sem((PAIRS, PAIR_COPIES)),
        ],
        compiler_params=params(62, collective_id=2, has_side_effects=True),
        cost_estimate=cost(100, 40),
    )(q, k, v, d, o, side, kb, xt, xa, xb, wq, wk, wv, adel)


def gelu_parts(x):
    bell = jnp.exp2(x * x * (-0.5 * LOG2E))
    t = 1.0 / (1.0 + (0.3275911 * 0.7071067811865476) * jnp.abs(x))
    poly = 0.5 * 1.061405429
    for term in (-1.453152027, 1.421413741, -0.284496736, 0.254829592):
        poly = poly * t + 0.5 * term
    below = poly * t * bell
    phi = jnp.where(x >= 0.0, 1.0 - below, below)
    return x * phi, phi + x * bell * 0.3989422804014327


def normed_of(values):
    centered = values - jnp.mean(values, axis=-1, keepdims=True)
    spread = lax.rsqrt(jnp.mean(centered * centered, axis=-1, keepdims=True) + EPSILON)
    return centered * spread, spread


def norm_back(incoming, normed, spread, gain):
    scaled = incoming * gain
    centered = scaled - jnp.mean(scaled, axis=-1, keepdims=True)
    return (centered - normed * jnp.mean(scaled * normed, axis=-1, keepdims=True)) * spread


FCH = 768


def forward_back_kernel(
    mixed, tok, cot, teach, keep, scale, vecs, upb, up_full, down_full,
    result, hid_o, act_o, ddel_o, udel_o, adel_o, mdel_o, sums,
    wa_pieces, wu_pieces, wd_pieces, slope, sems,
):
    step = pl.program_id(0)
    width = tok.shape[1]
    hidden_units = upb.shape[1]

    loads = [
        pltpu.make_async_copy(up_full.at[:, :, pl.ds(0, width)], wa_pieces, sems.at[0]),
        pltpu.make_async_copy(up_full.at[:, :, pl.ds(width, hidden_units)], wu_pieces, sems.at[1]),
        pltpu.make_async_copy(down_full, wd_pieces, sems.at[2]),
    ]

    @pl.when(step == 0)
    def _():
        for load in loads:
            load.start()
        sums[...] = jnp.zeros_like(sums)
        for load in loads:
            load.wait()

    wa = wa_pieces.reshape(width, width)
    wu = wu_pieces.reshape(width, hidden_units)
    wd = wd_pieces.reshape(hidden_units, width)

    def vector(index):
        return vecs[index : index + 1].astype(f32)

    attn_b, gain1, shift1, down_b, gain2, shift2 = [vector(i) for i in range(2, 8)]

    def add_sum(index, values):
        sums[index : index + 1] += jnp.sum(values, axis=0, keepdims=True)

    x = tok[...].astype(f32)
    branch = attn_b + x + dot(mixed[...], wa[...], NN)
    normed1, inv1 = normed_of(branch)
    hidden = normed1 * gain1 + shift1
    hid_low = hidden.astype(bf16)
    hid_o[...] = hid_low
    for c in range(hidden_units // FCH):
        cols = slice(c * FCH, c * FCH + FCH)
        value, rise = gelu_parts(dot(hid_low, wu[:, cols], NN) + upb[:, cols].astype(f32))
        act_o[:, cols] = value.astype(bf16)
        slope[:, cols] = rise.astype(bf16)
    second = hidden + dot(act_o[...], wd[...], NN) + down_b
    normed2, inv2 = normed_of(second)
    final = normed2 * gain2 + shift2
    result[...] = final.astype(bf16)
    errors = final - teach[...].astype(f32)
    kept = errors * jnp.concatenate([keep[...]] * (width // 128), axis=1)
    add_sum(6, kept * errors)
    grad = cot[...].astype(f32) + kept * (2.0 * scale[...])
    add_sum(1, grad * normed2)
    add_sum(2, grad)
    grad2 = norm_back(grad, normed2, inv2, gain2)
    ddel = grad2.astype(bf16)
    ddel_o[...] = ddel
    add_sum(0, ddel.astype(f32))
    for c in range(hidden_units // FCH):
        cols = slice(c * FCH, c * FCH + FCH)
        delta = dot(ddel, wd[cols], NT) * slope[:, cols].astype(f32)
        low = delta.astype(bf16)
        udel_o[:, cols] = low
        add_sum(8 + c, low.astype(f32))
    hgrad = grad2 + dot(udel_o[...], wu[...], NT)
    add_sum(4, hgrad * normed1)
    add_sum(5, hgrad)
    grad1 = norm_back(hgrad, normed1, inv1, gain1)
    adel = grad1.astype(bf16)
    adel_o[...] = adel
    add_sum(3, adel.astype(f32))
    mdel = dot(adel, wa[...], NT).astype(bf16)
    mdel_o[...] = mdel
    add_sum(7, mdel.astype(f32))


def forward_back(mixed, tok, cot, teach, keep, scale, vecs, upb, up_full, down_full):
    rows, width = tok.shape
    hidden_units = upb.shape[1]
    half = 512

    def block(columns):
        return pl.BlockSpec((half, columns), lambda i, *_: (i, 0))

    def fixed(*shape):
        return pl.BlockSpec(shape, lambda i, *_: (0,) * len(shape))

    def out(columns):
        return jax.ShapeDtypeStruct((rows, columns), bf16)

    return pl.pallas_call(
        forward_back_kernel,
        grid=(rows // half,),
        in_specs=[
            block(width), block(width), block(width), block(width),
            block(128), fixed(1, 1), fixed(8, width), fixed(1, hidden_units), ANY, ANY,
        ],
        out_specs=[
            block(width), block(width), block(hidden_units), block(width),
            block(hidden_units), block(width), block(width), fixed(16, width),
        ],
        scratch_shapes=[
            pltpu.VMEM((16, width // 16, width), bf16),
            pltpu.VMEM((16, width // 16, hidden_units), bf16),
            pltpu.VMEM((16, hidden_units // 16, width), bf16),
            pltpu.VMEM((half, hidden_units), bf16),
            pltpu.SemaphoreType.DMA((3,)),
        ],
        out_shape=[
            out(width), out(width), out(hidden_units), out(width), out(hidden_units),
            out(width), out(width), jax.ShapeDtypeStruct((16, width), f32),
        ],
        compiler_params=params(60),
        cost_estimate=cost(32.6, 30),
    )(mixed, tok, cot, teach, keep, scale, vecs, upb, up_full, down_full)


def up_grad_kernel(order, mixed, adel, hid, udel, mine, other, whole):
    step = pl.program_id(0)

    @pl.when(step == 0)
    def _():
        whole[...] = dot(mixed[...], adel[...], TN).astype(bf16)

    @pl.when(step > 0)
    def _():
        whole[...] = dot(hid[...], udel[...], TN).astype(bf16)

    store_pieces(order, whole, mine, other, 48)


def store_pieces(order, source, mine, other, piece):
    for i in range(8):
        at = pl.multiple_of(order[i] * piece, 16)
        mine[i, :piece] = source[pl.ds(at, piece)]
        at = pl.multiple_of(order[i + 8] * piece, 16)
        other[i, :piece] = source[pl.ds(at, piece)]


def up_grad(order, mixed, adel, hid, udel):
    rows, width = adel.shape
    columns = udel.shape[1]
    shape = jax.ShapeDtypeStruct((8, 48, width + columns), bf16)
    out = pl.BlockSpec((8, 48, width), lambda i, *_: (0, 0, i))
    full = pl.BlockSpec((rows, width), lambda i, *_: (0, 0))
    return pl.pallas_call(
        up_grad_kernel,
        grid_spec=pltpu.PrefetchScalarGridSpec(
            num_scalar_prefetch=1,
            grid=(1 + columns // width,),
            in_specs=[
                full, full, full,
                pl.BlockSpec((rows, width), lambda i, *_: (0, jnp.maximum(i - 1, 0))),
            ],
            out_specs=[out, out],
            scratch_shapes=[pltpu.VMEM((width, width), bf16)],
        ),
        out_shape=[shape, shape],
        compiler_params=params(),
        cost_estimate=cost(6, 20),
    )(order, mixed, adel, hid, udel)


def down_grad_kernel(order, act, ddel, sums, mine, other, whole):
    whole[...] = dot(act[...], ddel[...], TN).astype(bf16)
    store_pieces(order, whole, mine, other, 192)
    low = sums[...].astype(bf16)
    for i in range(8):
        mine[i, 192:] = low
        other[i, 192:] = low


def down_grad(order, act, ddel, sums):
    rows, columns = ddel.shape
    total = act.shape[1]
    chunk = 256
    shape = jax.ShapeDtypeStruct((8, 208, columns), bf16)
    out = pl.BlockSpec((8, 208, chunk), lambda i, *_: (0, 0, i))
    return pl.pallas_call(
        down_grad_kernel,
        grid_spec=pltpu.PrefetchScalarGridSpec(
            num_scalar_prefetch=1,
            grid=(columns // chunk,),
            in_specs=[
                pl.BlockSpec(act.shape, lambda i, *_: (0, 0)),
                pl.BlockSpec((rows, chunk), lambda i, *_: (0, i)),
                pl.BlockSpec((16, chunk), lambda i, *_: (0, i)),
            ],
            out_specs=[out, out],
            scratch_shapes=[pltpu.VMEM((total, chunk), bf16)],
        ),
        out_shape=[shape, shape],
        compiler_params=params(),
        cost_estimate=cost(5, 20),
    )(order, act, ddel, sums)


def tokens_grad_kernel(adel, dq, own, cont, wq, wk, wv, out):
    for half, low in enumerate((own, cont)):
        rows = slice(512 * half, 512 * half + 512)
        total = adel[rows].astype(f32) + dot(dq[rows], wq[...], NT)
        for p in range(wq.shape[1] // 128):
            cols = slice(128 * p, 128 * p + 128)
            both = jnp.concatenate([wk[:, cols], wv[:, cols]], axis=1)
            total = total + dot(low[:, 256 * p : 256 * p + 256], both, NT)
        out[rows] = total.astype(bf16)


def tokens_grad(adel, dq, own, cont, wq, wk, wv):
    args = (adel, dq, own, cont, wq, wk, wv)
    return pl.pallas_call(
        tokens_grad_kernel,
        grid=(1,),
        in_specs=[pl.BlockSpec(a.shape, lambda i: (0, 0)) for a in args],
        out_specs=pl.BlockSpec(adel.shape, lambda i: (0, 0)),
        out_shape=jax.ShapeDtypeStruct(adel.shape, bf16),
        compiler_params=params(),
        cost_estimate=cost(3.6, 12),
    )(*args)


def finish_kernel(gq, gk, gv, qrow, ga, gb, scale, oq, ok, ov, oa, ou, od, loss, *rows):
    shard = lax.axis_index("shard")
    width = gq.shape[1]
    part = gq.shape[0]
    for low, out in ((gq, oq), (gk, ok), (gv, ov)):
        out[...] = low[...].astype(f32)
    oa[...] = ga[:, :width].astype(f32)
    ou[...] = ga[:, width:].astype(f32)
    od[...] = gb[:, :192].astype(f32)
    low = gb[0, 192:]

    def pick(values, size, first):
        row = lax.broadcasted_iota(jnp.int32, (width, size), 0)
        col = lax.broadcasted_iota(jnp.int32, (width, size), 1)
        return dot(values, jnp.where(row == col + first, 1.0, 0.0).astype(bf16), NN)

    own = pick(low, 128, shard * part)
    first = pick(qrow[...], 128, shard * part)
    for out, index in zip(rows[1:-1], (7, 3, 4, 5, 0, 1, 2)):
        out[...] = own[index : index + 1, :part]
    rows[0][...] = first[0:1, :part]
    up_part = rows[-1].shape[1]
    per_row = width // up_part
    lines = pick(low, up_part, shard % per_row * up_part)
    line = lax.broadcasted_iota(jnp.int32, lines.shape, 0)
    lines = jnp.where(line == 8 + shard // per_row, lines, 0.0)
    rows[-1][...] = jnp.sum(lines, axis=0, keepdims=True)
    total = jnp.sum(low[6:7].astype(f32), axis=1, keepdims=True)
    loss[...] = total * scale[...]


def finish(gq, gk, gv, qrow, ga, gb, scale):
    part, width = gq.shape
    up = ga.shape[1] - width

    def out(*shape):
        return jax.ShapeDtypeStruct(shape, f32)

    square = out(part, width)
    return pl.pallas_call(
        finish_kernel,
        out_shape=[
            square, square, square, square, out(part, up), out(2, 192, width), out(1, 1),
        ] + [out(1, part)] * 8 + [out(1, up * part // width)],
        compiler_params=params(60),
        cost_estimate=cost(0.1, 6),
    )(gq, gk, gv, qrow, ga, gb, scale)


def swap(values, axis, bit):
    size = lax.axis_size(axis)
    return lax.ppermute(values, axis, [(i, i ^ bit) for i in range(size)])


def local(
    tokens, cotangent, teacher, valid_mask, valid_count,
    query_weight, query_bias, key_weight, value_weight, value_bias,
    attn_weight, attn_bias, first_gain, first_shift,
    up_weight, up_bias, down_weight, down_bias, second_gain, second_shift,
):
    rows, width = tokens.shape[2:]
    shards = lax.axis_size("shard")
    split = shards == 8
    rep = lax.axis_index("rep")
    shard = lax.axis_index("shard")
    core = rep % 2
    z, y = shard // 2, shard % 2
    tok = tokens.reshape(rows, width)
    keep = valid_mask.reshape(rows)
    if split:
        i = jnp.arange(16, dtype=jnp.int32)
        order = (((z ^ (i % 4)) * 2 + (y ^ (i // 4 % 2))) * 2 + (core ^ (i // 8))).astype(jnp.int32)
    else:
        order = jnp.arange(16, dtype=jnp.int32)

    small = [
        query_bias, value_bias, attn_bias, first_gain, first_shift, down_bias, second_gain,
        second_shift, up_bias,
    ]
    part = query_bias.shape[0]
    vec = jnp.concatenate([v[None] for v in small], axis=1)[0]
    keep_low = keep[:PPIECE].astype(f32).reshape(4, 128)
    if split:
        keep_low = jnp.concatenate([keep_low, keep_low])
        vec = jnp.pad(vec, (0, 2048 - vec.shape[0])).reshape(16, 128)
        up_own = jnp.concatenate([attn_weight, up_weight], axis=1).reshape(2, 48, -1)
        wq, wk, wv, vecs, oth, others_keep, up_full = first_gather(
            query_weight, key_weight, value_weight, vec, tok, keep_low, up_own
        )
        vecs = vecs.reshape(8, 2048)
    else:
        wq, wk, wv, vecs = [
            lax.all_gather(w, "shard", axis=0, tiled=True)
            for w in (query_weight, key_weight, value_weight, vec[None])
        ]
        prompt = tok[:PPIECE]
        oth = jnp.concatenate([swap(prompt, "rep", bit) for bit in (1, 2, 3)])
        others_keep = jnp.stack([swap(keep_low, "rep", bit) for bit in (1, 2, 3)])
    others_keep = others_keep[:, :4].reshape(3 * PPIECE)
    upb = vecs[:, 8 * part : 8 * part + up_bias.shape[0]].reshape(1, -1)
    vecs = vecs[:, : 8 * part].reshape(shards, 8, part).transpose(1, 0, 2).reshape(8, width)

    all_keep = jnp.concatenate(
        [keep[:PPIECE].astype(f32), others_keep, keep[PPIECE:].astype(f32)]
    )
    bias = jnp.where(all_keep > 0.5, 0.0, NEGATIVE)
    brow = jnp.broadcast_to(bias[None], (8, bias.shape[0]))
    lane = jnp.arange(128)[None]
    kb = jnp.where(lane == 0, bias[:, None], jnp.where(lane < 4, 1.0, 0.0)).astype(bf16)

    own_parts = ()
    if split:
        own_parts = (up_own, down_weight.reshape(2, 192, width), up_full)
    outs = attend_near(tok, oth, wq, wk, wv, vecs[0:1], vecs[1:2], kb, brow, own_parts)
    q, k, v, xt, qn, kn, mixed, sides = outs[:8]
    if split:
        up_full, down_full = outs[8:]
    else:
        up_full = jnp.concatenate(
            [
                lax.all_gather(w, "shard", axis=0, tiled=True)
                for w in (attn_weight, up_weight)
            ],
            axis=1,
        ).reshape(16, 48, -1)
        down_full = lax.all_gather(down_weight, "shard", axis=0, tiled=True)
        down_full = down_full.reshape(16, 192, width)
    mixed, sides = attend_far(q, k, v, kb, brow, qn, kn, mixed, sides)

    keep_wide = jnp.broadcast_to(keep.astype(f32)[:, None], (rows, 128))
    scale = (1.0 / valid_count.astype(f32)).reshape(1, 1)
    result, hid, act, ddel, udel, adel, mdel, sums = forward_back(
        mixed, tok, cotangent.reshape(rows, width), teacher.reshape(rows, width),
        keep_wide, scale, vecs, upb, up_full, down_full,
    )
    down_mine, down_other = down_grad(order, act, ddel, sums)
    up_mine, up_other = up_grad(order, mixed, adel, hid, udel)
    if split:
        down_sum = (down_mine.astype(f32) + swap(down_other, "rep", 1).astype(f32)).astype(bf16)
        up_sum = (up_mine.astype(f32) + swap(up_other, "rep", 1).astype(f32)).astype(bf16)
        token_grad, query_low, key_low, value_low, qrow, up_low, down_low = attend_back(
            q, k, v, mdel, mixed, sides, kb, xt, up_sum, down_sum, wq, wk, wv, adel
        )
        outs = finish(query_low, key_low, value_low, qrow, up_low, down_low, scale)
        query_grad, key_grad, value_grad, attn_grad, up_final, down_final, loss = outs[:7]
        (
            query_vec, value_vec, attn_vec, gain1_vec, shift1_vec, down_vec, gain2_vec, shift2_vec,
            up_vec,
        ) = [row.reshape(-1) for row in outs[7:]]
        return (
            result.reshape(tokens.shape),
            loss.reshape(()),
            token_grad.reshape(tokens.shape),
            query_grad,
            query_vec,
            key_grad,
            value_grad,
            value_vec,
            attn_grad,
            attn_vec,
            gain1_vec,
            shift1_vec,
            up_final,
            up_vec,
            down_final.reshape(-1, width),
            down_vec,
            gain2_vec,
            shift2_vec,
        )
    else:
        dq, cont, partial_rows, whole = attend_back_alone(q, k, v, mdel, mixed, sides, kb, xt)

        def scatter(part):
            part = lax.psum_scatter(part, "shard", scatter_dimension=0, tiled=True)
            return lax.psum(part, "rep").astype(f32)

        def joined(mine, other, piece):
            return jnp.concatenate([mine, other])[:, :piece].reshape(16 * piece, -1)

        turned = partial_rows.reshape(2, 2, PPIECE, -1)
        turned = jnp.where(core == 1, turned[:, ::-1], turned)
        turned = jnp.where(rep // 2 == 1, turned[::-1], turned)
        own = lax.psum_scatter(
            turned.reshape(4 * PPIECE, -1), "rep", scatter_dimension=0, tiled=True
        )
        whole = scatter(whole).reshape(part, width // 128, 3, 128)
        query_grad, key_grad, value_grad = [whole[:, :, j].reshape(part, width) for j in range(3)]
        up_all = scatter(joined(up_mine, up_other, 48))
        down_all = scatter(joined(down_mine, down_other, 192))
        sums = lax.psum(sums, ("rep", "shard"))
        query_row = lax.psum(jnp.sum(dq.astype(f32), axis=0), ("rep", "shard"))
        token_grad = tokens_grad(adel, dq, own, cont, wq, wk, wv)

    def owned(row):
        return lax.dynamic_slice(row, (shard * part,), (part,))

    up_part = up_bias.shape[0]
    loss = jnp.sum(sums[6]) / valid_count.astype(f32)
    return (
        result.reshape(tokens.shape),
        loss,
        token_grad.reshape(tokens.shape),
        query_grad,
        owned(query_row),
        key_grad,
        value_grad,
        owned(sums[7]),
        up_all[:, :width],
        owned(sums[3]),
        owned(sums[4]),
        owned(sums[5]),
        up_all[:, width:],
        lax.dynamic_slice(sums[8:12].reshape(-1), (shard * up_part,), (up_part,)),
        down_all,
        owned(sums[0]),
        owned(sums[1]),
        owned(sums[2]),
    )


def solution(mesh):
    wide = P("shard", "rep", None, None)
    matrix, vector = P("shard", None), P("shard")
    return jax.shard_map(
        local,
        mesh=mesh,
        in_specs=(
            wide, wide, wide, P("shard", "rep", None), P(),
            matrix, vector, matrix, matrix, vector, matrix, vector, vector, vector,
            matrix, vector, matrix, vector, vector, vector,
        ),
        out_specs=(
            wide, P(), wide,
            matrix, vector, matrix, matrix, vector, matrix, vector, vector, vector,
            matrix, vector, matrix, vector, vector, vector,
        ),
        check_vma=False,
    )
```

```python
import functools

import jax
import jax.numpy as jnp
from jax import lax
from jax.experimental import pallas as pl
from jax.experimental.pallas import tpu as pltpu
from jax.sharding import PartitionSpec as P

HDIM = 64
PPIECE = 512
CLEN = 256
EPSILON = 1e-05
NEGATIVE = -1e30
LOG2E = 1.4426950408889634
SCALE = 1.0 / 8.0
LIMIT = 100.0

f32 = jnp.float32
bf16 = jnp.bfloat16
NT = (((1,), (1,)), ((), ()))
NN = (((1,), (0,)), ((), ()))
TN = (((0,), (0,)), ((), ()))
ANY = pl.BlockSpec(memory_space=pl.ANY)
MESH = pl.DeviceIdType.MESH


def dot(left, right, dims):
    return lax.dot_general(left, right, dims, preferred_element_type=f32)


def params(mib=56, **more):
    return pltpu.CompilerParams(vmem_limit_bytes=mib * 2**20, **more)


def cost(gflop, mbytes):
    return pl.CostEstimate(
        flops=int(gflop * 1e9), bytes_accessed=int(mbytes * 1e6), transcendentals=0
    )


def lane_of(rows):
    return lax.broadcasted_iota(jnp.int32, (rows, 128), 1)


def split3(values):
    hi = values.astype(bf16).astype(f32)
    mid = (values - hi).astype(bf16).astype(f32)
    low = values - hi - mid
    return hi, mid, low


def side_lanes(first, values):
    lane = lane_of(values.shape[0])
    hi, mid, low = split3(values)
    out = jnp.where(lane == 1, -hi, jnp.where(lane == 2, -mid, jnp.where(lane == 3, -low, 0.0)))
    return jnp.where(lane == 0, first, out).astype(bf16)


def gather_kernel(
    wq, wk, wv, vec, tok, keep, up_own,
    fq, fk, fv, fvec, ptok, pkeep, up_full,
    asend, arecv, local_sem, zrecv, yrecv, crecv, usend, dsend, ysend, csend, tsend, trecv,
):
    depth = 4
    rep = lax.axis_index("rep")
    shard = lax.axis_index("shard")
    core = rep % 2
    z = shard // 2
    y = shard % 2
    other_core = {"rep": rep + 1 - 2 * core}
    other_x = {"rep": (rep + 2) % 4}
    other_y = {"shard": z * 2 + 1 - y}
    up = {"shard": (shard + 2) % 8}
    down = {"shard": (shard + 6) % 8}

    barrier = pltpu.get_barrier_semaphore()
    for place in (other_core, other_x, other_y):
        pl.semaphore_signal(barrier, inc=1, device_id=place, device_id_type=MESH)

    @pl.when(z < depth - 1)
    def _():
        pl.semaphore_signal(barrier, inc=1, device_id=up, device_id_type=MESH)

    @pl.when(z > 0)
    def _():
        pl.semaphore_signal(barrier, inc=1, device_id=down, device_id_type=MESH)

    inner = jnp.where((z > 0) & (z < depth - 1), 5, 4)
    pl.semaphore_wait(barrier, inner)

    sources = (wq, wk, wv, vec)
    targets = (fq, fk, fv, fvec)

    def place_of(u, zz, yy, cc):
        if u == 3:
            return targets[u].at[zz * 2 + yy]
        return targets[u].at[(zz * 2 + yy) * 2 + cc]

    def own_of(u):
        return sources[u] if u == 3 else sources[u].at[core]

    def move(src, dst, send, recv, where):
        return pltpu.make_async_remote_copy(
            src_ref=src, dst_ref=dst, send_sem=send, recv_sem=recv,
            device_id=where, device_id_type=MESH,
        )

    def to_up(u, zz, src):
        return move(src, place_of(u, zz, y, core), usend.at[u, zz], zrecv.at[u, zz], up)

    def to_down(u, zz, src):
        return move(src, place_of(u, zz, y, core), dsend.at[u, zz], zrecv.at[u, zz], down)

    def to_y(u, zz, src):
        return move(src, place_of(u, zz, y, core), ysend.at[u, zz], yrecv.at[u, zz], other_y)

    def to_core(u, zz, yy):
        at = place_of(u, zz, yy, core)
        index = zz * 2 + yy
        return move(at, at, csend.at[u, index], crecv.at[u, index], other_core)

    for u in range(4):
        @pl.when(z < depth - 1)
        def _():
            to_up(u, z, own_of(u)).start()

        @pl.when(z > 0)
        def _():
            to_down(u, z, own_of(u)).start()

        to_y(u, z, own_of(u)).start()

    prompt = tok.at[pl.ds(0, PPIECE)]
    copies = [
        move(prompt, ptok.at[1], tsend.at[0], trecv.at[0], other_x),
        move(keep, pkeep.at[1], tsend.at[1], trecv.at[1], other_x),
        move(prompt, ptok.at[0], tsend.at[2], trecv.at[2], other_core),
        move(keep, pkeep.at[0], tsend.at[3], trecv.at[3], other_core),
    ]
    for copy in copies:
        copy.start()
    locals_ = []
    for u in range(4):
        if u == 3:
            dst = fvec.at[shard]
        else:
            dst = targets[u].at[pl.ds(shard * 2, 2)]
        locals_.append(pltpu.make_async_copy(sources[u], dst, local_sem.at[u]))
        locals_[-1].start()

    columns = pl.ds(pl.multiple_of(rep // 2 * HALF_UP, 128), HALF_UP)

    def up_place(zz):
        return up_full.at[(zz * 2 + y) * 2 + core, :, columns]

    def up_up(zz, src):
        return move(src, up_place(zz), asend.at[0, zz], arecv.at[zz], up)

    def up_down(zz, src):
        return move(src, up_place(zz), asend.at[1, zz], arecv.at[zz], down)

    def up_start():
        src = up_own.at[core, :, columns]

        @pl.when(z < depth - 1)
        def _():
            up_up(z, src).start()

        @pl.when(z > 0)
        def _():
            up_down(z, src).start()

    def up_hop(step):
        @pl.when(z - step >= 0)
        def _():
            at = up_place(z - step)
            up_up(z - step, at).wait_recv()
            if step == 1:
                @pl.when(z < depth - 1)
                def _():
                    up_up(z - step, at).start()

        @pl.when(z + step < depth)
        def _():
            at = up_place(z + step)
            up_down(z + step, at).wait_recv()
            if step == 1:
                @pl.when(z > 0)
                def _():
                    up_down(z + step, at).start()

    for step in range(1, depth + 1):
        if step == 2:
            up_start()
        if step == 4:
            up_hop(1)
        for u in range(4):
            if step < depth:
                @pl.when(z - step >= 0)
                def _():
                    zz = z - step
                    at = place_of(u, zz, y, core)
                    to_up(u, zz, at).wait_recv()

                    @pl.when(z < depth - 1)
                    def _():
                        to_up(u, zz, at).start()

                    to_y(u, zz, at).start()
                    if u < 3:
                        to_core(u, zz, y).start()

                @pl.when(z + step < depth)
                def _():
                    zz = z + step
                    at = place_of(u, zz, y, core)
                    to_down(u, zz, at).wait_recv()

                    @pl.when(z > 0)
                    def _():
                        to_down(u, zz, at).start()

                    to_y(u, zz, at).start()
                    if u < 3:
                        to_core(u, zz, y).start()

        for u in range(4):
            def from_y(zz):
                at = targets[u].at[zz * 2 + 1 - y] if u == 3 else place_of(u, zz, 1 - y, core)
                move(at, at, ysend.at[u, zz], yrecv.at[u, zz], other_y).wait_recv()
                if u < 3:
                    to_core(u, zz, 1 - y).start()

            if step == 1:
                from_y(z)
            else:
                @pl.when(z - (step - 1) >= 0)
                def _():
                    from_y(z - (step - 1))

                @pl.when(z + (step - 1) < depth)
                def _():
                    from_y(z + (step - 1))

    up_hop(2)
    copies[0].wait_recv()
    copies[1].wait_recv()
    forward = [
        move(ptok.at[1], ptok.at[2], tsend.at[4], trecv.at[4], other_core),
        move(pkeep.at[1], pkeep.at[2], tsend.at[5], trecv.at[5], other_core),
    ]
    for copy in forward:
        copy.start()

    def others(act):
        for zz in range(depth):
            for yy in range(2):
                @pl.when((zz != z) | (yy != y))
                def _():
                    act(zz, yy)

    for u in range(3):
        def arrived(zz, yy):
            at = place_of(u, zz, yy, 1 - core)
            index = zz * 2 + yy
            move(at, at, csend.at[u, index], crecv.at[u, index], other_core).wait_recv()

        others(arrived)
    copies[2].wait_recv()
    copies[3].wait_recv()
    for copy in forward:
        copy.wait_recv()

    for copy in copies + forward:
        copy.wait_send()
    for zz in range(depth):
        at = up_place(zz)

        @pl.when((zz <= z) & (zz >= z - 1) & (z < depth - 1))
        def _():
            up_up(zz, at).wait_send()

        @pl.when((zz >= z) & (zz <= z + 1) & (z > 0))
        def _():
            up_down(zz, at).wait_send()

    for copy in locals_:
        copy.wait()
    for u in range(4):
        for zz in range(depth):
            at = place_of(u, zz, y, core)
            to_y(u, zz, at).wait_send()

            @pl.when((zz <= z) & (z < depth - 1))
            def _():
                to_up(u, zz, at).wait_send()

            @pl.when((zz >= z) & (z > 0))
            def _():
                to_down(u, zz, at).wait_send()

        if u < 3:
            others(lambda zz, yy: to_core(u, zz, yy).wait_send())


def first_gather(wq, wk, wv, vec, tok, keep, up_own):
    width = wq.shape[1]
    sem = pltpu.SemaphoreType.DMA
    halves = [w.reshape(2, 48, width) for w in (wq, wk, wv)]
    full = jax.ShapeDtypeStruct((16, 48, width), bf16)
    outs = pl.pallas_call(
        gather_kernel,
        in_specs=[ANY] * 7,
        out_specs=[ANY] * 7,
        out_shape=[
            full, full, full,
            jax.ShapeDtypeStruct((8, 16, 128), bf16),
            jax.ShapeDtypeStruct((3, PPIECE, width), bf16),
            jax.ShapeDtypeStruct((3, 8, 128), f32),
            jax.ShapeDtypeStruct((16, 48, up_own.shape[2]), bf16),
        ],
        scratch_shapes=[
            sem((2, 4)), sem((4,)), sem((4,)), sem((4, 4)), sem((4, 4)), sem((3, 8)), sem((4, 4)), sem((4, 4)),
            sem((4, 4)), sem((3, 8)), sem((6,)), sem((6,)),
        ],
        compiler_params=params(60, collective_id=1, has_side_effects=True),
        cost_estimate=cost(0, 20),
    )(*halves, vec, tok, keep, up_own)
    fq, fk, fv, fvec, ptok, pkeep, up_full = outs
    return (
        fq.reshape(width, width), fk.reshape(width, width), fv.reshape(width, width),
        fvec, ptok.reshape(3 * PPIECE, width), pkeep, up_full,
    )


class Link:
    def __init__(self):
        rep = lax.axis_index("rep")
        shard = lax.axis_index("shard")
        self.core = rep % 2
        self.x = rep // 2
        self.z = shard // 2
        self.y = shard % 2
        self.shard = shard
        self.to_core = {"rep": rep + 1 - 2 * self.core}
        self.to_x = {"rep": (rep + 2) % 4}
        self.to_y = {"shard": self.z * 2 + 1 - self.y}
        self.to_up = {"shard": (shard + 2) % 8}
        self.to_down = {"shard": (shard + 6) % 8}

    def greet(self):
        barrier = pltpu.get_barrier_semaphore()
        for place in (self.to_core, self.to_x, self.to_y):
            pl.semaphore_signal(barrier, inc=1, device_id=place, device_id_type=MESH)

        @pl.when(self.z < 3)
        def _():
            pl.semaphore_signal(barrier, inc=1, device_id=self.to_up, device_id_type=MESH)

        @pl.when(self.z > 0)
        def _():
            pl.semaphore_signal(barrier, inc=1, device_id=self.to_down, device_id_type=MESH)

        count = jnp.where((self.z > 0) & (self.z < 3), 5, 4)
        pl.semaphore_wait(barrier, count)


def move(src, dst, send, recv, where):
    return pltpu.make_async_remote_copy(
        src_ref=src, dst_ref=dst, send_sem=send, recv_sem=recv,
        device_id=where, device_id_type=MESH,
    )


class Spread:
    def __init__(self, own, full, sems):
        self.at = Link()
        self.own, self.full = own, full
        (
            self.local, self.zrecv, self.yrecv, self.usend, self.dsend, self.ysend,
            self.xrecv, self.xsend, self.crecv, self.csend,
        ) = sems

    def columns(self, xx):
        return pl.ds(pl.multiple_of(xx * HALF_UP, 128), HALF_UP)

    def place(self, u, zz, yy, cc, xx):
        index = (zz * 2 + yy) * 2 + cc
        if u == 0:
            return self.full[0].at[index, :, self.columns(xx)]
        return self.full[1].at[index]

    def mine(self, u, zz, yy):
        return self.place(u, zz, yy, self.at.core, self.at.x)

    def source(self, u):
        if u == 0:
            return self.own[0].at[self.at.core, :, self.columns(self.at.x)]
        return self.own[1].at[self.at.core]

    def up(self, u, zz, src):
        return move(
            src, self.mine(u, zz, self.at.y), self.usend.at[u, zz], self.zrecv.at[u, zz],
            self.at.to_up,
        )

    def down(self, u, zz, src):
        return move(
            src, self.mine(u, zz, self.at.y), self.dsend.at[u, zz], self.zrecv.at[u, zz],
            self.at.to_down,
        )

    def side(self, u, zz, src):
        return move(
            src, self.mine(u, zz, self.at.y), self.ysend.at[u, zz], self.yrecv.at[u, zz],
            self.at.to_y,
        )

    def across(self, zz, yy):
        at = self.mine(0, zz, yy)
        index = zz * 2 + yy
        return move(at, at, self.xsend.at[index], self.xrecv.at[index], self.at.to_x)

    def twin(self, kind, zz, yy):
        if kind == 1:
            at = self.place(0, zz, yy, self.at.core, 1 - self.at.x)
        else:
            at = self.mine(0 if kind == 0 else 1, zz, yy)
        index = zz * 2 + yy
        return move(
            at, at, self.csend.at[kind, index], self.crecv.at[kind, index], self.at.to_core
        )

    def twin_in(self, kind, zz, yy):
        cc = 1 - self.at.core
        xx = 1 - self.at.x if kind == 1 else self.at.x
        at = self.place(1 if kind == 2 else 0, zz, yy, cc, xx)
        index = zz * 2 + yy
        return move(
            at, at, self.csend.at[kind, index], self.crecv.at[kind, index], self.at.to_core
        )

    def locals_(self):
        return [
            pltpu.make_async_copy(
                self.own[u], self.full[u].at[pl.ds(self.at.shard * 2, 2)], self.local.at[u]
            )
            for u in range(2)
        ]

    def begin(self):
        z, y = self.at.z, self.at.y
        self.at.greet()

        @pl.when(z < 3)
        def _():
            self.up(1, z, self.source(1)).start()

        @pl.when(z > 0)
        def _():
            self.down(1, z, self.source(1)).start()

        @pl.when((z >= 2) & (z < 3))
        def _():
            self.up(0, z - 2, self.mine(0, z - 2, y)).start()

        @pl.when((z <= 1) & (z > 0))
        def _():
            self.down(0, z + 2, self.mine(0, z + 2, y)).start()

        self.side(0, z, self.source(0)).start()
        for step in (1, 2):
            @pl.when(z - step >= 0)
            def _():
                self.side(0, z - step, self.mine(0, z - step, y)).start()
                self.got(0, z - step, y)

            @pl.when(z + step < 4)
            def _():
                self.side(0, z + step, self.mine(0, z + step, y)).start()
                self.got(0, z + step, y)

        self.side(1, z, self.source(1)).start()
        for copy in self.locals_():
            copy.start()

    def got(self, u, zz, yy):
        if u == 0:
            self.across(zz, yy).start()
            self.twin(0, zz, yy).start()
        else:
            self.twin(2, zz, yy).start()

    def hop(self, u, step):
        z, y = self.at.z, self.at.y

        @pl.when(z - step >= 0)
        def _():
            zz = z - step
            at = self.mine(u, zz, y)
            self.up(u, zz, at).wait_recv()
            if step < 3:
                @pl.when(z < 3)
                def _():
                    self.up(u, zz, at).start()

            self.side(u, zz, at).start()
            self.got(u, zz, y)

        @pl.when(z + step < 4)
        def _():
            zz = z + step
            at = self.mine(u, zz, y)
            self.down(u, zz, at).wait_recv()
            if step < 3:
                @pl.when(z > 0)
                def _():
                    self.down(u, zz, at).start()

            self.side(u, zz, at).start()
            self.got(u, zz, y)

    def from_side(self, u, step):
        z, yy = self.at.z, 1 - self.at.y

        def take(zz):
            at = self.mine(u, zz, yy)
            move(at, at, self.ysend.at[u, zz], self.yrecv.at[u, zz], self.at.to_y).wait_recv()
            self.got(u, zz, yy)

        if step == 0:
            take(z)
        else:
            @pl.when(z - step >= 0)
            def _():
                take(z - step)

            @pl.when(z + step < 4)
            def _():
                take(z + step)

    def others(self, act):
        for zz in range(4):
            for yy in range(2):
                @pl.when((zz != self.at.z) | (yy != self.at.y))
                def _():
                    act(zz, yy)

    def from_across(self):
        def take(zz, yy):
            at = self.place(0, zz, yy, self.at.core, 1 - self.at.x)
            index = zz * 2 + yy
            move(at, at, self.xsend.at[index], self.xrecv.at[index], self.at.to_x).wait_recv()
            self.twin(1, zz, yy).start()

        self.others(take)

    def end(self):
        z, y = self.at.z, self.at.y

        def take(zz, yy):
            for kind in range(3):
                self.twin_in(kind, zz, yy).wait_recv()
                self.twin(kind, zz, yy).wait_send()
            self.across(zz, yy).wait_send()

        self.others(take)
        for copy in self.locals_():
            copy.wait()
        for u in range(2):
            for zz in range(4):
                at = self.mine(u, zz, y)
                self.side(u, zz, at).wait_send()

                rising = (zz <= z) & (z < 3)
                falling = (zz >= z) & (z > 0)
                if u == 0:
                    rising = (zz == z - 2) & (z < 3)
                    falling = (zz == z + 2) & (z > 0)

                @pl.when(rising)
                def _():
                    self.up(u, zz, at).wait_send()

                @pl.when(falling)
                def _():
                    self.down(u, zz, at).wait_send()


HALF_UP = 1920


def head_twice(values, head):
    wide = values.astype(f32)
    turned = pltpu.roll(wide, 64, 1)
    first = lane_of(values.shape[0]) < 64
    if head == 0:
        return jnp.where(first, wide, turned).astype(bf16)
    return jnp.where(first, turned, wide).astype(bf16)


def head_parts(values, head):
    wide = values.astype(f32) * (SCALE * LOG2E)
    hi = wide.astype(bf16).astype(f32)
    low = wide - hi
    first = lane_of(values.shape[0]) < 64
    if head == 0:
        return jnp.where(first, hi, pltpu.roll(low, 64, 1)).astype(bf16)
    return jnp.where(first, pltpu.roll(hi, 64, 1), low).astype(bf16)


def head_only(values, head):
    first = lane_of(values.shape[0]) < 64
    keep = first if head == 0 else jnp.logical_not(first)
    return jnp.where(keep, values, jnp.zeros_like(values))


def off_diagonal(size, bias):
    row = lax.broadcasted_iota(jnp.int32, (size, size), 0)
    col = lax.broadcasted_iota(jnp.int32, (size, size), 1)
    return jnp.where(row == col, 0.0, bias)


def attend_setup(kb, brow, kx, vx, bown, bcont):
    for head in range(2):
        kx[head, :, 128:] = kb[...]
    vx[:, 128:] = jnp.ones((2560, 128), bf16)
    bown[...] = off_diagonal(512, brow[0:1, 0:512])
    for c in range(2):
        bcont[c] = off_diagonal(256, brow[0:1, 2048 + 256 * c : 2304 + 256 * c])


def attend_fill(q, k, v, qx, kx, vx):
    ones = jnp.where(lane_of(1024) == 0, 1.0, 0.0).astype(bf16)
    vx[:, :128] = v
    for head in range(2):
        qx[head, :, :128] = head_parts(q, head)
        kx[head, :, :128] = head_twice(k, head)
        qx[head, :, 128:] = ones


def own_scores(head, qx, kx, bown):
    return dot(qx[head, :512, :128], kx[head, :512, :128], NT) + bown[...]


def cont_scores(head, c, qx, kx, bcont):
    rows = slice(512 + 256 * c, 768 + 256 * c)
    keys = slice(2048 + 256 * c, 2304 + 256 * c)
    return dot(qx[head, rows, :128], kx[head, keys, :128], NT) + bcont[c]


def attend_head(head, o, side, qx, kx, vx, pm, pc, bown, bcont, top=None):
    def below(scores, rows):
        if top is None:
            return jnp.exp2(scores).astype(bf16)
        return jnp.exp2(scores - top[head, rows, 0:1]).astype(bf16)

    lane = lane_of(256)
    for c in range(3):
        keys = slice(512 + 512 * c, 1024 + 512 * c)
        pm[head, :, keys] = jnp.exp2(dot(qx[head], kx[head, keys], NT)).astype(bf16)
    pm[head, 512:, :512] = jnp.exp2(dot(qx[head, 512:], kx[head, :512], NT)).astype(bf16)
    pm[head, :512, :512] = below(own_scores(head, qx, kx, bown), slice(0, 512))
    for c in range(2):
        rows = slice(512 + 256 * c, 768 + 256 * c)
        pc[head, c] = below(cont_scores(head, c, qx, kx, bcont), rows)
    for r in range(4):
        rows = slice(256 * r, 256 * r + 256)
        total = dot(pm[head, rows], vx[:2048], NN)
        if r >= 2:
            total = total + dot(pc[head, r - 2], vx[1536 + 256 * r : 1792 + 256 * r], NN)
        mass = total[:, 128:]
        value = total[:, :128] / mass
        if head == 0:
            o[rows] = value.astype(bf16)
        else:
            o[rows] = jnp.where(lane < 64, o[rows].astype(f32), value).astype(bf16)
        logs = jnp.log2(mass)
        if top is not None:
            logs = logs + top[head, rows]
        side[head, rows] = side_lanes(1.0, logs)


ROW_STEPS = 5


def near_kernel(
    tok, oth, wq, wk, wv, vecs, kb, brow, *refs, linked
):
    if linked:
        own_parts, refs = refs[:2], refs[3:]
    q, k, v, xt, qn, kn, o, side = refs[:8]
    refs = refs[8:]
    if linked:
        full, refs = refs[:2], refs[2:]
    qs, ks, vs, qx, kx, vx, pm, pc, bown, bcont = refs[:10]
    step = pl.program_id(0)
    spread = Spread(own_parts, full, refs[10:]) if linked else None

    def comm(at, act):
        if linked:
            @pl.when(step == at)
            def _():
                act()

    comm(0, lambda: spread.begin())
    width = wq.shape[0]

    @pl.when(step < ROW_STEPS)
    def _():
        own = (step == 0) | (step == 4)
        row = lax.broadcasted_iota(jnp.int32, (width, 128), 0)
        lane = lax.broadcasted_iota(jnp.int32, (width, 128), 1)
        heads = jnp.where(row // HDIM == lane, 1.0, 0.0).astype(bf16)
        at = pl.ds(pl.multiple_of(step * PPIECE, PPIECE), PPIECE)

        @pl.when(step == 0)
        def _():
            qn[...] = jnp.zeros_like(qn)
            kn[...] = jnp.zeros_like(kn)
            attend_setup(kb, brow, kx, vx, bown, bcont)

        def norms(values):
            wide = values.astype(f32)
            sums = dot((wide * wide).astype(bf16), heads, NN)
            return jnp.broadcast_to(jnp.max(sums, axis=0, keepdims=True), (8, 128))

        def keep(low, out, held, where):
            out[...] = low
            for p in range(width // 128):
                held[p, where] = low[:, 128 * p : 128 * p + 128]

        def keys(rows):
            low = dot(rows, wk[...], NN).astype(bf16)
            keep(low, k, ks, at)
            kn[...] = jnp.maximum(kn[...], norms(low))
            keep((dot(rows, wv[...], NN) + vecs[1:2].astype(f32)).astype(bf16), v, vs, at)
            xt[...] = jnp.transpose(rows)

        @pl.when(own)
        def _():
            rows = tok[...]
            keys(rows)
            low = (dot(rows, wq[...], NN) + vecs[0:1].astype(f32)).astype(bf16)
            keep(low, q, qs, pl.ds(pl.multiple_of(step // 4 * PPIECE, PPIECE), PPIECE))
            qn[...] = jnp.maximum(qn[...], norms(low))

        @pl.when(jnp.logical_not(own))
        def _():
            keys(oth[...])

    comm(4, lambda: (spread.hop(0, 3), spread.hop(1, 1)))

    @pl.when(step >= ROW_STEPS)
    def _():
        p = step - ROW_STEPS
        attend_fill(qs[p], ks[p], vs[p], qx, kx, vx)
        attend_head(0, o, side, qx, kx, vx, pm, pc, bown, bcont)

    comm(5, lambda: [spread.from_side(0, j) for j in range(3)])
    comm(6, lambda: spread.hop(1, 2))
    comm(7, lambda: (spread.from_side(1, 0), spread.from_side(0, 3)))
    comm(9, lambda: spread.from_side(1, 1))
    comm(10, lambda: spread.from_side(1, 2))

    @pl.when(step >= ROW_STEPS)
    def _():
        attend_head(1, o, side, qx, kx, vx, pm, pc, bown, bcont)

    comm(7, lambda: spread.hop(1, 3))
    comm(8, lambda: spread.from_across())
    comm(10, lambda: (spread.from_side(1, 3), spread.end()))


def attend_near(tok, oth, wq, wk, wv, vecs, kb, brow, own_parts):
    width = tok.shape[1]
    linked = bool(own_parts)
    pairs = width // 128
    block = (PPIECE, width)

    def once(*shape):
        return pl.BlockSpec(shape, lambda i: (0,) * len(shape), pipeline_mode=pl.Buffered(1))

    def rows_at(i):
        return jnp.minimum(i, ROW_STEPS - 1)

    def pair_at(i):
        return jnp.maximum(i - ROW_STEPS, 0)

    small = pl.BlockSpec((8, 128), lambda i: (0, 0))
    extra_shape, extra_sems, more = [], [], {}
    if linked:
        sem = pltpu.SemaphoreType.DMA
        extra_shape = [
            jax.ShapeDtypeStruct((16, 48, own_parts[0].shape[2]), bf16),
            jax.ShapeDtypeStruct((16, 192, width), bf16),
        ]
        extra_sems = [
            sem((2,)), sem((2, 4)), sem((2, 4)), sem((2, 4)), sem((2, 4)), sem((2, 4)),
            sem((8,)), sem((8,)), sem((3, 8)), sem((3, 8)),
        ]
        more = {"collective_id": 3, "has_side_effects": True}
    return pl.pallas_call(
        functools.partial(near_kernel, linked=linked),
        grid=(ROW_STEPS + pairs,),
        in_specs=[
            pl.BlockSpec(block, lambda i: (rows_at(i) // 4, 0)),
            pl.BlockSpec(block, lambda i: (jnp.clip(i - 1, 0, 2), 0)),
            once(width, width), once(width, width), once(width, width),
            once(8, width), once(2560, 128), once(8, 2560),
        ] + [ANY] * len(own_parts),
        out_specs=[
            pl.BlockSpec(block, lambda i: (rows_at(i) // 4, 0)),
            pl.BlockSpec(block, lambda i: (rows_at(i), 0)),
            pl.BlockSpec(block, lambda i: (rows_at(i), 0)),
            pl.BlockSpec((width, PPIECE), lambda i: (0, rows_at(i))),
            small, small,
            pl.BlockSpec((1024, 128), lambda i: (0, pair_at(i))),
            pl.BlockSpec((2, 1024, 128), lambda i: (pair_at(i), 0, 0)),
        ] + [ANY] * len(extra_shape),
        out_shape=[
            jax.ShapeDtypeStruct((1024, width), bf16),
            jax.ShapeDtypeStruct((2560, width), bf16),
            jax.ShapeDtypeStruct((2560, width), bf16),
            jax.ShapeDtypeStruct((width, 2560), bf16),
            jax.ShapeDtypeStruct((8, 128), f32),
            jax.ShapeDtypeStruct((8, 128), f32),
            jax.ShapeDtypeStruct((1024, width), bf16),
            jax.ShapeDtypeStruct((2 * pairs, 1024, 128), bf16),
        ] + extra_shape,
        scratch_shapes=[
            pltpu.VMEM((pairs, 1024, 128), bf16),
            pltpu.VMEM((pairs, 2560, 128), bf16),
            pltpu.VMEM((pairs, 2560, 128), bf16),
            pltpu.VMEM((2, 1024, 256), bf16),
            pltpu.VMEM((2, 2560, 256), bf16),
            pltpu.VMEM((2560, 256), bf16),
            pltpu.VMEM((2, 1024, 2048), bf16),
            pltpu.VMEM((2, 2, 256, 256), bf16),
            pltpu.VMEM((512, 512), f32),
            pltpu.VMEM((2, 256, 256), f32),
        ] + extra_sems,
        input_output_aliases={10: 8} if linked else {},
        compiler_params=params(60, **more),
        cost_estimate=cost(50, 50),
    )(tok, oth, wq, wk, wv, vecs, kb, brow, *own_parts)


def far_kernel(
    q, k, v, kb, brow, qn, kn, o_in, side_in, o_out, side_out,
    qs, ks, vs, o, side, qx, kx, vx, pm, pc, bown, bcont, top, sems,
):
    pair = pl.program_id(0)
    widest_product = jnp.max(qn[...] * kn[...]) * ((SCALE * LOG2E) ** 2 * 1.1)

    @pl.when(widest_product > LIMIT * LIMIT)
    def _():
        at = pl.ds(pl.multiple_of(pair * 128, 128), 128)
        copies = [
            pltpu.make_async_copy(ref.at[:, at], held, sems.at[i])
            for i, (ref, held) in enumerate(((q, qs), (k, ks), (v, vs)))
        ]
        for copy in copies:
            copy.start()
        for copy in copies:
            copy.wait()
        attend_setup(kb, brow, kx, vx, bown, bcont)
        attend_fill(qs[...], ks[...], vs[...], qx, kx, vx)

        def widest(scores):
            return jnp.broadcast_to(
                jnp.max(scores, axis=1, keepdims=True), (scores.shape[0], 128)
            )

        for head in range(2):
            def more(c, carry):
                found = widest(dot(qx[head], kx[head, pl.ds(512 + c * 256, 256)], NT))
                top[head] = jnp.maximum(top[head], found)
                return carry

            top[head] = jnp.full((1024, 128), -3e38, f32)
            lax.fori_loop(0, 6, more, 0)
            top[head, 0:512] = jnp.maximum(
                top[head, 0:512], widest(own_scores(head, qx, kx, bown))
            )
            top[head, 512:1024] = jnp.maximum(
                top[head, 512:1024], widest(dot(qx[head, 512:], kx[head, :512], NT))
            )
            for c in range(2):
                rows = slice(512 + 256 * c, 768 + 256 * c)
                top[head, rows] = jnp.maximum(
                    top[head, rows], widest(cont_scores(head, c, qx, kx, bcont))
                )
            qx[head, :, 128:] = side_lanes(1.0, top[head])
            attend_head(head, o, side, qx, kx, vx, pm, pc, bown, bcont, top)
        copies = [
            pltpu.make_async_copy(o, o_out.at[:, at], sems.at[0]),
            pltpu.make_async_copy(side, side_out.at[pl.ds(pair * 2, 2)], sems.at[1]),
        ]
        for copy in copies:
            copy.start()
        for copy in copies:
            copy.wait()


def attend_far(q, k, v, kb, brow, qn, kn, o, side):
    def fixed(*shape):
        return pl.BlockSpec(shape, lambda i: (0,) * len(shape), pipeline_mode=pl.Buffered(1))

    return pl.pallas_call(
        far_kernel,
        grid=(q.shape[1] // 128,),
        in_specs=[
            ANY, ANY, ANY, fixed(2560, 128), fixed(8, 2560), fixed(8, 128), fixed(8, 128),
            ANY, ANY,
        ],
        out_specs=[ANY, ANY],
        out_shape=[
            jax.ShapeDtypeStruct(o.shape, bf16), jax.ShapeDtypeStruct(side.shape, bf16),
        ],
        scratch_shapes=[
            pltpu.VMEM((1024, 128), bf16),
            pltpu.VMEM((2560, 128), bf16),
            pltpu.VMEM((2560, 128), bf16),
            pltpu.VMEM((1024, 128), bf16),
            pltpu.VMEM((2, 1024, 128), bf16),
            pltpu.VMEM((2, 1024, 256), bf16),
            pltpu.VMEM((2, 2560, 256), bf16),
            pltpu.VMEM((2560, 256), bf16),
            pltpu.VMEM((2, 1024, 2048), bf16),
            pltpu.VMEM((2, 2, 256, 256), bf16),
            pltpu.VMEM((512, 512), f32),
            pltpu.VMEM((2, 256, 256), f32),
            pltpu.VMEM((2, 1024, 128), f32),
            pltpu.SemaphoreType.DMA((3,)),
        ],
        input_output_aliases={7: 0, 8: 1},
        compiler_params=params(),
        cost_estimate=cost(0.1, 1),
    )(q, k, v, kb, brow, qn, kn, o, side)


def back_fill(q, k, v, d, o, side, kb, qx, qd, kx, vx, dx, qm, kt, bown, bcont):
    @pl.when(pl.program_id(0) == 0)
    def _():
        for head in range(2):
            kx[head, :, 128:] = kb[...]
        vx[:, 128:] = kb[...]
        column = kb[:, 0:1].astype(f32)
        bown[...] = off_diagonal(512, column[:512]).astype(bf16)
        for c in range(2):
            keys = slice(2048 + 256 * c, 2304 + 256 * c)
            bcont[c] = off_diagonal(256, column[keys]).astype(bf16)

    lane = lane_of(1024)
    vx[:, :128] = v[...]
    kt[...] = jnp.transpose(k[...].astype(f32)).astype(bf16)
    product = d[...].astype(f32) * o[...].astype(f32)
    for head in range(2):
        parts = head_parts(q[...], head)
        qx[head, :, :128] = parts
        qd[head, :, :128] = parts
        tail = side[head]
        qx[head, :, 128:] = tail
        qd[head, :, 128:] = jnp.where(lane == 0, jnp.zeros_like(tail), tail)
        kx[head, :, :128] = head_twice(k[...], head)
        qm[head] = head_only(q[...], head)
        dx[head, :, :128] = head_only(d[...], head)
        inner = jnp.sum(head_only(product, head), axis=1, keepdims=True)
        dx[head, :, 128:] = side_lanes(0.0, jnp.broadcast_to(inner, (1024, 128)))


def back_head(head, qx, qd, kx, vx, dx, qm, kt, pt, st, pc, sc, bown, bcont):
    def tile(keys, rows, queries, bias=None):
        scores = dot(kx[head, keys], queries[head, rows], NT)
        if bias is not None:
            scores = scores + bias.astype(f32)
        probs = jnp.exp2(scores)
        return probs.astype(bf16), (probs * dot(vx[keys], dx[head, rows], NT)).astype(bf16)

    for c in range(3):
        keys = slice(512 + 512 * c, 1024 + 512 * c)
        pt[keys], st[keys] = tile(keys, slice(0, 1024), qx)
    pt[:512, 512:], st[:512, 512:] = tile(slice(0, 512), slice(512, 1024), qx)
    pt[:512, :512], st[:512, :512] = tile(slice(0, 512), slice(0, 512), qd, bown[...])
    for c in range(2):
        keys = slice(2048 + 256 * c, 2304 + 256 * c)
        pc[c], sc[c] = tile(keys, slice(512 + 256 * c, 768 + 256 * c), qd, bcont[c])
    kth = kt[64 * head : 64 * head + 64]
    main = dot(kth[:, :2048], st[...], NN)
    extra = [dot(kth[:, 2048 + 256 * c : 2304 + 256 * c], sc[c], NN) for c in range(2)]
    rows = jnp.concatenate(
        [main[:, :512], main[:, 512:768] + extra[0], main[:, 768:] + extra[1]], axis=1
    )
    return rows


def back_keys(head, dx, qm, pt, st, pc, sc, acc):
    def put(keys, cols, value):
        if head == 0:
            acc[keys, cols] = value
        else:
            acc[keys, cols] += value

    left, right = slice(0, 128), slice(128, 256)
    for c in range(4):
        keys = slice(512 * c, 512 * c + 512)
        put(keys, left, dot(st[keys], qm[head], NN) * SCALE)
        put(keys, right, dot(pt[keys], dx[head, :, :128], NN))
    for c in range(2):
        keys = slice(2048 + 256 * c, 2304 + 256 * c)
        rows = slice(512 + 256 * c, 768 + 256 * c)
        put(keys, left, dot(sc[c], qm[head, rows], NN) * SCALE)
        put(keys, right, dot(pc[c], dx[head, rows, :128], NN))


BACK_SCRATCH = [
    pltpu.VMEM((2, 1024, 256), bf16),
    pltpu.VMEM((2, 1024, 256), bf16),
    pltpu.VMEM((2, 2560, 256), bf16),
    pltpu.VMEM((2560, 256), bf16),
    pltpu.VMEM((2, 1024, 256), bf16),
    pltpu.VMEM((2, 1024, 128), bf16),
    pltpu.VMEM((128, 2560), bf16),
    pltpu.VMEM((2048, 1024), bf16),
    pltpu.VMEM((2048, 1024), bf16),
    pltpu.VMEM((2, 256, 256), bf16),
    pltpu.VMEM((2, 256, 256), bf16),
    pltpu.VMEM((512, 512), bf16),
    pltpu.VMEM((2, 256, 256), bf16),
    pltpu.VMEM((2560, 256), f32),
]


def back_specs():
    def pair(rows):
        return pl.BlockSpec((rows, 128), lambda i: (0, i))

    def once(*shape):
        return pl.BlockSpec(shape, lambda i: (0,) * len(shape), pipeline_mode=pl.Buffered(1))

    return [
        pair(1024), pair(2560), pair(2560), pair(1024), pair(1024),
        pl.BlockSpec((2, 1024, 128), lambda i: (i, 0, 0)),
        once(2560, 128), once(768, 2560),
    ]


def back_alone_kernel(q, k, v, d, o, side, kb, xt, dq, cont, partial_rows, whole, *scratch):
    (qx, qd, kx, vx, dx, qm, kt, pt, st, pc, sc, bown, bcont, acc) = scratch
    back_fill(q, k, v, d, o, side, kb, qx, qd, kx, vx, dx, qm, kt, bown, bcont)
    rows = []
    for head in range(2):
        rows.append(back_head(head, qx, qd, kx, vx, dx, qm, kt, pt, st, pc, sc, bown, bcont))
        back_keys(head, dx, qm, pt, st, pc, sc, acc)
    delta = jnp.transpose(jnp.concatenate(rows, axis=0) * SCALE).astype(bf16)
    dq[...] = delta
    low = acc[...].astype(bf16)
    partial_rows[...] = low[:2048]
    cont[...] = low[2048:]
    grad = dot(xt[:, :512], delta[:512], NN) + dot(xt[:, 2048:], delta[512:], NN)
    whole[:, :128] = grad.astype(bf16)
    whole[:, 128:] = dot(xt[...], low, NN).astype(bf16)


def attend_back_alone(q, k, v, d, o, side, kb, xt):
    width = q.shape[1]
    count = width // 128
    return pl.pallas_call(
        back_alone_kernel,
        grid=(count,),
        in_specs=back_specs(),
        out_specs=[
            pl.BlockSpec((1024, 128), lambda i: (0, i)),
            pl.BlockSpec((512, 256), lambda i: (0, i)),
            pl.BlockSpec((2048, 256), lambda i: (0, i)),
            pl.BlockSpec((width, 384), lambda i: (0, i)),
        ],
        out_shape=[
            jax.ShapeDtypeStruct((1024, width), bf16),
            jax.ShapeDtypeStruct((512, 2 * width), bf16),
            jax.ShapeDtypeStruct((2048, 2 * width), bf16),
            jax.ShapeDtypeStruct((width, 3 * width), bf16),
        ],
        scratch_shapes=BACK_SCRATCH,
        compiler_params=params(60),
        cost_estimate=cost(100, 40),
    )(q, k, v, d, o, side, kb, xt)


PAIRS = 6
A_X = 2
B_Y = 2
AB_COPIES = 15
PAIR_COPIES = 11


def back_linked_kernel(
    q, k, v, d, o, side, kb, xt, xa, xb, wq, wk, wv, adel,
    token_grad, gq, gk, gv, qrow, ga, gb,
    qx, qd, kx, vx, dx, qm, kt, pt, st, pc, sc, bown, bcont, acc,
    a_mine, a_x, a_y, a_z, a_q, b_mine, b_y, b_z, b_r,
    p_mine, p_other, c_in, y_in, z_in, r_in, keys_low, k_in, k_far, k_x, dw,
    dq, cont_k, cont_v, own_k, own_v, wsem, lsem, ab_send, ab_recv, p_send, p_recv,
):
    step = pl.program_id(0)
    rep = lax.axis_index("rep")
    shard = lax.axis_index("shard")
    core = rep % 2
    x = rep // 2
    z = shard // 2
    y = shard % 2
    rep1 = rep + 1 - 2 * core
    to_rep = [None, {"rep": rep1}, {"rep": (rep + 2) % 4}, {"rep": (rep1 + 2) % 4}]
    to_y = {"shard": z * 2 + 1 - y}
    zs = [z, z + 1 - 2 * (z % 2), (z + 2) % 4, 3 - z]
    to_z = [None] + [{"shard": zs[j] * 2 + y} for j in range(1, 4)]

    def move(src, dst, send, recv, where):
        return pltpu.make_async_remote_copy(
            src_ref=src, dst_ref=dst, send_sem=send, recv_sem=recv,
            device_id=where, device_id_type=MESH,
        )

    def ab(index, src, dst, where):
        return move(src, dst, ab_send.at[index], ab_recv.at[index], where)

    def columns(which):
        return pl.ds(pl.multiple_of(which * HALF_UP, 128), HALF_UP)

    def copy_ax():
        return ab(0, xa.at[:, :, columns(1 - x)], a_x, to_rep[2])

    def copy_ay():
        return ab(1, a_mine.at[pl.ds(4, 4)], a_y, to_y)

    def copy_az(j):
        return ab(1 + j, a_mine.at[j], a_z.at[j - 1], to_z[j])

    def copy_aq(j):
        src = a_q.at[1] if j == 3 else a_q.at[0]
        return ab(4 + j, src, a_q.at[j], to_rep[2 if j == 1 else 1])

    def copy_by():
        return ab(8, xb.at[pl.ds(4, 4)], b_y, to_y)

    def copy_bz(j):
        return ab(8 + j, b_mine.at[j], b_z.at[j - 1], to_z[j])

    def copy_br(j):
        return ab(12 + j, b_r.at[2 * j], b_r.at[2 * j + 1], to_rep[2 - j])

    def pair_copy(p, index, src, dst, where):
        return move(src, dst, p_send.at[p, index], p_recv.at[p, index], where)

    def copy_core(p):
        return pair_copy(p, 0, p_other, c_in.at[p % 2], to_rep[1])

    def copy_y(p):
        return pair_copy(p, 1, p_mine.at[p % 3, pl.ds(4, 4)], y_in.at[p % 2], to_y)

    def copy_z(p, j):
        return pair_copy(p, 1 + j, p_mine.at[p % 3, j], z_in.at[p % 2, j - 1], to_z[j])

    def copy_rep(p, j):
        return pair_copy(
            p, 5 + j, r_in.at[p % 2, 2 * j], r_in.at[p % 2, 2 * j + 1], to_rep[2 - j]
        )

    def copy_near(p):
        return pair_copy(p, 8, keys_low.at[p % 2, pl.ds(512, 512)], k_in.at[p % 2], to_rep[1])

    def copy_far(p):
        return pair_copy(p, 9, keys_low.at[p % 2, pl.ds(1536, 512)], k_far.at[p % 2], to_rep[1])

    def copy_turn(p):
        return pair_copy(p, 10, keys_low.at[p % 2, pl.ds(1024, 512)], k_x.at[p % 2], to_rep[2])

    def after_core(p):
        slot = p % 2
        copy_core(p).wait()
        for i in range(8):
            p_mine[p % 3, i] = p_mine[p % 3, i] + c_in[slot, i]
        copy_y(p).start()
        copy_near(p).wait()
        copy_far(p).wait()
        keys_low[slot, 1024:1536] = keys_low[slot, 1024:1536] + k_far[slot]
        copy_turn(p).start()
        keys_low[slot, :512] = keys_low[slot, :512] + k_in[slot]

    def after_y(p):
        copy_y(p).wait()
        for i in range(4):
            p_mine[p % 3, i] = p_mine[p % 3, i] + y_in[p % 2, i]
        for j in range(1, 4):
            copy_z(p, j).start()

    def own_keys(p):
        slot = p % 2
        copy_turn(p).wait()
        total = keys_low[slot, :512] + k_x[slot]
        at = pl.ds(pl.multiple_of(p * 128, 128), 128)
        own_k[:, at] = total[:, :128]
        own_v[:, at] = total[:, 128:]

    def after_z(p):
        slot = p % 2
        for j in range(1, 4):
            copy_z(p, j).wait()
        total = p_mine[p % 3, 0].astype(f32)
        for j in range(3):
            total = total + z_in[slot, j].astype(f32)
        r_in[slot, 0] = total.astype(bf16)
        copy_rep(p, 0).start()

    def after_x(p):
        slot = p % 2
        copy_rep(p, 0).wait()
        r_in[slot, 2] = r_in[slot, 0] + r_in[slot, 1]
        copy_rep(p, 1).start()

    def after_twin(p):
        slot = p % 2
        copy_rep(p, 1).wait()
        at = pl.ds(pl.multiple_of(p * 128, 128), 128)
        for half in range(2):
            total = r_in[slot, 2 + half]
            rows = core if half == 0 else 1 - core
            rows = pl.ds(pl.multiple_of(rows * 48, 16), 48)
            for j, out in enumerate((gq, gk, gv)):
                out[rows, at] = total[:48, 128 * j : 128 * j + 128]
            if half == 0:
                qrow[:, at] = total[48:64, :128]

    stages = (
        (5, after_twin), (4, after_x), (3, after_z), (2, after_y), (2, own_keys), (1, after_core),
    )

    def sum_pieces(total, more, count):
        def sum_piece(i, carry):
            total[i] = total[i] + more[i]
            return carry

        lax.fori_loop(0, count, sum_piece, 0)

    def sum_four(first, rest, out):
        total = first[0].astype(f32)
        for j in range(3):
            total = total + rest[j].astype(f32)
        out[0] = total.astype(bf16)

    @pl.when(step == 0)
    def _():
        barrier = pltpu.get_barrier_semaphore()
        for place in to_rep[1:] + [to_y] + to_z[1:]:
            pl.semaphore_signal(barrier, inc=1, device_id=place, device_id_type=MESH)
        pl.semaphore_wait(barrier, 7)
        copy_by().start()
        copy_ax().start()
        for copy in (
            pltpu.make_async_copy(xa.at[:, :, columns(x)], a_mine, lsem.at[0]),
            pltpu.make_async_copy(xb.at[pl.ds(0, 4)], b_mine, lsem.at[1]),
        ):
            copy.start()

    back_fill(q, k, v, d, o, side, kb, qx, qd, kx, vx, dx, qm, kt, bown, bcont)
    turned = []
    turned.append(back_head(0, qx, qd, kx, vx, dx, qm, kt, pt, st, pc, sc, bown, bcont))
    back_keys(0, dx, qm, pt, st, pc, sc, acc)

    for back, stage in stages:
        @pl.when(step >= back)
        def _():
            stage(step - back)

    @pl.when(step == 4)
    def _():
        copy_ay().wait()
        sum_pieces(a_mine, a_y, 4)
        for j in range(1, 4):
            copy_az(j).start()

    turned.append(back_head(1, qx, qd, kx, vx, dx, qm, kt, pt, st, pc, sc, bown, bcont))
    back_keys(1, dx, qm, pt, st, pc, sc, acc)

    @pl.when(step == A_X)
    def _():
        copy_ax().wait()
        pltpu.make_async_copy(xa.at[:, :, columns(x)], a_mine, lsem.at[0]).wait()
        sum_pieces(a_mine, a_x, 8)
        copy_ay().start()

    @pl.when(step == B_Y)
    def _():
        copy_by().wait()
        pltpu.make_async_copy(xb.at[pl.ds(0, 4)], b_mine, lsem.at[1]).wait()
        sum_pieces(b_mine, b_y, 4)
        for j in range(1, 4):
            copy_bz(j).start()

    @pl.when(step == 4)
    def _():
        for j in range(1, 4):
            copy_bz(j).wait()
        sum_four(b_mine, b_z, b_r)
        copy_br(0).start()

    def loads():
        wide = pl.ds(0, 768)
        return [
            pltpu.make_async_copy(wq, pt.at[pl.ds(0, 768), wide], wsem.at[0]),
            pltpu.make_async_copy(wk, pt.at[pl.ds(1024, 768), wide], wsem.at[1]),
            pltpu.make_async_copy(wv, st.at[pl.ds(0, 768), wide], wsem.at[2]),
            pltpu.make_async_copy(adel, st.at[pl.ds(1024, 1024), wide], wsem.at[3]),
        ]

    def results(half):
        rows = pl.ds(512 * half, 512)
        return pltpu.make_async_copy(dq.at[rows], token_grad.at[rows], wsem.at[4 + half])

    def tokens_half(half):
        rows = slice(512 * half, 512 * half + 512)
        far_rows = slice(1024 + 512 * half, 1536 + 512 * half)
        total = st[far_rows, :768].astype(f32) + dot(dq[rows], pt[:768, :768], NT)
        total = total + dot((own_k if half == 0 else cont_k)[...], pt[1024:1792, :768], NT)
        total = total + dot((own_v if half == 0 else cont_v)[...], st[:768, :768], NT)
        dq[rows] = total.astype(bf16)
        results(half).start()

    @pl.when(step == PAIRS - 1)
    def _():
        for load in loads():
            load.start()

    delta = jnp.transpose(jnp.concatenate(turned, axis=0) * SCALE)
    low = delta.astype(bf16)
    pair_at = pl.ds(pl.multiple_of(step * 128, 128), 128)
    dq[:, pair_at] = low
    slot = step % 2
    keys_low[slot] = acc[:2048].astype(bf16)
    tail = acc[2048:].astype(bf16)
    cont_k[:, pair_at] = tail[:, :128]
    cont_v[:, pair_at] = tail[:, 128:]
    copy_near(step).start()
    copy_far(step).start()
    grad = dot(xt[:, :512], low[:512], NN) + dot(xt[:, 2048:], low[512:], NN)
    dw[:, :128] = grad.astype(bf16)
    dw[:, 128:] = (dot(xt[:, :2048], keys_low[slot], NN) + dot(xt[:, 2048:], tail, NN)).astype(bf16)
    extra = jnp.sum(low.astype(f32), axis=0, keepdims=True)
    extra = jnp.concatenate([jnp.broadcast_to(extra, (16, 128)), jnp.zeros((16, 256), f32)], axis=1)
    extra = extra.astype(bf16)
    for i in range(8):
        place = (zs[i % 4] * 2 + (y if i < 4 else 1 - y)) * 2
        at = pl.multiple_of((place + core) * 48, 16)
        p_mine[step % 3, i, :48] = dw[pl.ds(at, 48)]
        p_mine[step % 3, i, 48:] = extra
        at = pl.multiple_of((place + 1 - core) * 48, 16)
        p_other[i, :48] = dw[pl.ds(at, 48)]
        p_other[i, 48:] = extra
    copy_core(step).start()

    @pl.when(step == PAIRS - 1)
    def _():
        def late(at):
            for back, stage in stages:
                if 0 <= at - back < PAIRS:
                    stage(at - back)

        late(PAIRS)
        for load in loads():
            load.wait()
        tokens_half(1)
        copy_br(0).wait()
        b_r[2] = b_r[0] + b_r[1]
        copy_br(1).start()
        late(PAIRS + 1)
        for j in range(1, 4):
            copy_az(j).wait()
        sum_four(a_mine, a_z, a_q)
        copy_aq(1).start()
        copy_aq(2).start()
        tokens_half(0)
        late(PAIRS + 2)
        copy_aq(1).wait()
        copy_aq(3).start()
        copy_br(1).wait()
        gb[core] = b_r[2]
        gb[1 - core] = b_r[3]
        late(PAIRS + 3)
        copy_aq(2).wait()
        copy_aq(3).wait()
        for j, (rows, which) in enumerate(
            ((core, x), (core, 1 - x), (1 - core, x), (1 - core, 1 - x))
        ):
            rows = pl.ds(pl.multiple_of(rows * 48, 16), 48)
            ga[rows, columns(which)] = a_q[j]
        late(PAIRS + 4)
        for half in range(2):
            results(half).wait()


def attend_back(q, k, v, d, o, side, kb, xt, xa, xb, wq, wk, wv, adel):
    width = q.shape[1]
    count = width // 128
    full = xa.shape[2]

    def held(*shape):
        return pl.BlockSpec(shape, lambda i: (0,) * len(shape), pipeline_mode=pl.Buffered(1))

    def vm(*shape):
        return pltpu.VMEM(shape, bf16)

    def out(*shape):
        return jax.ShapeDtypeStruct(shape, bf16)

    sem = pltpu.SemaphoreType.DMA
    piece = (64, 384)
    return pl.pallas_call(
        back_linked_kernel,
        grid=(count,),
        in_specs=back_specs() + [ANY] * 6,
        out_specs=[
            ANY, held(96, width), held(96, width), held(96, width),
            held(16, width), held(96, full), held(2, 208, width),
        ],
        out_shape=[
            out(1024, width), out(96, width), out(96, width), out(96, width),
            out(16, width), out(96, full), out(2, 208, width),
        ],
        scratch_shapes=BACK_SCRATCH
        + [
            vm(8, 48, HALF_UP), vm(8, 48, HALF_UP), vm(4, 48, HALF_UP), vm(3, 48, HALF_UP),
            vm(4, 48, HALF_UP), vm(4, 208, width), vm(4, 208, width), vm(3, 208, width),
            vm(4, 208, width),
            vm(3, 8, *piece), vm(8, *piece), vm(2, 8, *piece), vm(2, 4, *piece),
            vm(2, 3, *piece), vm(2, 4, *piece), vm(2, 2048, 256), vm(2, 512, 256),
            vm(2, 512, 256), vm(2, 512, 256), vm(width, 384),
            vm(1024, width), vm(512, width), vm(512, width), vm(512, width), vm(512, width),
            sem((6,)), sem((2,)), sem((AB_COPIES,)), sem((AB_COPIES,)), sem((PAIRS, PAIR_COPIES)),
            sem((PAIRS, PAIR_COPIES)),
        ],
        compiler_params=params(62, collective_id=2, has_side_effects=True),
        cost_estimate=cost(100, 40),
    )(q, k, v, d, o, side, kb, xt, xa, xb, wq, wk, wv, adel)


def gelu_parts(x):
    bell = jnp.exp2(x * x * (-0.5 * LOG2E))
    t = 1.0 / (1.0 + (0.3275911 * 0.7071067811865476) * jnp.abs(x))
    poly = 0.5 * 1.061405429
    for term in (-1.453152027, 1.421413741, -0.284496736, 0.254829592):
        poly = poly * t + 0.5 * term
    below = poly * t * bell
    phi = jnp.where(x >= 0.0, 1.0 - below, below)
    return x * phi, phi + x * bell * 0.3989422804014327


def normed_of(values):
    centered = values - jnp.mean(values, axis=-1, keepdims=True)
    spread = lax.rsqrt(jnp.mean(centered * centered, axis=-1, keepdims=True) + EPSILON)
    return centered * spread, spread


def norm_back(incoming, normed, spread, gain):
    scaled = incoming * gain
    centered = scaled - jnp.mean(scaled, axis=-1, keepdims=True)
    return (centered - normed * jnp.mean(scaled * normed, axis=-1, keepdims=True)) * spread


FCH = 768


def forward_back_kernel(
    mixed, tok, cot, teach, keep, scale, vecs, upb, up_full, down_full,
    result, hid_o, act_o, ddel_o, udel_o, adel_o, mdel_o, sums,
    wa_pieces, wu_pieces, wd_pieces, slope, sems,
):
    step = pl.program_id(0)
    width = tok.shape[1]
    hidden_units = upb.shape[1]

    loads = [
        pltpu.make_async_copy(up_full.at[:, :, pl.ds(0, width)], wa_pieces, sems.at[0]),
        pltpu.make_async_copy(up_full.at[:, :, pl.ds(width, hidden_units)], wu_pieces, sems.at[1]),
        pltpu.make_async_copy(down_full, wd_pieces, sems.at[2]),
    ]

    @pl.when(step == 0)
    def _():
        for load in loads:
            load.start()
        sums[...] = jnp.zeros_like(sums)
        for load in loads:
            load.wait()

    wa = wa_pieces.reshape(width, width)
    wu = wu_pieces.reshape(width, hidden_units)
    wd = wd_pieces.reshape(hidden_units, width)

    def vector(index):
        return vecs[index : index + 1].astype(f32)

    attn_b, gain1, shift1, down_b, gain2, shift2 = [vector(i) for i in range(2, 8)]

    def add_sum(index, values):
        sums[index : index + 1] += jnp.sum(values, axis=0, keepdims=True)

    x = tok[...].astype(f32)
    branch = attn_b + x + dot(mixed[...], wa[...], NN)
    normed1, inv1 = normed_of(branch)
    hidden = normed1 * gain1 + shift1
    hid_low = hidden.astype(bf16)
    hid_o[...] = hid_low
    for c in range(hidden_units // FCH):
        cols = slice(c * FCH, c * FCH + FCH)
        value, rise = gelu_parts(dot(hid_low, wu[:, cols], NN) + upb[:, cols].astype(f32))
        act_o[:, cols] = value.astype(bf16)
        slope[:, cols] = rise.astype(bf16)
    second = hidden + dot(act_o[...], wd[...], NN) + down_b
    normed2, inv2 = normed_of(second)
    final = normed2 * gain2 + shift2
    result[...] = final.astype(bf16)
    errors = final - teach[...].astype(f32)
    kept = errors * jnp.concatenate([keep[...]] * (width // 128), axis=1)
    add_sum(6, kept * errors)
    grad = cot[...].astype(f32) + kept * (2.0 * scale[...])
    add_sum(1, grad * normed2)
    add_sum(2, grad)
    grad2 = norm_back(grad, normed2, inv2, gain2)
    ddel = grad2.astype(bf16)
    ddel_o[...] = ddel
    add_sum(0, ddel.astype(f32))
    for c in range(hidden_units // FCH):
        cols = slice(c * FCH, c * FCH + FCH)
        delta = dot(ddel, wd[cols], NT) * slope[:, cols].astype(f32)
        low = delta.astype(bf16)
        udel_o[:, cols] = low
        add_sum(8 + c, low.astype(f32))
    hgrad = grad2 + dot(udel_o[...], wu[...], NT)
    add_sum(4, hgrad * normed1)
    add_sum(5, hgrad)
    grad1 = norm_back(hgrad, normed1, inv1, gain1)
    adel = grad1.astype(bf16)
    adel_o[...] = adel
    add_sum(3, adel.astype(f32))
    mdel = dot(adel, wa[...], NT).astype(bf16)
    mdel_o[...] = mdel
    add_sum(7, mdel.astype(f32))


def forward_back(mixed, tok, cot, teach, keep, scale, vecs, upb, up_full, down_full):
    rows, width = tok.shape
    hidden_units = upb.shape[1]
    half = 512

    def block(columns):
        return pl.BlockSpec((half, columns), lambda i, *_: (i, 0))

    def fixed(*shape):
        return pl.BlockSpec(shape, lambda i, *_: (0,) * len(shape))

    def out(columns):
        return jax.ShapeDtypeStruct((rows, columns), bf16)

    return pl.pallas_call(
        forward_back_kernel,
        grid=(rows // half,),
        in_specs=[
            block(width), block(width), block(width), block(width),
            block(128), fixed(1, 1), fixed(8, width), fixed(1, hidden_units), ANY, ANY,
        ],
        out_specs=[
            block(width), block(width), block(hidden_units), block(width),
            block(hidden_units), block(width), block(width), fixed(16, width),
        ],
        scratch_shapes=[
            pltpu.VMEM((16, width // 16, width), bf16),
            pltpu.VMEM((16, width // 16, hidden_units), bf16),
            pltpu.VMEM((16, hidden_units // 16, width), bf16),
            pltpu.VMEM((half, hidden_units), bf16),
            pltpu.SemaphoreType.DMA((3,)),
        ],
        out_shape=[
            out(width), out(width), out(hidden_units), out(width), out(hidden_units),
            out(width), out(width), jax.ShapeDtypeStruct((16, width), f32),
        ],
        compiler_params=params(60),
        cost_estimate=cost(32.6, 30),
    )(mixed, tok, cot, teach, keep, scale, vecs, upb, up_full, down_full)


def up_grad_kernel(order, mixed, adel, hid, udel, mine, other, whole):
    step = pl.program_id(0)

    @pl.when(step == 0)
    def _():
        whole[...] = dot(mixed[...], adel[...], TN).astype(bf16)

    @pl.when(step > 0)
    def _():
        whole[...] = dot(hid[...], udel[...], TN).astype(bf16)

    store_pieces(order, whole, mine, other, 48)


def store_pieces(order, source, mine, other, piece):
    for i in range(8):
        at = pl.multiple_of(order[i] * piece, 16)
        mine[i, :piece] = source[pl.ds(at, piece)]
        at = pl.multiple_of(order[i + 8] * piece, 16)
        other[i, :piece] = source[pl.ds(at, piece)]


def up_grad(order, mixed, adel, hid, udel):
    rows, width = adel.shape
    columns = udel.shape[1]
    shape = jax.ShapeDtypeStruct((8, 48, width + columns), bf16)
    out = pl.BlockSpec((8, 48, width), lambda i, *_: (0, 0, i))
    full = pl.BlockSpec((rows, width), lambda i, *_: (0, 0))
    return pl.pallas_call(
        up_grad_kernel,
        grid_spec=pltpu.PrefetchScalarGridSpec(
            num_scalar_prefetch=1,
            grid=(1 + columns // width,),
            in_specs=[
                full, full, full,
                pl.BlockSpec((rows, width), lambda i, *_: (0, jnp.maximum(i - 1, 0))),
            ],
            out_specs=[out, out],
            scratch_shapes=[pltpu.VMEM((width, width), bf16)],
        ),
        out_shape=[shape, shape],
        compiler_params=params(),
        cost_estimate=cost(6, 20),
    )(order, mixed, adel, hid, udel)


def down_grad_kernel(order, act, ddel, sums, mine, other, whole):
    whole[...] = dot(act[...], ddel[...], TN).astype(bf16)
    store_pieces(order, whole, mine, other, 192)
    low = sums[...].astype(bf16)
    for i in range(8):
        mine[i, 192:] = low
        other[i, 192:] = low


def down_grad(order, act, ddel, sums):
    rows, columns = ddel.shape
    total = act.shape[1]
    chunk = 256
    shape = jax.ShapeDtypeStruct((8, 208, columns), bf16)
    out = pl.BlockSpec((8, 208, chunk), lambda i, *_: (0, 0, i))
    return pl.pallas_call(
        down_grad_kernel,
        grid_spec=pltpu.PrefetchScalarGridSpec(
            num_scalar_prefetch=1,
            grid=(columns // chunk,),
            in_specs=[
                pl.BlockSpec(act.shape, lambda i, *_: (0, 0)),
                pl.BlockSpec((rows, chunk), lambda i, *_: (0, i)),
                pl.BlockSpec((16, chunk), lambda i, *_: (0, i)),
            ],
            out_specs=[out, out],
            scratch_shapes=[pltpu.VMEM((total, chunk), bf16)],
        ),
        out_shape=[shape, shape],
        compiler_params=params(),
        cost_estimate=cost(5, 20),
    )(order, act, ddel, sums)


def tokens_grad_kernel(adel, dq, own, cont, wq, wk, wv, out):
    for half, low in enumerate((own, cont)):
        rows = slice(512 * half, 512 * half + 512)
        total = adel[rows].astype(f32) + dot(dq[rows], wq[...], NT)
        for p in range(wq.shape[1] // 128):
            cols = slice(128 * p, 128 * p + 128)
            both = jnp.concatenate([wk[:, cols], wv[:, cols]], axis=1)
            total = total + dot(low[:, 256 * p : 256 * p + 256], both, NT)
        out[rows] = total.astype(bf16)


def tokens_grad(adel, dq, own, cont, wq, wk, wv):
    args = (adel, dq, own, cont, wq, wk, wv)
    return pl.pallas_call(
        tokens_grad_kernel,
        grid=(1,),
        in_specs=[pl.BlockSpec(a.shape, lambda i: (0, 0)) for a in args],
        out_specs=pl.BlockSpec(adel.shape, lambda i: (0, 0)),
        out_shape=jax.ShapeDtypeStruct(adel.shape, bf16),
        compiler_params=params(),
        cost_estimate=cost(3.6, 12),
    )(*args)


def finish_kernel(gq, gk, gv, qrow, ga, gb, scale, oq, ok, ov, oa, ou, od, loss, *rows):
    shard = lax.axis_index("shard")
    width = gq.shape[1]
    part = gq.shape[0]
    for low, out in ((gq, oq), (gk, ok), (gv, ov)):
        out[...] = low[...].astype(f32)
    oa[...] = ga[:, :width].astype(f32)
    ou[...] = ga[:, width:].astype(f32)
    od[...] = gb[:, :192].astype(f32)
    low = gb[0, 192:]

    def pick(values, size, first):
        row = lax.broadcasted_iota(jnp.int32, (width, size), 0)
        col = lax.broadcasted_iota(jnp.int32, (width, size), 1)
        return dot(values, jnp.where(row == col + first, 1.0, 0.0).astype(bf16), NN)

    own = pick(low, 128, shard * part)
    first = pick(qrow[...], 128, shard * part)
    for out, index in zip(rows[1:-1], (7, 3, 4, 5, 0, 1, 2)):
        out[...] = own[index : index + 1, :part]
    rows[0][...] = first[0:1, :part]
    up_part = rows[-1].shape[1]
    per_row = width // up_part
    lines = pick(low, up_part, shard % per_row * up_part)
    line = lax.broadcasted_iota(jnp.int32, lines.shape, 0)
    lines = jnp.where(line == 8 + shard // per_row, lines, 0.0)
    rows[-1][...] = jnp.sum(lines, axis=0, keepdims=True)
    total = jnp.sum(low[6:7].astype(f32), axis=1, keepdims=True)
    loss[...] = total * scale[...]


def finish(gq, gk, gv, qrow, ga, gb, scale):
    part, width = gq.shape
    up = ga.shape[1] - width

    def out(*shape):
        return jax.ShapeDtypeStruct(shape, f32)

    square = out(part, width)
    return pl.pallas_call(
        finish_kernel,
        out_shape=[
            square, square, square, square, out(part, up), out(2, 192, width), out(1, 1),
        ] + [out(1, part)] * 8 + [out(1, up * part // width)],
        compiler_params=params(60),
        cost_estimate=cost(0.1, 6),
    )(gq, gk, gv, qrow, ga, gb, scale)


def swap(values, axis, bit):
    size = lax.axis_size(axis)
    return lax.ppermute(values, axis, [(i, i ^ bit) for i in range(size)])


def local(
    tokens, cotangent, teacher, valid_mask, valid_count,
    query_weight, query_bias, key_weight, value_weight, value_bias,
    attn_weight, attn_bias, first_gain, first_shift,
    up_weight, up_bias, down_weight, down_bias, second_gain, second_shift,
):
    rows, width = tokens.shape[2:]
    shards = lax.axis_size("shard")
    split = shards == 8
    rep = lax.axis_index("rep")
    shard = lax.axis_index("shard")
    core = rep % 2
    z, y = shard // 2, shard % 2
    tok = tokens.reshape(rows, width)
    keep = valid_mask.reshape(rows)
    if split:
        i = jnp.arange(16, dtype=jnp.int32)
        order = (((z ^ (i % 4)) * 2 + (y ^ (i // 4 % 2))) * 2 + (core ^ (i // 8))).astype(jnp.int32)
    else:
        order = jnp.arange(16, dtype=jnp.int32)

    small = [
        query_bias, value_bias, attn_bias, first_gain, first_shift, down_bias, second_gain,
        second_shift, up_bias,
    ]
    part = query_bias.shape[0]
    vec = jnp.concatenate([v[None] for v in small], axis=1)[0]
    keep_low = keep[:PPIECE].astype(f32).reshape(4, 128)
    if split:
        keep_low = jnp.concatenate([keep_low, keep_low])
        vec = jnp.pad(vec, (0, 2048 - vec.shape[0])).reshape(16, 128)
        up_own = jnp.concatenate([attn_weight, up_weight], axis=1).reshape(2, 48, -1)
        wq, wk, wv, vecs, oth, others_keep, up_full = first_gather(
            query_weight, key_weight, value_weight, vec, tok, keep_low, up_own
        )
        vecs = vecs.reshape(8, 2048)
    else:
        wq, wk, wv, vecs = [
            lax.all_gather(w, "shard", axis=0, tiled=True)
            for w in (query_weight, key_weight, value_weight, vec[None])
        ]
        prompt = tok[:PPIECE]
        oth = jnp.concatenate([swap(prompt, "rep", bit) for bit in (1, 2, 3)])
        others_keep = jnp.stack([swap(keep_low, "rep", bit) for bit in (1, 2, 3)])
    others_keep = others_keep[:, :4].reshape(3 * PPIECE)
    upb = vecs[:, 8 * part : 8 * part + up_bias.shape[0]].reshape(1, -1)
    vecs = vecs[:, : 8 * part].reshape(shards, 8, part).transpose(1, 0, 2).reshape(8, width)

    all_keep = jnp.concatenate(
        [keep[:PPIECE].astype(f32), others_keep, keep[PPIECE:].astype(f32)]
    )
    bias = jnp.where(all_keep > 0.5, 0.0, NEGATIVE)
    brow = jnp.broadcast_to(bias[None], (8, bias.shape[0]))
    lane = jnp.arange(128)[None]
    kb = jnp.where(lane == 0, bias[:, None], jnp.where(lane < 4, 1.0, 0.0)).astype(bf16)

    own_parts = ()
    if split:
        own_parts = (up_own, down_weight.reshape(2, 192, width), up_full)
    outs = attend_near(tok, oth, wq, wk, wv, vecs, kb, brow, own_parts)
    q, k, v, xt, qn, kn, mixed, sides = outs[:8]
    if split:
        up_full, down_full = outs[8:]
    else:
        up_full = jnp.concatenate(
            [
                lax.all_gather(w, "shard", axis=0, tiled=True)
                for w in (attn_weight, up_weight)
            ],
            axis=1,
        ).reshape(16, 48, -1)
        down_full = lax.all_gather(down_weight, "shard", axis=0, tiled=True)
        down_full = down_full.reshape(16, 192, width)
    mixed, sides = attend_far(q, k, v, kb, brow, qn, kn, mixed, sides)

    keep_wide = jnp.broadcast_to(keep.astype(f32)[:, None], (rows, 128))
    scale = (1.0 / valid_count.astype(f32)).reshape(1, 1)
    result, hid, act, ddel, udel, adel, mdel, sums = forward_back(
        mixed, tok, cotangent.reshape(rows, width), teacher.reshape(rows, width),
        keep_wide, scale, vecs, upb, up_full, down_full,
    )
    down_mine, down_other = down_grad(order, act, ddel, sums)
    up_mine, up_other = up_grad(order, mixed, adel, hid, udel)
    if split:
        down_sum = (down_mine.astype(f32) + swap(down_other, "rep", 1).astype(f32)).astype(bf16)
        up_sum = (up_mine.astype(f32) + swap(up_other, "rep", 1).astype(f32)).astype(bf16)
        token_grad, query_low, key_low, value_low, qrow, up_low, down_low = attend_back(
            q, k, v, mdel, mixed, sides, kb, xt, up_sum, down_sum, wq, wk, wv, adel
        )
        outs = finish(query_low, key_low, value_low, qrow, up_low, down_low, scale)
        query_grad, key_grad, value_grad, attn_grad, up_final, down_final, loss = outs[:7]
        (
            query_vec, value_vec, attn_vec, gain1_vec, shift1_vec, down_vec, gain2_vec, shift2_vec,
            up_vec,
        ) = [row.reshape(-1) for row in outs[7:]]
        return (
            result.reshape(tokens.shape),
            loss.reshape(()),
            token_grad.reshape(tokens.shape),
            query_grad,
            query_vec,
            key_grad,
            value_grad,
            value_vec,
            attn_grad,
            attn_vec,
            gain1_vec,
            shift1_vec,
            up_final,
            up_vec,
            down_final.reshape(-1, width),
            down_vec,
            gain2_vec,
            shift2_vec,
        )
    else:
        dq, cont, partial_rows, whole = attend_back_alone(q, k, v, mdel, mixed, sides, kb, xt)

        def scatter(part):
            part = lax.psum_scatter(part, "shard", scatter_dimension=0, tiled=True)
            return lax.psum(part, "rep").astype(f32)

        def joined(mine, other, piece):
            return jnp.concatenate([mine, other])[:, :piece].reshape(16 * piece, -1)

        turned = partial_rows.reshape(2, 2, PPIECE, -1)
        turned = jnp.where(core == 1, turned[:, ::-1], turned)
        turned = jnp.where(rep // 2 == 1, turned[::-1], turned)
        own = lax.psum_scatter(
            turned.reshape(4 * PPIECE, -1), "rep", scatter_dimension=0, tiled=True
        )
        whole = scatter(whole).reshape(part, width // 128, 3, 128)
        query_grad, key_grad, value_grad = [whole[:, :, j].reshape(part, width) for j in range(3)]
        up_all = scatter(joined(up_mine, up_other, 48))
        down_all = scatter(joined(down_mine, down_other, 192))
        sums = lax.psum(sums, ("rep", "shard"))
        query_row = lax.psum(jnp.sum(dq.astype(f32), axis=0), ("rep", "shard"))
        token_grad = tokens_grad(adel, dq, own, cont, wq, wk, wv)

    def owned(row):
        return lax.dynamic_slice(row, (shard * part,), (part,))

    up_part = up_bias.shape[0]
    loss = jnp.sum(sums[6]) / valid_count.astype(f32)
    return (
        result.reshape(tokens.shape),
        loss,
        token_grad.reshape(tokens.shape),
        query_grad,
        owned(query_row),
        key_grad,
        value_grad,
        owned(sums[7]),
        up_all[:, :width],
        owned(sums[3]),
        owned(sums[4]),
        owned(sums[5]),
        up_all[:, width:],
        lax.dynamic_slice(sums[8:12].reshape(-1), (shard * up_part,), (up_part,)),
        down_all,
        owned(sums[0]),
        owned(sums[1]),
        owned(sums[2]),
    )


def solution(mesh):
    wide = P("shard", "rep", None, None)
    matrix, vector = P("shard", None), P("shard")
    return jax.shard_map(
        local,
        mesh=mesh,
        in_specs=(
            wide, wide, wide, P("shard", "rep", None), P(),
            matrix, vector, matrix, matrix, vector, matrix, vector, vector, vector,
            matrix, vector, matrix, vector, vector, vector,
        ),
        out_specs=(
            wide, P(), wide,
            matrix, vector, matrix, matrix, vector, matrix, vector, vector, vector,
            matrix, vector, matrix, vector, vector, vector,
        ),
        check_vma=False,
    )
```
